32 devices in a mesh: dp: 8 (over z, x), head: 4 (over y, core).
Axes of the slice: x: 2, y: 2, z: 4, core: 2. Of those that a mesh axis runs over, the one named last changes fastest.
Arguments:
- tokens: float32 [25088, 384], P(('dp', 'head')), may hold values from -6 to 6
- outputs_grad: bfloat16 [25088, 384], P(('dp', 'head')), may hold values from -6 to 6
- image_kind: int32 [8, 16], P('dp'), may hold values from 0 to 2, as said below
- qkv_weight: bfloat16 [2, 384, 3, 384], P(None, None, None, 'head'), may hold values from -0.3125 to 0.3125
- qv_bias: float32 [2, 2, 384], P(None, None, 'head'), may hold values from -3 to 3
- bias_table: float32 [2, 169, 12], P(None, None, 'head'), may hold values from -4 to 4
- proj_weight: bfloat16 [2, 384, 384], P(None, 'head'), may hold values from -1.25 to 1.25
- fc1_weight: bfloat16 [2, 384, 1536], P(None, None, 'head'), may hold values from -0.3125 to 0.3125
- fc1_bias: float32 [2, 1536], P(None, 'head'), may hold values from -3 to 3
- fc2_weight: bfloat16 [2, 1536, 384], P(None, 'head'), may hold values from -0.15625 to 0.15625
- gains: float32 [2, 2, 384], replicated, may hold values from 0.5 to 1.5
- shifts: float32 [2, 4, 384], replicated, may hold values from -2 to 2
Outputs:
- outputs: float32 [25088, 384], P(('dp', 'head'))
- tokens_grad: float32 [25088, 384], P(('dp', 'head'))
- qkv_weight_grad: float32 [2, 384, 3, 384], P(None, None, None, 'head')
- qv_bias_grad: float32 [2, 2, 384], P(None, None, 'head')
- bias_table_grad: float32 [2, 169, 12], P(None, None, 'head')
- proj_weight_grad: float32 [2, 384, 384], P(None, 'head')
- fc1_weight_grad: float32 [2, 384, 1536], P(None, None, 'head')
- fc1_bias_grad: float32 [2, 1536], P(None, 'head')
- fc2_weight_grad: float32 [2, 1536, 384], P(None, 'head')
- gains_grad: float32 [2, 2, 384], replicated
- shifts_grad: float32 [2, 4, 384], replicated
The draws below stay inside these ranges and needn't reach their ends.
Inputs may be any that keep to these rules, and one draw needn't show every extreme that they name: `image_kind`: row d lists the images of dp index d: 1 a 14 x 14 map in 4 windows, 2 a 21 x 21 map in 9 windows, 0 none. Zeros only follow images, the first entry is an image, a row's windows total at most 64 and fill slots from the first on; the remaining slots are empty. Some row is filled exactly, by images of kind 1.
All inputs are finite; a program needn't handle non-finite values.
Results may differ from the reference program's by a relative error of at most 0.03.
Values may be sent and summed in bfloat16 or wider, within the bound.
No kernel may reach another device: no remote copies, remote signals or barrier semaphores. Data moves between devices by JAX's collectives and lax.ppermute only.
A program may use at most 192 MiB of HBM per device.

```python
import jax
import jax.numpy as jnp
from jax import lax

D = 384
HEADS = 12
FF = 1536
LAYERS = 2
SLOTS = 64
IMG_MAX = 16
TOKENS = 25088
N_DP = 8


def draw_image_kind(key, part):
    key = jax.random.fold_in(key, 11)
    key_kind, key_limit, key_full = jax.random.split(key, 3)
    image_kinds = jax.random.randint(key_kind, (N_DP, IMG_MAX), 1, 3).astype(jnp.int32)
    limit = jax.random.randint(key_limit, (N_DP, 1), max(IMG_MAX // 2, 1), IMG_MAX + 1).astype(jnp.int32)
    full_row = jax.random.randint(key_full, (), 0, N_DP).astype(jnp.int32)
    row_ids = jnp.arange(N_DP, dtype=jnp.int32)[:, None]
    slot_ids = jnp.arange(IMG_MAX, dtype=jnp.int32)[None, :]
    image_kinds = jnp.where(row_ids == full_row, 1, image_kinds)
    image_kinds = jnp.where((row_ids == (full_row + 1) % N_DP) & (slot_ids == 0), 2, image_kinds)
    limit = jnp.where(row_ids == full_row, IMG_MAX, limit)
    counts = jnp.where(image_kinds == 2, 9, 4).astype(jnp.int32)
    end_slots = jnp.cumsum(counts, axis=1).astype(jnp.int32)
    keep = (slot_ids < limit) & (end_slots <= SLOTS)
    return jnp.where(keep, image_kinds, 0).astype(jnp.int32)


def block_scale(rng, extent, cuts, least, top_value):
    level = 1.0
    for dim, shards_of in cuts:
        heights = jax.random.uniform(jax.random.fold_in(jax.random.fold_in(rng, 6), dim), (shards_of,), jnp.float32, least / len(cuts), top_value / len(cuts))
        level = level * jnp.repeat(jnp.exp(heights), extent[dim] // shards_of).reshape((-1,) + (1,) * (len(extent) - 1 - dim))
    return level


def bell_draw(own_key, dims, width, reach, shards=(), kind=jnp.bfloat16):
    entries = jax.random.normal(own_key, dims, jnp.float32) * width
    if len(shards) > 0:
        entries = block_scale(own_key, dims, shards, -0.22, 0.18) * entries
    return jnp.clip(entries, min=-reach, max=reach).astype(kind)


def setup_inputs(seed: int = 0) -> dict:
    key_of = jax.random.split(jax.random.key(seed), 13)
    tokens = bell_draw(key_of[0], (TOKENS, D), 1.0, 6.0, ((0, 32),), jnp.float32)
    outputs_grad = bell_draw(key_of[1], (TOKENS, D), 1.0, 6.0, ((0, 32),))
    image_kind = draw_image_kind(jax.random.fold_in(key_of[12], 71), 0)
    qkv_weight = bell_draw(key_of[3], (LAYERS, D, 3, D), D ** -0.5, 0.3125, ((3, 4),))
    qv_bias = bell_draw(key_of[4], (LAYERS, 2, D), 0.5, 3.0, ((2, 4),), jnp.float32)
    bias_table = bell_draw(key_of[5], (LAYERS, 169, HEADS), 1.0, 4.0, ((2, 4),), jnp.float32)
    proj_weight = bell_draw(key_of[6], (LAYERS, D, D), (max(D // 16, 1)) ** -0.5, 1.25, ((1, 4),))
    fc1_weight = bell_draw(key_of[7], (LAYERS, D, FF), D ** -0.5, 0.3125, ((2, 4),))
    fc1_bias = bell_draw(key_of[8], (LAYERS, FF), 0.5, 3.0, ((1, 4),), jnp.float32)
    fc2_weight = bell_draw(key_of[9], (LAYERS, FF, D), FF ** -0.5, 0.15625, ((1, 4),))
    gains = jnp.clip(1.0 + 0.1 * jax.random.normal(key_of[10], (LAYERS, 2, D), jnp.float32), 0.5, 1.5)
    shifts = bell_draw(key_of[11], (LAYERS, 4, D), 0.3, 2.0, (), jnp.float32)
    return {"tokens": tokens, "outputs_grad": outputs_grad, "image_kind": image_kind, "qkv_weight": qkv_weight, "qv_bias": qv_bias, "bias_table": bias_table, "proj_weight": proj_weight, "fc1_weight": fc1_weight, "fc1_bias": fc1_bias, "fc2_weight": fc2_weight, "gains": gains, "shifts": shifts}


ln_eps = 1e-05
mask_fill = -100.0
highest = lax.Precision.HIGHEST

@jax.custom_vjp
def low(v):
    return lax.optimization_barrier(v.astype(jnp.bfloat16)).astype(jnp.float32)

@jax.custom_vjp
def low_back(v):
    return v

def low_keep(v):
    return (low(v), None)

def low_pass(kept, grad):
    return (grad,)

def back_keep(v):
    return (v, None)

def back_low(kept, grad):
    return (low(grad),)
low.defvjp(low_keep, low_pass)
low_back.defvjp(back_keep, back_low)

def window_plan(image_kinds, slot_count, offset):
    counts = jnp.where(image_kinds == 2, 9, jnp.where(image_kinds == 1, 4, 0)).astype(jnp.int32)
    end_slots = jnp.cumsum(counts).astype(jnp.int32)
    starts = (end_slots - counts).astype(jnp.int32)
    side_count = jnp.where(image_kinds == 2, 3, 2).astype(jnp.int32)
    slot_ids = jnp.arange(slot_count, dtype=jnp.int32)
    inside = (slot_ids[:, None] >= starts[None, :]) & (slot_ids[:, None] < end_slots[None, :])
    live_slots = jnp.any(inside, axis=1)
    first_slot = lax.optimization_barrier(jnp.sum(jnp.where(inside, starts[None, :], 0), axis=1)).astype(jnp.int32)
    image_side = jnp.maximum(lax.optimization_barrier(jnp.sum(jnp.where(inside, side_count[None, :], 0), axis=1)), 1).astype(jnp.int32)
    local_slot = slot_ids - first_slot
    map_span = (image_side * 7)[:, None]
    places = jnp.arange(49, dtype=jnp.int32)
    image_row = (local_slot // image_side)[:, None] * 7 + (places // 7)[None, :]
    image_col = (local_slot % image_side)[:, None] * 7 + (places % 7)[None, :]
    from_row = (image_row + offset + map_span) % map_span
    from_col = (image_col + offset + map_span) % map_span
    source = (first_slot[:, None] + from_row // 7 * image_side[:, None] + from_col // 7) * 49 + from_row % 7 * 7 + from_col % 7
    same_row = slot_ids[:, None] * 49 + places[None, :]
    source = jnp.where(live_slots[:, None], source, same_row).astype(jnp.int32)
    band_row = (image_row >= map_span - 7).astype(jnp.int32) + (image_row >= map_span - 3).astype(jnp.int32)
    band_col = (image_col >= map_span - 7).astype(jnp.int32) + (image_col >= map_span - 3).astype(jnp.int32)
    region = jnp.where(live_slots[:, None], band_row * 3 + band_col, 0).astype(jnp.int32)
    return (source.reshape(-1), region, live_slots)

def relative_index():
    places = jnp.arange(49, dtype=jnp.int32)
    place_row = places // 7
    place_col = places % 7
    return ((place_row[:, None] - place_row[None, :] + 6) * 13 + place_col[:, None] - place_col[None, :] + 6).astype(jnp.int32)

def layer_norm(values, gain_row, shift_row):
    average = lax.optimization_barrier(jnp.mean(values, axis=-1, keepdims=True))
    centred = values - average
    spread = lax.optimization_barrier(jnp.mean(centred * centred, axis=-1, keepdims=True))
    return centred * lax.rsqrt(spread + ln_eps) * gain_row + shift_row

def take_group(matrix, order):
    return jnp.take(matrix, order, axis=0)

def swin_block(hidden, layer_weights, shifted, source, inverse, mask_now):
    qkv_now, qv_now, table_now, proj_now, fc1_now, fc1_bias_now, fc2_now, gain_now, shift_now = layer_weights
    groups = hidden.shape[0]
    head_dim = D // HEADS
    normed = low(layer_norm(hidden, gain_now[0], shift_now[0]))
    if shifted:
        normed = jax.vmap(take_group)(normed, source)
    project = jnp.einsum('grd,dce->grce', normed, qkv_now, precision=highest)
    grid_shape = (groups, SLOTS, 49, HEADS, head_dim)
    queries = low_back(low(project[:, :, 0] + qv_now[0])).reshape(grid_shape)
    keys_low = low_back(low(project[:, :, 1])).reshape(grid_shape)
    values_low = low_back(low(project[:, :, 2] + qv_now[1])).reshape(grid_shape)
    scores = jnp.einsum('gwphe,gwqhe->gwhpq', queries, keys_low, precision=highest) * head_dim ** (-0.5)
    scores = scores + jnp.transpose(table_now[relative_index()], (2, 0, 1))[None, None]
    if shifted:
        scores = scores + mask_now[:, :, None]
    scores = low_back(scores)
    attention_probs = low(jax.nn.softmax(scores, axis=-1))
    attended = jnp.einsum('gwhpq,gwqhe->gwphe', attention_probs, values_low, precision=highest).reshape(groups, SLOTS * 49, D)
    attended = low_back(low(attended))
    if shifted:
        attended = jax.vmap(take_group)(attended, inverse)
    middle = hidden + low_back(jnp.einsum('grd,de->gre', attended, proj_now, precision=highest) + shift_now[2])
    normed_mlp = low(layer_norm(middle, gain_now[1], shift_now[1]))
    preact = low_back(jnp.einsum('grd,df->grf', normed_mlp, fc1_now, precision=highest) + fc1_bias_now)
    active = low(jax.nn.gelu(preact, approximate=False))
    return middle + low_back(jnp.einsum('grf,fd->grd', active, fc2_now, precision=highest) + shift_now[3])

def shifted_plan(row_kinds):
    return window_plan(row_kinds, SLOTS, 3)

def back_plan(row_kinds):
    return window_plan(row_kinds, SLOTS, -3)[0]

def reference(tokens, outputs_grad, image_kind, qkv_weight, qv_bias, bias_table, proj_weight, fc1_weight, fc1_bias, fc2_weight, gains, shifts):
    source, region, live_slots = jax.vmap(shifted_plan)(image_kind)
    inverse = jax.vmap(back_plan)(image_kind)
    mask_now = jnp.where(region[:, :, :, None] != region[:, :, None, :], mask_fill, 0.0).astype(jnp.float32)
    row_live = jnp.repeat(live_slots.astype(jnp.float32), 49, axis=1)[:, :, None]

    def forward(inputs, qkv_all, qv_all, table_all, proj_all, fc1_all, fc1_bias_all, fc2_all, gain_all, shift_all):
        hidden = inputs.reshape(N_DP, SLOTS * 49, D)
        for layer_index in range(LAYERS):
            layer_weights = (qkv_all[layer_index], qv_all[layer_index], table_all[layer_index], proj_all[layer_index], fc1_all[layer_index], fc1_bias_all[layer_index], fc2_all[layer_index], gain_all[layer_index], shift_all[layer_index])
            hidden = swin_block(hidden, layer_weights, layer_index % 2 == 1, source, inverse, mask_now)
        return (hidden * row_live).reshape(TOKENS, D)
    primals = (tokens.astype(jnp.float32), qkv_weight.astype(jnp.float32), qv_bias.astype(jnp.float32), bias_table.astype(jnp.float32), proj_weight.astype(jnp.float32), fc1_weight.astype(jnp.float32), fc1_bias.astype(jnp.float32), fc2_weight.astype(jnp.float32), gains.astype(jnp.float32), shifts.astype(jnp.float32))
    result, pull_back = jax.vjp(forward, *primals)
    grads = pull_back(outputs_grad.astype(jnp.float32))
    return (result, grads[0], grads[1], grads[2], grads[3], grads[4], grads[5], grads[6], grads[7], grads[8], grads[9])
```

```python
import jax
import jax.numpy as jnp
import numpy as np
from jax import lax
from jax.experimental import pallas as pl
from jax.experimental.pallas import tpu as pltpu
from jax.sharding import PartitionSpec as P

D = 384
FF = 1536
LAYERS = 2
PLACES = 49
PAD = 56
WIDE = 64
QUADS = 3
HEAD_DIM = 32
SCORE_SCALE = HEAD_DIM**-0.5
LN_EPS = 1e-05
LOW = jnp.bfloat16
F32 = jnp.float32
VMEM_BYTES = 56 * 1024 * 1024

SRC, SIDE, WROW, WCOL, FIRST, RET, SEND = 0, 24, 48, 72, 96, 120, 140
TABLE = 144


def vmem():
    return pl.BlockSpec(memory_space=pltpu.VMEM)


def smem():
    return pl.BlockSpec(memory_space=pltpu.SMEM)


def params(limit=VMEM_BYTES):
    return pltpu.CompilerParams(vmem_limit_bytes=limit)


def cost(flops, size):
    return pl.CostEstimate(flops=int(flops), bytes_accessed=int(size), transcendentals=0)


def dot_nn(a, b):
    return lax.dot_general(a, b, (((1,), (0,)), ((), ())), preferred_element_type=F32)


def dot_nt(a, b):
    return lax.dot_general(a, b, (((1,), (1,)), ((), ())), preferred_element_type=F32)


def dot_tn(a, b):
    return lax.dot_general(a, b, (((0,), (0,)), ((), ())), preferred_element_type=F32)


def plan_kernel(own, bins, kind_ref, me_ref, out_ref, load_ref):
    me = me_ref[0]
    half = 2 * own
    for i in range(TABLE):
        out_ref[i] = -1 if i < bins or RET <= i < RET + own else 0
    for i in range(bins):
        out_ref[SIDE + i] = 1
        out_ref[FIRST + i] = i
    for i in range(4):
        load_ref[i] = 0

    def place(start, count, side, bin_id):
        base = load_ref[bin_id]
        load_ref[bin_id] = base + count

        def step(k, carry):
            slot = start + k
            owner = slot // own
            inner = slot - owner * own
            local = base + k
            mine = bin_id == me
            halo = jnp.where(me == 1, slot - half, slot - half + 4)
            code = jnp.where(
                owner == me, inner, jnp.where(owner == (me ^ 1), own + inner, 2 * own + halo)
            )

            @pl.when(mine)
            def _():
                wrow = k // side
                out_ref[SRC + local] = code
                out_ref[SIDE + local] = side
                out_ref[WROW + local] = wrow
                out_ref[WCOL + local] = k - wrow * side
                out_ref[FIRST + local] = base

            @pl.when(owner == me)
            def _():
                back = jnp.where(me == 2, slot - half, k)
                out_ref[RET + inner] = jnp.where(
                    mine, local, jnp.where(bin_id == (me ^ 1), bins + local, 2 * bins + back)
                )

            return carry

        lax.fori_loop(0, count, step, 0)

    for turn in range(3):

        def visit(i, start, turn=turn):
            kind = kind_ref[0, i]
            count = jnp.where(kind == 2, 9, jnp.where(kind == 1, 4, 0))
            side = jnp.where(kind == 2, 3, 2)
            cut = half - start
            across = (cut > 0) & (cut < count)
            second = (start >= half) | (across & (cut < count - cut))
            chip = jnp.where(second, 1, 0)
            left, right = load_ref[2 * chip], load_ref[2 * chip + 1]
            emptier = 2 * chip + jnp.where(left <= right, 0, 1)
            if turn == 0:
                chosen, bin_id = across, 1 + chip
            else:
                chosen, bin_id = (kind == 3 - turn) & jnp.logical_not(across), emptier

            @pl.when(chosen)
            def _():
                place(start, count, side, bin_id)
                if turn == 0:
                    out_ref[SEND] = jnp.where((me == 1) & (chip == 0), cut, 0)

            return start + count

        lax.fori_loop(0, kind_ref.shape[1], visit, jnp.int32(0))


def make_plan(image_kind, me, own, bins):
    def kernel(kind_ref, me_ref, out_ref, load_ref):
        plan_kernel(own, bins, kind_ref, me_ref, out_ref, load_ref)

    return pl.pallas_call(
        kernel,
        out_shape=jax.ShapeDtypeStruct((TABLE,), jnp.int32),
        in_specs=[smem(), smem()],
        out_specs=smem(),
        scratch_shapes=[pltpu.SMEM((4,), jnp.int32)],
        name="plan",
    )(image_kind, me.reshape(1))


def gather_slots(table, mine, partner, halo, bins):
    own = mine.shape[0] // PLACES

    def kernel(table_ref, mine_ref, partner_ref, halo_ref, out_ref, spread_ref):
        spread_ref[...] = jnp.zeros(spread_ref.shape, F32)
        at = 0
        for ref in (mine_ref, partner_ref, halo_ref):
            for s in range(ref.shape[0] // PLACES):
                spread_ref[at, 0:PLACES] = ref[s * PLACES : (s + 1) * PLACES].astype(F32)
                at += 1

        def step(j, carry):
            src = table_ref[SRC + j]

            @pl.when(src < 0)
            def _():
                out_ref[j] = jnp.zeros((PAD, D), F32)

            @pl.when(src >= 0)
            def _():
                out_ref[j] = spread_ref[src]

            return carry

        lax.fori_loop(0, bins, step, 0)

    out = pl.pallas_call(
        kernel,
        out_shape=jax.ShapeDtypeStruct((bins, PAD, D), F32),
        in_specs=[smem(), vmem(), vmem(), vmem()],
        out_specs=vmem(),
        scratch_shapes=[pltpu.VMEM((2 * own + 4, PAD, D), F32)],
        compiler_params=params(),
        cost_estimate=cost(0, 5e6),
        name="gather_slots",
    )(table, mine, partner, halo)
    return out.reshape(bins * PAD, D)


def return_slots(table, mine, partner, halo, own):
    bins = mine.shape[0]

    def kernel(table_ref, mine_ref, partner_ref, halo_ref, out_ref):
        for s in range(own):
            src = table_ref[RET + s]
            rows = pl.ds(s * PLACES, PLACES)

            @pl.when(src < 0)
            def _():
                out_ref[rows] = jnp.zeros((PLACES, D), F32)

            @pl.when((src >= 0) & (src < bins))
            def _():
                out_ref[rows] = mine_ref[src, 0:PLACES]

            @pl.when((src >= bins) & (src < 2 * bins))
            def _():
                out_ref[rows] = partner_ref[src - bins, 0:PLACES]

            @pl.when(src >= 2 * bins)
            def _():
                out_ref[rows] = halo_ref[src - 2 * bins, 0:PLACES]

    return pl.pallas_call(
        kernel,
        out_shape=jax.ShapeDtypeStruct((own * PLACES, D), F32),
        in_specs=[smem(), vmem(), vmem(), vmem()],
        out_specs=vmem(),
        compiler_params=params(),
        cost_estimate=cost(0, 5e6),
        name="return_slots",
    )(table, mine, partner, halo)


def norm_rows(rows):
    average = jnp.mean(rows, axis=-1, keepdims=True)
    centred = rows - average
    inverse = lax.rsqrt(jnp.mean(centred * centred, axis=-1, keepdims=True) + LN_EPS)
    return centred * inverse, inverse


def norm_back(incoming, scaled, inverse, gain):
    weighted = incoming * gain
    return inverse * (
        weighted
        - jnp.mean(weighted, axis=-1, keepdims=True)
        - scaled * jnp.mean(weighted * scaled, axis=-1, keepdims=True)
    )


def gelu_parts(x):
    size = jnp.abs(x) * 0.7071067811865476
    t = 1.0 / (1.0 + 0.3275911 * size)
    bell = jnp.exp(-0.5 * x * x)
    poly = t * (
        0.127414796 + t * (-0.142248368 + t * (0.7107068705 + t * (-0.7265760135 + t * 0.5307027145)))
    )
    tail = poly * bell
    phi = jnp.where(x >= 0, 1.0 - tail, tail)
    return x * phi, phi + x * bell * 0.3989422804014327


def place_parts(shape, dim):
    place = lax.broadcasted_iota(jnp.int32, shape, dim)
    row = (place * 37) >> 8
    return place, row, place - 7 * row


def fill_moves(table_ref, out_ref, bins, back):
    width = out_ref.shape[1]
    place, row, col = place_parts((PAD, 1), 0)
    if back:
        row_other, col_other = row < 3, col < 3
        inner = 7 * jnp.where(row_other, row + 4, row - 3) + jnp.where(col_other, col + 4, col - 3)
    else:
        row_other, col_other = row >= 4, col >= 4
        inner = 7 * jnp.where(row_other, row - 4, row + 3) + jnp.where(col_other, col - 4, col + 3)
    lanes = lax.broadcasted_iota(jnp.int32, (2 * PAD, width), 1)

    def source(w):
        side, wrow, wcol = table_ref[SIDE + w], table_ref[WROW + w], table_ref[WCOL + w]
        first = table_ref[FIRST + w]
        if back:
            orow = jnp.where(wrow == 0, side - 1, wrow - 1)
            ocol = jnp.where(wcol == 0, side - 1, wcol - 1)
        else:
            orow = jnp.where(wrow == side - 1, 0, wrow + 1)
            ocol = jnp.where(wcol == side - 1, 0, wcol + 1)
        slot = first + jnp.where(row_other, orow, wrow) * side + jnp.where(col_other, ocol, wcol)
        return jnp.where(place < PLACES, slot * PAD + inner, w * PAD + place)

    def step(j, carry):
        rows = jnp.concatenate([source(2 * j), source(2 * j + 1)], axis=0)
        hot = jnp.where(lanes == rows, 1.0, 0.0).astype(LOW)
        out_ref[pl.ds(pl.multiple_of(j * 2 * PAD, 16), 2 * PAD)] = hot
        return carry

    lax.fori_loop(0, bins // 2, step, 0)


def head_marks():
    lane = lax.broadcasted_iota(jnp.int32, (WIDE, 128), 1) // HEAD_DIM
    return [jnp.where(lane == h, 1.0, 0.0).astype(LOW) for h in range(4)]


def spread(block, marks):
    return jnp.concatenate([block * mark for mark in marks], axis=0)


def fold(product, marks):
    total = None
    for h, mark in enumerate(marks):
        part = product[h * WIDE : (h + 1) * WIDE] * mark.astype(F32)
        total = part if total is None else total + part
    return total


def by_segment(values, reduce, neutral):
    lane = lax.broadcasted_iota(jnp.int32, (values.shape[0], 128), 1) < WIDE
    parts = []
    for half in range(2):
        part = values[:, half * 128 : (half + 1) * 128]
        left = reduce(jnp.where(lane, part, neutral), axis=-1, keepdims=True)
        right = reduce(jnp.where(lane, neutral, part), axis=-1, keepdims=True)
        parts.append(jnp.where(lane, left, right))
    return jnp.concatenate(parts, axis=1)


def pad_rows(rows):
    return jnp.concatenate([rows, jnp.zeros((WIDE - PAD, rows.shape[1]), rows.dtype)], axis=0)


def stack_qkv(pieces, out_ref):
    for k, piece in enumerate(pieces):
        for c in range(3):
            out_ref[c * D + k * 96 : c * D + (k + 1) * 96] = piece[c * 96 : (c + 1) * 96]


def stack_proj(pieces, out_ref):
    for k, piece in enumerate(pieces):
        out_ref[k * 96 : (k + 1) * 96] = piece[288:384]


def stack_mlp(pieces, fc1_ref, fc2_ref):
    for k, piece in enumerate(pieces):
        fc1_ref[:, k * D : (k + 1) * D] = piece[0:D]
        fc2_ref[k * D : (k + 1) * D] = piece[D : 2 * D]


def attn_forward(table, hidden, weights, qv_bias, bias, norms, shifted):
    rows = hidden.shape[0]
    bins = rows // PAD
    chunk_slots = 6
    chunk = chunk_slots * PAD
    wide_rows = -(-rows // 128) * 128

    def kernel(
        table_ref, hidden_ref, w0, w1, w2, w3, qv_ref, bias_ref, norm_ref,
        mid_ref, a_ref, qkv_ref, p_ref, attn_ref,
        wqkv, wproj, wide_attn, moves,
    ):
        pieces = (w0, w1, w2, w3)
        stack_qkv(pieces, wqkv)
        stack_proj(pieces, wproj)
        gain, shift, proj_shift = norm_ref[0:1], norm_ref[1:2], norm_ref[2:3]
        marks = head_marks()
        dest = attn_ref if shifted else a_ref

        def norm_step(i, carry):
            at = pl.ds(pl.multiple_of(i * chunk, 16), chunk)
            scaled, _ = norm_rows(hidden_ref[at])
            dest[at] = (scaled * gain + shift).astype(LOW)
            return carry

        lax.fori_loop(0, bins // chunk_slots, norm_step, 0)
        if shifted:
            fill_moves(table_ref, moves, bins, False)
            a_ref[...] = dot_nn(moves[:, 0:rows], dest[...]).astype(LOW)
            fill_moves(table_ref, moves, bins, True)

        def qkv_step(i, carry):
            at = pl.ds(pl.multiple_of(i * chunk, 16), chunk)
            project = dot_nt(a_ref[at], wqkv[...]) + qv_ref[...]
            for j in range(chunk_slots):
                block = project[j * PAD : (j + 1) * PAD]
                qkv_ref[i * chunk_slots + j] = pad_rows(block).astype(LOW)
            return carry

        lax.fori_loop(0, bins // chunk_slots, qkv_step, 0)

        if shifted:
            _, prow, pcol = place_parts((PAD, 1), 0)
            lane = lax.broadcasted_iota(jnp.int32, (1, 4 * WIDE), 1)
            qplace = lane - (lane >> 6) * WIDE
            qrow = (qplace * 37) >> 8
            qcol = qplace - 7 * qrow
            pband = 1 + (prow >= 4).astype(jnp.int32), 1 + (pcol >= 4).astype(jnp.int32)
            qband = 1 + (qrow >= 4).astype(jnp.int32), 1 + (qcol >= 4).astype(jnp.int32)

        def window(w, carry):
            if shifted:
                side = table_ref[SIDE + w]
                low_row = jnp.where(table_ref[WROW + w] == side - 1, 3, 0)
                low_col = jnp.where(table_ref[WCOL + w] == side - 1, 1, 0)
                pregion = low_row * pband[0] + low_col * pband[1]
                qregion = low_row * qband[0] + low_col * qband[1]
                mask = jnp.where(pregion != qregion, -100.0, 0.0)
            for t in range(QUADS):
                cols = slice(t * 128, (t + 1) * 128)
                q = qkv_ref[w, :, t * 128 : (t + 1) * 128]
                k = qkv_ref[w, :, D + t * 128 : D + (t + 1) * 128]
                v = qkv_ref[w, :, 2 * D + t * 128 : 2 * D + (t + 1) * 128]
                scores = dot_nt(q, spread(k, marks))[0:PAD] * SCORE_SCALE + bias_ref[t]
                if shifted:
                    scores = scores + mask
                exponent = jnp.exp(scores - by_segment(scores, jnp.max, -3e38))
                total = by_segment(exponent, jnp.sum, 0.0)
                probs = pad_rows(exponent / total).astype(LOW)
                p_ref[w, t] = probs
                at = pl.ds(pl.multiple_of(w * PAD, 8), PAD)
                wide_attn[at, cols] = dot_nn(probs, spread(v, marks))[0:PAD]
            return carry

        lax.fori_loop(0, bins, window, 0)
        if shifted:
            attn_ref[...] = dot_nn(moves[:, 0:rows], wide_attn[...].astype(LOW)).astype(LOW)
        else:
            attn_ref[...] = wide_attn[...].astype(LOW)

        def proj_step(i, carry):
            at = pl.ds(pl.multiple_of(i * chunk, 16), chunk)
            mid_ref[at] = hidden_ref[at] + dot_nn(attn_ref[at], wproj[...]) + proj_shift
            return carry

        lax.fori_loop(0, bins // chunk_slots, proj_step, 0)

    return pl.pallas_call(
        kernel,
        out_shape=(
            jax.ShapeDtypeStruct((rows, D), F32),
            jax.ShapeDtypeStruct((rows, D), LOW),
            jax.ShapeDtypeStruct((bins, WIDE, 3 * D), LOW),
            jax.ShapeDtypeStruct((bins, QUADS, WIDE, 4 * WIDE), LOW),
            jax.ShapeDtypeStruct((rows, D), LOW),
        ),
        in_specs=[smem()] + [vmem()] * 8,
        out_specs=[vmem()] * 5,
        scratch_shapes=[
            pltpu.VMEM((3 * D, D), LOW),
            pltpu.VMEM((D, D), LOW),
            pltpu.VMEM((rows, D), F32),
            pltpu.VMEM((rows if shifted else 16, wide_rows), LOW),
        ],
        compiler_params=params(),
        cost_estimate=cost(8e9, 1.2e7),
        name="attn_forward",
    )(table, hidden, *weights, qv_bias, bias, norms)


def attn_backward(table, grad, hidden, a, qkv, probs, attn, weights, norms, shifted):
    rows = hidden.shape[0]
    bins = rows // PAD
    chunk_slots = 6
    chunk = chunk_slots * PAD
    wide_rows = -(-rows // 128) * 128

    def kernel(
        table_ref, grad_ref, hidden_ref, a_ref, qkv_ref, p_ref, attn_ref, w0, w1, w2, w3, norm_ref,
        out_ref, keep_ref, send_ref, small_ref, bias_ref,
        wqkv, wproj, low_grad, wide_attn, low_wide, gqkv, moves,
    ):
        pieces = (w0, w1, w2, w3)
        stack_qkv(pieces, wqkv)
        stack_proj(pieces, wproj)
        gain = norm_ref[0:1]
        marks = head_marks()
        steps = bins // chunk_slots
        if shifted:
            fill_moves(table_ref, moves, bins, False)

        def proj_step(i, total):
            at = pl.ds(pl.multiple_of(i * chunk, 16), chunk)
            gz = grad_ref[at].astype(LOW)
            low_grad[at] = gz
            gattn = dot_nt(gz, wproj[...])
            if shifted:
                low_wide[at] = gattn.astype(LOW)
            else:
                for j in range(chunk_slots):
                    block = gattn[j * PAD : (j + 1) * PAD]
                    wide_attn[i * chunk_slots + j] = pad_rows(block).astype(LOW)
            return total + jnp.sum(gz.astype(F32), axis=0, keepdims=True)

        proj_shift = lax.fori_loop(0, steps, proj_step, jnp.zeros((1, D), F32))
        if shifted:

            def move_step(i, carry):
                at = pl.ds(pl.multiple_of(i * chunk, 16), chunk)
                moved = dot_nn(moves[at, 0:rows], low_wide[...])
                for j in range(chunk_slots):
                    block = moved[j * PAD : (j + 1) * PAD]
                    wide_attn[i * chunk_slots + j] = pad_rows(block).astype(LOW)
                return carry

            lax.fori_loop(0, steps, move_step, 0)
            fill_moves(table_ref, moves, bins, True)
        dproj = dot_tn(attn_ref[...], low_grad[...]).astype(LOW)
        for k in range(4):
            dest = keep_ref if k < 2 else send_ref
            dest[k % 2, 288:384] = dproj[k * 96 : (k + 1) * 96]

        bias_ref[...] = jnp.zeros((QUADS, PAD, 4 * WIDE), F32)

        def window(w, carry):
            for t in range(QUADS):
                q = qkv_ref[w, :, t * 128 : (t + 1) * 128]
                k = qkv_ref[w, :, D + t * 128 : D + (t + 1) * 128]
                v = qkv_ref[w, :, 2 * D + t * 128 : 2 * D + (t + 1) * 128]
                low_probs = p_ref[w, t]
                p = low_probs.astype(F32)
                go = wide_attn[w, :, t * 128 : (t + 1) * 128]
                gp = dot_nt(go, spread(v, marks))
                ds = p * (gp - by_segment(gp * p, jnp.sum, 0.0))
                low_ds = ds.astype(LOW)
                bias_ref[t] += low_ds.astype(F32)[0:PAD]
                gq = dot_nn(low_ds, spread(k, marks)) * SCORE_SCALE
                gk = fold(dot_tn(low_ds, q), marks) * SCORE_SCALE
                gv = fold(dot_tn(low_probs, go), marks)
                at = pl.ds(pl.multiple_of(w * PAD, 8), PAD)
                gqkv[at, t * 128 : (t + 1) * 128] = gq[0:PAD]
                gqkv[at, D + t * 128 : D + (t + 1) * 128] = gk[0:PAD]
                gqkv[at, 2 * D + t * 128 : 2 * D + (t + 1) * 128] = gv[0:PAD]
            return carry

        lax.fori_loop(0, bins, window, 0)

        low_qkv = gqkv[...].astype(LOW)
        sums = jnp.sum(low_qkv.astype(F32), axis=0, keepdims=True)
        dqkv = dot_tn(a_ref[...], low_qkv)
        for c in range(3):
            turned = dqkv[:, c * D : (c + 1) * D].T.astype(LOW)
            for k in range(4):
                dest = keep_ref if k < 2 else send_ref
                dest[k % 2, c * 96 : (c + 1) * 96] = turned[k * 96 : (k + 1) * 96]
        if shifted:
            low_wide[...] = dot_nn(low_qkv, wqkv[...]).astype(LOW)

        def back_step(i, totals):
            at = pl.ds(pl.multiple_of(i * chunk, 16), chunk)
            if shifted:
                ga = dot_nn(moves[at, 0:rows], low_wide[...])
            else:
                ga = dot_nn(gqkv[at].astype(LOW), wqkv[...])
            scaled, inverse = norm_rows(hidden_ref[at])
            out_ref[at] = grad_ref[at] + norm_back(ga, scaled, inverse, gain)
            return (
                totals[0] + jnp.sum(ga * scaled, axis=0, keepdims=True),
                totals[1] + jnp.sum(ga, axis=0, keepdims=True),
            )

        zero = jnp.zeros((1, D), F32)
        dgain, dshift = lax.fori_loop(0, steps, back_step, (zero, zero))
        small_ref[0:1] = dgain
        small_ref[1:2] = dshift
        small_ref[2:3] = proj_shift
        small_ref[3:4] = sums[:, 0:D]
        small_ref[4:5] = sums[:, 2 * D : 3 * D]
        small_ref[5:8] = jnp.zeros((3, D), F32)

    return pl.pallas_call(
        kernel,
        out_shape=(
            jax.ShapeDtypeStruct((rows, D), F32),
            jax.ShapeDtypeStruct((2, D, D), LOW),
            jax.ShapeDtypeStruct((2, D, D), LOW),
            jax.ShapeDtypeStruct((8, D), F32),
            jax.ShapeDtypeStruct((QUADS, PAD, 4 * WIDE), F32),
        ),
        in_specs=[smem()] + [vmem()] * 11,
        out_specs=[vmem()] * 5,
        scratch_shapes=[
            pltpu.VMEM((3 * D, D), LOW),
            pltpu.VMEM((D, D), LOW),
            pltpu.VMEM((rows, D), LOW),
            pltpu.VMEM((bins, WIDE, D), LOW),
            pltpu.VMEM((rows, D), LOW),
            pltpu.VMEM((rows, 3 * D), F32),
            pltpu.VMEM((rows if shifted else 16, wide_rows), LOW),
        ],
        compiler_params=params(),
        cost_estimate=cost(1.6e10, 1.2e7),
        name="attn_backward",
    )(table, grad, hidden, a, qkv, probs, attn, *weights, norms)


def mlp_forward(mid, weights, fc1_bias, norms):
    rows = mid.shape[0]
    chunk = 3 * PAD * 2
    steps = rows // chunk

    def kernel(
        mid_ref, w0, w1, w2, w3, fc1_bias_ref, norm_ref,
        out_ref, a_ref, act_ref, slope_ref, fc1, fc2,
    ):
        stack_mlp((w0, w1, w2, w3), fc1, fc2)
        gain, shift, out_shift = norm_ref[0:1], norm_ref[1:2], norm_ref[2:3]

        def step(i, carry):
            at = pl.ds(pl.multiple_of(i * chunk, 16), chunk)
            rows_now = mid_ref[at]
            scaled, _ = norm_rows(rows_now)
            a = (scaled * gain + shift).astype(LOW)
            a_ref[at] = a
            act, slope = gelu_parts(dot_nn(a, fc1[...]) + fc1_bias_ref[...])
            act = act.astype(LOW)
            act_ref[at] = act
            slope_ref[at] = slope.astype(LOW)
            out_ref[at] = rows_now + dot_nn(act, fc2[...]) + out_shift
            return carry

        lax.fori_loop(0, steps, step, 0)

    return pl.pallas_call(
        kernel,
        out_shape=(
            jax.ShapeDtypeStruct((rows, D), F32),
            jax.ShapeDtypeStruct((rows, D), LOW),
            jax.ShapeDtypeStruct((rows, FF), LOW),
            jax.ShapeDtypeStruct((rows, FF), LOW),
        ),
        in_specs=[vmem()] * 7,
        out_specs=[vmem()] * 4,
        scratch_shapes=[pltpu.VMEM((D, FF), LOW), pltpu.VMEM((FF, D), LOW)],
        compiler_params=params(),
        cost_estimate=cost(8e9, 1.2e7),
        name="mlp_forward",
    )(mid, *weights, fc1_bias, norms)


def mlp_backward(grad, mid, a, act, slope, weights, norms):
    rows = mid.shape[0]
    chunk = 3 * PAD * 2
    steps = rows // chunk

    def kernel(
        grad_ref, mid_ref, a_ref, act_ref, slope_ref, w0, w1, w2, w3, norm_ref,
        out_ref, keep_ref, send_ref, small_ref, bias_ref, fc1, fc2, low_grad, gpre_ref,
    ):
        stack_mlp((w0, w1, w2, w3), fc1, fc2)
        gain = norm_ref[0:1]

        def step(i, totals):
            at = pl.ds(pl.multiple_of(i * chunk, 16), chunk)
            grad_now = grad_ref[at]
            gz = grad_now.astype(LOW)
            low_grad[at] = gz
            gpre = (dot_nt(gz, fc2[...]) * slope_ref[at].astype(F32)).astype(LOW)
            gpre_ref[at] = gpre
            ga = dot_nt(gpre, fc1[...])
            scaled, inverse = norm_rows(mid_ref[at])
            out_ref[at] = grad_now + norm_back(ga, scaled, inverse, gain)
            return (
                totals[0] + jnp.sum(ga * scaled, axis=0, keepdims=True),
                totals[1] + jnp.sum(ga, axis=0, keepdims=True),
                totals[2] + jnp.sum(gz.astype(F32), axis=0, keepdims=True),
                totals[3] + jnp.sum(gpre.astype(F32), axis=0, keepdims=True),
            )

        zero = jnp.zeros((1, D), F32)
        sums = lax.fori_loop(0, steps, step, (zero, zero, zero, jnp.zeros((1, FF), F32)))
        for i in range(3):
            small_ref[i : i + 1] = sums[i]
        small_ref[3:8] = jnp.zeros((5, D), F32)
        bias_ref[...] = sums[3]
        for k in range(4):
            dest = keep_ref if k < 2 else send_ref
            cols = slice(k * D, (k + 1) * D)
            dest[k % 2, 0:D] = dot_tn(a_ref[...], gpre_ref[:, cols]).astype(LOW)
            dest[k % 2, D : 2 * D] = dot_tn(low_grad[...], act_ref[:, cols]).astype(LOW)

    return pl.pallas_call(
        kernel,
        out_shape=(
            jax.ShapeDtypeStruct((rows, D), F32),
            jax.ShapeDtypeStruct((2, 2 * D, D), LOW),
            jax.ShapeDtypeStruct((2, 2 * D, D), LOW),
            jax.ShapeDtypeStruct((8, D), F32),
            jax.ShapeDtypeStruct((1, FF), F32),
        ),
        in_specs=[vmem()] * 10,
        out_specs=[vmem()] * 5,
        scratch_shapes=[
            pltpu.VMEM((D, FF), LOW),
            pltpu.VMEM((FF, D), LOW),
            pltpu.VMEM((rows, D), LOW),
            pltpu.VMEM((rows, FF), LOW),
        ],
        compiler_params=params(),
        cost_estimate=cost(1.6e10, 1.5e7),
        name="mlp_backward",
    )(grad, mid, a, act, slope, *weights, norms)


def swap_core(value):
    return lax.ppermute(value, "head", [(i, i ^ 1) for i in range(4)])


def swap_chip(value):
    return lax.ppermute(value, "head", [(i, i ^ 2) for i in range(4)])


def swap_border(value):
    return lax.ppermute(value, "head", [(1, 2), (2, 1)])


def swap_dp(value, step, size):
    return lax.ppermute(value, "dp", [(i, i ^ step) for i in range(size)])


def sum_head(keep, send):
    halves = keep.astype(F32) + swap_core(send).astype(F32)
    other = swap_chip(halves[1].astype(send.dtype))
    return halves[0] + other.astype(F32)


def sum_dp(value, low):
    size = lax.axis_size("dp")
    me = lax.axis_index("dp")
    bits = [1 << b for b in range(size.bit_length() - 1)]
    for bit in bits:
        mine = (me // bit) % 2
        half = value.shape[0] // 2
        sent = lax.dynamic_slice_in_dim(value, (1 - mine) * half, half, 0).astype(low)
        kept = lax.dynamic_slice_in_dim(value, mine * half, half, 0)
        value = kept + swap_dp(sent, bit, size).astype(F32)
    value = value.astype(low)
    for bit in reversed(bits):
        mine = (me // bit) % 2
        other = swap_dp(value, bit, size)
        value = jnp.where(
            mine == 0, jnp.concatenate([value, other]), jnp.concatenate([other, value])
        )
    return value.astype(F32)


def sum_dp_small(value):
    size = lax.axis_size("dp")
    for b in range(size.bit_length() - 1):
        value = value + swap_dp(value, 1 << b, size)
    return value


def relative_hot():
    place = np.arange(PLACES)
    row, col = place // 7, place % 7
    index = (row[:, None] - row[None, :] + 6) * 13 + col[:, None] - col[None, :] + 6
    return jnp.asarray((index.reshape(-1)[:, None] == np.arange(169)[None, :]).astype(np.float32))


def body(
    tokens, outputs_grad, image_kind, qkv_weight, qv_bias, bias_table, proj_weight,
    fc1_weight, fc1_bias, fc2_weight, gains, shifts,
):
    highest = lax.Precision.HIGHEST
    own = tokens.shape[0] // PLACES
    bins = own + 2
    me = lax.axis_index("head").astype(jnp.int32)
    table = make_plan(image_kind, me, own, bins)

    turned = jnp.transpose(qkv_weight, (0, 2, 3, 1)).reshape(LAYERS, 288, D)
    packs = []
    for l in range(LAYERS):
        packs.append(jnp.concatenate([turned[l], proj_weight[l]], axis=0))
        packs.append(jnp.concatenate([fc1_weight[l], fc2_weight[l]], axis=0))
    small = jnp.concatenate(
        [qv_bias.reshape(1, -1), fc1_bias, jnp.pad(bias_table.reshape(-1), (0, 138)).reshape(3, D)]
    )
    small_pair = jnp.stack([small, swap_chip(small)])
    smalls = jnp.concatenate([small_pair, swap_core(small_pair)])
    gathered = []
    for pack in packs:
        chip = swap_chip(pack)
        gathered.append((pack, chip, swap_core(pack), swap_core(chip)))

    qv_all = smalls[:, 0].reshape(4, LAYERS, 2, 96).transpose(1, 2, 0, 3).reshape(LAYERS, 2, D)
    qkv_bias = jnp.stack([qv_all[:, 0], jnp.zeros_like(qv_all[:, 0]), qv_all[:, 1]], axis=1)
    qkv_bias = qkv_bias.reshape(LAYERS, 1, 3 * D)
    fc1_all = smalls[:, 1:3].transpose(1, 0, 2).reshape(LAYERS, 1, FF)
    tables = smalls[:, 3:6].reshape(4, -1)[:, : LAYERS * 169 * 3].reshape(4, LAYERS, 169, 3)
    hot = relative_hot()
    looked = jnp.einsum("nt,kltj->lkjn", hot, tables, precision=highest)
    looked = looked.reshape(LAYERS, QUADS, 4, PLACES, PLACES)
    looked = jnp.pad(looked, ((0, 0),) * 4 + ((0, WIDE - PLACES),), constant_values=-1e30)
    looked = jnp.pad(looked, ((0, 0),) * 3 + ((0, PAD - PLACES), (0, 0)))
    bias = looked.transpose(0, 1, 3, 2, 4).reshape(LAYERS, QUADS, PAD, 4 * WIDE)

    def border(value):
        edge = 4 * PLACES
        return swap_border(jnp.where(me == 1, value[-edge:], value[:edge]))

    hidden = gather_slots(table, tokens, swap_core(tokens), border(tokens), bins)
    grad = gather_slots(
        table, outputs_grad, swap_core(outputs_grad), border(outputs_grad), bins
    )

    def norm_pack(l, which, bias_row):
        rows = jnp.stack([gains[l, which], shifts[l, which], shifts[l, bias_row]])
        return jnp.pad(rows, ((0, 5), (0, 0)))

    saved = []
    for l in range(LAYERS):
        norms = norm_pack(l, 0, 2)
        mid, a, qkv, probs, attn = attn_forward(
            table, hidden, gathered[2 * l], qkv_bias[l], bias[l], norms, l % 2 == 1
        )
        mlp_norms = norm_pack(l, 1, 3)
        out, a2, act, slope = mlp_forward(mid, gathered[2 * l + 1], fc1_all[l], mlp_norms)
        saved.append((hidden, mid, a, qkv, probs, attn, a2, act, slope, norms, mlp_norms))
        hidden = out

    def give_back(value):
        slots = value.reshape(bins, PAD, D)
        edge = lax.dynamic_slice_in_dim(slots, table[SEND], 4, 0)
        return return_slots(table, slots, swap_core(slots), swap_border(edge), own)

    output = give_back(hidden)

    mlp_grads, attn_grads = [None] * LAYERS, [None] * LAYERS
    keep_small, send_small = [None] * LAYERS, [None] * LAYERS
    for l in reversed(range(LAYERS)):
        hidden, mid, a, qkv, probs, attn, a2, act, slope, norms, mlp_norms = saved[l]
        grad, keep, send, small_mlp, dfc1_bias = mlp_backward(
            grad, mid, a2, act, slope, gathered[2 * l + 1], mlp_norms
        )
        mlp_grads[l] = sum_dp(sum_head(keep, send), LOW)
        grad, keep, send, small_attn, dscores = attn_backward(
            table, grad, hidden, a, qkv, probs, attn, gathered[2 * l], norms, l % 2 == 1
        )
        attn_grads[l] = sum_dp(sum_head(keep, send), LOW)
        dscores = dscores.reshape(QUADS, PAD, 4, WIDE)[:, :PLACES, :, :PLACES]
        dscores = dscores.transpose(0, 2, 1, 3).reshape(12, PLACES * PLACES)
        dtable = jnp.einsum("nt,hn->ht", hot, dscores, precision=highest).reshape(4, 3, 169)
        dtable = jnp.pad(dtable.reshape(4, 507), ((0, 0), (0, 261))).reshape(4, 2, D)
        dqv = small_attn[3:5].reshape(2, 4, 96).transpose(1, 0, 2).reshape(4, 192)
        dqv = jnp.pad(dqv, ((0, 0), (0, 192))).reshape(4, 1, D)
        shared = jnp.concatenate([small_attn[0:3], small_mlp[0:3]])
        shared = jnp.broadcast_to(shared[None], (4, 6, D))
        rows = jnp.concatenate([shared, dfc1_bias.reshape(4, 1, D), dqv, dtable], axis=1)
        keep_small[l], send_small[l] = rows[:2], rows[2:]
    tokens_grad = give_back(grad)

    total = sum_head(jnp.concatenate(keep_small, axis=1), jnp.concatenate(send_small, axis=1))
    total = sum_dp_small(total).reshape(LAYERS, 10, D)
    gains_out = jnp.stack([total[:, 0], total[:, 3]], axis=1)
    shifts_out = jnp.stack([total[:, 1], total[:, 4], total[:, 2], total[:, 5]], axis=1)
    fc1_bias_out = total[:, 6]
    qv_out = total[:, 7, :192].reshape(LAYERS, 2, 96)
    table_out = total[:, 8:10].reshape(LAYERS, 2 * D)[:, :507].reshape(LAYERS, 3, 169)
    table_out = table_out.transpose(0, 2, 1)
    attn_all = jnp.stack(attn_grads)
    qkv_out = attn_all[:, :288].reshape(LAYERS, 3, 96, D).transpose(0, 3, 1, 2)
    proj_out = attn_all[:, 288:]
    mlp_all = jnp.stack(mlp_grads)
    fc1_out = mlp_all[:, :D]
    fc2_out = mlp_all[:, D:].transpose(0, 2, 1)
    return (
        output, tokens_grad, qkv_out, qv_out, table_out, proj_out, fc1_out, fc1_bias_out,
        fc2_out, gains_out, shifts_out,
    )


def solution(mesh):
    rows = P(("dp", "head"), None)
    placed = (
        rows,
        rows,
        P("dp", None),
        P(None, None, None, "head"),
        P(None, None, "head"),
        P(None, None, "head"),
        P(None, "head", None),
        P(None, None, "head"),
        P(None, "head"),
        P(None, "head", None),
        P(),
        P(),
    )
    return jax.shard_map(
        body,
        mesh=mesh,
        in_specs=placed,
        out_specs=(
            rows,
            rows,
            P(None, None, None, "head"),
            P(None, None, "head"),
            P(None, None, "head"),
            P(None, "head", None),
            P(None, None, "head"),
            P(None, "head"),
            P(None, "head", None),
            P(),
            P(),
        ),
        check_vma=False,
    )
```

```python
import jax
import jax.numpy as jnp
from jax import lax
from jax.experimental import pallas as pl
from jax.experimental.pallas import tpu as pltpu
from jax.sharding import PartitionSpec as P

D = 384
FF = 1536
LAYERS = 2
PLACES = 49
PAD = 56
WIDE = 64
QUADS = 3
HEAD_DIM = 32
SCORE_SCALE = HEAD_DIM**-0.5
LN_EPS = 1e-05
LOW = jnp.bfloat16
F32 = jnp.float32
MIB = 1024 * 1024
SMALL = 16

SRC, SIDE, WROW, WCOL, FIRST, RET, SEND = 0, 24, 48, 72, 96, 120, 140
TABLE = 144


def vmem():
    return pl.BlockSpec(memory_space=pltpu.VMEM)


def smem():
    return pl.BlockSpec(memory_space=pltpu.SMEM)


def anywhere():
    return pl.BlockSpec(memory_space=pl.ANY)


def params(limit):
    return pltpu.CompilerParams(vmem_limit_bytes=limit * MIB)


def cost(flops, size):
    return pl.CostEstimate(flops=int(flops * 0.02), bytes_accessed=int(size * 0.02), transcendentals=0)


def dot_nn(a, b):
    return lax.dot_general(a, b, (((1,), (0,)), ((), ())), preferred_element_type=F32)


def dot_nt(a, b):
    return lax.dot_general(a, b, (((1,), (1,)), ((), ())), preferred_element_type=F32)


def dot_tn(a, b):
    return lax.dot_general(a, b, (((0,), (0,)), ((), ())), preferred_element_type=F32)


def plan_kernel(own, bins, kind_ref, me_ref, out_ref, load_ref):
    me = me_ref[0]
    half = 2 * own
    for i in range(TABLE):
        out_ref[i] = -1 if i < bins or RET <= i < RET + own else 0
    for i in range(bins):
        out_ref[SIDE + i] = 1
        out_ref[FIRST + i] = i
    for i in range(4):
        load_ref[i] = 0

    def place(start, count, side, bin_id):
        base = load_ref[bin_id]
        load_ref[bin_id] = base + count

        def step(k, carry):
            slot = start + k
            owner = slot // own
            inner = slot - owner * own
            local = base + k
            mine = bin_id == me
            halo = jnp.where(me == 1, slot - half, slot - half + 4)
            code = jnp.where(
                owner == me, inner, jnp.where(owner == (me ^ 1), own + inner, 2 * own + halo)
            )

            @pl.when(mine)
            def _():
                wrow = k // side
                out_ref[SRC + local] = code
                out_ref[SIDE + local] = side
                out_ref[WROW + local] = wrow
                out_ref[WCOL + local] = k - wrow * side
                out_ref[FIRST + local] = base

            @pl.when(owner == me)
            def _():
                back = jnp.where(me == 2, slot - half, k)
                out_ref[RET + inner] = jnp.where(
                    mine, local, jnp.where(bin_id == (me ^ 1), bins + local, 2 * bins + back)
                )

            return carry

        lax.fori_loop(0, count, step, 0)

    for turn in range(3):

        def visit(i, start, turn=turn):
            kind = kind_ref[0, i]
            count = jnp.where(kind == 2, 9, jnp.where(kind == 1, 4, 0))
            side = jnp.where(kind == 2, 3, 2)
            cut = half - start
            across = (cut > 0) & (cut < count)
            second = (start >= half) | (across & (cut < count - cut))
            chip = jnp.where(second, 1, 0)
            left, right = load_ref[2 * chip], load_ref[2 * chip + 1]
            emptier = 2 * chip + jnp.where(left <= right, 0, 1)
            if turn == 0:
                chosen, bin_id = across, 1 + chip
            else:
                chosen, bin_id = (kind == 3 - turn) & jnp.logical_not(across), emptier

            @pl.when(chosen)
            def _():
                place(start, count, side, bin_id)
                if turn == 0:
                    out_ref[SEND] = jnp.where((me == 1) & (chip == 0), cut, 0)

            return start + count

        lax.fori_loop(0, kind_ref.shape[1], visit, jnp.int32(0))


def gather_kernel(bins, table_ref, refs, out_ref, spread_ref):
    spread_ref[...] = jnp.zeros(spread_ref.shape, F32)
    at = 0
    for ref in refs:
        for s in range(ref.shape[0] // PLACES):
            spread_ref[at, 0:PLACES] = ref[s * PLACES : (s + 1) * PLACES].astype(F32)
            at += 1

    def step(j, carry):
        src = table_ref[SRC + j]

        @pl.when(src < 0)
        def _():
            out_ref[j] = jnp.zeros((PAD, D), F32)

        @pl.when(src >= 0)
        def _():
            out_ref[j] = spread_ref[src]

        return carry

    lax.fori_loop(0, bins, step, 0)


def make_plan(image_kind, me, own, bins):
    def kernel(kind_ref, me_ref, table_ref, load_ref):
        plan_kernel(own, bins, kind_ref, me_ref, table_ref, load_ref)

    return pl.pallas_call(
        kernel,
        out_shape=jax.ShapeDtypeStruct((TABLE,), jnp.int32),
        in_specs=[smem(), smem()],
        out_specs=smem(),
        scratch_shapes=[pltpu.SMEM((4,), jnp.int32)],
        compiler_params=params(1),
        cost_estimate=cost(0, 1.5e7),
        name="plan",
    )(image_kind, me.reshape(1))


def gather_slots(table, mine, partner, halo, bins):
    own = mine.shape[0] // PLACES

    def kernel(table_ref, *refs):
        gather_kernel(bins, table_ref, refs[:3], refs[3], refs[4])

    out = pl.pallas_call(
        kernel,
        out_shape=jax.ShapeDtypeStruct((bins, PAD, D), F32),
        in_specs=[smem()] + [vmem()] * 3,
        out_specs=vmem(),
        scratch_shapes=[pltpu.VMEM((2 * own + 4, PAD, D), F32)],
        compiler_params=params(8),
        cost_estimate=cost(0, 8e6),
        name="gather_slots",
    )(table, mine, partner, halo)
    return out.reshape(bins * PAD, D)


def return_slots(table, mine, partner, halo, own):
    bins = mine.shape[0]

    def kernel(table_ref, mine_ref, partner_ref, halo_ref, out_ref):
        for s in range(own):
            src = table_ref[RET + s]
            rows = pl.ds(s * PLACES, PLACES)

            @pl.when(src < 0)
            def _():
                out_ref[rows] = jnp.zeros((PLACES, D), F32)

            @pl.when((src >= 0) & (src < bins))
            def _():
                out_ref[rows] = mine_ref[src, 0:PLACES]

            @pl.when((src >= bins) & (src < 2 * bins))
            def _():
                out_ref[rows] = partner_ref[src - bins, 0:PLACES]

            @pl.when(src >= 2 * bins)
            def _():
                out_ref[rows] = halo_ref[src - 2 * bins, 0:PLACES]

    return pl.pallas_call(
        kernel,
        out_shape=jax.ShapeDtypeStruct((own * PLACES, D), F32),
        in_specs=[smem(), vmem(), vmem(), vmem()],
        out_specs=vmem(),
        compiler_params=params(2),
        cost_estimate=cost(0, 8e6),
        name="return_slots",
    )(table, mine, partner, halo)


def norm_rows(rows):
    average = jnp.mean(rows, axis=-1, keepdims=True)
    centred = rows - average
    inverse = lax.rsqrt(jnp.mean(centred * centred, axis=-1, keepdims=True) + LN_EPS)
    return centred * inverse, inverse


def norm_back(incoming, scaled, inverse, gain):
    weighted = incoming * gain
    return inverse * (
        weighted
        - jnp.mean(weighted, axis=-1, keepdims=True)
        - scaled * jnp.mean(weighted * scaled, axis=-1, keepdims=True)
    )


def gelu_parts(x):
    size = jnp.abs(x) * 0.7071067811865476
    t = 1.0 / (1.0 + 0.3275911 * size)
    bell = jnp.exp(-0.5 * x * x)
    poly = t * (
        0.127414796 + t * (-0.142248368 + t * (0.7107068705 + t * (-0.7265760135 + t * 0.5307027145)))
    )
    tail = poly * bell
    phi = jnp.where(x >= 0, 1.0 - tail, tail)
    return x * phi, phi + x * bell * 0.3989422804014327


def place_parts(shape, dim):
    place = lax.broadcasted_iota(jnp.int32, shape, dim)
    row = (place * 37) >> 8
    return place, row, place - 7 * row


def fill_moves(table_ref, out_ref, bins, back):
    width = out_ref.shape[1]
    place, row, col = place_parts((PAD, 1), 0)
    if back:
        row_other, col_other = row < 3, col < 3
        inner = 7 * jnp.where(row_other, row + 4, row - 3) + jnp.where(col_other, col + 4, col - 3)
    else:
        row_other, col_other = row >= 4, col >= 4
        inner = 7 * jnp.where(row_other, row - 4, row + 3) + jnp.where(col_other, col - 4, col + 3)
    lanes = lax.broadcasted_iota(jnp.int32, (2 * PAD, width), 1)

    def source(w):
        side, wrow, wcol = table_ref[SIDE + w], table_ref[WROW + w], table_ref[WCOL + w]
        first = table_ref[FIRST + w]
        if back:
            orow = jnp.where(wrow == 0, side - 1, wrow - 1)
            ocol = jnp.where(wcol == 0, side - 1, wcol - 1)
        else:
            orow = jnp.where(wrow == side - 1, 0, wrow + 1)
            ocol = jnp.where(wcol == side - 1, 0, wcol + 1)
        slot = first + jnp.where(row_other, orow, wrow) * side + jnp.where(col_other, ocol, wcol)
        return jnp.where(place < PLACES, slot * PAD + inner, w * PAD + place)

    def step(j, carry):
        rows = jnp.concatenate([source(2 * j), source(2 * j + 1)], axis=0)
        hot = jnp.where(lanes == rows, 1.0, 0.0).astype(LOW)
        out_ref[pl.ds(pl.multiple_of(j * 2 * PAD, 16), 2 * PAD)] = hot
        return carry

    lax.fori_loop(0, bins // 2, step, 0)


def head_marks():
    lane = lax.broadcasted_iota(jnp.int32, (WIDE, 128), 1) // HEAD_DIM
    return [jnp.where(lane == h, 1.0, 0.0).astype(LOW) for h in range(4)]


def spread(block, marks):
    return jnp.concatenate([block * mark for mark in marks], axis=0)


def fold(product, marks):
    total = None
    for h, mark in enumerate(marks):
        part = product[h * WIDE : (h + 1) * WIDE] * mark.astype(F32)
        total = part if total is None else total + part
    return total


def spread_pair(block, marks):
    return jnp.concatenate([spread(block[0:WIDE], marks), spread(block[WIDE:], marks)], axis=1)


def diagonal(block):
    zero = jnp.zeros((WIDE, 128), block.dtype)
    top = jnp.concatenate([block[0:WIDE], zero], axis=1)
    return jnp.concatenate([top, jnp.concatenate([zero, block[WIDE:]], axis=1)], axis=0)


def by_head(values):
    return values.reshape(4, WIDE, 128)


def pad_rows(rows):
    return jnp.concatenate([rows, jnp.zeros((WIDE - PAD, rows.shape[1]), rows.dtype)], axis=0)


def split(values):
    high = values.astype(LOW)
    return high, (values - high.astype(F32)).astype(LOW)


def marks_where(rows, cols, test):
    row = lax.broadcasted_iota(jnp.int32, (rows, cols), 0)
    col = lax.broadcasted_iota(jnp.int32, (rows, cols), 1)
    return jnp.where(test(row, col), 1.0, 0.0).astype(LOW)


def far(place):
    row = (place * 37) >> 8
    return 13 * row + (place - 7 * row)


def tables_to_bias(tables):
    heads = tables.shape[0]

    def kernel(table_ref, out_ref):
        to_lane = marks_where(
            128, 128, lambda r, c: (far(c & 63) == r) & ((c & 63) < PLACES)
        )
        to_row = marks_where(WIDE, 96, lambda r, c: (far(r) == c) & (r < PLACES))
        place = lax.broadcasted_iota(jnp.int32, (WIDE, 128), 0)
        empty = jnp.where(place < PLACES, 0.0, -1e30)
        turned = pltpu.roll(table_ref[...], 172, 1)
        skewed = []
        for n in range(heads):
            row = jnp.broadcast_to(turned[n : n + 1], (96, 256))
            skewed.append(pltpu.roll(row, 0, 1, stride=1, stride_axis=0)[:, 0:128])
        skewed = jnp.concatenate(skewed, axis=1)
        total = None
        for part in split(skewed):
            rows = dot_nn(to_row, part).astype(LOW)
            rows = jnp.concatenate([rows[:, n * 128 : (n + 1) * 128] for n in range(heads)], axis=0)
            part = dot_nn(rows, to_lane)
            total = part if total is None else total + part
        for n in range(heads):
            l, t, h = n // 12, n % 12 // 4, n % 4
            out_ref[l, t, h * WIDE : (h + 1) * WIDE] = total[n * WIDE : (n + 1) * WIDE] + empty

    return pl.pallas_call(
        kernel,
        out_shape=jax.ShapeDtypeStruct((LAYERS, QUADS, 4 * WIDE, 128), F32),
        in_specs=[vmem()],
        out_specs=vmem(),
        compiler_params=params(4),
        cost_estimate=cost(0, 1e7),
        name="tables_to_bias",
    )(tables)


def scores_to_table(scores_ref):
    to_far = marks_where(128, 128, lambda r, c: (far(r & 63) == c) & ((r & 63) < PLACES))
    to_row = marks_where(96, WIDE, lambda r, c: (84 - far(c) == r) & (c < PLACES))
    wide = None
    for part in split(scores_ref[...].reshape(12 * WIDE, 128)):
        part = dot_nn(part, to_far)
        wide = part if wide is None else wide + part
    wide = jnp.concatenate([wide[h * WIDE : (h + 1) * WIDE] for h in range(12)], axis=1)
    rows = None
    for part in split(wide):
        part = dot_nn(to_row, part)
        rows = part if rows is None else rows + part
    out = []
    for h in range(12):
        one = rows[:, h * 128 : (h + 1) * 128]
        one = jnp.concatenate([one, jnp.zeros_like(one)], axis=1)
        one = pltpu.roll(one, 0, 1, stride=1, stride_axis=0)
        out.append(jnp.sum(one, axis=0, keepdims=True))
    return out


def stack_qkv(pieces, out_ref):
    for k, piece in enumerate(pieces):
        for c in range(3):
            out_ref[c * D + k * 96 : c * D + (k + 1) * 96] = piece[c * 96 : (c + 1) * 96]


def stack_proj(pieces, out_ref):
    for k, piece in enumerate(pieces):
        out_ref[k * 96 : (k + 1) * 96] = piece[288:384]


def stack_mlp(pieces, fc1_ref, fc2_ref):
    for k, piece in enumerate(pieces):
        fc1_ref[:, k * D : (k + 1) * D] = piece[0:D]
        fc2_ref[k * D : (k + 1) * D] = piece[D : 2 * D]


def attn_forward(table, hidden, weights, qv_bias, bias, norms, shifted):
    rows = hidden.shape[0]
    bins = rows // PAD
    chunk_slots = 6
    chunk = chunk_slots * PAD
    wide_rows = -(-rows // 128) * 128

    def kernel(
        table_ref, hidden_ref, w0, w1, w2, w3, qv_ref, bias_ref, norm_ref,
        mid_ref, a_ref, qkv_out, p_out, attn_ref,
        wqkv, wproj, wide_attn, moves, qkv_ref, p_ref, sems,
    ):
        pieces = (w0, w1, w2, w3)
        stack_qkv(pieces, wqkv)
        stack_proj(pieces, wproj)
        gain, shift, proj_shift = norm_ref[0:1], norm_ref[1:2], norm_ref[2:3]
        marks = head_marks()
        dest = attn_ref if shifted else a_ref

        def norm_step(i, carry):
            at = pl.ds(pl.multiple_of(i * chunk, 16), chunk)
            scaled, _ = norm_rows(hidden_ref[at])
            dest[at] = (scaled * gain + shift).astype(LOW)
            return carry

        lax.fori_loop(0, bins // chunk_slots, norm_step, 0)
        if shifted:
            fill_moves(table_ref, moves, bins, False)
            a_ref[...] = dot_nn(moves[:, 0:rows], dest[...]).astype(LOW)
            fill_moves(table_ref, moves, bins, True)

        def qkv_step(i, carry):
            at = pl.ds(pl.multiple_of(i * chunk, 16), chunk)
            project = dot_nt(a_ref[at], wqkv[...]) + qv_ref[...]
            for j in range(chunk_slots):
                block = project[j * PAD : (j + 1) * PAD]
                at = pl.ds((j % 2) * WIDE, WIDE)
                qkv_ref[i * (chunk_slots // 2) + j // 2, at] = pad_rows(block).astype(LOW)
            return carry

        lax.fori_loop(0, bins // chunk_slots, qkv_step, 0)
        keep_qkv = pltpu.make_async_copy(qkv_ref, qkv_out, sems.at[0])
        keep_qkv.start()

        if shifted:
            _, qrow, qcol = place_parts((WIDE, 1), 0)
            lane = lax.broadcasted_iota(jnp.int32, (1, 128), 1)
            second = lane >= WIDE
            pplace = jnp.where(second, lane - WIDE, lane)
            prow = (pplace * 37) >> 8
            pcol = pplace - 7 * prow
            pband = 1 + (prow >= 4).astype(jnp.int32), 1 + (pcol >= 4).astype(jnp.int32)
            qband = 1 + (qrow >= 4).astype(jnp.int32), 1 + (qcol >= 4).astype(jnp.int32)

        def window(j, carry):
            if shifted:
                low = []
                for w in (2 * j, 2 * j + 1):
                    side = table_ref[SIDE + w]
                    low.append(
                        (
                            jnp.where(table_ref[WROW + w] == side - 1, 3, 0),
                            jnp.where(table_ref[WCOL + w] == side - 1, 1, 0),
                        )
                    )
                low_row = jnp.where(second, low[1][0], low[0][0])
                low_col = jnp.where(second, low[1][1], low[0][1])
                pregion = low_row * pband[0] + low_col * pband[1]
                qregion = low_row * qband[0] + low_col * qband[1]
                mask = jnp.where(pregion != qregion, -100.0, 0.0)[None]
            for t in range(QUADS):
                cols = slice(t * 128, (t + 1) * 128)
                q = qkv_ref[j, :, t * 128 : (t + 1) * 128]
                k = qkv_ref[j, :, D + t * 128 : D + (t + 1) * 128]
                v = qkv_ref[j, :, 2 * D + t * 128 : 2 * D + (t + 1) * 128]
                scores = dot_nt(spread_pair(k, marks), diagonal(q)) * SCORE_SCALE + bias_ref[t]
                scores = by_head(scores)
                if shifted:
                    scores = scores + mask
                exponent = jnp.exp(scores - jnp.max(scores, axis=1, keepdims=True))
                total = jnp.sum(exponent, axis=1, keepdims=True)
                probs = (exponent * (1.0 / total)).reshape(4 * WIDE, 128).astype(LOW)
                p_ref[j, t] = probs
                both = dot_tn(probs, spread_pair(v, marks))
                at = pl.multiple_of(j * 2 * PAD, 16)
                wide_attn[pl.ds(at, PAD), cols] = both[0:PAD, 0:128]
                wide_attn[pl.ds(at + PAD, PAD), cols] = both[WIDE : WIDE + PAD, 128:256]
            return carry

        lax.fori_loop(0, bins // 2, window, 0)
        keep_p = pltpu.make_async_copy(p_ref, p_out, sems.at[1])
        keep_p.start()
        if shifted:
            attn_ref[...] = dot_nn(moves[:, 0:rows], wide_attn[...].astype(LOW)).astype(LOW)
        else:
            attn_ref[...] = wide_attn[...].astype(LOW)

        def proj_step(i, carry):
            at = pl.ds(pl.multiple_of(i * chunk, 16), chunk)
            mid_ref[at] = hidden_ref[at] + dot_nn(attn_ref[at], wproj[...]) + proj_shift
            return carry

        lax.fori_loop(0, bins // chunk_slots, proj_step, 0)
        keep_qkv.wait()
        keep_p.wait()

    return pl.pallas_call(
        kernel,
        out_shape=(
            jax.ShapeDtypeStruct((rows, D), F32),
            jax.ShapeDtypeStruct((rows, D), LOW),
            jax.ShapeDtypeStruct((bins // 2, 2 * WIDE, 3 * D), LOW),
            jax.ShapeDtypeStruct((bins // 2, QUADS, 4 * WIDE, 128), LOW),
            jax.ShapeDtypeStruct((rows, D), LOW),
        ),
        in_specs=[smem()] + [vmem()] * 8,
        out_specs=[vmem(), vmem(), anywhere(), anywhere(), vmem()],
        scratch_shapes=[
            pltpu.VMEM((3 * D, D), LOW),
            pltpu.VMEM((D, D), LOW),
            pltpu.VMEM((rows, D), F32),
            pltpu.VMEM((rows if shifted else 16, wide_rows), LOW),
            pltpu.VMEM((bins // 2, 2 * WIDE, 3 * D), LOW),
            pltpu.VMEM((bins // 2, QUADS, 4 * WIDE, 128), LOW),
            pltpu.SemaphoreType.DMA((2,)),
        ],
        compiler_params=params(13),
        cost_estimate=cost(1e10, 2e7),
        name="attn_forward",
    )(table, hidden, *weights, qv_bias, bias, norms)


def attn_backward(table, grad, qkv, probs, weights, shifted):
    rows = grad.shape[0]
    bins = rows // PAD
    chunk_slots = 6
    chunk = chunk_slots * PAD
    wide_rows = -(-rows // 128) * 128

    def kernel(
        table_ref, grad_ref, qkv_in, p_in, w0, w1, w2, w3,
        gqkv_ref, scores_ref, wproj, wide_attn, low_wide, moves, qkv_ref, p_ref, sems,
    ):
        fetch_qkv = pltpu.make_async_copy(qkv_in, qkv_ref, sems.at[0])
        fetch_p = pltpu.make_async_copy(p_in, p_ref, sems.at[1])
        fetch_qkv.start()
        fetch_p.start()
        stack_proj((w0, w1, w2, w3), wproj)
        marks = head_marks()
        steps = bins // chunk_slots
        if shifted:
            fill_moves(table_ref, moves, bins, False)

        def keep_windows(i, block_rows):
            for j in range(chunk_slots):
                block = block_rows[j * PAD : (j + 1) * PAD]
                dest = pl.ds((j % 2) * WIDE, WIDE)
                wide_attn[i * (chunk_slots // 2) + j // 2, dest] = pad_rows(block).astype(LOW)

        def proj_step(i, carry):
            at = pl.ds(pl.multiple_of(i * chunk, 16), chunk)
            gattn = dot_nt(grad_ref[at].astype(LOW), wproj[...])
            if shifted:
                low_wide[at] = gattn.astype(LOW)
            else:
                keep_windows(i, gattn)
            return carry

        lax.fori_loop(0, steps, proj_step, 0)
        if shifted:

            def move_step(i, carry):
                at = pl.ds(pl.multiple_of(i * chunk, 16), chunk)
                keep_windows(i, dot_nn(moves[at, 0:rows], low_wide[...]))
                return carry

            lax.fori_loop(0, steps, move_step, 0)

        scores_ref[...] = jnp.zeros((QUADS, 4 * WIDE, 128), F32)
        fetch_qkv.wait()
        fetch_p.wait()

        def window(j, carry):
            for t in range(QUADS):
                q = qkv_ref[j, :, t * 128 : (t + 1) * 128]
                k = qkv_ref[j, :, D + t * 128 : D + (t + 1) * 128]
                v = qkv_ref[j, :, 2 * D + t * 128 : 2 * D + (t + 1) * 128]
                low_probs = p_ref[j, t]
                p = by_head(low_probs.astype(F32))
                go = diagonal(wide_attn[j, :, t * 128 : (t + 1) * 128])
                gp = by_head(dot_nt(spread_pair(v, marks), go))
                ds = p * (gp - jnp.sum(gp * p, axis=1, keepdims=True))
                low_ds = ds.reshape(4 * WIDE, 128).astype(LOW)
                scores_ref[t] += low_ds.astype(F32)
                gq = dot_tn(low_ds, spread_pair(k, marks)) * SCORE_SCALE
                gk = dot_nn(low_ds, diagonal(q)) * SCORE_SCALE
                gv = dot_nn(low_probs, go)
                at = pl.ds(pl.multiple_of(j * 2 * PAD, 16), 2 * PAD)
                left, right = slice(0, 128), slice(128, 256)
                parts = (
                    (gq[0:PAD, left], gq[WIDE : WIDE + PAD, right]),
                    (fold(gk[:, left], marks)[0:PAD], fold(gk[:, right], marks)[0:PAD]),
                    (fold(gv[:, left], marks)[0:PAD], fold(gv[:, right], marks)[0:PAD]),
                )
                for c, part in enumerate(parts):
                    cols = slice(c * D + t * 128, c * D + (t + 1) * 128)
                    gqkv_ref[at, cols] = jnp.concatenate(part, axis=0).astype(LOW)
            return carry

        lax.fori_loop(0, bins // 2, window, 0)

    return pl.pallas_call(
        kernel,
        out_shape=(
            jax.ShapeDtypeStruct((rows, 3 * D), LOW),
            jax.ShapeDtypeStruct((QUADS, 4 * WIDE, 128), F32),
        ),
        in_specs=[smem(), vmem(), anywhere(), anywhere()] + [vmem()] * 4,
        out_specs=[vmem()] * 2,
        scratch_shapes=[
            pltpu.VMEM((D, D), LOW),
            pltpu.VMEM((bins // 2, 2 * WIDE, D), LOW),
            pltpu.VMEM((rows, D), LOW),
            pltpu.VMEM((rows if shifted else 16, wide_rows), LOW),
            pltpu.VMEM((bins // 2, 2 * WIDE, 3 * D), LOW),
            pltpu.VMEM((bins // 2, QUADS, 4 * WIDE, 128), LOW),
            pltpu.SemaphoreType.DMA((2,)),
        ],
        compiler_params=params(13),
        cost_estimate=cost(1e10, 2e7),
        name="attn_backward",
    )(table, grad, qkv, probs, *weights)


def attn_grads(
    table, grad, hidden, a, attn, gqkv, scores, small_mlp, fc1_bias_grad, weights, norms, shifted
):
    rows = hidden.shape[0]
    bins = rows // PAD
    chunk = 6 * PAD
    steps = rows // chunk
    wide_rows = -(-rows // 128) * 128

    def kernel(
        table_ref, grad_ref, hidden_ref, a_ref, attn_ref, gqkv_ref, scores_ref, mlp_ref, fc1b_ref,
        w0, w1, w2, w3, norm_ref,
        out_ref, keep_ref, send_ref, wqkv, low_wide, small, moves,
    ):
        stack_qkv((w0, w1, w2, w3), wqkv)
        gain = norm_ref[0:1]
        if shifted:
            fill_moves(table_ref, moves, bins, True)
            low_wide[...] = dot_nn(gqkv_ref[...], wqkv[...]).astype(LOW)

        def back_step(i, totals):
            at = pl.ds(pl.multiple_of(i * chunk, 16), chunk)
            if shifted:
                ga = dot_nn(moves[at, 0:rows], low_wide[...])
            else:
                ga = dot_nn(gqkv_ref[at], wqkv[...])
            scaled, inverse = norm_rows(hidden_ref[at])
            grad_now = grad_ref[at]
            out_ref[at] = grad_now + norm_back(ga, scaled, inverse, gain)
            return (
                totals[0] + jnp.sum(ga * scaled, axis=0, keepdims=True),
                totals[1] + jnp.sum(ga, axis=0, keepdims=True),
                totals[2] + jnp.sum(grad_now.astype(LOW).astype(F32), axis=0, keepdims=True),
                totals[3] + jnp.sum(gqkv_ref[at].astype(F32), axis=0, keepdims=True),
            )

        zero = jnp.zeros((1, D), F32)
        sums = lax.fori_loop(0, steps, back_step, (zero, zero, zero, jnp.zeros((1, 3 * D), F32)))
        table_rows = scores_to_table(scores_ref)
        dproj = dot_tn(attn_ref[...], grad_ref[...].astype(LOW)).astype(LOW)
        dqkv = dot_tn(a_ref[...], gqkv_ref[...])
        turned = [dqkv[:, c * D : (c + 1) * D].T.astype(LOW) for c in range(3)]
        small[...] = jnp.zeros((SMALL, D), F32)
        for i in range(3):
            small[i : i + 1] = sums[i]
        small[3:6] = mlp_ref[0:3]
        gq_sum = jnp.broadcast_to(sums[3][:, 0:D], (8, D))
        gv_sum = jnp.broadcast_to(sums[3][:, 2 * D : 3 * D], (8, D))
        for k in range(4):
            dest = keep_ref if k < 2 else send_ref
            for c in range(3):
                dest[k % 2, c * 96 : (c + 1) * 96] = turned[c][k * 96 : (k + 1) * 96]
            dest[k % 2, 288:384] = dproj[k * 96 : (k + 1) * 96]
            small[6:7] = fc1b_ref[:, k * D : (k + 1) * D]
            small[7:8] = pltpu.roll(gq_sum, (D - k * 96) % D, 1)[0:1]
            small[8:9] = pltpu.roll(gv_sum, (D - k * 96) % D, 1)[0:1]
            for h in range(3):
                small[9 + h : 10 + h, 0:256] = table_rows[3 * k + h]
            dest[k % 2, D : D + SMALL] = small[...].astype(LOW)

    return pl.pallas_call(
        kernel,
        out_shape=(
            jax.ShapeDtypeStruct((rows, D), F32),
            jax.ShapeDtypeStruct((2, D + SMALL, D), LOW),
            jax.ShapeDtypeStruct((2, D + SMALL, D), LOW),
        ),
        in_specs=[smem()] + [vmem()] * 13,
        out_specs=[vmem()] * 3,
        scratch_shapes=[
            pltpu.VMEM((3 * D, D), LOW),
            pltpu.VMEM((rows, D), LOW),
            pltpu.VMEM((SMALL, D), F32),
            pltpu.VMEM((rows if shifted else 16, wide_rows), LOW),
        ],
        compiler_params=params(10),
        cost_estimate=cost(6e9, 2e7),
        name="attn_grads",
    )(
        table, grad, hidden, a, attn, gqkv, scores, small_mlp, fc1_bias_grad, *weights, norms
    )


def mlp_forward(mid, weights, fc1_bias, norms):
    rows = mid.shape[0]
    chunk = 3 * PAD * 2
    steps = rows // chunk

    def kernel(
        mid_ref, w0, w1, w2, w3, fc1_bias_ref, norm_ref,
        out_ref, a_ref, act_out, slope_out, fc1, fc2, act_ref, slope_ref, sems,
    ):
        stack_mlp((w0, w1, w2, w3), fc1, fc2)
        gain, shift, out_shift = norm_ref[0:1], norm_ref[1:2], norm_ref[2:3]

        def keep(i, source, dest, which):
            at = pl.ds(pl.multiple_of(i * chunk, 16), chunk)
            return pltpu.make_async_copy(source.at[at], dest.at[at], sems.at[which, i])

        def step(i, carry):
            at = pl.ds(pl.multiple_of(i * chunk, 16), chunk)
            rows_now = mid_ref[at]
            scaled, _ = norm_rows(rows_now)
            a = (scaled * gain + shift).astype(LOW)
            a_ref[at] = a
            act, slope = gelu_parts(dot_nn(a, fc1[...]) + fc1_bias_ref[...])
            act = act.astype(LOW)
            act_ref[at] = act
            slope_ref[at] = slope.astype(LOW)
            keep(i, act_ref, act_out, 0).start()
            keep(i, slope_ref, slope_out, 1).start()
            out_ref[at] = rows_now + dot_nn(act, fc2[...]) + out_shift
            return carry

        lax.fori_loop(0, steps, step, 0)
        for i in range(steps):
            keep(i, act_ref, act_out, 0).wait()
            keep(i, slope_ref, slope_out, 1).wait()

    return pl.pallas_call(
        kernel,
        out_shape=(
            jax.ShapeDtypeStruct((rows, D), F32),
            jax.ShapeDtypeStruct((rows, D), LOW),
            jax.ShapeDtypeStruct((rows, FF), LOW),
            jax.ShapeDtypeStruct((rows, FF), LOW),
        ),
        in_specs=[vmem()] * 7,
        out_specs=[vmem(), vmem(), anywhere(), anywhere()],
        scratch_shapes=[
            pltpu.VMEM((D, FF), LOW),
            pltpu.VMEM((FF, D), LOW),
            pltpu.VMEM((rows, FF), LOW),
            pltpu.VMEM((rows, FF), LOW),
            pltpu.SemaphoreType.DMA((2, steps)),
        ],
        compiler_params=params(15),
        cost_estimate=cost(7e9, 2e7),
        name="mlp_forward",
    )(mid, *weights, fc1_bias, norms)


def mlp_backward(grad, mid, a, act, slope, weights, norms):
    rows = mid.shape[0]
    chunk = 3 * PAD * 2
    steps = rows // chunk

    def kernel(
        grad_ref, mid_ref, a_ref, act_in, slope_in, w0, w1, w2, w3, norm_ref,
        out_ref, keep_ref, send_ref, small_ref, bias_ref,
        fc1, fc2, low_grad, gpre_ref, act_ref, slope_ref, sems,
    ):
        def fetch_slope(i):
            at = pl.ds(pl.multiple_of(i * chunk, 16), chunk)
            return pltpu.make_async_copy(slope_in.at[at], slope_ref.at[at], sems.at[i])

        for i in range(steps):
            fetch_slope(i).start()
        fetch_act = pltpu.make_async_copy(act_in, act_ref, sems.at[steps])
        fetch_act.start()
        stack_mlp((w0, w1, w2, w3), fc1, fc2)
        gain = norm_ref[0:1]

        def step(i, totals):
            at = pl.ds(pl.multiple_of(i * chunk, 16), chunk)
            grad_now = grad_ref[at]
            gz = grad_now.astype(LOW)
            low_grad[at] = gz
            fetch_slope(i).wait()
            gpre = (dot_nt(gz, fc2[...]) * slope_ref[at].astype(F32)).astype(LOW)
            gpre_ref[at] = gpre
            ga = dot_nt(gpre, fc1[...])
            scaled, inverse = norm_rows(mid_ref[at])
            out_ref[at] = grad_now + norm_back(ga, scaled, inverse, gain)
            return (
                totals[0] + jnp.sum(ga * scaled, axis=0, keepdims=True),
                totals[1] + jnp.sum(ga, axis=0, keepdims=True),
                totals[2] + jnp.sum(gz.astype(F32), axis=0, keepdims=True),
                totals[3] + jnp.sum(gpre.astype(F32), axis=0, keepdims=True),
            )

        zero = jnp.zeros((1, D), F32)
        sums = lax.fori_loop(0, steps, step, (zero, zero, zero, jnp.zeros((1, FF), F32)))
        for i in range(3):
            small_ref[i : i + 1] = sums[i]
        small_ref[3:8] = jnp.zeros((5, D), F32)
        bias_ref[...] = sums[3]
        fetch_act.wait()
        for k in range(4):
            dest = keep_ref if k < 2 else send_ref
            cols = slice(k * D, (k + 1) * D)
            dest[k % 2, 0:D] = dot_tn(a_ref[...], gpre_ref[:, cols]).astype(LOW)
            dest[k % 2, D : 2 * D] = dot_tn(low_grad[...], act_ref[:, cols]).astype(LOW)

    return pl.pallas_call(
        kernel,
        out_shape=(
            jax.ShapeDtypeStruct((rows, D), F32),
            jax.ShapeDtypeStruct((2, 2 * D, D), LOW),
            jax.ShapeDtypeStruct((2, 2 * D, D), LOW),
            jax.ShapeDtypeStruct((8, D), F32),
            jax.ShapeDtypeStruct((1, FF), F32),
        ),
        in_specs=[vmem()] * 3 + [anywhere()] * 2 + [vmem()] * 5,
        out_specs=[vmem()] * 5,
        scratch_shapes=[
            pltpu.VMEM((D, FF), LOW),
            pltpu.VMEM((FF, D), LOW),
            pltpu.VMEM((rows, D), LOW),
            pltpu.VMEM((rows, FF), LOW),
            pltpu.VMEM((rows, FF), LOW),
            pltpu.VMEM((rows, FF), LOW),
            pltpu.SemaphoreType.DMA((steps + 1,)),
        ],
        compiler_params=params(19),
        cost_estimate=cost(7e9, 2e7),
        name="mlp_backward",
    )(grad, mid, a, act, slope, *weights, norms)


def mlp_turn(mid, grad, weights, fc1_bias, norms):
    rows = mid.shape[0]
    chunk = 3 * PAD * 2
    steps = rows // chunk

    def kernel(
        mid_ref, grad_ref, w0, w1, w2, w3, fc1_bias_ref, norm_ref,
        out_ref, grad_out_ref, keep_ref, send_ref, small_ref, bias_ref,
        fc1, fc2, a_all, act_all, low_grad, gpre_all,
    ):
        stack_mlp((w0, w1, w2, w3), fc1, fc2)
        gain, shift, out_shift = norm_ref[0:1], norm_ref[1:2], norm_ref[2:3]

        def step(i, totals):
            at = pl.ds(pl.multiple_of(i * chunk, 16), chunk)
            rows_now = mid_ref[at]
            scaled, inverse = norm_rows(rows_now)
            a = (scaled * gain + shift).astype(LOW)
            a_all[at] = a
            act, slope = gelu_parts(dot_nn(a, fc1[...]) + fc1_bias_ref[...])
            act = act.astype(LOW)
            act_all[at] = act
            out_ref[at] = rows_now + dot_nn(act, fc2[...]) + out_shift
            grad_now = grad_ref[at]
            gz = grad_now.astype(LOW)
            low_grad[at] = gz
            gpre = (dot_nt(gz, fc2[...]) * slope).astype(LOW)
            gpre_all[at] = gpre
            ga = dot_nt(gpre, fc1[...])
            grad_out_ref[at] = grad_now + norm_back(ga, scaled, inverse, gain)
            return (
                totals[0] + jnp.sum(ga * scaled, axis=0, keepdims=True),
                totals[1] + jnp.sum(ga, axis=0, keepdims=True),
                totals[2] + jnp.sum(gz.astype(F32), axis=0, keepdims=True),
                totals[3] + jnp.sum(gpre.astype(F32), axis=0, keepdims=True),
            )

        zero = jnp.zeros((1, D), F32)
        sums = lax.fori_loop(0, steps, step, (zero, zero, zero, jnp.zeros((1, FF), F32)))
        for i in range(3):
            small_ref[i : i + 1] = sums[i]
        small_ref[3:8] = jnp.zeros((5, D), F32)
        bias_ref[...] = sums[3]
        for k in range(4):
            dest = keep_ref if k < 2 else send_ref
            cols = slice(k * D, (k + 1) * D)
            dest[k % 2, 0:D] = dot_tn(a_all[...], gpre_all[:, cols]).astype(LOW)
            dest[k % 2, D : 2 * D] = dot_tn(low_grad[...], act_all[:, cols]).astype(LOW)

    return pl.pallas_call(
        kernel,
        out_shape=(
            jax.ShapeDtypeStruct((rows, D), F32),
            jax.ShapeDtypeStruct((rows, D), F32),
            jax.ShapeDtypeStruct((2, 2 * D, D), LOW),
            jax.ShapeDtypeStruct((2, 2 * D, D), LOW),
            jax.ShapeDtypeStruct((8, D), F32),
            jax.ShapeDtypeStruct((1, FF), F32),
        ),
        in_specs=[vmem()] * 8,
        out_specs=[vmem()] * 6,
        scratch_shapes=[
            pltpu.VMEM((D, FF), LOW),
            pltpu.VMEM((FF, D), LOW),
            pltpu.VMEM((rows, D), LOW),
            pltpu.VMEM((rows, FF), LOW),
            pltpu.VMEM((rows, D), LOW),
            pltpu.VMEM((rows, FF), LOW),
        ],
        compiler_params=params(18),
        cost_estimate=cost(1.5e10, 4e7),
        name="mlp_turn",
    )(mid, grad, *weights, fc1_bias, norms)


def swap_core(value):
    return lax.ppermute(value, "head", [(i, i ^ 1) for i in range(4)])


def swap_chip(value):
    return lax.ppermute(value, "head", [(i, i ^ 2) for i in range(4)])


def swap_border(value):
    return lax.ppermute(value, "head", [(1, 2), (2, 1)])


def swap_dp(value, step, size):
    return lax.ppermute(value, "dp", [(i, i ^ step) for i in range(size)])


def tie(*values):
    return lax.optimization_barrier(values)


def pick(first, one, other):
    return jnp.where(first, one, other), jnp.where(first, other, one)


def dp_start(parts):
    first = lax.axis_index("dp") % 2 == 0
    half = parts[0].shape[0] // 2
    low = sum(p[:half].astype(F32) for p in parts)
    high = sum(p[half:].astype(F32) for p in parts)
    kept, sent = pick(first, low, high)
    return kept, swap_dp(sent.astype(LOW), 1, lax.axis_size("dp"))


def dp_middle(kept, other, step):
    value = (kept.astype(F32) + other.astype(F32)).astype(LOW)
    return value, swap_dp(value, step, lax.axis_size("dp"))


def dp_last(kept, other):
    value = (kept.astype(F32) + other.astype(F32)).astype(LOW)
    return value, swap_dp(value, 1, lax.axis_size("dp"))


def dp_join(value, other):
    first = lax.axis_index("dp") % 2 == 0
    low, high = pick(first, value, other)
    return jnp.concatenate([low, high])


def dp_steps():
    return [(2 << b) - 2 for b in range(1, lax.axis_size("dp").bit_length() - 1)]


def dp_finish(state, steps):
    for step in steps:
        state = dp_middle(*state, step)
    return dp_join(*dp_last(*state))


def body(
    tokens, outputs_grad, image_kind, qkv_weight, qv_bias, bias_table, proj_weight,
    fc1_weight, fc1_bias, fc2_weight, gains, shifts,
):
    own = tokens.shape[0] // PLACES
    bins = own + 2
    me = lax.axis_index("head").astype(jnp.int32)

    def border(value):
        edge = 4 * PLACES
        return swap_border(jnp.where(me == 1, value[-edge:], value[:edge]))

    def attn_pack(l):
        turned = jnp.transpose(qkv_weight[l], (1, 2, 0)).reshape(288, D)
        return jnp.concatenate([turned, proj_weight[l]], axis=0)

    def mlp_pack(l):
        return jnp.concatenate([fc1_weight[l], fc2_weight[l]], axis=0)

    def norm_pack(l, which, bias_row):
        rows = jnp.stack([gains[l, which], shifts[l, which], shifts[l, bias_row]])
        return jnp.pad(rows, ((0, 5), (0, 0)))

    partner = swap_core(tokens)
    own_pack, chip_pack = [attn_pack(0)], []
    chip_pack.append(swap_chip(own_pack[0]))
    rows = jnp.pad(jnp.transpose(bias_table, (0, 2, 1)).reshape(6, 169), ((0, 0), (0, D - 169)))
    small = jnp.concatenate([rows, qv_bias.reshape(1, D), fc1_bias])
    small = jnp.pad(small, ((0, 7), (0, 0)))
    small, edges, _ = tie(small, tokens, own_pack[0])
    small_chip = swap_chip(small)
    halo = border(edges)
    table = make_plan(image_kind, me, own, bins)
    smalls = jnp.stack([small, small_chip, swap_core(small), swap_core(small_chip)])
    chip_pack[0], table = tie(chip_pack[0], table)
    hidden = gather_slots(table, tokens, partner, halo, bins)
    pack, _ = tie(mlp_pack(0), chip_pack[0])
    own_pack.append(pack)
    chip_pack.append(swap_chip(pack))

    def gathered(i):
        p, c = own_pack[i], chip_pack[i]
        return p, c, swap_core(p), swap_core(c)

    qv_all = smalls[:, 6].reshape(4, LAYERS, 2, 96).transpose(1, 2, 0, 3).reshape(LAYERS, 2, D)
    qkv_bias = jnp.stack([qv_all[:, 0], jnp.zeros_like(qv_all[:, 0]), qv_all[:, 1]], axis=1)
    qkv_bias = qkv_bias.reshape(LAYERS, 1, 3 * D)
    fc1_all = smalls[:, 7:9].transpose(1, 0, 2).reshape(LAYERS, 1, FF)
    tables = smalls[:, 0:6, 0:256].reshape(4, LAYERS, 3, 256).transpose(1, 0, 2, 3)
    bias = tables_to_bias(tables.reshape(LAYERS * 12, 256))

    saved, weights = [], []
    last = LAYERS - 1
    for l in range(LAYERS):
        norms, mlp_norms = norm_pack(l, 0, 2), norm_pack(l, 1, 3)
        weights.append(gathered(2 * l))
        mid, a, qkv, probs, attn = attn_forward(
            table, hidden, weights[2 * l], qkv_bias[l], bias[l], norms, l % 2 == 1
        )
        mid, chip_pack[2 * l + 1] = tie(mid, chip_pack[2 * l + 1])
        weights.append(gathered(2 * l + 1))
        if l == last:
            saved.append((hidden, mid, a, qkv, probs, attn, norms, mlp_norms))
            break
        pack, outputs_grad, mid = tie(attn_pack(1), outputs_grad, mid)
        own_pack.append(pack)
        chip_pack.append(swap_chip(pack))
        out, a2, act, slope = mlp_forward(mid, weights[2 * l + 1], fc1_all[l], mlp_norms)
        pack, out, chip_pack[2] = tie(mlp_pack(1), out, chip_pack[2])
        own_pack.append(pack)
        chip_pack.append(swap_chip(pack))
        saved.append((hidden, mid, a, qkv, probs, attn, norms, mlp_norms, a2, act, slope))
        hidden = out
    grad = gather_slots(table, outputs_grad, swap_core(outputs_grad), border(outputs_grad), bins)

    def give_back(value):
        slots = value.reshape(bins, PAD, D)
        edge = lax.dynamic_slice_in_dim(slots, table[SEND], 4, 0)
        return slots, swap_core(slots), swap_border(edge)

    def mlp_back(l, grad):
        return mlp_backward(
            grad, saved[l][1], saved[l][8], saved[l][9], saved[l][10], weights[2 * l + 1],
            saved[l][7],
        )

    def attn_back(l, grad):
        return attn_backward(table, grad, saved[l][3], saved[l][4], weights[2 * l], l % 2 == 1)

    def attn_sums(l, grad, gqkv, scores, small_mlp, fc1_bias_grad):
        return attn_grads(
            table, grad, saved[l][0], saved[l][2], saved[l][5], gqkv, scores, small_mlp,
            fc1_bias_grad, weights[2 * l], saved[l][6], l % 2 == 1,
        )

    def core_sum(keep, other):
        return [(keep[i].astype(F32) + other[i].astype(F32)).astype(LOW) for i in range(2)]

    steps = dp_steps()
    out, grad, keep_a, send_a, small_mlp, fc1_bias_grad = mlp_turn(
        saved[last][1], grad, weights[2 * last + 1], fc1_all[last], saved[last][7]
    )
    core_a = swap_core(send_a)
    gqkv, scores = attn_back(1, grad)
    gqkv, core_a = tie(gqkv, core_a)
    half_a, out_a = core_sum(keep_a, core_a)
    gqkv, out_a = tie(gqkv, out_a)
    chip_a = swap_chip(out_a)
    grad, keep_b, send_b = attn_sums(1, grad, gqkv, scores, small_mlp, fc1_bias_grad)
    core_b = swap_core(send_b)
    grad, keep_c, send_c, small_mlp, fc1_bias_grad = mlp_back(0, grad)
    send_c, chip_a, core_b = tie(send_c, chip_a, core_b)
    core_c = swap_core(send_c)
    state_a = dp_start((half_a, chip_a))
    half_b, out_b = core_sum(keep_b, core_b)
    half_c, out_c = core_sum(keep_c, core_c)
    grad, out_b, out_c = tie(grad, out_b, out_c)
    chip_b, chip_c = swap_chip(out_b), swap_chip(out_c)
    gqkv, scores = attn_back(0, grad)
    gqkv, other_a = tie(gqkv, state_a[1])
    state_a = dp_middle(state_a[0], other_a, steps[0])
    grad, keep_d, send_d = attn_sums(0, grad, gqkv, scores, small_mlp, fc1_bias_grad)
    send_d, other_a, chip_b, chip_c = tie(send_d, state_a[1], chip_b, chip_c)
    core_d = swap_core(send_d)
    core_d, out = tie(core_d, out)
    output_parts = give_back(out)
    half_d, out_d = core_sum(keep_d, core_d)
    chip_d = swap_chip(out_d)
    total_a = dp_finish((state_a[0], other_a), steps[1:])
    total_b = dp_finish(dp_start((half_b, chip_b)), steps)
    total_c = dp_finish(dp_start((half_c, chip_c)), steps)
    output = return_slots(table, *output_parts, own)
    tokens_grad = return_slots(table, *give_back(grad), own)
    mlp_all = jnp.stack([total_c, total_a]).astype(F32)
    fc1_out = mlp_all[:, :D]
    fc2_out = mlp_all[:, D:].transpose(0, 2, 1)
    state_d = dp_start((half_d, chip_d))
    for step in steps:
        state_d = dp_middle(*state_d, step)
    value_d, other_d = dp_last(*state_d)
    value_d, fc1_out, fc2_out, output, tokens_grad = tie(
        value_d, fc1_out, fc2_out, output, tokens_grad
    )
    total_d = dp_join(value_d, other_d)

    attn_all = jnp.stack([total_d, total_b]).astype(F32)
    total = attn_all[:, D:]
    gains_out = jnp.stack([total[:, 0], total[:, 3]], axis=1)
    shifts_out = jnp.stack([total[:, 1], total[:, 4], total[:, 2], total[:, 5]], axis=1)
    fc1_bias_out = total[:, 6]
    qv_out = total[:, 7:9, 0:96]
    table_out = total[:, 9:12, 0:169].transpose(0, 2, 1)
    qkv_out = attn_all[:, 0:288].reshape(LAYERS, 3, 96, D).transpose(0, 3, 1, 2)
    proj_out = attn_all[:, 288:384]
    return (
        output, tokens_grad, qkv_out, qv_out, table_out, proj_out, fc1_out, fc1_bias_out,
        fc2_out, gains_out, shifts_out,
    )


def solution(mesh):
    rows = P(("dp", "head"), None)
    placed = (
        rows,
        rows,
        P("dp", None),
        P(None, None, None, "head"),
        P(None, None, "head"),
        P(None, None, "head"),
        P(None, "head", None),
        P(None, None, "head"),
        P(None, "head"),
        P(None, "head", None),
        P(),
        P(),
    )
    return jax.shard_map(
        body,
        mesh=mesh,
        in_specs=placed,
        out_specs=(
            rows,
            rows,
            P(None, None, None, "head"),
            P(None, None, "head"),
            P(None, None, "head"),
            P(None, "head", None),
            P(None, None, "head"),
            P(None, "head"),
            P(None, "head", None),
            P(),
            P(),
        ),
        check_vma=False,
    )
```

```python
import jax
import jax.numpy as jnp
from jax import lax
from jax.experimental import pallas as pl
from jax.experimental.pallas import tpu as pltpu
from jax.sharding import PartitionSpec as P

D = 384
FF = 1536
LAYERS = 2
PLACES = 49
PAD = 56
WIDE = 64
QUADS = 3
HEAD_DIM = 32
SCORE_SCALE = HEAD_DIM**-0.5
LN_EPS = 1e-05
LOW = jnp.bfloat16
F32 = jnp.float32
MIB = 1024 * 1024
SMALL = 16

SRC, SIDE, WROW, WCOL, FIRST, RET, SEND = 0, 24, 48, 72, 96, 120, 140
TABLE = 144


def vmem():
    return pl.BlockSpec(memory_space=pltpu.VMEM)


def smem():
    return pl.BlockSpec(memory_space=pltpu.SMEM)


def anywhere():
    return pl.BlockSpec(memory_space=pl.ANY)


def params(limit):
    return pltpu.CompilerParams(vmem_limit_bytes=limit * MIB)


def cost(flops, size):
    return pl.CostEstimate(flops=int(flops * 0.02), bytes_accessed=int(size * 0.02), transcendentals=0)


def dot_nn(a, b):
    return lax.dot_general(a, b, (((1,), (0,)), ((), ())), preferred_element_type=F32)


def dot_nt(a, b):
    return lax.dot_general(a, b, (((1,), (1,)), ((), ())), preferred_element_type=F32)


def dot_tn(a, b):
    return lax.dot_general(a, b, (((0,), (0,)), ((), ())), preferred_element_type=F32)


def plan_kernel(own, bins, kind_ref, me_ref, out_ref, load_ref):
    me = me_ref[0]
    half = 2 * own
    for i in range(TABLE):
        out_ref[i] = -1 if i < bins or RET <= i < RET + own else 0
    for i in range(bins):
        out_ref[SIDE + i] = 1
        out_ref[FIRST + i] = i
    for i in range(4):
        load_ref[i] = 0

    def place(start, count, side, bin_id):
        base = load_ref[bin_id]
        load_ref[bin_id] = base + count

        def step(k, carry):
            slot = start + k
            owner = slot // own
            inner = slot - owner * own
            local = base + k
            mine = bin_id == me
            halo = jnp.where(me == 1, slot - half, slot - half + 4)
            code = jnp.where(
                owner == me, inner, jnp.where(owner == (me ^ 1), own + inner, 2 * own + halo)
            )

            @pl.when(mine)
            def _():
                wrow = k // side
                out_ref[SRC + local] = code
                out_ref[SIDE + local] = side
                out_ref[WROW + local] = wrow
                out_ref[WCOL + local] = k - wrow * side
                out_ref[FIRST + local] = base

            @pl.when(owner == me)
            def _():
                back = jnp.where(me == 2, slot - half, k)
                out_ref[RET + inner] = jnp.where(
                    mine, local, jnp.where(bin_id == (me ^ 1), bins + local, 2 * bins + back)
                )

            return carry

        lax.fori_loop(0, count, step, 0)

    for turn in range(3):

        def visit(i, start, turn=turn):
            kind = kind_ref[0, i]
            count = jnp.where(kind == 2, 9, jnp.where(kind == 1, 4, 0))
            side = jnp.where(kind == 2, 3, 2)
            cut = half - start
            across = (cut > 0) & (cut < count)
            second = (start >= half) | (across & (cut < count - cut))
            chip = jnp.where(second, 1, 0)
            left, right = load_ref[2 * chip], load_ref[2 * chip + 1]
            emptier = 2 * chip + jnp.where(left <= right, 0, 1)
            if turn == 0:
                chosen, bin_id = across, 1 + chip
            else:
                chosen, bin_id = (kind == 3 - turn) & jnp.logical_not(across), emptier

            @pl.when(chosen)
            def _():
                place(start, count, side, bin_id)
                if turn == 0:
                    out_ref[SEND] = jnp.where((me == 1) & (chip == 0), cut, 0)

            return start + count

        lax.fori_loop(0, kind_ref.shape[1], visit, jnp.int32(0))


def gather_kernel(bins, table_ref, refs, out_ref, spread_ref):
    spread_ref[...] = jnp.zeros(spread_ref.shape, F32)
    at = 0
    for ref in refs:
        for s in range(ref.shape[0] // PLACES):
            spread_ref[at, 0:PLACES] = ref[s * PLACES : (s + 1) * PLACES].astype(F32)
            at += 1

    def step(j, carry):
        src = table_ref[SRC + j]

        @pl.when(src < 0)
        def _():
            out_ref[j] = jnp.zeros((PAD, D), F32)

        @pl.when(src >= 0)
        def _():
            out_ref[j] = spread_ref[src]

        return carry

    lax.fori_loop(0, bins, step, 0)


def make_plan(image_kind, me, own, bins):
    def kernel(kind_ref, me_ref, table_ref, load_ref):
        plan_kernel(own, bins, kind_ref, me_ref, table_ref, load_ref)

    return pl.pallas_call(
        kernel,
        out_shape=jax.ShapeDtypeStruct((TABLE,), jnp.int32),
        in_specs=[smem(), smem()],
        out_specs=smem(),
        scratch_shapes=[pltpu.SMEM((4,), jnp.int32)],
        compiler_params=params(1),
        cost_estimate=cost(0, 1.5e7),
        name="plan",
    )(image_kind, me.reshape(1))


def gather_slots(table, mine, partner, halo, bins):
    own = mine.shape[0] // PLACES

    def kernel(table_ref, *refs):
        gather_kernel(bins, table_ref, refs[:3], refs[3], refs[4])

    out = pl.pallas_call(
        kernel,
        out_shape=jax.ShapeDtypeStruct((bins, PAD, D), F32),
        in_specs=[smem()] + [vmem()] * 3,
        out_specs=vmem(),
        scratch_shapes=[pltpu.VMEM((2 * own + 4, PAD, D), F32)],
        compiler_params=params(8),
        cost_estimate=cost(0, 8e6),
        name="gather_slots",
    )(table, mine, partner, halo)
    return out.reshape(bins * PAD, D)


def border_slots(table, slots):
    def kernel(table_ref, slots_ref, out_ref):
        start = table_ref[SEND]
        for j in range(4):
            out_ref[j] = slots_ref[start + j]

    return pl.pallas_call(
        kernel,
        out_shape=jax.ShapeDtypeStruct((4,) + slots.shape[1:], F32),
        in_specs=[smem(), vmem()],
        out_specs=vmem(),
        compiler_params=params(1),
        cost_estimate=cost(0, 1e6),
        name="border_slots",
    )(table, slots)


def return_slots(table, mine, partner, halo, own):
    bins = mine.shape[0]

    def kernel(table_ref, mine_ref, partner_ref, halo_ref, out_ref):
        for s in range(own):
            src = table_ref[RET + s]
            rows = pl.ds(s * PLACES, PLACES)

            @pl.when(src < 0)
            def _():
                out_ref[rows] = jnp.zeros((PLACES, D), F32)

            @pl.when((src >= 0) & (src < bins))
            def _():
                out_ref[rows] = mine_ref[src, 0:PLACES]

            @pl.when((src >= bins) & (src < 2 * bins))
            def _():
                out_ref[rows] = partner_ref[src - bins, 0:PLACES]

            @pl.when(src >= 2 * bins)
            def _():
                out_ref[rows] = halo_ref[src - 2 * bins, 0:PLACES]

    return pl.pallas_call(
        kernel,
        out_shape=jax.ShapeDtypeStruct((own * PLACES, D), F32),
        in_specs=[smem(), vmem(), vmem(), vmem()],
        out_specs=vmem(),
        compiler_params=params(2),
        cost_estimate=cost(0, 8e6),
        name="return_slots",
    )(table, mine, partner, halo)


def norm_rows(rows):
    average = jnp.mean(rows, axis=-1, keepdims=True)
    centred = rows - average
    inverse = lax.rsqrt(jnp.mean(centred * centred, axis=-1, keepdims=True) + LN_EPS)
    return centred * inverse, inverse


def norm_back(incoming, scaled, inverse, gain):
    weighted = incoming * gain
    return inverse * (
        weighted
        - jnp.mean(weighted, axis=-1, keepdims=True)
        - scaled * jnp.mean(weighted * scaled, axis=-1, keepdims=True)
    )


def gelu_parts(x):
    size = jnp.abs(x) * 0.7071067811865476
    t = 1.0 / (1.0 + 0.3275911 * size)
    bell = jnp.exp(-0.5 * x * x)
    poly = t * (
        0.127414796 + t * (-0.142248368 + t * (0.7107068705 + t * (-0.7265760135 + t * 0.5307027145)))
    )
    tail = poly * bell
    phi = jnp.where(x >= 0, 1.0 - tail, tail)
    return x * phi, phi + x * bell * 0.3989422804014327


def place_parts(shape, dim):
    place = lax.broadcasted_iota(jnp.int32, shape, dim)
    row = (place * 37) >> 8
    return place, row, place - 7 * row


def fill_moves(table_ref, out_ref, bins, back):
    width = out_ref.shape[1]
    place, row, col = place_parts((PAD, 1), 0)
    if back:
        row_other, col_other = row < 3, col < 3
        inner = 7 * jnp.where(row_other, row + 4, row - 3) + jnp.where(col_other, col + 4, col - 3)
    else:
        row_other, col_other = row >= 4, col >= 4
        inner = 7 * jnp.where(row_other, row - 4, row + 3) + jnp.where(col_other, col - 4, col + 3)
    lanes = lax.broadcasted_iota(jnp.int32, (2 * PAD, width), 1)

    def source(w):
        side, wrow, wcol = table_ref[SIDE + w], table_ref[WROW + w], table_ref[WCOL + w]
        first = table_ref[FIRST + w]
        if back:
            orow = jnp.where(wrow == 0, side - 1, wrow - 1)
            ocol = jnp.where(wcol == 0, side - 1, wcol - 1)
        else:
            orow = jnp.where(wrow == side - 1, 0, wrow + 1)
            ocol = jnp.where(wcol == side - 1, 0, wcol + 1)
        slot = first + jnp.where(row_other, orow, wrow) * side + jnp.where(col_other, ocol, wcol)
        return jnp.where(place < PLACES, slot * PAD + inner, w * PAD + place)

    def step(j, carry):
        rows = jnp.concatenate([source(2 * j), source(2 * j + 1)], axis=0)
        hot = jnp.where(lanes == rows, 1.0, 0.0).astype(LOW)
        out_ref[pl.ds(pl.multiple_of(j * 2 * PAD, 16), 2 * PAD)] = hot
        return carry

    lax.fori_loop(0, bins // 2, step, 0)


def head_marks():
    lane = lax.broadcasted_iota(jnp.int32, (WIDE, 128), 1) // HEAD_DIM
    return [jnp.where(lane == h, 1.0, 0.0).astype(LOW) for h in range(4)]


def spread(block, marks):
    return jnp.concatenate([block * mark for mark in marks], axis=0)


def fold(product, marks):
    total = None
    for h, mark in enumerate(marks):
        part = product[h * WIDE : (h + 1) * WIDE] * mark.astype(F32)
        total = part if total is None else total + part
    return total


def spread_pair(block, marks):
    return jnp.concatenate([spread(block[0:WIDE], marks), spread(block[WIDE:], marks)], axis=1)


def diagonal(block):
    zero = jnp.zeros((WIDE, 128), block.dtype)
    top = jnp.concatenate([block[0:WIDE], zero], axis=1)
    return jnp.concatenate([top, jnp.concatenate([zero, block[WIDE:]], axis=1)], axis=0)


def by_head(values):
    return values.reshape(4, WIDE, 128)


def pad_rows(rows):
    return jnp.concatenate([rows, jnp.zeros((WIDE - PAD, rows.shape[1]), rows.dtype)], axis=0)


def split(values):
    high = values.astype(LOW)
    return high, (values - high.astype(F32)).astype(LOW)


def marks_where(rows, cols, test):
    row = lax.broadcasted_iota(jnp.int32, (rows, cols), 0)
    col = lax.broadcasted_iota(jnp.int32, (rows, cols), 1)
    return jnp.where(test(row, col), 1.0, 0.0).astype(LOW)


def far(place):
    row = (place * 37) >> 8
    return 13 * row + (place - 7 * row)


def spread_smalls(smalls):
    heads = LAYERS * 12

    def kernel(s0, s1, s2, s3, out_ref, qkv_ref, fc1_ref, table_ref):
        quarters = (s0, s1, s2, s3)
        for k, ref in enumerate(quarters):
            for l in range(LAYERS):
                at = l * 12 + k * 3
                table_ref[at : at + 3] = ref[l * 3 : l * 3 + 3, 0:256]
        lane = lax.broadcasted_iota(jnp.int32, (8, D), 1)
        for l in range(LAYERS):
            for c in range(3):
                total = jnp.zeros((8, D), F32)
                for k, ref in enumerate(quarters):
                    if c != 1:
                        row = jnp.broadcast_to(ref[6:7], (8, D))
                        row = pltpu.roll(row, (k * 96 - l * 192 - (c // 2) * 96) % D, 1)
                        own_lanes = (lane >= k * 96) & (lane < k * 96 + 96)
                        total = total + jnp.where(own_lanes, row, 0.0)
                qkv_ref[l, :, c * D : (c + 1) * D] = total
            for k, ref in enumerate(quarters):
                row = jnp.broadcast_to(ref[7 + l : 8 + l], (8, D))
                fc1_ref[l, :, k * D : (k + 1) * D] = row
        to_lane = marks_where(128, 128, lambda r, c: (far(c & 63) == r) & ((c & 63) < PLACES))
        to_row = marks_where(WIDE, 96, lambda r, c: (far(r) == c) & (r < PLACES))
        place = lax.broadcasted_iota(jnp.int32, (WIDE, 128), 0)
        empty = jnp.where(place < PLACES, 0.0, -1e30)
        turned = pltpu.roll(table_ref[...], 172, 1)
        skewed = []
        for n in range(heads):
            row = jnp.broadcast_to(turned[n : n + 1], (96, 256))
            skewed.append(pltpu.roll(row, 0, 1, stride=1, stride_axis=0)[:, 0:128])
        skewed = jnp.concatenate(skewed, axis=1)
        total = None
        for part in split(skewed):
            rows = dot_nn(to_row, part).astype(LOW)
            rows = jnp.concatenate([rows[:, n * 128 : (n + 1) * 128] for n in range(heads)], axis=0)
            part = dot_nn(rows, to_lane)
            total = part if total is None else total + part
        for n in range(heads):
            l, t, h = n // 12, n % 12 // 4, n % 4
            out_ref[l, t, h * WIDE : (h + 1) * WIDE] = total[n * WIDE : (n + 1) * WIDE] + empty

    return pl.pallas_call(
        kernel,
        out_shape=(
            jax.ShapeDtypeStruct((LAYERS, QUADS, 4 * WIDE, 128), F32),
            jax.ShapeDtypeStruct((LAYERS, 8, 3 * D), F32),
            jax.ShapeDtypeStruct((LAYERS, 8, FF), F32),
        ),
        in_specs=[vmem()] * 4,
        out_specs=[vmem()] * 3,
        scratch_shapes=[pltpu.VMEM((heads, 256), F32)],
        compiler_params=params(6),
        cost_estimate=cost(0, 1e7),
        name="spread_smalls",
    )(*smalls)


def scores_to_table(scores_ref):
    to_far = marks_where(128, 128, lambda r, c: (far(r & 63) == c) & ((r & 63) < PLACES))
    to_row = marks_where(96, WIDE, lambda r, c: (84 - far(c) == r) & (c < PLACES))
    wide = None
    for part in split(scores_ref[...].reshape(12 * WIDE, 128)):
        part = dot_nn(part, to_far)
        wide = part if wide is None else wide + part
    wide = jnp.concatenate([wide[h * WIDE : (h + 1) * WIDE] for h in range(12)], axis=1)
    rows = None
    for part in split(wide):
        part = dot_nn(to_row, part)
        rows = part if rows is None else rows + part
    out = []
    for h in range(12):
        one = rows[:, h * 128 : (h + 1) * 128]
        one = jnp.concatenate([one, jnp.zeros_like(one)], axis=1)
        one = pltpu.roll(one, 0, 1, stride=1, stride_axis=0)
        out.append(jnp.sum(one, axis=0, keepdims=True))
    return out


def stack_qkv(pieces, out_ref):
    for k, piece in enumerate(pieces):
        for c in range(3):
            out_ref[c * D + k * 96 : c * D + (k + 1) * 96] = piece[c * 96 : (c + 1) * 96]


def stack_proj(pieces, out_ref):
    for k, piece in enumerate(pieces):
        out_ref[k * 96 : (k + 1) * 96] = piece[288:384]


def stack_mlp(pieces, fc1_ref, fc2_ref):
    for k, piece in enumerate(pieces):
        fc1_ref[:, k * D : (k + 1) * D] = piece[0:D]
        fc2_ref[k * D : (k + 1) * D] = piece[D : 2 * D]


def attn_forward(table, hidden, weights, qv_bias, bias, norms, layer):
    shifted = layer % 2 == 1
    rows = hidden.shape[0]
    bins = rows // PAD
    chunk_slots = 6
    chunk = chunk_slots * PAD
    wide_rows = -(-rows // 128) * 128

    def kernel(
        table_ref, hidden_ref, w0, w1, w2, w3, qv_ref, bias_ref, norm_ref,
        mid_ref, a_ref, qkv_ref, p_ref, attn_ref,
        wqkv, wproj, wide_attn, moves,
    ):
        pieces = (w0, w1, w2, w3)
        stack_qkv(pieces, wqkv)
        stack_proj(pieces, wproj)
        gain, shift, proj_shift = norm_ref[0:1], norm_ref[1:2], norm_ref[2:3]
        marks = head_marks()
        dest = attn_ref if shifted else a_ref

        def norm_step(i, carry):
            at = pl.ds(pl.multiple_of(i * chunk, 16), chunk)
            scaled, _ = norm_rows(hidden_ref[at])
            dest[at] = (scaled * gain + shift).astype(LOW)
            return carry

        lax.fori_loop(0, bins // chunk_slots, norm_step, 0)
        if shifted:
            fill_moves(table_ref, moves, bins, False)
            a_ref[...] = dot_nn(moves[:, 0:rows], dest[...]).astype(LOW)
            fill_moves(table_ref, moves, bins, True)

        def qkv_step(i, carry):
            at = pl.ds(pl.multiple_of(i * chunk, 16), chunk)
            project = dot_nt(a_ref[at], wqkv[...]) + qv_ref[layer, 0:1]
            for j in range(chunk_slots):
                block = project[j * PAD : (j + 1) * PAD]
                at = pl.ds((j % 2) * WIDE, WIDE)
                qkv_ref[i * (chunk_slots // 2) + j // 2, at] = pad_rows(block).astype(LOW)
            return carry

        lax.fori_loop(0, bins // chunk_slots, qkv_step, 0)

        if shifted:
            _, qrow, qcol = place_parts((WIDE, 1), 0)
            lane = lax.broadcasted_iota(jnp.int32, (1, 128), 1)
            second = lane >= WIDE
            pplace = jnp.where(second, lane - WIDE, lane)
            prow = (pplace * 37) >> 8
            pcol = pplace - 7 * prow
            pband = 1 + (prow >= 4).astype(jnp.int32), 1 + (pcol >= 4).astype(jnp.int32)
            qband = 1 + (qrow >= 4).astype(jnp.int32), 1 + (qcol >= 4).astype(jnp.int32)

        def window(j, carry):
            if shifted:
                low = []
                for w in (2 * j, 2 * j + 1):
                    side = table_ref[SIDE + w]
                    low.append(
                        (
                            jnp.where(table_ref[WROW + w] == side - 1, 3, 0),
                            jnp.where(table_ref[WCOL + w] == side - 1, 1, 0),
                        )
                    )
                low_row = jnp.where(second, low[1][0], low[0][0])
                low_col = jnp.where(second, low[1][1], low[0][1])
                pregion = low_row * pband[0] + low_col * pband[1]
                qregion = low_row * qband[0] + low_col * qband[1]
                mask = jnp.where(pregion != qregion, -100.0, 0.0)[None]
            for t in range(QUADS):
                cols = slice(t * 128, (t + 1) * 128)
                q = qkv_ref[j, :, t * 128 : (t + 1) * 128]
                k = qkv_ref[j, :, D + t * 128 : D + (t + 1) * 128]
                v = qkv_ref[j, :, 2 * D + t * 128 : 2 * D + (t + 1) * 128]
                scores = dot_nt(spread_pair(k, marks), diagonal(q)) * SCORE_SCALE + bias_ref[layer, t]
                scores = by_head(scores)
                if shifted:
                    scores = scores + mask
                exponent = jnp.exp(scores - jnp.max(scores, axis=1, keepdims=True))
                total = jnp.sum(exponent, axis=1, keepdims=True)
                probs = (exponent * (1.0 / total)).reshape(4 * WIDE, 128).astype(LOW)
                p_ref[j, t] = probs
                both = dot_tn(probs, spread_pair(v, marks))
                at = pl.multiple_of(j * 2 * PAD, 16)
                wide_attn[pl.ds(at, PAD), cols] = both[0:PAD, 0:128]
                wide_attn[pl.ds(at + PAD, PAD), cols] = both[WIDE : WIDE + PAD, 128:256]
            return carry

        lax.fori_loop(0, bins // 2, window, 0)
        if shifted:
            attn_ref[...] = dot_nn(moves[:, 0:rows], wide_attn[...].astype(LOW)).astype(LOW)
        else:
            attn_ref[...] = wide_attn[...].astype(LOW)

        def proj_step(i, carry):
            at = pl.ds(pl.multiple_of(i * chunk, 16), chunk)
            mid_ref[at] = hidden_ref[at] + dot_nn(attn_ref[at], wproj[...]) + proj_shift
            return carry

        lax.fori_loop(0, bins // chunk_slots, proj_step, 0)

    return pl.pallas_call(
        kernel,
        out_shape=(
            jax.ShapeDtypeStruct((rows, D), F32),
            jax.ShapeDtypeStruct((rows, D), LOW),
            jax.ShapeDtypeStruct((bins // 2, 2 * WIDE, 3 * D), LOW),
            jax.ShapeDtypeStruct((bins // 2, QUADS, 4 * WIDE, 128), LOW),
            jax.ShapeDtypeStruct((rows, D), LOW),
        ),
        in_specs=[smem()] + [vmem()] * 8,
        out_specs=[vmem()] * 5,
        scratch_shapes=[
            pltpu.VMEM((3 * D, D), LOW),
            pltpu.VMEM((D, D), LOW),
            pltpu.VMEM((rows, D), F32),
            pltpu.VMEM((rows if shifted else 16, wide_rows), LOW),
        ],
        compiler_params=params(8),
        cost_estimate=cost(1e10, 2e7),
        name="attn_forward",
    )(table, hidden, *weights, qv_bias, bias, norms)


def attn_backward(table, grad, qkv, probs, weights, shifted):
    rows = grad.shape[0]
    bins = rows // PAD
    chunk_slots = 6
    chunk = chunk_slots * PAD
    wide_rows = -(-rows // 128) * 128

    def kernel(
        table_ref, grad_ref, qkv_ref, p_ref, w0, w1, w2, w3,
        gqkv_ref, scores_ref, wproj, wide_attn, low_wide, moves,
    ):
        stack_proj((w0, w1, w2, w3), wproj)
        marks = head_marks()
        steps = bins // chunk_slots
        if shifted:
            fill_moves(table_ref, moves, bins, False)

        def keep_windows(i, block_rows):
            for j in range(chunk_slots):
                block = block_rows[j * PAD : (j + 1) * PAD]
                dest = pl.ds((j % 2) * WIDE, WIDE)
                wide_attn[i * (chunk_slots // 2) + j // 2, dest] = pad_rows(block).astype(LOW)

        def proj_step(i, carry):
            at = pl.ds(pl.multiple_of(i * chunk, 16), chunk)
            gattn = dot_nt(grad_ref[at].astype(LOW), wproj[...])
            if shifted:
                low_wide[at] = gattn.astype(LOW)
            else:
                keep_windows(i, gattn)
            return carry

        lax.fori_loop(0, steps, proj_step, 0)
        if shifted:

            def move_step(i, carry):
                at = pl.ds(pl.multiple_of(i * chunk, 16), chunk)
                keep_windows(i, dot_nn(moves[at, 0:rows], low_wide[...]))
                return carry

            lax.fori_loop(0, steps, move_step, 0)

        scores_ref[...] = jnp.zeros((QUADS, 4 * WIDE, 128), F32)

        def window(j, carry):
            for t in range(QUADS):
                q = qkv_ref[j, :, t * 128 : (t + 1) * 128]
                k = qkv_ref[j, :, D + t * 128 : D + (t + 1) * 128]
                v = qkv_ref[j, :, 2 * D + t * 128 : 2 * D + (t + 1) * 128]
                low_probs = p_ref[j, t]
                p = by_head(low_probs.astype(F32))
                go = diagonal(wide_attn[j, :, t * 128 : (t + 1) * 128])
                gp = by_head(dot_nt(spread_pair(v, marks), go))
                ds = p * (gp - jnp.sum(gp * p, axis=1, keepdims=True))
                low_ds = ds.reshape(4 * WIDE, 128).astype(LOW)
                scores_ref[t] += low_ds.astype(F32)
                gq = dot_tn(low_ds, spread_pair(k, marks)) * SCORE_SCALE
                gk = dot_nn(low_ds, diagonal(q)) * SCORE_SCALE
                gv = dot_nn(low_probs, go)
                at = pl.ds(pl.multiple_of(j * 2 * PAD, 16), 2 * PAD)
                left, right = slice(0, 128), slice(128, 256)
                parts = (
                    (gq[0:PAD, left], gq[WIDE : WIDE + PAD, right]),
                    (fold(gk[:, left], marks)[0:PAD], fold(gk[:, right], marks)[0:PAD]),
                    (fold(gv[:, left], marks)[0:PAD], fold(gv[:, right], marks)[0:PAD]),
                )
                for c, part in enumerate(parts):
                    cols = slice(c * D + t * 128, c * D + (t + 1) * 128)
                    gqkv_ref[at, cols] = jnp.concatenate(part, axis=0).astype(LOW)
            return carry

        lax.fori_loop(0, bins // 2, window, 0)

    return pl.pallas_call(
        kernel,
        out_shape=(
            jax.ShapeDtypeStruct((rows, 3 * D), LOW),
            jax.ShapeDtypeStruct((QUADS, 4 * WIDE, 128), F32),
        ),
        in_specs=[smem()] + [vmem()] * 7,
        out_specs=[vmem()] * 2,
        scratch_shapes=[
            pltpu.VMEM((D, D), LOW),
            pltpu.VMEM((bins // 2, 2 * WIDE, D), LOW),
            pltpu.VMEM((rows, D), LOW),
            pltpu.VMEM((rows if shifted else 16, wide_rows), LOW),
        ],
        compiler_params=params(8),
        cost_estimate=cost(1e10, 2e7),
        name="attn_backward",
    )(table, grad, qkv, probs, *weights)


def attn_grads(
    table, grad, hidden, a, attn, gqkv, scores, small_mlp, fc1_bias_grad, weights, norms, shifted
):
    rows = hidden.shape[0]
    bins = rows // PAD
    chunk = 6 * PAD
    steps = rows // chunk
    wide_rows = -(-rows // 128) * 128

    def kernel(
        table_ref, grad_ref, hidden_ref, a_ref, attn_ref, gqkv_ref, scores_ref, mlp_ref, fc1b_ref,
        w0, w1, w2, w3, norm_ref,
        out_ref, keep_ref, send_ref, wqkv, low_wide, small, moves,
    ):
        stack_qkv((w0, w1, w2, w3), wqkv)
        gain = norm_ref[0:1]
        if shifted:
            fill_moves(table_ref, moves, bins, True)
            low_wide[...] = dot_nn(gqkv_ref[...], wqkv[...]).astype(LOW)

        def back_step(i, totals):
            at = pl.ds(pl.multiple_of(i * chunk, 16), chunk)
            if shifted:
                ga = dot_nn(moves[at, 0:rows], low_wide[...])
            else:
                ga = dot_nn(gqkv_ref[at], wqkv[...])
            scaled, inverse = norm_rows(hidden_ref[at])
            grad_now = grad_ref[at]
            out_ref[at] = grad_now + norm_back(ga, scaled, inverse, gain)
            return (
                totals[0] + jnp.sum(ga * scaled, axis=0, keepdims=True),
                totals[1] + jnp.sum(ga, axis=0, keepdims=True),
                totals[2] + jnp.sum(grad_now.astype(LOW).astype(F32), axis=0, keepdims=True),
                totals[3] + jnp.sum(gqkv_ref[at].astype(F32), axis=0, keepdims=True),
            )

        zero = jnp.zeros((1, D), F32)
        sums = lax.fori_loop(0, steps, back_step, (zero, zero, zero, jnp.zeros((1, 3 * D), F32)))
        table_rows = scores_to_table(scores_ref)
        dproj = dot_tn(attn_ref[...], grad_ref[...].astype(LOW)).astype(LOW)
        dqkv = dot_tn(a_ref[...], gqkv_ref[...])
        turned = [dqkv[:, c * D : (c + 1) * D].T.astype(LOW) for c in range(3)]
        small[...] = jnp.zeros((SMALL, D), F32)
        for i in range(3):
            small[i : i + 1] = sums[i]
        small[3:6] = mlp_ref[0:3]
        gq_sum = jnp.broadcast_to(sums[3][:, 0:D], (8, D))
        gv_sum = jnp.broadcast_to(sums[3][:, 2 * D : 3 * D], (8, D))
        for k in range(4):
            dest = keep_ref if k < 2 else send_ref
            for c in range(3):
                dest[k % 2, c * 96 : (c + 1) * 96] = turned[c][k * 96 : (k + 1) * 96]
            dest[k % 2, 288:384] = dproj[k * 96 : (k + 1) * 96]
            small[6:7] = fc1b_ref[:, k * D : (k + 1) * D]
            small[7:8] = pltpu.roll(gq_sum, (D - k * 96) % D, 1)[0:1]
            small[8:9] = pltpu.roll(gv_sum, (D - k * 96) % D, 1)[0:1]
            for h in range(3):
                small[9 + h : 10 + h, 0:256] = table_rows[3 * k + h]
            dest[k % 2, D : D + SMALL] = small[...].astype(LOW)

    return pl.pallas_call(
        kernel,
        out_shape=(
            jax.ShapeDtypeStruct((rows, D), F32),
            jax.ShapeDtypeStruct((2, D + SMALL, D), LOW),
            jax.ShapeDtypeStruct((2, D + SMALL, D), LOW),
        ),
        in_specs=[smem()] + [vmem()] * 13,
        out_specs=[vmem()] * 3,
        scratch_shapes=[
            pltpu.VMEM((3 * D, D), LOW),
            pltpu.VMEM((rows, D), LOW),
            pltpu.VMEM((SMALL, D), F32),
            pltpu.VMEM((rows if shifted else 16, wide_rows), LOW),
        ],
        compiler_params=params(10),
        cost_estimate=cost(6e9, 2e7),
        name="attn_grads",
    )(
        table, grad, hidden, a, attn, gqkv, scores, small_mlp, fc1_bias_grad, *weights, norms
    )


def mlp_forward(mid, weights, fc1_bias, norms, layer):
    rows = mid.shape[0]
    chunk = 3 * PAD * 2
    steps = rows // chunk

    def kernel(
        mid_ref, w0, w1, w2, w3, fc1_bias_ref, norm_ref,
        out_ref, act_ref, slope_ref, fc1, fc2,
    ):
        stack_mlp((w0, w1, w2, w3), fc1, fc2)
        gain, shift, out_shift = norm_ref[0:1], norm_ref[1:2], norm_ref[2:3]

        def step(i, carry):
            at = pl.ds(pl.multiple_of(i * chunk, 16), chunk)
            rows_now = mid_ref[at]
            scaled, _ = norm_rows(rows_now)
            a = (scaled * gain + shift).astype(LOW)
            act, slope = gelu_parts(dot_nn(a, fc1[...]) + fc1_bias_ref[layer, 0:1])
            act = act.astype(LOW)
            act_ref[at] = act
            slope_ref[at] = slope.astype(LOW)
            out_ref[at] = rows_now + dot_nn(act, fc2[...]) + out_shift
            return carry

        lax.fori_loop(0, steps, step, 0)

    return pl.pallas_call(
        kernel,
        out_shape=(
            jax.ShapeDtypeStruct((rows, D), F32),
            jax.ShapeDtypeStruct((rows, FF), LOW),
            jax.ShapeDtypeStruct((rows, FF), LOW),
        ),
        in_specs=[vmem()] * 7,
        out_specs=[vmem()] * 3,
        scratch_shapes=[pltpu.VMEM((D, FF), LOW), pltpu.VMEM((FF, D), LOW)],
        compiler_params=params(8),
        cost_estimate=cost(7e9, 2e7),
        name="mlp_forward",
    )(mid, *weights, fc1_bias, norms)


def mlp_backward(grad, mid, act, slope, weights, norms):
    rows = mid.shape[0]
    chunk = 3 * PAD * 2
    steps = rows // chunk

    def kernel(
        grad_ref, mid_ref, act_ref, slope_ref, w0, w1, w2, w3, norm_ref,
        out_ref, keep_ref, send_ref, small_ref, bias_ref, fc1, fc2, low_grad, gpre_ref, a_ref,
    ):
        stack_mlp((w0, w1, w2, w3), fc1, fc2)
        gain, shift = norm_ref[0:1], norm_ref[1:2]

        def step(i, totals):
            at = pl.ds(pl.multiple_of(i * chunk, 16), chunk)
            grad_now = grad_ref[at]
            gz = grad_now.astype(LOW)
            low_grad[at] = gz
            gpre = (dot_nt(gz, fc2[...]) * slope_ref[at].astype(F32)).astype(LOW)
            gpre_ref[at] = gpre
            ga = dot_nt(gpre, fc1[...])
            scaled, inverse = norm_rows(mid_ref[at])
            a_ref[at] = (scaled * gain + shift).astype(LOW)
            out_ref[at] = grad_now + norm_back(ga, scaled, inverse, gain)
            return (
                totals[0] + jnp.sum(ga * scaled, axis=0, keepdims=True),
                totals[1] + jnp.sum(ga, axis=0, keepdims=True),
                totals[2] + jnp.sum(gz.astype(F32), axis=0, keepdims=True),
                totals[3] + jnp.sum(gpre.astype(F32), axis=0, keepdims=True),
            )

        zero = jnp.zeros((1, D), F32)
        sums = lax.fori_loop(0, steps, step, (zero, zero, zero, jnp.zeros((1, FF), F32)))
        for i in range(3):
            small_ref[i : i + 1] = sums[i]
        small_ref[3:8] = jnp.zeros((5, D), F32)
        bias_ref[...] = sums[3]
        for k in range(4):
            dest = keep_ref if k < 2 else send_ref
            cols = slice(k * D, (k + 1) * D)
            dest[k % 2, 0:D] = dot_tn(a_ref[...], gpre_ref[:, cols]).astype(LOW)
            dest[k % 2, D : 2 * D] = dot_tn(low_grad[...], act_ref[:, cols]).astype(LOW)

    return pl.pallas_call(
        kernel,
        out_shape=(
            jax.ShapeDtypeStruct((rows, D), F32),
            jax.ShapeDtypeStruct((2, 2 * D, D), LOW),
            jax.ShapeDtypeStruct((2, 2 * D, D), LOW),
            jax.ShapeDtypeStruct((8, D), F32),
            jax.ShapeDtypeStruct((1, FF), F32),
        ),
        in_specs=[vmem()] * 9,
        input_output_aliases={0: 0},
        out_specs=[vmem()] * 5,
        scratch_shapes=[
            pltpu.VMEM((D, FF), LOW),
            pltpu.VMEM((FF, D), LOW),
            pltpu.VMEM((rows, D), LOW),
            pltpu.VMEM((rows, FF), LOW),
            pltpu.VMEM((rows, D), LOW),
        ],
        compiler_params=params(13),
        cost_estimate=cost(7e9, 2e7),
        name="mlp_backward",
    )(grad, mid, act, slope, *weights, norms)


def mlp_turn(mid, grad, weights, fc1_bias, norms, layer):
    rows = mid.shape[0]
    chunk = 6 * PAD
    steps = rows // chunk

    def kernel(
        mid_ref, grad_ref, w0, w1, w2, w3, fc1_bias_ref, norm_ref,
        out_ref, grad_out_ref, keep_ref, send_ref, small_ref, bias_ref,
        fc1, fc2, a_all, act_all, low_grad, gpre_all,
    ):
        stack_mlp((w0, w1, w2, w3), fc1, fc2)
        gain, shift, out_shift = norm_ref[0:1], norm_ref[1:2], norm_ref[2:3]

        def step(i, totals):
            at = pl.ds(pl.multiple_of(i * chunk, 16), chunk)
            rows_now = mid_ref[at]
            scaled, inverse = norm_rows(rows_now)
            a = (scaled * gain + shift).astype(LOW)
            a_all[at] = a
            act, slope = gelu_parts(dot_nn(a, fc1[...]) + fc1_bias_ref[layer, 0:1])
            act = act.astype(LOW)
            act_all[at] = act
            out_ref[at] = rows_now + dot_nn(act, fc2[...]) + out_shift
            grad_now = grad_ref[at]
            gz = grad_now.astype(LOW)
            low_grad[at] = gz
            gpre = (dot_nt(gz, fc2[...]) * slope).astype(LOW)
            gpre_all[at] = gpre
            ga = dot_nt(gpre, fc1[...])
            grad_out_ref[at] = grad_now + norm_back(ga, scaled, inverse, gain)
            return (
                totals[0] + jnp.sum(ga * scaled, axis=0, keepdims=True),
                totals[1] + jnp.sum(ga, axis=0, keepdims=True),
                totals[2] + jnp.sum(gz.astype(F32), axis=0, keepdims=True),
                totals[3] + jnp.sum(gpre.astype(F32), axis=0, keepdims=True),
            )

        zero = jnp.zeros((1, D), F32)
        sums = lax.fori_loop(0, steps, step, (zero, zero, zero, jnp.zeros((1, FF), F32)))
        for i in range(3):
            small_ref[i : i + 1] = sums[i]
        small_ref[3:8] = jnp.zeros((5, D), F32)
        bias_ref[...] = sums[3]
        for k in range(4):
            dest = keep_ref if k < 2 else send_ref
            cols = slice(k * D, (k + 1) * D)
            dest[k % 2, 0:D] = dot_tn(a_all[...], gpre_all[:, cols]).astype(LOW)
            dest[k % 2, D : 2 * D] = dot_tn(low_grad[...], act_all[:, cols]).astype(LOW)

    return pl.pallas_call(
        kernel,
        out_shape=(
            jax.ShapeDtypeStruct((rows, D), F32),
            jax.ShapeDtypeStruct((rows, D), F32),
            jax.ShapeDtypeStruct((2, 2 * D, D), LOW),
            jax.ShapeDtypeStruct((2, 2 * D, D), LOW),
            jax.ShapeDtypeStruct((8, D), F32),
            jax.ShapeDtypeStruct((1, FF), F32),
        ),
        in_specs=[vmem()] * 8,
        input_output_aliases={0: 0, 1: 1},
        out_specs=[vmem()] * 6,
        scratch_shapes=[
            pltpu.VMEM((D, FF), LOW),
            pltpu.VMEM((FF, D), LOW),
            pltpu.VMEM((rows, D), LOW),
            pltpu.VMEM((rows, FF), LOW),
            pltpu.VMEM((rows, D), LOW),
            pltpu.VMEM((rows, FF), LOW),
        ],
        compiler_params=params(18),
        cost_estimate=cost(1.5e10, 4e7),
        name="mlp_turn",
    )(mid, grad, *weights, fc1_bias, norms)


def swap_core(value):
    return lax.ppermute(value, "head", [(i, i ^ 1) for i in range(4)])


def swap_chip(value):
    return lax.ppermute(value, "head", [(i, i ^ 2) for i in range(4)])


def swap_border(value):
    return lax.ppermute(value, "head", [(1, 2), (2, 1)])


def swap_dp(value, step, size):
    return lax.ppermute(value, "dp", [(i, i ^ step) for i in range(size)])


def tie(*values):
    return lax.optimization_barrier(values)


def pick(first, one, other):
    first = first > 0
    return jnp.where(first, one, other), jnp.where(first, other, one)


def dp_start(parts, first):
    half = parts[0].shape[0] // 2
    low = sum(p[:half].astype(F32) for p in parts)
    high = sum(p[half:].astype(F32) for p in parts)
    kept, sent = pick(first, low, high)
    return kept, swap_dp(sent.astype(LOW), 1, lax.axis_size("dp"))


def dp_middle(kept, other, step):
    value = (kept.astype(F32) + other.astype(F32)).astype(LOW)
    return value, swap_dp(value, step, lax.axis_size("dp"))


def dp_last(kept, other):
    value = (kept.astype(F32) + other.astype(F32)).astype(LOW)
    return value, swap_dp(value, 1, lax.axis_size("dp"))


def dp_join(value, other, first):
    low, high = pick(first, value, other)
    return jnp.concatenate([low, high])


def dp_steps():
    return [(2 << b) - 2 for b in range(1, lax.axis_size("dp").bit_length() - 1)]


def dp_finish(state, steps, first):
    for step in steps:
        state = dp_middle(*state, step)
    return dp_join(*dp_last(*state), first)


def body(
    tokens, outputs_grad, image_kind, qkv_weight, qv_bias, bias_table, proj_weight,
    fc1_weight, fc1_bias, fc2_weight, gains, shifts,
):
    own = tokens.shape[0] // PLACES
    bins = own + 2
    me = lax.axis_index("head").astype(jnp.int32)

    def border(value):
        edge = 4 * PLACES
        return swap_border(jnp.where(me == 1, value[-edge:], value[:edge]))

    def attn_pack(l):
        turned = jnp.transpose(qkv_weight[l], (1, 2, 0)).reshape(288, D)
        return jnp.concatenate([turned, proj_weight[l]], axis=0)

    def mlp_pack(l):
        return jnp.concatenate([fc1_weight[l], fc2_weight[l]], axis=0)

    def norm_pack(l, which, bias_row):
        rows = jnp.stack([gains[l, which], shifts[l, which], shifts[l, bias_row]])
        return jnp.pad(rows, ((0, 5), (0, 0)))

    partner = swap_core(tokens)
    own_pack, chip_pack = [attn_pack(0)], []
    chip_pack.append(swap_chip(own_pack[0]))
    rows = jnp.pad(jnp.transpose(bias_table, (0, 2, 1)).reshape(6, 169), ((0, 0), (0, D - 169)))
    small = jnp.concatenate([rows, qv_bias.reshape(1, D), fc1_bias])
    small = jnp.pad(small, ((0, 7), (0, 0)))
    edges, _ = tie(tokens, own_pack[0])
    halo = border(edges)
    small_chip = swap_chip(small)
    first = jnp.broadcast_to(1 - (lax.axis_index("dp") & 1).astype(jnp.int32), (1, D))
    table = make_plan(image_kind, me, own, bins)
    table, first, chip_pack[0], halo, partner, small_chip = tie(
        table, first, chip_pack[0], halo, partner, small_chip
    )
    smalls = (small, small_chip, swap_core(small), swap_core(small_chip))
    bias, qkv_bias, fc1_all = spread_smalls(smalls)
    hidden = gather_slots(table, tokens, partner, halo, bins)
    pack, _ = tie(mlp_pack(0), chip_pack[0])
    own_pack.append(pack)
    chip_pack.append(swap_chip(pack))

    def gathered(i):
        p, c = own_pack[i], chip_pack[i]
        return p, c, swap_core(p), swap_core(c)

    saved, weights = [], []
    last = LAYERS - 1
    for l in range(LAYERS):
        norms, mlp_norms = norm_pack(l, 0, 2), norm_pack(l, 1, 3)
        weights.append(gathered(2 * l))
        mid, a, qkv, probs, attn = attn_forward(
            table, hidden, weights[2 * l], qkv_bias, bias, norms, l
        )
        mid, chip_pack[2 * l + 1] = tie(mid, chip_pack[2 * l + 1])
        weights.append(gathered(2 * l + 1))
        if l == last:
            saved.append((hidden, mid, a, qkv, probs, attn, norms, mlp_norms))
            break
        pack, outputs_grad, mid = tie(attn_pack(1), outputs_grad, mid)
        grad_partner, grad_halo = swap_core(outputs_grad), border(outputs_grad)
        own_pack.append(pack)
        chip_pack.append(swap_chip(pack))
        out, act, slope = mlp_forward(mid, weights[2 * l + 1], fc1_all, mlp_norms, l)
        pack, out, chip_pack[2], grad_partner, grad_halo = tie(
            mlp_pack(1), out, chip_pack[2], grad_partner, grad_halo
        )
        own_pack.append(pack)
        chip_pack.append(swap_chip(pack))
        saved.append((hidden, mid, a, qkv, probs, attn, norms, mlp_norms, act, slope))
        hidden = out
    grad = gather_slots(table, outputs_grad, grad_partner, grad_halo, bins)

    def give_back(value):
        slots = value.reshape(bins, PAD, D)
        return slots, swap_core(slots), swap_border(border_slots(table, slots))

    def mlp_back(l, grad):
        return mlp_backward(
            grad, saved[l][1], saved[l][8], saved[l][9], weights[2 * l + 1], saved[l][7]
        )

    def attn_back(l, grad):
        return attn_backward(table, grad, saved[l][3], saved[l][4], weights[2 * l], l % 2 == 1)

    def attn_sums(l, grad, gqkv, scores, small_mlp, fc1_bias_grad):
        return attn_grads(
            table, grad, saved[l][0], saved[l][2], saved[l][5], gqkv, scores, small_mlp,
            fc1_bias_grad, weights[2 * l], saved[l][6], l % 2 == 1,
        )

    def core_sum(keep, other):
        return [(keep[i].astype(F32) + other[i].astype(F32)).astype(LOW) for i in range(2)]

    steps = dp_steps()
    out, grad, keep_a, send_a, small_mlp, fc1_bias_grad = mlp_turn(
        saved[last][1], grad, weights[2 * last + 1], fc1_all, saved[last][7], last
    )
    half_a, out_a = core_sum(keep_a, swap_core(send_a))
    grad, out_a = tie(grad, out_a)
    chip_a = swap_chip(out_a)
    gqkv, scores = attn_back(1, grad)
    gqkv, chip_a = tie(gqkv, chip_a)
    state_a = dp_start((half_a, chip_a), first)
    grad, keep_b, send_b = attn_sums(1, grad, gqkv, scores, small_mlp, fc1_bias_grad)
    grad, state_a, send_b = tie(grad, state_a, send_b)
    core_b = swap_core(send_b)
    state_a = dp_middle(*state_a, steps[0])
    grad, keep_c, send_c, small_mlp, fc1_bias_grad = mlp_back(0, grad)
    grad, send_c, state_a, core_b = tie(grad, send_c, state_a, core_b)
    core_c = swap_core(send_c)
    half_b, out_b = core_sum(keep_b, core_b)
    half_c, out_c = core_sum(keep_c, core_c)
    grad, out_b, out_c = tie(grad, out_b, out_c)
    chip_b, chip_c = swap_chip(out_b), swap_chip(out_c)
    for step in steps[1:]:
        state_a = dp_middle(*state_a, step)
    gqkv, scores = attn_back(0, grad)
    gqkv, state_a, chip_b, chip_c = tie(gqkv, state_a, chip_b, chip_c)
    state_a = dp_last(*state_a)
    state_bc = dp_start((jnp.concatenate([half_b, half_c]), jnp.concatenate([chip_b, chip_c])), first)
    grad, keep_d, send_d = attn_sums(0, grad, gqkv, scores, small_mlp, fc1_bias_grad)
    send_d, state_a, state_bc = tie(send_d, state_a, state_bc)
    half_d, out_d = core_sum(keep_d, swap_core(send_d))
    chip_d = swap_chip(out_d)
    out_d, out = tie(out_d, out)
    total_a = dp_join(*state_a, first)
    output_parts = give_back(out)
    total_bc = dp_finish(state_bc, steps, first)
    output = return_slots(table, *output_parts, own)
    tokens_grad = return_slots(table, *give_back(grad), own)
    mlp_all = jnp.stack([total_bc[D + SMALL :], total_a]).astype(F32)
    fc1_out = mlp_all[:, :D]
    fc2_out = mlp_all[:, D:].transpose(0, 2, 1)
    state_d = dp_start((half_d, chip_d), first)
    for step in steps:
        state_d = dp_middle(*state_d, step)
    value_d, other_d = dp_last(*state_d)
    value_d, fc1_out, fc2_out, output, tokens_grad = tie(
        value_d, fc1_out, fc2_out, output, tokens_grad
    )
    total_d = dp_join(value_d, other_d, first)

    attn_all = jnp.stack([total_d, total_bc[: D + SMALL]]).astype(F32)
    total = attn_all[:, D:]
    gains_out = jnp.stack([total[:, 0], total[:, 3]], axis=1)
    shifts_out = jnp.stack([total[:, 1], total[:, 4], total[:, 2], total[:, 5]], axis=1)
    fc1_bias_out = total[:, 6]
    qv_out = total[:, 7:9, 0:96]
    table_out = total[:, 9:12, 0:169].transpose(0, 2, 1)
    qkv_out = attn_all[:, 0:288].reshape(LAYERS, 3, 96, D).transpose(0, 3, 1, 2)
    proj_out = attn_all[:, 288:384]
    return (
        output, tokens_grad, qkv_out, qv_out, table_out, proj_out, fc1_out, fc1_bias_out,
        fc2_out, gains_out, shifts_out,
    )


def solution(mesh):
    rows = P(("dp", "head"), None)
    placed = (
        rows,
        rows,
        P("dp", None),
        P(None, None, None, "head"),
        P(None, None, "head"),
        P(None, None, "head"),
        P(None, "head", None),
        P(None, None, "head"),
        P(None, "head"),
        P(None, "head", None),
        P(),
        P(),
    )
    return jax.shard_map(
        body,
        mesh=mesh,
        in_specs=placed,
        out_specs=(
            rows,
            rows,
            P(None, None, None, "head"),
            P(None, None, "head"),
            P(None, None, "head"),
            P(None, "head", None),
            P(None, None, "head"),
            P(None, "head"),
            P(None, "head", None),
            P(),
            P(),
        ),
        check_vma=False,
    )
```

```python
import jax
import jax.numpy as jnp
from jax import lax
from jax.experimental import pallas as pl
from jax.experimental.pallas import tpu as pltpu
from jax.sharding import PartitionSpec as P

D = 384
FF = 1536
LAYERS = 2
PLACES = 49
PAD = 56
WIDE = 64
QUADS = 3
HEAD_DIM = 32
SCORE_SCALE = HEAD_DIM**-0.5
LN_EPS = 1e-05
LOW = jnp.bfloat16
F32 = jnp.float32
MIB = 1024 * 1024
SMALL = 16

SRC, SIDE, WROW, WCOL, FIRST, RET, SEND = 0, 24, 48, 72, 96, 120, 140
TABLE = 144


def vmem():
    return pl.BlockSpec(memory_space=pltpu.VMEM)


def smem():
    return pl.BlockSpec(memory_space=pltpu.SMEM)


def anywhere():
    return pl.BlockSpec(memory_space=pl.ANY)


def params(limit):
    return pltpu.CompilerParams(vmem_limit_bytes=limit * MIB)


def cost(flops, size):
    return pl.CostEstimate(flops=int(flops * 0.02), bytes_accessed=int(size * 0.02), transcendentals=0)


def dot_nn(a, b):
    return lax.dot_general(a, b, (((1,), (0,)), ((), ())), preferred_element_type=F32)


def dot_nt(a, b):
    return lax.dot_general(a, b, (((1,), (1,)), ((), ())), preferred_element_type=F32)


def dot_tn(a, b):
    return lax.dot_general(a, b, (((0,), (0,)), ((), ())), preferred_element_type=F32)


def plan_kernel(own, bins, kind_ref, me_ref, out_ref, load_ref):
    me = me_ref[0]
    half = 2 * own
    for i in range(TABLE):
        out_ref[i] = -1 if i < bins or RET <= i < RET + own else 0
    for i in range(bins):
        out_ref[SIDE + i] = 1
        out_ref[FIRST + i] = i
    for i in range(4):
        load_ref[i] = 0

    def place(start, count, side, bin_id):
        base = load_ref[bin_id]
        load_ref[bin_id] = base + count

        def step(k, carry):
            slot = start + k
            owner = slot // own
            inner = slot - owner * own
            local = base + k
            mine = bin_id == me
            halo = jnp.where(me == 1, slot - half, slot - half + 4)
            code = jnp.where(
                owner == me, inner, jnp.where(owner == (me ^ 1), own + inner, 2 * own + halo)
            )

            @pl.when(mine)
            def _():
                wrow = k // side
                out_ref[SRC + local] = code
                out_ref[SIDE + local] = side
                out_ref[WROW + local] = wrow
                out_ref[WCOL + local] = k - wrow * side
                out_ref[FIRST + local] = base

            @pl.when(owner == me)
            def _():
                back = jnp.where(me == 2, slot - half, k)
                out_ref[RET + inner] = jnp.where(
                    mine, local, jnp.where(bin_id == (me ^ 1), bins + local, 2 * bins + back)
                )

            return carry

        lax.fori_loop(0, count, step, 0)

    for turn in range(3):

        def visit(i, start, turn=turn):
            kind = kind_ref[0, i]
            count = jnp.where(kind == 2, 9, jnp.where(kind == 1, 4, 0))
            side = jnp.where(kind == 2, 3, 2)
            cut = half - start
            across = (cut > 0) & (cut < count)
            second = (start >= half) | (across & (cut < count - cut))
            chip = jnp.where(second, 1, 0)
            left, right = load_ref[2 * chip], load_ref[2 * chip + 1]
            emptier = 2 * chip + jnp.where(left <= right, 0, 1)
            if turn == 0:
                chosen, bin_id = across, 1 + chip
            else:
                chosen, bin_id = (kind == 3 - turn) & jnp.logical_not(across), emptier

            @pl.when(chosen)
            def _():
                place(start, count, side, bin_id)
                if turn == 0:
                    out_ref[SEND] = jnp.where((me == 1) & (chip == 0), cut, 0)

            return start + count

        lax.fori_loop(0, kind_ref.shape[1], visit, jnp.int32(0))


def gather_kernel(bins, table_ref, refs, out_ref, spread_ref):
    spread_ref[...] = jnp.zeros(spread_ref.shape, F32)
    at = 0
    for ref in refs:
        for s in range(ref.shape[0] // PLACES):
            spread_ref[at, 0:PLACES] = ref[s * PLACES : (s + 1) * PLACES].astype(F32)
            at += 1

    def step(j, carry):
        src = table_ref[SRC + j]

        @pl.when(src < 0)
        def _():
            out_ref[j] = jnp.zeros((PAD, D), F32)

        @pl.when(src >= 0)
        def _():
            out_ref[j] = spread_ref[src]

        return carry

    lax.fori_loop(0, bins, step, 0)


def make_plan(image_kind, me, own, bins):
    def kernel(kind_ref, me_ref, table_ref, load_ref):
        plan_kernel(own, bins, kind_ref, me_ref, table_ref, load_ref)

    return pl.pallas_call(
        kernel,
        out_shape=jax.ShapeDtypeStruct((TABLE,), jnp.int32),
        in_specs=[smem(), smem()],
        out_specs=smem(),
        scratch_shapes=[pltpu.SMEM((4,), jnp.int32)],
        compiler_params=params(1),
        cost_estimate=cost(0, 1.5e7),
        name="plan",
    )(image_kind, me.reshape(1))


def gather_slots(table, mine, partner, halo, bins):
    own = mine.shape[0] // PLACES

    def kernel(table_ref, *refs):
        gather_kernel(bins, table_ref, refs[:3], refs[3], refs[4])

    out = pl.pallas_call(
        kernel,
        out_shape=jax.ShapeDtypeStruct((bins, PAD, D), F32),
        in_specs=[smem()] + [vmem()] * 3,
        out_specs=vmem(),
        scratch_shapes=[pltpu.VMEM((2 * own + 4, PAD, D), F32)],
        compiler_params=params(8),
        cost_estimate=cost(0, 8e6),
        name="gather_slots",
    )(table, mine, partner, halo)
    return out.reshape(bins * PAD, D)


def border_slots(table, slots):
    def kernel(table_ref, slots_ref, out_ref):
        start = table_ref[SEND]
        for j in range(4):
            out_ref[j] = slots_ref[start + j]

    return pl.pallas_call(
        kernel,
        out_shape=jax.ShapeDtypeStruct((4,) + slots.shape[1:], F32),
        in_specs=[smem(), vmem()],
        out_specs=vmem(),
        compiler_params=params(1),
        cost_estimate=cost(0, 1e6),
        name="border_slots",
    )(table, slots)


def return_slots(table, mine, partner, halo, own):
    bins = mine.shape[0]

    def kernel(table_ref, mine_ref, partner_ref, halo_ref, out_ref):
        for s in range(own):
            src = table_ref[RET + s]
            rows = pl.ds(s * PLACES, PLACES)

            @pl.when(src < 0)
            def _():
                out_ref[rows] = jnp.zeros((PLACES, D), F32)

            @pl.when((src >= 0) & (src < bins))
            def _():
                out_ref[rows] = mine_ref[src, 0:PLACES]

            @pl.when((src >= bins) & (src < 2 * bins))
            def _():
                out_ref[rows] = partner_ref[src - bins, 0:PLACES]

            @pl.when(src >= 2 * bins)
            def _():
                out_ref[rows] = halo_ref[src - 2 * bins, 0:PLACES]

    return pl.pallas_call(
        kernel,
        out_shape=jax.ShapeDtypeStruct((own * PLACES, D), F32),
        in_specs=[smem(), vmem(), vmem(), vmem()],
        out_specs=vmem(),
        compiler_params=params(2),
        cost_estimate=cost(0, 8e6),
        name="return_slots",
    )(table, mine, partner, halo)


def norm_rows(rows):
    average = jnp.mean(rows, axis=-1, keepdims=True)
    centred = rows - average
    inverse = lax.rsqrt(jnp.mean(centred * centred, axis=-1, keepdims=True) + LN_EPS)
    return centred * inverse, inverse


def norm_back(incoming, scaled, inverse, gain):
    weighted = incoming * gain
    return inverse * (
        weighted
        - jnp.mean(weighted, axis=-1, keepdims=True)
        - scaled * jnp.mean(weighted * scaled, axis=-1, keepdims=True)
    )


def gelu_parts(x):
    size = jnp.abs(x) * 0.7071067811865476
    t = 1.0 / (1.0 + 0.3275911 * size)
    bell = jnp.exp(-0.5 * x * x)
    poly = t * (
        0.127414796 + t * (-0.142248368 + t * (0.7107068705 + t * (-0.7265760135 + t * 0.5307027145)))
    )
    tail = poly * bell
    phi = jnp.where(x >= 0, 1.0 - tail, tail)
    return x * phi, phi + x * bell * 0.3989422804014327


def place_parts(shape, dim):
    place = lax.broadcasted_iota(jnp.int32, shape, dim)
    row = (place * 37) >> 8
    return place, row, place - 7 * row


def fill_moves(table_ref, out_ref, bins, back):
    width = out_ref.shape[1]
    place, row, col = place_parts((PAD, 1), 0)
    if back:
        row_other, col_other = row < 3, col < 3
        inner = 7 * jnp.where(row_other, row + 4, row - 3) + jnp.where(col_other, col + 4, col - 3)
    else:
        row_other, col_other = row >= 4, col >= 4
        inner = 7 * jnp.where(row_other, row - 4, row + 3) + jnp.where(col_other, col - 4, col + 3)
    lanes = lax.broadcasted_iota(jnp.int32, (2 * PAD, width), 1)

    def source(w):
        side, wrow, wcol = table_ref[SIDE + w], table_ref[WROW + w], table_ref[WCOL + w]
        first = table_ref[FIRST + w]
        if back:
            orow = jnp.where(wrow == 0, side - 1, wrow - 1)
            ocol = jnp.where(wcol == 0, side - 1, wcol - 1)
        else:
            orow = jnp.where(wrow == side - 1, 0, wrow + 1)
            ocol = jnp.where(wcol == side - 1, 0, wcol + 1)
        slot = first + jnp.where(row_other, orow, wrow) * side + jnp.where(col_other, ocol, wcol)
        return jnp.where(place < PLACES, slot * PAD + inner, w * PAD + place)

    def step(j, carry):
        rows = jnp.concatenate([source(2 * j), source(2 * j + 1)], axis=0)
        hot = jnp.where(lanes == rows, 1.0, 0.0).astype(LOW)
        out_ref[pl.ds(pl.multiple_of(j * 2 * PAD, 16), 2 * PAD)] = hot
        return carry

    lax.fori_loop(0, bins // 2, step, 0)


def head_marks():
    lane = lax.broadcasted_iota(jnp.int32, (WIDE, 128), 1) // HEAD_DIM
    return [jnp.where(lane == h, 1.0, 0.0).astype(LOW) for h in range(4)]


def spread(block, marks):
    return jnp.concatenate([block * mark for mark in marks], axis=0)


def fold(product, marks):
    total = None
    for h, mark in enumerate(marks):
        part = product[h * WIDE : (h + 1) * WIDE] * mark.astype(F32)
        total = part if total is None else total + part
    return total


def spread_pair(block, marks):
    return jnp.concatenate([spread(block[0:WIDE], marks), spread(block[WIDE:], marks)], axis=1)


def diagonal(block):
    zero = jnp.zeros((WIDE, 128), block.dtype)
    top = jnp.concatenate([block[0:WIDE], zero], axis=1)
    return jnp.concatenate([top, jnp.concatenate([zero, block[WIDE:]], axis=1)], axis=0)


def by_head(values):
    return values.reshape(4, WIDE, 128)


def pad_rows(rows):
    return jnp.concatenate([rows, jnp.zeros((WIDE - PAD, rows.shape[1]), rows.dtype)], axis=0)


def split(values):
    high = values.astype(LOW)
    return high, (values - high.astype(F32)).astype(LOW)


def marks_where(rows, cols, test):
    row = lax.broadcasted_iota(jnp.int32, (rows, cols), 0)
    col = lax.broadcasted_iota(jnp.int32, (rows, cols), 1)
    return jnp.where(test(row, col), 1.0, 0.0).astype(LOW)


def far(place):
    row = (place * 37) >> 8
    return 13 * row + (place - 7 * row)


def spread_smalls(smalls):
    heads = LAYERS * 12

    def kernel(p0, p1, p2, p3, out_ref, qkv_ref, fc1_ref, table_ref, small_ref):
        quarters = []
        for k, ref in enumerate((p0, p1, p2, p3)):
            high, low = ref[D : D + SMALL], ref[D + SMALL : D + 2 * SMALL]
            small_ref[k] = high.astype(F32) + low.astype(F32)
            quarters.append(small_ref.at[k])
        for k, ref in enumerate(quarters):
            for l in range(LAYERS):
                at = l * 12 + k * 3
                table_ref[at : at + 3] = ref[l * 3 : l * 3 + 3, 0:256]
        lane = lax.broadcasted_iota(jnp.int32, (8, D), 1)
        for l in range(LAYERS):
            for c in range(3):
                total = jnp.zeros((8, D), F32)
                for k, ref in enumerate(quarters):
                    if c != 1:
                        row = jnp.broadcast_to(ref[6:7], (8, D))
                        row = pltpu.roll(row, (k * 96 - l * 192 - (c // 2) * 96) % D, 1)
                        own_lanes = (lane >= k * 96) & (lane < k * 96 + 96)
                        total = total + jnp.where(own_lanes, row, 0.0)
                qkv_ref[l, :, c * D : (c + 1) * D] = total
            for k, ref in enumerate(quarters):
                row = jnp.broadcast_to(ref[7 + l : 8 + l], (8, D))
                fc1_ref[l, :, k * D : (k + 1) * D] = row
        to_lane = marks_where(128, 128, lambda r, c: (far(c & 63) == r) & ((c & 63) < PLACES))
        to_row = marks_where(WIDE, 96, lambda r, c: (far(r) == c) & (r < PLACES))
        place = lax.broadcasted_iota(jnp.int32, (WIDE, 128), 0)
        empty = jnp.where(place < PLACES, 0.0, -1e30)
        turned = pltpu.roll(table_ref[...], 172, 1)
        skewed = []
        for n in range(heads):
            row = jnp.broadcast_to(turned[n : n + 1], (96, 256))
            skewed.append(pltpu.roll(row, 0, 1, stride=1, stride_axis=0)[:, 0:128])
        skewed = jnp.concatenate(skewed, axis=1)
        total = None
        for part in split(skewed):
            rows = dot_nn(to_row, part).astype(LOW)
            rows = jnp.concatenate([rows[:, n * 128 : (n + 1) * 128] for n in range(heads)], axis=0)
            part = dot_nn(rows, to_lane)
            total = part if total is None else total + part
        for n in range(heads):
            l, t, h = n // 12, n % 12 // 4, n % 4
            out_ref[l, t, h * WIDE : (h + 1) * WIDE] = total[n * WIDE : (n + 1) * WIDE] + empty

    return pl.pallas_call(
        kernel,
        out_shape=(
            jax.ShapeDtypeStruct((LAYERS, QUADS, 4 * WIDE, 128), F32),
            jax.ShapeDtypeStruct((LAYERS, 8, 3 * D), F32),
            jax.ShapeDtypeStruct((LAYERS, 8, FF), F32),
        ),
        in_specs=[vmem()] * 4,
        out_specs=[vmem()] * 3,
        scratch_shapes=[pltpu.VMEM((heads, 256), F32), pltpu.VMEM((4, SMALL, D), F32)],
        compiler_params=params(6),
        cost_estimate=cost(0, 1e7),
        name="spread_smalls",
    )(*smalls)


def scores_to_table(scores_ref):
    to_far = marks_where(128, 128, lambda r, c: (far(r & 63) == c) & ((r & 63) < PLACES))
    to_row = marks_where(96, WIDE, lambda r, c: (84 - far(c) == r) & (c < PLACES))
    wide = None
    for part in split(scores_ref[...].reshape(12 * WIDE, 128)):
        part = dot_nn(part, to_far)
        wide = part if wide is None else wide + part
    wide = jnp.concatenate([wide[h * WIDE : (h + 1) * WIDE] for h in range(12)], axis=1)
    rows = None
    for part in split(wide):
        part = dot_nn(to_row, part)
        rows = part if rows is None else rows + part
    out = []
    for h in range(12):
        one = rows[:, h * 128 : (h + 1) * 128]
        one = jnp.concatenate([one, jnp.zeros_like(one)], axis=1)
        one = pltpu.roll(one, 0, 1, stride=1, stride_axis=0)
        out.append(jnp.sum(one, axis=0, keepdims=True))
    return out


def stack_qkv(pieces, out_ref):
    for k, piece in enumerate(pieces):
        for c in range(3):
            out_ref[c * D + k * 96 : c * D + (k + 1) * 96] = piece[c * 96 : (c + 1) * 96]


def stack_proj(pieces, out_ref):
    for k, piece in enumerate(pieces):
        out_ref[k * 96 : (k + 1) * 96] = piece[288:384]


def stack_mlp(pieces, fc1_ref, fc2_ref):
    for k, piece in enumerate(pieces):
        fc1_ref[:, k * D : (k + 1) * D] = piece[0:D]
        fc2_ref[k * D : (k + 1) * D] = piece[D : 2 * D]


def attn_forward(table, hidden, weights, qv_bias, bias, norms, layer):
    shifted = layer % 2 == 1
    rows = hidden.shape[0]
    bins = rows // PAD
    chunk_slots = 6
    chunk = chunk_slots * PAD
    wide_rows = -(-rows // 128) * 128

    def kernel(
        table_ref, hidden_ref, w0, w1, w2, w3, qv_ref, bias_ref, norm_ref,
        mid_ref, a_ref, qkv_ref, p_ref, attn_ref,
        wqkv, wproj, wide_attn, moves,
    ):
        pieces = (w0, w1, w2, w3)
        stack_qkv(pieces, wqkv)
        stack_proj(pieces, wproj)
        gain, shift, proj_shift = norm_ref[0:1], norm_ref[1:2], norm_ref[2:3]
        marks = head_marks()
        dest = attn_ref if shifted else a_ref

        def norm_step(i, carry):
            at = pl.ds(pl.multiple_of(i * chunk, 16), chunk)
            scaled, _ = norm_rows(hidden_ref[at])
            dest[at] = (scaled * gain + shift).astype(LOW)
            return carry

        lax.fori_loop(0, bins // chunk_slots, norm_step, 0)
        if shifted:
            fill_moves(table_ref, moves, bins, False)
            a_ref[...] = dot_nn(moves[:, 0:rows], dest[...]).astype(LOW)
            fill_moves(table_ref, moves, bins, True)

        def qkv_step(i, carry):
            at = pl.ds(pl.multiple_of(i * chunk, 16), chunk)
            project = dot_nt(a_ref[at], wqkv[...]) + qv_ref[layer, 0:1]
            for j in range(chunk_slots):
                block = project[j * PAD : (j + 1) * PAD]
                at = pl.ds((j % 2) * WIDE, WIDE)
                qkv_ref[i * (chunk_slots // 2) + j // 2, at] = pad_rows(block).astype(LOW)
            return carry

        lax.fori_loop(0, bins // chunk_slots, qkv_step, 0)

        if shifted:
            _, qrow, qcol = place_parts((WIDE, 1), 0)
            lane = lax.broadcasted_iota(jnp.int32, (1, 128), 1)
            second = lane >= WIDE
            pplace = jnp.where(second, lane - WIDE, lane)
            prow = (pplace * 37) >> 8
            pcol = pplace - 7 * prow
            pband = 1 + (prow >= 4).astype(jnp.int32), 1 + (pcol >= 4).astype(jnp.int32)
            qband = 1 + (qrow >= 4).astype(jnp.int32), 1 + (qcol >= 4).astype(jnp.int32)

        def window(j, carry):
            if shifted:
                low = []
                for w in (2 * j, 2 * j + 1):
                    side = table_ref[SIDE + w]
                    low.append(
                        (
                            jnp.where(table_ref[WROW + w] == side - 1, 3, 0),
                            jnp.where(table_ref[WCOL + w] == side - 1, 1, 0),
                        )
                    )
                low_row = jnp.where(second, low[1][0], low[0][0])
                low_col = jnp.where(second, low[1][1], low[0][1])
                pregion = low_row * pband[0] + low_col * pband[1]
                qregion = low_row * qband[0] + low_col * qband[1]
                mask = jnp.where(pregion != qregion, -100.0, 0.0)[None]
            for t in range(QUADS):
                cols = slice(t * 128, (t + 1) * 128)
                q = qkv_ref[j, :, t * 128 : (t + 1) * 128]
                k = qkv_ref[j, :, D + t * 128 : D + (t + 1) * 128]
                v = qkv_ref[j, :, 2 * D + t * 128 : 2 * D + (t + 1) * 128]
                scores = dot_nt(spread_pair(k, marks), diagonal(q)) * SCORE_SCALE + bias_ref[layer, t]
                scores = by_head(scores)
                if shifted:
                    scores = scores + mask
                exponent = jnp.exp(scores - jnp.max(scores, axis=1, keepdims=True))
                total = jnp.sum(exponent, axis=1, keepdims=True)
                probs = (exponent * (1.0 / total)).reshape(4 * WIDE, 128).astype(LOW)
                p_ref[j, t] = probs
                both = dot_tn(probs, spread_pair(v, marks))
                at = pl.multiple_of(j * 2 * PAD, 16)
                wide_attn[pl.ds(at, PAD), cols] = both[0:PAD, 0:128]
                wide_attn[pl.ds(at + PAD, PAD), cols] = both[WIDE : WIDE + PAD, 128:256]
            return carry

        lax.fori_loop(0, bins // 2, window, 0, unroll=3)
        if shifted:
            attn_ref[...] = dot_nn(moves[:, 0:rows], wide_attn[...].astype(LOW)).astype(LOW)
        else:
            attn_ref[...] = wide_attn[...].astype(LOW)

        def proj_step(i, carry):
            at = pl.ds(pl.multiple_of(i * chunk, 16), chunk)
            mid_ref[at] = hidden_ref[at] + dot_nn(attn_ref[at], wproj[...]) + proj_shift
            return carry

        lax.fori_loop(0, bins // chunk_slots, proj_step, 0)

    return pl.pallas_call(
        kernel,
        out_shape=(
            jax.ShapeDtypeStruct((rows, D), F32),
            jax.ShapeDtypeStruct((rows, D), LOW),
            jax.ShapeDtypeStruct((bins // 2, 2 * WIDE, 3 * D), LOW),
            jax.ShapeDtypeStruct((bins // 2, QUADS, 4 * WIDE, 128), LOW),
            jax.ShapeDtypeStruct((rows, D), LOW),
        ),
        in_specs=[smem()] + [vmem()] * 8,
        out_specs=[vmem()] * 5,
        scratch_shapes=[
            pltpu.VMEM((3 * D, D), LOW),
            pltpu.VMEM((D, D), LOW),
            pltpu.VMEM((rows, D), F32),
            pltpu.VMEM((rows if shifted else 16, wide_rows), LOW),
        ],
        compiler_params=params(11),
        cost_estimate=cost(1e10, 2e7),
        name="attn_forward",
    )(table, hidden, *weights, qv_bias, bias, norms)


def attn_backward(table, grad, qkv, probs, weights, shifted):
    rows = grad.shape[0]
    bins = rows // PAD
    chunk_slots = 6
    chunk = chunk_slots * PAD
    wide_rows = -(-rows // 128) * 128

    def kernel(
        table_ref, grad_ref, qkv_ref, p_ref, w0, w1, w2, w3,
        gqkv_ref, scores_ref, wproj, wide_attn, low_wide, moves,
    ):
        stack_proj((w0, w1, w2, w3), wproj)
        marks = head_marks()
        steps = bins // chunk_slots
        if shifted:
            fill_moves(table_ref, moves, bins, False)

        def keep_windows(i, block_rows):
            for j in range(chunk_slots):
                block = block_rows[j * PAD : (j + 1) * PAD]
                dest = pl.ds((j % 2) * WIDE, WIDE)
                wide_attn[i * (chunk_slots // 2) + j // 2, dest] = pad_rows(block).astype(LOW)

        def proj_step(i, carry):
            at = pl.ds(pl.multiple_of(i * chunk, 16), chunk)
            gattn = dot_nt(grad_ref[at].astype(LOW), wproj[...])
            if shifted:
                low_wide[at] = gattn.astype(LOW)
            else:
                keep_windows(i, gattn)
            return carry

        lax.fori_loop(0, steps, proj_step, 0)
        if shifted:

            def move_step(i, carry):
                at = pl.ds(pl.multiple_of(i * chunk, 16), chunk)
                keep_windows(i, dot_nn(moves[at, 0:rows], low_wide[...]))
                return carry

            lax.fori_loop(0, steps, move_step, 0)

        scores_ref[...] = jnp.zeros((QUADS, 4 * WIDE, 128), F32)

        def window(j, carry):
            for t in range(QUADS):
                q = qkv_ref[j, :, t * 128 : (t + 1) * 128]
                k = qkv_ref[j, :, D + t * 128 : D + (t + 1) * 128]
                v = qkv_ref[j, :, 2 * D + t * 128 : 2 * D + (t + 1) * 128]
                low_probs = p_ref[j, t]
                p = by_head(low_probs.astype(F32))
                go = diagonal(wide_attn[j, :, t * 128 : (t + 1) * 128])
                gp = by_head(dot_nt(spread_pair(v, marks), go))
                ds = p * (gp - jnp.sum(gp * p, axis=1, keepdims=True))
                low_ds = ds.reshape(4 * WIDE, 128).astype(LOW)
                scores_ref[t] += low_ds.astype(F32)
                gq = dot_tn(low_ds, spread_pair(k, marks)) * SCORE_SCALE
                gk = dot_nn(low_ds, diagonal(q)) * SCORE_SCALE
                gv = dot_nn(low_probs, go)
                at = pl.ds(pl.multiple_of(j * 2 * PAD, 16), 2 * PAD)
                left, right = slice(0, 128), slice(128, 256)
                parts = (
                    (gq[0:PAD, left], gq[WIDE : WIDE + PAD, right]),
                    (fold(gk[:, left], marks)[0:PAD], fold(gk[:, right], marks)[0:PAD]),
                    (fold(gv[:, left], marks)[0:PAD], fold(gv[:, right], marks)[0:PAD]),
                )
                for c, part in enumerate(parts):
                    cols = slice(c * D + t * 128, c * D + (t + 1) * 128)
                    gqkv_ref[at, cols] = jnp.concatenate(part, axis=0).astype(LOW)
            return carry

        lax.fori_loop(0, bins // 2, window, 0, unroll=3)

    return pl.pallas_call(
        kernel,
        out_shape=(
            jax.ShapeDtypeStruct((rows, 3 * D), LOW),
            jax.ShapeDtypeStruct((QUADS, 4 * WIDE, 128), F32),
        ),
        in_specs=[smem()] + [vmem()] * 7,
        out_specs=[vmem()] * 2,
        scratch_shapes=[
            pltpu.VMEM((D, D), LOW),
            pltpu.VMEM((bins // 2, 2 * WIDE, D), LOW),
            pltpu.VMEM((rows, D), LOW),
            pltpu.VMEM((rows if shifted else 16, wide_rows), LOW),
        ],
        compiler_params=params(11),
        cost_estimate=cost(1e10, 2e7),
        name="attn_backward",
    )(table, grad, qkv, probs, *weights)


def attn_grads(
    table, grad, hidden, a, attn, gqkv, scores, small_mlp, fc1_bias_grad, weights, norms, shifted
):
    rows = hidden.shape[0]
    bins = rows // PAD
    chunk = 6 * PAD
    steps = rows // chunk
    wide_rows = -(-rows // 128) * 128

    def kernel(
        table_ref, grad_ref, hidden_ref, a_ref, attn_ref, gqkv_ref, scores_ref, mlp_ref, fc1b_ref,
        w0, w1, w2, w3, norm_ref,
        out_ref, keep_ref, send_ref, wqkv, low_wide, small, moves,
    ):
        stack_qkv((w0, w1, w2, w3), wqkv)
        gain = norm_ref[0:1]
        if shifted:
            fill_moves(table_ref, moves, bins, True)
            low_wide[...] = dot_nn(gqkv_ref[...], wqkv[...]).astype(LOW)

        def back_step(i, totals):
            at = pl.ds(pl.multiple_of(i * chunk, 16), chunk)
            if shifted:
                ga = dot_nn(moves[at, 0:rows], low_wide[...])
            else:
                ga = dot_nn(gqkv_ref[at], wqkv[...])
            scaled, inverse = norm_rows(hidden_ref[at])
            grad_now = grad_ref[at]
            out_ref[at] = grad_now + norm_back(ga, scaled, inverse, gain)
            return (
                totals[0] + jnp.sum(ga * scaled, axis=0, keepdims=True),
                totals[1] + jnp.sum(ga, axis=0, keepdims=True),
                totals[2] + jnp.sum(grad_now.astype(LOW).astype(F32), axis=0, keepdims=True),
                totals[3] + jnp.sum(gqkv_ref[at].astype(F32), axis=0, keepdims=True),
            )

        zero = jnp.zeros((1, D), F32)
        sums = lax.fori_loop(0, steps, back_step, (zero, zero, zero, jnp.zeros((1, 3 * D), F32)))
        table_rows = scores_to_table(scores_ref)
        dproj = dot_tn(attn_ref[...], grad_ref[...].astype(LOW)).astype(LOW)
        dqkv = dot_tn(a_ref[...], gqkv_ref[...])
        turned = [dqkv[:, c * D : (c + 1) * D].T.astype(LOW) for c in range(3)]
        small[...] = jnp.zeros((SMALL, D), F32)
        for i in range(3):
            small[i : i + 1] = sums[i]
        small[3:6] = mlp_ref[0:3]
        gq_sum = jnp.broadcast_to(sums[3][:, 0:D], (8, D))
        gv_sum = jnp.broadcast_to(sums[3][:, 2 * D : 3 * D], (8, D))
        for k in range(4):
            dest = keep_ref if k < 2 else send_ref
            for c in range(3):
                dest[k % 2, c * 96 : (c + 1) * 96] = turned[c][k * 96 : (k + 1) * 96]
            dest[k % 2, 288:384] = dproj[k * 96 : (k + 1) * 96]
            small[6:7] = fc1b_ref[:, k * D : (k + 1) * D]
            small[7:8] = pltpu.roll(gq_sum, (D - k * 96) % D, 1)[0:1]
            small[8:9] = pltpu.roll(gv_sum, (D - k * 96) % D, 1)[0:1]
            for h in range(3):
                small[9 + h : 10 + h, 0:256] = table_rows[3 * k + h]
            dest[k % 2, D : D + SMALL] = small[...].astype(LOW)

    return pl.pallas_call(
        kernel,
        out_shape=(
            jax.ShapeDtypeStruct((rows, D), F32),
            jax.ShapeDtypeStruct((2, D + SMALL, D), LOW),
            jax.ShapeDtypeStruct((2, D + SMALL, D), LOW),
        ),
        in_specs=[smem()] + [vmem()] * 13,
        out_specs=[vmem()] * 3,
        scratch_shapes=[
            pltpu.VMEM((3 * D, D), LOW),
            pltpu.VMEM((rows, D), LOW),
            pltpu.VMEM((SMALL, D), F32),
            pltpu.VMEM((rows if shifted else 16, wide_rows), LOW),
        ],
        compiler_params=params(10),
        cost_estimate=cost(6e9, 2e7),
        name="attn_grads",
    )(
        table, grad, hidden, a, attn, gqkv, scores, small_mlp, fc1_bias_grad, *weights, norms
    )


def mlp_forward(mid, weights, fc1_bias, norms, layer):
    rows = mid.shape[0]
    chunk = 3 * PAD * 2
    steps = rows // chunk

    def kernel(
        mid_ref, w0, w1, w2, w3, fc1_bias_ref, norm_ref,
        out_ref, act_ref, slope_ref, fc1, fc2,
    ):
        stack_mlp((w0, w1, w2, w3), fc1, fc2)
        gain, shift, out_shift = norm_ref[0:1], norm_ref[1:2], norm_ref[2:3]

        def step(i, carry):
            at = pl.ds(pl.multiple_of(i * chunk, 16), chunk)
            rows_now = mid_ref[at]
            scaled, _ = norm_rows(rows_now)
            a = (scaled * gain + shift).astype(LOW)
            act, slope = gelu_parts(dot_nn(a, fc1[...]) + fc1_bias_ref[layer, 0:1])
            act = act.astype(LOW)
            act_ref[at] = act
            slope_ref[at] = slope.astype(LOW)
            out_ref[at] = rows_now + dot_nn(act, fc2[...]) + out_shift
            return carry

        lax.fori_loop(0, steps, step, 0, unroll=True)

    return pl.pallas_call(
        kernel,
        out_shape=(
            jax.ShapeDtypeStruct((rows, D), F32),
            jax.ShapeDtypeStruct((rows, FF), LOW),
            jax.ShapeDtypeStruct((rows, FF), LOW),
        ),
        in_specs=[vmem()] * 7,
        out_specs=[vmem()] * 3,
        scratch_shapes=[pltpu.VMEM((D, FF), LOW), pltpu.VMEM((FF, D), LOW)],
        compiler_params=params(14),
        cost_estimate=cost(7e9, 2e7),
        name="mlp_forward",
    )(mid, *weights, fc1_bias, norms)


def mlp_backward(grad, mid, act, slope, weights, norms):
    rows = mid.shape[0]
    chunk = 3 * PAD * 2
    steps = rows // chunk

    def kernel(
        grad_ref, mid_ref, act_ref, slope_ref, w0, w1, w2, w3, norm_ref,
        out_ref, keep_ref, send_ref, small_ref, bias_ref, fc1, fc2, low_grad, gpre_ref, a_ref,
    ):
        stack_mlp((w0, w1, w2, w3), fc1, fc2)
        gain, shift = norm_ref[0:1], norm_ref[1:2]

        def step(i, totals):
            at = pl.ds(pl.multiple_of(i * chunk, 16), chunk)
            grad_now = grad_ref[at]
            gz = grad_now.astype(LOW)
            low_grad[at] = gz
            gpre = (dot_nt(gz, fc2[...]) * slope_ref[at].astype(F32)).astype(LOW)
            gpre_ref[at] = gpre
            ga = dot_nt(gpre, fc1[...])
            scaled, inverse = norm_rows(mid_ref[at])
            a_ref[at] = (scaled * gain + shift).astype(LOW)
            out_ref[at] = grad_now + norm_back(ga, scaled, inverse, gain)
            return (
                totals[0] + jnp.sum(ga * scaled, axis=0, keepdims=True),
                totals[1] + jnp.sum(ga, axis=0, keepdims=True),
                totals[2] + jnp.sum(gz.astype(F32), axis=0, keepdims=True),
                totals[3] + jnp.sum(gpre.astype(F32), axis=0, keepdims=True),
            )

        zero = jnp.zeros((1, D), F32)
        sums = lax.fori_loop(
            0, steps, step, (zero, zero, zero, jnp.zeros((1, FF), F32)), unroll=True
        )
        for i in range(3):
            small_ref[i : i + 1] = sums[i]
        small_ref[3:8] = jnp.zeros((5, D), F32)
        bias_ref[...] = sums[3]
        for k in range(4):
            dest = keep_ref if k < 2 else send_ref
            cols = slice(k * D, (k + 1) * D)
            dest[k % 2, 0:D] = dot_tn(a_ref[...], gpre_ref[:, cols]).astype(LOW)
            dest[k % 2, D : 2 * D] = dot_tn(low_grad[...], act_ref[:, cols]).astype(LOW)

    return pl.pallas_call(
        kernel,
        out_shape=(
            jax.ShapeDtypeStruct((rows, D), F32),
            jax.ShapeDtypeStruct((2, 2 * D, D), LOW),
            jax.ShapeDtypeStruct((2, 2 * D, D), LOW),
            jax.ShapeDtypeStruct((8, D), F32),
            jax.ShapeDtypeStruct((1, FF), F32),
        ),
        in_specs=[vmem()] * 9,
        input_output_aliases={0: 0},
        out_specs=[vmem()] * 5,
        scratch_shapes=[
            pltpu.VMEM((D, FF), LOW),
            pltpu.VMEM((FF, D), LOW),
            pltpu.VMEM((rows, D), LOW),
            pltpu.VMEM((rows, FF), LOW),
            pltpu.VMEM((rows, D), LOW),
        ],
        compiler_params=params(20),
        cost_estimate=cost(7e9, 2e7),
        name="mlp_backward",
    )(grad, mid, act, slope, *weights, norms)


def mlp_turn(mid, grad, weights, fc1_bias, norms, layer):
    rows = mid.shape[0]
    chunk = 6 * PAD
    steps = rows // chunk

    def kernel(
        mid_ref, grad_ref, w0, w1, w2, w3, fc1_bias_ref, norm_ref,
        out_ref, grad_out_ref, keep_ref, send_ref, small_ref, bias_ref,
        fc1, fc2, a_all, act_all, low_grad, gpre_all,
    ):
        stack_mlp((w0, w1, w2, w3), fc1, fc2)
        gain, shift, out_shift = norm_ref[0:1], norm_ref[1:2], norm_ref[2:3]

        def step(i, totals):
            at = pl.ds(pl.multiple_of(i * chunk, 16), chunk)
            rows_now = mid_ref[at]
            scaled, inverse = norm_rows(rows_now)
            a = (scaled * gain + shift).astype(LOW)
            a_all[at] = a
            act, slope = gelu_parts(dot_nn(a, fc1[...]) + fc1_bias_ref[layer, 0:1])
            act = act.astype(LOW)
            act_all[at] = act
            out_ref[at] = rows_now + dot_nn(act, fc2[...]) + out_shift
            grad_now = grad_ref[at]
            gz = grad_now.astype(LOW)
            low_grad[at] = gz
            gpre = (dot_nt(gz, fc2[...]) * slope).astype(LOW)
            gpre_all[at] = gpre
            ga = dot_nt(gpre, fc1[...])
            grad_out_ref[at] = grad_now + norm_back(ga, scaled, inverse, gain)
            return (
                totals[0] + jnp.sum(ga * scaled, axis=0, keepdims=True),
                totals[1] + jnp.sum(ga, axis=0, keepdims=True),
                totals[2] + jnp.sum(gz.astype(F32), axis=0, keepdims=True),
                totals[3] + jnp.sum(gpre.astype(F32), axis=0, keepdims=True),
            )

        zero = jnp.zeros((1, D), F32)
        sums = lax.fori_loop(
            0, steps, step, (zero, zero, zero, jnp.zeros((1, FF), F32))
        )
        for i in range(3):
            small_ref[i : i + 1] = sums[i]
        small_ref[3:8] = jnp.zeros((5, D), F32)
        bias_ref[...] = sums[3]
        for k in range(4):
            dest = keep_ref if k < 2 else send_ref
            cols = slice(k * D, (k + 1) * D)
            dest[k % 2, 0:D] = dot_tn(a_all[...], gpre_all[:, cols]).astype(LOW)
            dest[k % 2, D : 2 * D] = dot_tn(low_grad[...], act_all[:, cols]).astype(LOW)

    return pl.pallas_call(
        kernel,
        out_shape=(
            jax.ShapeDtypeStruct((rows, D), F32),
            jax.ShapeDtypeStruct((rows, D), F32),
            jax.ShapeDtypeStruct((2, 2 * D, D), LOW),
            jax.ShapeDtypeStruct((2, 2 * D, D), LOW),
            jax.ShapeDtypeStruct((8, D), F32),
            jax.ShapeDtypeStruct((1, FF), F32),
        ),
        in_specs=[vmem()] * 8,
        input_output_aliases={0: 0, 1: 1},
        out_specs=[vmem()] * 6,
        scratch_shapes=[
            pltpu.VMEM((D, FF), LOW),
            pltpu.VMEM((FF, D), LOW),
            pltpu.VMEM((rows, D), LOW),
            pltpu.VMEM((rows, FF), LOW),
            pltpu.VMEM((rows, D), LOW),
            pltpu.VMEM((rows, FF), LOW),
        ],
        compiler_params=params(18),
        cost_estimate=cost(1.5e10, 4e7),
        name="mlp_turn",
    )(mid, grad, *weights, fc1_bias, norms)


def small_outputs(rows):
    def kernel(rows_ref, gains_ref, shifts_ref, fc1_ref, qv_ref, table_ref):
        for l in range(LAYERS):
            now = rows_ref[l]
            for i, row in enumerate((0, 3)):
                gains_ref[l, i : i + 1] = now[row : row + 1]
            for i, row in enumerate((1, 4, 2, 5)):
                shifts_ref[l, i : i + 1] = now[row : row + 1]
            fc1_ref[l : l + 1] = now[6:7]
            qv_ref[l] = now[7:9, 0:96]
            turned = rows_ref[l, 8:SMALL, 0:256].T
            table_ref[l] = turned[0:169, 1:4]

    return pl.pallas_call(
        kernel,
        out_shape=(
            jax.ShapeDtypeStruct((LAYERS, 2, D), F32),
            jax.ShapeDtypeStruct((LAYERS, 4, D), F32),
            jax.ShapeDtypeStruct((LAYERS, D), F32),
            jax.ShapeDtypeStruct((LAYERS, 2, 96), F32),
            jax.ShapeDtypeStruct((LAYERS, 169, 3), F32),
        ),
        in_specs=[vmem()],
        out_specs=[vmem()] * 5,
        compiler_params=params(2),
        cost_estimate=cost(0, 1e6),
        name="small_outputs",
    )(rows)


def swap_core(value):
    return lax.ppermute(value, "head", [(i, i ^ 1) for i in range(4)])


def swap_chip(value):
    return lax.ppermute(value, "head", [(i, i ^ 2) for i in range(4)])


def swap_border(value):
    return lax.ppermute(value, "head", [(1, 2), (2, 1)])


def swap_dp(value, step, size):
    return lax.ppermute(value, "dp", [(i, i ^ step) for i in range(size)])


def tie(*values):
    return lax.optimization_barrier(values)


def pick(first, one, other):
    first = first > 0
    return jnp.where(first, one, other), jnp.where(first, other, one)


def dp_masks(across):
    size = lax.axis_size("dp")
    upper = [(2 << b) - 2 for b in range(1, size.bit_length() - 1)]
    if across and upper:
        return [upper[-1]] + upper[:-1] + [1]
    return [1] + upper


def dp_start(parts, sides, across=False):
    half = parts[0].shape[0] // 2
    low = sum(p[:half].astype(F32) for p in parts)
    high = sum(p[half:].astype(F32) for p in parts)
    masks = dp_masks(across)
    kept, sent = pick(sides[int(across)], low, high)
    return kept, swap_dp(sent.astype(LOW), masks[0], lax.axis_size("dp"))


def dp_next(kept, other, across, stage):
    masks = dp_masks(across)
    value = (kept.astype(F32) + other.astype(F32)).astype(LOW)
    return value, swap_dp(value, (masks + masks[:1])[stage], lax.axis_size("dp"))


def dp_join(value, other, sides, across=False):
    low, high = pick(sides[int(across)], value, other)
    return jnp.concatenate([low, high])


def body(
    tokens, outputs_grad, image_kind, qkv_weight, qv_bias, bias_table, proj_weight,
    fc1_weight, fc1_bias, fc2_weight, gains, shifts,
):
    own = tokens.shape[0] // PLACES
    bins = own + 2
    me = lax.axis_index("head").astype(jnp.int32)

    def border(value):
        edge = 4 * PLACES
        return swap_border(jnp.where(me == 1, value[-edge:], value[:edge]))

    def attn_pack(l):
        turned = jnp.transpose(qkv_weight[l], (1, 2, 0)).reshape(288, D)
        return jnp.concatenate([turned, proj_weight[l]], axis=0)

    def mlp_pack(l):
        return jnp.concatenate([fc1_weight[l], fc2_weight[l]], axis=0)

    def norm_pack(l, which, bias_row):
        rows = jnp.stack([gains[l, which], shifts[l, which], shifts[l, bias_row]])
        return jnp.pad(rows, ((0, 5), (0, 0)))

    partner = swap_core(tokens)
    rows = jnp.pad(jnp.transpose(bias_table, (0, 2, 1)).reshape(6, 169), ((0, 0), (0, D - 169)))
    small = jnp.concatenate([rows, qv_bias.reshape(1, D), fc1_bias])
    small = jnp.pad(small, ((0, SMALL - 9), (0, 0)))
    own_pack = [jnp.concatenate([attn_pack(0), *split(small)])]
    chip_pack = [swap_chip(own_pack[0])]
    edges, _ = tie(tokens, own_pack[0])
    halo = border(edges)
    place = lax.axis_index("dp")
    top = lax.axis_size("dp") // 2
    sides = [1 - (place & 1), (place < top).astype(jnp.int32)]
    first = jnp.broadcast_to(jnp.stack(sides).astype(jnp.int32)[:, None], (2, D))
    table = make_plan(image_kind, me, own, bins)
    mlp_first = mlp_pack(0)
    table, first, chip_pack[0], halo, partner, mlp_first = tie(
        table, first, chip_pack[0], halo, partner, mlp_first
    )
    sides = [first[0:1], first[1:2]]
    hidden = gather_slots(table, tokens, partner, halo, bins)

    def gathered(i):
        p, c = own_pack[i], chip_pack[i]
        return p, c, swap_core(p), swap_core(c)

    first_weights = gathered(0)
    bias, qkv_bias, fc1_all = spread_smalls(first_weights)
    pack, hidden, *first_weights = tie(mlp_first, hidden, *first_weights)
    own_pack.append(pack)
    chip_pack.append(swap_chip(pack))

    saved, weights = [], []
    last = LAYERS - 1
    for l in range(LAYERS):
        norms, mlp_norms = norm_pack(l, 0, 2), norm_pack(l, 1, 3)
        weights.append(first_weights if l == 0 else gathered(2 * l))
        mid, a, qkv, probs, attn = attn_forward(
            table, hidden, weights[2 * l], qkv_bias, bias, norms, l
        )
        mid, chip_pack[2 * l + 1] = tie(mid, chip_pack[2 * l + 1])
        weights.append(gathered(2 * l + 1))
        if l == last:
            saved.append((hidden, mid, a, qkv, probs, attn, norms, mlp_norms))
            break
        pack, outputs_grad, mid = tie(attn_pack(1), outputs_grad, mid)
        grad_partner, grad_halo = swap_core(outputs_grad), border(outputs_grad)
        own_pack.append(pack)
        chip_pack.append(swap_chip(pack))
        out, act, slope = mlp_forward(mid, weights[2 * l + 1], fc1_all, mlp_norms, l)
        pack, out, chip_pack[2], grad_partner, grad_halo = tie(
            mlp_pack(1), out, chip_pack[2], grad_partner, grad_halo
        )
        own_pack.append(pack)
        chip_pack.append(swap_chip(pack))
        saved.append((hidden, mid, a, qkv, probs, attn, norms, mlp_norms, act, slope))
        hidden = out
    grad = gather_slots(table, outputs_grad, grad_partner, grad_halo, bins)

    def give_back(value):
        slots = value.reshape(bins, PAD, D)
        return slots, swap_core(slots), swap_border(border_slots(table, slots))

    def mlp_back(l, grad):
        return mlp_backward(
            grad, saved[l][1], saved[l][8], saved[l][9], weights[2 * l + 1], saved[l][7]
        )

    def attn_back(l, grad):
        return attn_backward(table, grad, saved[l][3], saved[l][4], weights[2 * l], l % 2 == 1)

    def attn_sums(l, grad, gqkv, scores, small_mlp, fc1_bias_grad):
        return attn_grads(
            table, grad, saved[l][0], saved[l][2], saved[l][5], gqkv, scores, small_mlp,
            fc1_bias_grad, weights[2 * l], saved[l][6], l % 2 == 1,
        )

    def core_sum(keep, other):
        return [(keep[i].astype(F32) + other[i].astype(F32)).astype(LOW) for i in range(2)]

    out, grad, keep_a, send_a, small_mlp, fc1_bias_grad = mlp_turn(
        saved[last][1], grad, weights[2 * last + 1], fc1_all, saved[last][7], last
    )
    half_a, out_a = core_sum(keep_a, swap_core(send_a))
    grad, out_a = tie(grad, out_a)
    chip_a = swap_chip(out_a)
    gqkv, scores = attn_back(1, grad)
    gqkv, chip_a = tie(gqkv, chip_a)
    state_a = dp_start((half_a, chip_a), sides)
    grad, keep_b, send_b = attn_sums(1, grad, gqkv, scores, small_mlp, fc1_bias_grad)
    grad, state_a, send_b = tie(grad, state_a, send_b)
    half_b, out_b = core_sum(keep_b, swap_core(send_b))
    state_a = dp_next(*state_a, False, 1)
    grad, out_b = tie(grad, out_b)
    chip_b = swap_chip(out_b)
    grad, keep_c, send_c, small_mlp, fc1_bias_grad = mlp_back(0, grad)
    grad, send_c, state_a, chip_b = tie(grad, send_c, state_a, chip_b)
    half_c, out_c = core_sum(keep_c, swap_core(send_c))
    grad, out_c = tie(grad, out_c)
    chip_c = swap_chip(out_c)
    state_a = dp_next(*state_a, False, 2)
    state_b = dp_start((half_b, chip_b), sides)
    gqkv, scores = attn_back(0, grad)
    gqkv, state_a, state_b, chip_c = tie(gqkv, state_a, state_b, chip_c)
    state_a = dp_next(*state_a, False, 3)
    state_b = dp_next(*state_b, False, 1)
    state_c = dp_start((half_c, chip_c), sides, True)
    grad, keep_d, send_d = attn_sums(0, grad, gqkv, scores, small_mlp, fc1_bias_grad)
    half_d, out_d = core_sum(keep_d, swap_core(send_d))
    chip_d = swap_chip(out_d)
    out, _ = tie(out, out_d)
    output_parts = give_back(out)
    chip_d, state_a, state_b, state_c = tie(chip_d, state_a, state_b, state_c)
    state_d = dp_start((half_d, chip_d), sides, True)
    state_c = dp_next(*state_c, True, 1)
    state_b = dp_next(*state_b, False, 2)
    total_a = dp_join(*state_a, sides)
    output = return_slots(table, *output_parts, own)
    tokens_parts = give_back(grad)
    state_d, state_c = tie(state_d, state_c)
    state_d = dp_next(*state_d, True, 1)
    state_c = dp_next(*state_c, True, 2)
    state_d, state_c, state_b = tie(state_d, state_c, state_b)
    state_d = dp_next(*state_d, True, 2)
    state_c = dp_next(*state_c, True, 3)
    state_b = dp_next(*state_b, False, 3)
    tokens_grad = return_slots(table, *tokens_parts, own)
    state_d = dp_next(*state_d, True, 3)
    total_b = dp_join(*state_b, sides)
    total_c = dp_join(*state_c, sides, True)
    mlp_all = jnp.stack([total_c, total_a]).astype(F32)
    fc1_out = mlp_all[:, :D]
    fc2_out = mlp_all[:, D:].transpose(0, 2, 1)
    value_d, other_d = state_d
    value_d, fc1_out, fc2_out, output, tokens_grad = tie(
        value_d, fc1_out, fc2_out, output, tokens_grad
    )
    total_d = dp_join(value_d, other_d, sides, True)

    attn_all = jnp.stack([total_d, total_b]).astype(F32)
    gains_out, shifts_out, fc1_bias_out, qv_out, table_out = small_outputs(attn_all[:, D:])
    qkv_out = attn_all[:, 0:288].reshape(LAYERS, 3, 96, D).transpose(0, 3, 1, 2)
    proj_out = attn_all[:, 288:384]
    return (
        output, tokens_grad, qkv_out, qv_out, table_out, proj_out, fc1_out, fc1_bias_out,
        fc2_out, gains_out, shifts_out,
    )


def solution(mesh):
    rows = P(("dp", "head"), None)
    placed = (
        rows,
        rows,
        P("dp", None),
        P(None, None, None, "head"),
        P(None, None, "head"),
        P(None, None, "head"),
        P(None, "head", None),
        P(None, None, "head"),
        P(None, "head"),
        P(None, "head", None),
        P(),
        P(),
    )
    return jax.shard_map(
        body,
        mesh=mesh,
        in_specs=placed,
        out_specs=(
            rows,
            rows,
            P(None, None, None, "head"),
            P(None, None, "head"),
            P(None, None, "head"),
            P(None, "head", None),
            P(None, None, "head"),
            P(None, "head"),
            P(None, "head", None),
            P(),
            P(),
        ),
        check_vma=False,
    )
```

```python
import jax
import jax.numpy as jnp
from jax import lax
from jax.experimental import pallas as pl
from jax.experimental.pallas import tpu as pltpu
from jax.sharding import PartitionSpec as P

D = 384
FF = 1536
LAYERS = 2
PLACES = 49
PAD = 56
WIDE = 64
QUADS = 3
HEAD_DIM = 32
SCORE_SCALE = HEAD_DIM**-0.5
LN_EPS = 1e-05
LOW = jnp.bfloat16
F32 = jnp.float32
MIB = 1024 * 1024
SMALL = 16

SRC, SIDE, WROW, WCOL, FIRST, RET, SEND = 0, 24, 48, 72, 96, 120, 140
TABLE = 144


def vmem():
    return pl.BlockSpec(memory_space=pltpu.VMEM)


def smem():
    return pl.BlockSpec(memory_space=pltpu.SMEM)


def anywhere():
    return pl.BlockSpec(memory_space=pl.ANY)


def params(limit):
    return pltpu.CompilerParams(vmem_limit_bytes=limit * MIB)


def cost(flops, size):
    return pl.CostEstimate(flops=int(flops * 0.02), bytes_accessed=int(size * 0.02), transcendentals=0)


def dot_nn(a, b):
    return lax.dot_general(a, b, (((1,), (0,)), ((), ())), preferred_element_type=F32)


def dot_nt(a, b):
    return lax.dot_general(a, b, (((1,), (1,)), ((), ())), preferred_element_type=F32)


def dot_tn(a, b):
    return lax.dot_general(a, b, (((0,), (0,)), ((), ())), preferred_element_type=F32)


def plan_kernel(own, bins, kind_ref, me_ref, out_ref, load_ref):
    me = me_ref[0]
    half = 2 * own
    for i in range(TABLE):
        out_ref[i] = -1 if i < bins or RET <= i < RET + own else 0
    for i in range(bins):
        out_ref[SIDE + i] = 1
        out_ref[FIRST + i] = i
    for i in range(4):
        load_ref[i] = 0

    def place(start, count, side, bin_id):
        base = load_ref[bin_id]
        load_ref[bin_id] = base + count

        def step(k, carry):
            slot = start + k
            owner = slot // own
            inner = slot - owner * own
            local = base + k
            mine = bin_id == me
            halo = jnp.where(me == 1, slot - half, slot - half + 4)
            code = jnp.where(
                owner == me, inner, jnp.where(owner == (me ^ 1), own + inner, 2 * own + halo)
            )

            @pl.when(mine)
            def _():
                wrow = k // side
                out_ref[SRC + local] = code
                out_ref[SIDE + local] = side
                out_ref[WROW + local] = wrow
                out_ref[WCOL + local] = k - wrow * side
                out_ref[FIRST + local] = base

            @pl.when(owner == me)
            def _():
                back = jnp.where(me == 2, slot - half, k)
                out_ref[RET + inner] = jnp.where(
                    mine, local, jnp.where(bin_id == (me ^ 1), bins + local, 2 * bins + back)
                )

            return carry

        lax.fori_loop(0, count, step, 0)

    for turn in range(3):

        def visit(i, start, turn=turn):
            kind = kind_ref[0, i]
            count = jnp.where(kind == 2, 9, jnp.where(kind == 1, 4, 0))
            side = jnp.where(kind == 2, 3, 2)
            cut = half - start
            across = (cut > 0) & (cut < count)
            second = (start >= half) | (across & (cut < count - cut))
            chip = jnp.where(second, 1, 0)
            left, right = load_ref[2 * chip], load_ref[2 * chip + 1]
            emptier = 2 * chip + jnp.where(left <= right, 0, 1)
            if turn == 0:
                chosen, bin_id = across, 1 + chip
            else:
                chosen, bin_id = (kind == 3 - turn) & jnp.logical_not(across), emptier

            @pl.when(chosen)
            def _():
                place(start, count, side, bin_id)
                if turn == 0:
                    out_ref[SEND] = jnp.where((me == 1) & (chip == 0), cut, 0)

            return start + count

        lax.fori_loop(0, kind_ref.shape[1], visit, jnp.int32(0))


def gather_kernel(bins, table_ref, refs, out_ref, spread_ref):
    spread_ref[...] = jnp.zeros(spread_ref.shape, F32)
    at = 0
    for ref in refs:
        for s in range(ref.shape[0] // PLACES):
            spread_ref[at, 0:PLACES] = ref[s * PLACES : (s + 1) * PLACES].astype(F32)
            at += 1

    def step(j, carry):
        src = table_ref[SRC + j]

        @pl.when(src < 0)
        def _():
            out_ref[j] = jnp.zeros((PAD, D), F32)

        @pl.when(src >= 0)
        def _():
            out_ref[j] = spread_ref[src]

        return carry

    lax.fori_loop(0, bins, step, 0)


def make_plan(image_kind, me, own, bins):
    def kernel(kind_ref, me_ref, table_ref, load_ref):
        plan_kernel(own, bins, kind_ref, me_ref, table_ref, load_ref)

    return pl.pallas_call(
        kernel,
        out_shape=jax.ShapeDtypeStruct((TABLE,), jnp.int32),
        in_specs=[smem(), smem()],
        out_specs=smem(),
        scratch_shapes=[pltpu.SMEM((4,), jnp.int32)],
        compiler_params=params(1),
        cost_estimate=cost(0, 1.5e7),
        name="plan",
    )(image_kind, me.reshape(1))


def gather_slots(table, mine, partner, halo, bins):
    own = mine.shape[0] // PLACES

    def kernel(table_ref, *refs):
        gather_kernel(bins, table_ref, refs[:3], refs[3], refs[4])

    out = pl.pallas_call(
        kernel,
        out_shape=jax.ShapeDtypeStruct((bins, PAD, D), F32),
        in_specs=[smem()] + [vmem()] * 3,
        out_specs=vmem(),
        scratch_shapes=[pltpu.VMEM((2 * own + 4, PAD, D), F32)],
        compiler_params=params(8),
        cost_estimate=cost(0, 8e6),
        name="gather_slots",
    )(table, mine, partner, halo)
    return out.reshape(bins * PAD, D)


def border_slots(table, slots):
    def kernel(table_ref, slots_ref, out_ref):
        start = table_ref[SEND]
        for j in range(4):
            out_ref[j] = slots_ref[start + j]

    return pl.pallas_call(
        kernel,
        out_shape=jax.ShapeDtypeStruct((4,) + slots.shape[1:], F32),
        in_specs=[smem(), vmem()],
        out_specs=vmem(),
        compiler_params=params(4),
        cost_estimate=cost(0, 1e6),
        name="border_slots",
    )(table, slots)


def return_slots(table, mine, partner, halo, own):
    bins = mine.shape[0]

    def kernel(table_ref, mine_ref, partner_ref, halo_ref, out_ref):
        for s in range(own):
            src = table_ref[RET + s]
            rows = pl.ds(s * PLACES, PLACES)

            @pl.when(src < 0)
            def _():
                out_ref[rows] = jnp.zeros((PLACES, D), F32)

            @pl.when((src >= 0) & (src < bins))
            def _():
                out_ref[rows] = mine_ref[src, 0:PLACES]

            @pl.when((src >= bins) & (src < 2 * bins))
            def _():
                out_ref[rows] = partner_ref[src - bins, 0:PLACES]

            @pl.when(src >= 2 * bins)
            def _():
                out_ref[rows] = halo_ref[src - 2 * bins, 0:PLACES]

    return pl.pallas_call(
        kernel,
        out_shape=jax.ShapeDtypeStruct((own * PLACES, D), F32),
        in_specs=[smem(), vmem(), vmem(), vmem()],
        out_specs=vmem(),
        compiler_params=params(8),
        cost_estimate=cost(0, 8e6),
        name="return_slots",
    )(table, mine, partner, halo)


def norm_rows(rows):
    average = jnp.mean(rows, axis=-1, keepdims=True)
    centred = rows - average
    inverse = lax.rsqrt(jnp.mean(centred * centred, axis=-1, keepdims=True) + LN_EPS)
    return centred * inverse, inverse


def norm_back(incoming, scaled, inverse, gain):
    weighted = incoming * gain
    return inverse * (
        weighted
        - jnp.mean(weighted, axis=-1, keepdims=True)
        - scaled * jnp.mean(weighted * scaled, axis=-1, keepdims=True)
    )


def gelu_parts(x):
    t = 1.0 / (1.0 + 0.23164189 * jnp.abs(x))
    bell = jnp.exp2(x * x * -0.7213475204444817)
    poly = t * (
        0.127414796 + t * (-0.142248368 + t * (0.7107068705 + t * (-0.7265760135 + t * 0.5307027145)))
    )
    tail = poly * bell
    phi = jnp.where(x >= 0, 1.0 - tail, tail)
    return x * phi, phi + x * bell * 0.3989422804014327


def place_parts(shape, dim):
    place = lax.broadcasted_iota(jnp.int32, shape, dim)
    row = (place * 37) >> 8
    return place, row, place - 7 * row


def neighbour(table_ref, w, back, down):
    side, wrow, wcol = table_ref[SIDE + w], table_ref[WROW + w], table_ref[WCOL + w]
    at = wrow if down else wcol
    if back:
        other = jnp.where(at == 0, side - 1, at - 1)
    else:
        other = jnp.where(at == side - 1, 0, at + 1)
    if down:
        return table_ref[FIRST + w] + other * side + wcol
    return table_ref[FIRST + w] + wrow * side + other


def move_windows(table_ref, src, tmp, out, back):
    bins = src.shape[0]
    tmp[...] = jnp.zeros(tmp.shape, F32)
    out[...] = jnp.zeros(out.shape, F32)

    def rows(w, carry):
        other = neighbour(table_ref, w, back, True)
        if back:
            tmp[w, 21:49] = src[w, 0:28]
            tmp[w, 0:21] = src[other, 28:49]
        else:
            tmp[w, 0:28] = src[w, 21:49]
            tmp[w, 28:49] = src[other, 0:21]
        return carry

    lax.fori_loop(0, bins, rows, 0, unroll=2)
    _, _, col = place_parts((PAD, 1), 0)

    def cols(w, carry):
        other = neighbour(table_ref, w, back, False)
        if back:
            out[w, 0:49] = tmp[other, 4:53]
            out[w, 3:49] = jnp.where(col[3:49] >= 3, tmp[w, 0:46], out[w, 3:49])
        else:
            out[w, 0:49] = tmp[w, 3:52]
            out[w, 4:49] = jnp.where(col[4:49] < 4, out[w, 4:49], tmp[other, 0:45])
        return carry

    lax.fori_loop(0, bins, cols, 0, unroll=2)


def head_marks():
    lane = lax.broadcasted_iota(jnp.int32, (WIDE, 128), 1) // HEAD_DIM
    return [jnp.where(lane == h, 1.0, 0.0).astype(LOW) for h in range(4)]


def spread(block, marks):
    return jnp.concatenate([block * mark for mark in marks], axis=0)


def fold(product, marks):
    total = None
    for h, mark in enumerate(marks):
        part = product[h * WIDE : (h + 1) * WIDE] * mark.astype(F32)
        total = part if total is None else total + part
    return total


def spread_pair(block, marks):
    return jnp.concatenate([spread(block[0:WIDE], marks), spread(block[WIDE:], marks)], axis=1)


def diagonal(block):
    zero = jnp.zeros((WIDE, 128), block.dtype)
    top = jnp.concatenate([block[0:WIDE], zero], axis=1)
    return jnp.concatenate([top, jnp.concatenate([zero, block[WIDE:]], axis=1)], axis=0)


def by_head(values):
    return values.reshape(4, WIDE, 128)


def pad_rows(rows):
    return jnp.concatenate([rows, jnp.zeros((WIDE - PAD, rows.shape[1]), rows.dtype)], axis=0)


def split(values):
    high = values.astype(LOW)
    return high, (values - high.astype(F32)).astype(LOW)


def marks_where(rows, cols, test):
    row = lax.broadcasted_iota(jnp.int32, (rows, cols), 0)
    col = lax.broadcasted_iota(jnp.int32, (rows, cols), 1)
    return jnp.where(test(row, col), 1.0, 0.0).astype(LOW)


def far(place):
    row = (place * 37) >> 8
    return 13 * row + (place - 7 * row)


def spread_smalls(smalls):
    heads = LAYERS * 12

    def kernel(p0, p1, p2, p3, out_ref, qkv_ref, fc1_ref, table_ref, small_ref):
        quarters = []
        for k, ref in enumerate((p0, p1, p2, p3)):
            high, low = ref[D : D + SMALL], ref[D + SMALL : D + 2 * SMALL]
            small_ref[k] = high.astype(F32) + low.astype(F32)
            quarters.append(small_ref.at[k])
        for k, ref in enumerate(quarters):
            for l in range(LAYERS):
                at = l * 12 + k * 3
                table_ref[at : at + 3] = ref[l * 3 : l * 3 + 3, 0:256]
        lane = lax.broadcasted_iota(jnp.int32, (8, D), 1)
        for l in range(LAYERS):
            for c in range(3):
                total = jnp.zeros((8, D), F32)
                for k, ref in enumerate(quarters):
                    if c != 1:
                        row = jnp.broadcast_to(ref[6:7], (8, D))
                        row = pltpu.roll(row, (k * 96 - l * 192 - (c // 2) * 96) % D, 1)
                        own_lanes = (lane >= k * 96) & (lane < k * 96 + 96)
                        total = total + jnp.where(own_lanes, row, 0.0)
                qkv_ref[l, :, c * D : (c + 1) * D] = total
            for k, ref in enumerate(quarters):
                row = jnp.broadcast_to(ref[7 + l : 8 + l], (8, D))
                fc1_ref[l, :, k * D : (k + 1) * D] = row
        to_lane = marks_where(128, 128, lambda r, c: (far(c & 63) == r) & ((c & 63) < PLACES))
        to_row = marks_where(WIDE, 96, lambda r, c: (far(r) == c) & (r < PLACES))
        place = lax.broadcasted_iota(jnp.int32, (WIDE, 128), 0)
        empty = jnp.where(place < PLACES, 0.0, -1e30)
        turned = pltpu.roll(table_ref[...], 172, 1)
        skewed = []
        for n in range(heads):
            row = jnp.broadcast_to(turned[n : n + 1], (96, 256))
            skewed.append(pltpu.roll(row, 0, 1, stride=1, stride_axis=0)[:, 0:128])
        skewed = jnp.concatenate(skewed, axis=1)
        total = None
        for part in split(skewed):
            rows = dot_nn(to_row, part).astype(LOW)
            rows = jnp.concatenate([rows[:, n * 128 : (n + 1) * 128] for n in range(heads)], axis=0)
            part = dot_nn(rows, to_lane)
            total = part if total is None else total + part
        for n in range(heads):
            l, t, h = n // 12, n % 12 // 4, n % 4
            out_ref[l, t, h * WIDE : (h + 1) * WIDE] = total[n * WIDE : (n + 1) * WIDE] + empty

    return pl.pallas_call(
        kernel,
        out_shape=(
            jax.ShapeDtypeStruct((LAYERS, QUADS, 4 * WIDE, 128), F32),
            jax.ShapeDtypeStruct((LAYERS, 8, 3 * D), F32),
            jax.ShapeDtypeStruct((LAYERS, 8, FF), F32),
        ),
        in_specs=[vmem()] * 4,
        out_specs=[vmem()] * 3,
        scratch_shapes=[pltpu.VMEM((heads, 256), F32), pltpu.VMEM((4, SMALL, D), F32)],
        compiler_params=params(6),
        cost_estimate=cost(0, 1e7),
        name="spread_smalls",
    )(*smalls)


def scores_to_table(scores_ref):
    to_far = marks_where(128, 128, lambda r, c: (far(r & 63) == c) & ((r & 63) < PLACES))
    to_row = marks_where(96, WIDE, lambda r, c: (84 - far(c) == r) & (c < PLACES))
    wide = None
    for part in split(scores_ref[...].reshape(12 * WIDE, 128)):
        part = dot_nn(part, to_far)
        wide = part if wide is None else wide + part
    wide = jnp.concatenate([wide[h * WIDE : (h + 1) * WIDE] for h in range(12)], axis=1)
    rows = None
    for part in split(wide):
        part = dot_nn(to_row, part)
        rows = part if rows is None else rows + part
    out = []
    for h in range(12):
        one = rows[:, h * 128 : (h + 1) * 128]
        one = jnp.concatenate([one, jnp.zeros_like(one)], axis=1)
        one = pltpu.roll(one, 0, 1, stride=1, stride_axis=0)
        out.append(jnp.sum(one, axis=0, keepdims=True))
    return out


def stack_qkv(pieces, out_ref):
    for k, piece in enumerate(pieces):
        for c in range(3):
            out_ref[c * D + k * 96 : c * D + (k + 1) * 96] = piece[c * 96 : (c + 1) * 96]


def stack_proj(pieces, out_ref):
    for k, piece in enumerate(pieces):
        out_ref[k * 96 : (k + 1) * 96] = piece[288:384]


def stack_mlp(pieces, fc1_ref, fc2_ref):
    for k, piece in enumerate(pieces):
        fc1_ref[:, k * D : (k + 1) * D] = piece[0:D]
        fc2_ref[k * D : (k + 1) * D] = piece[D : 2 * D]


def attn_forward(table, hidden, weights, qv_bias, bias, norms, layer):
    shifted = layer % 2 == 1
    rows = hidden.shape[0]
    bins = rows // PAD
    chunk_slots = 6
    chunk = chunk_slots * PAD
    spare = bins if shifted else 2

    def kernel(
        table_ref, hidden_ref, w0, w1, w2, w3, qv_ref, bias_ref, norm_ref,
        mid_ref, a_ref, qkv_ref, p_ref, attn_ref,
        wqkv, wproj, wide, tmp, moved,
    ):
        pieces = (w0, w1, w2, w3)
        stack_qkv(pieces, wqkv)
        stack_proj(pieces, wproj)
        gain, shift, proj_shift = norm_ref[0:1], norm_ref[1:2], norm_ref[2:3]
        marks = head_marks()
        def norm_step(i, carry):
            at = pl.ds(pl.multiple_of(i * chunk, 16), chunk)
            scaled, _ = norm_rows(hidden_ref[at])
            normed = scaled * gain + shift
            if shifted:
                slots = pl.ds(i * chunk_slots, chunk_slots)
                wide[slots] = normed.reshape(chunk_slots, PAD, D)
            else:
                a_ref[at] = normed.astype(LOW)
            return carry

        lax.fori_loop(0, bins // chunk_slots, norm_step, 0)
        if shifted:
            move_windows(table_ref, wide, tmp, moved, False)
            a_ref[...] = moved[...].reshape(rows, D).astype(LOW)

        def qkv_step(i, carry):
            at = pl.ds(pl.multiple_of(i * chunk, 16), chunk)
            project = dot_nt(a_ref[at], wqkv[...]) + qv_ref[layer, 0:1]
            for j in range(chunk_slots):
                block = project[j * PAD : (j + 1) * PAD]
                at = pl.ds((j % 2) * WIDE, WIDE)
                qkv_ref[i * (chunk_slots // 2) + j // 2, at] = pad_rows(block).astype(LOW)
            return carry

        lax.fori_loop(0, bins // chunk_slots, qkv_step, 0)

        if shifted:
            _, qrow, qcol = place_parts((WIDE, 1), 0)
            lane = lax.broadcasted_iota(jnp.int32, (1, 128), 1)
            second = lane >= WIDE
            pplace = jnp.where(second, lane - WIDE, lane)
            prow = (pplace * 37) >> 8
            pcol = pplace - 7 * prow
            pband = 1 + (prow >= 4).astype(jnp.int32), 1 + (pcol >= 4).astype(jnp.int32)
            qband = 1 + (qrow >= 4).astype(jnp.int32), 1 + (qcol >= 4).astype(jnp.int32)

        def window(j, carry):
            if shifted:
                low = []
                for w in (2 * j, 2 * j + 1):
                    side = table_ref[SIDE + w]
                    low.append(
                        (
                            jnp.where(table_ref[WROW + w] == side - 1, 3, 0),
                            jnp.where(table_ref[WCOL + w] == side - 1, 1, 0),
                        )
                    )
                low_row = jnp.where(second, low[1][0], low[0][0])
                low_col = jnp.where(second, low[1][1], low[0][1])
                pregion = low_row * pband[0] + low_col * pband[1]
                qregion = low_row * qband[0] + low_col * qband[1]
                mask = jnp.where(pregion != qregion, -100.0, 0.0)[None]
            scores, probs = [], []
            for t in range(QUADS):
                q = qkv_ref[j, :, t * 128 : (t + 1) * 128]
                k = qkv_ref[j, :, D + t * 128 : D + (t + 1) * 128]
                scores.append(dot_nt(spread_pair(k, marks), diagonal(q)))
            for t in range(QUADS):
                now = by_head(scores[t] * SCORE_SCALE + bias_ref[layer, t])
                if shifted:
                    now = now + mask
                exponent = jnp.exp(now - jnp.max(now, axis=1, keepdims=True))
                total = jnp.sum(exponent, axis=1, keepdims=True)
                probs.append((exponent * (1.0 / total)).reshape(4 * WIDE, 128).astype(LOW))
                p_ref[j, t] = probs[t]
            for t in range(QUADS):
                cols = slice(t * 128, (t + 1) * 128)
                v = qkv_ref[j, :, 2 * D + t * 128 : 2 * D + (t + 1) * 128]
                both = dot_tn(probs[t], spread_pair(v, marks))
                wide[2 * j, :, cols] = both[0:PAD, 0:128]
                wide[2 * j + 1, :, cols] = both[WIDE : WIDE + PAD, 128:256]
            return carry

        lax.fori_loop(0, bins // 2, window, 0, unroll=9)
        if shifted:
            move_windows(table_ref, wide, tmp, moved, True)
            attn_ref[...] = moved[...].reshape(rows, D).astype(LOW)
        else:
            attn_ref[...] = wide[...].reshape(rows, D).astype(LOW)

        def proj_step(i, carry):
            at = pl.ds(pl.multiple_of(i * chunk, 16), chunk)
            mid_ref[at] = hidden_ref[at] + dot_nn(attn_ref[at], wproj[...]) + proj_shift
            return carry

        lax.fori_loop(0, bins // chunk_slots, proj_step, 0)

    return pl.pallas_call(
        kernel,
        out_shape=(
            jax.ShapeDtypeStruct((rows, D), F32),
            jax.ShapeDtypeStruct((rows, D), LOW),
            jax.ShapeDtypeStruct((bins // 2, 2 * WIDE, 3 * D), LOW),
            jax.ShapeDtypeStruct((bins // 2, QUADS, 4 * WIDE, 128), LOW),
            jax.ShapeDtypeStruct((rows, D), LOW),
        ),
        in_specs=[smem()] + [vmem()] * 8,
        out_specs=[vmem()] * 5,
        scratch_shapes=[
            pltpu.VMEM((3 * D, D), LOW),
            pltpu.VMEM((D, D), LOW),
            pltpu.VMEM((bins, PAD, D), F32),
            pltpu.VMEM((spare, PAD, D), F32),
            pltpu.VMEM((spare, PAD, D), F32),
        ],
        compiler_params=params(11),
        cost_estimate=cost(1e10, 2e7),
        name="attn_forward",
    )(table, hidden, *weights, qv_bias, bias, norms)


def attn_backward(table, grad, qkv, probs, weights, shifted):
    rows = grad.shape[0]
    bins = rows // PAD
    chunk_slots = 6
    chunk = chunk_slots * PAD
    spare = bins if shifted else 2

    def kernel(
        table_ref, grad_ref, qkv_ref, p_ref, w0, w1, w2, w3,
        gqkv_ref, scores_ref, wproj, wide_attn, wide, tmp, moved,
    ):
        stack_proj((w0, w1, w2, w3), wproj)
        marks = head_marks()
        steps = bins // chunk_slots
        def keep_windows(i, block_rows):
            for j in range(chunk_slots):
                block = block_rows[j * PAD : (j + 1) * PAD]
                dest = pl.ds((j % 2) * WIDE, WIDE)
                wide_attn[i * (chunk_slots // 2) + j // 2, dest] = pad_rows(block).astype(LOW)

        def proj_step(i, carry):
            at = pl.ds(pl.multiple_of(i * chunk, 16), chunk)
            gattn = dot_nt(grad_ref[at].astype(LOW), wproj[...])
            if shifted:
                slots = pl.ds(i * chunk_slots, chunk_slots)
                wide[slots] = gattn.reshape(chunk_slots, PAD, D)
            else:
                keep_windows(i, gattn)
            return carry

        lax.fori_loop(0, steps, proj_step, 0)
        if shifted:
            move_windows(table_ref, wide, tmp, moved, False)

            def move_step(i, carry):
                slots = pl.ds(i * chunk_slots, chunk_slots)
                keep_windows(i, moved[slots].reshape(chunk, D))
                return carry

            lax.fori_loop(0, steps, move_step, 0)

        scores_ref[...] = jnp.zeros((QUADS, 4 * WIDE, 128), F32)

        def window(j, carry):
            at = pl.ds(pl.multiple_of(j * 2 * PAD, 16), 2 * PAD)

            def keep(c, t, left, right):
                cols = slice(c * D + t * 128, c * D + (t + 1) * 128)
                gqkv_ref[at, cols] = jnp.concatenate([left, right], axis=0).astype(LOW)

            go, gp, gv, low_ds, gq, gk = [], [], [], [], [], []
            for t in range(QUADS):
                v = qkv_ref[j, :, 2 * D + t * 128 : 2 * D + (t + 1) * 128]
                go.append(diagonal(wide_attn[j, :, t * 128 : (t + 1) * 128]))
                gp.append(dot_nt(spread_pair(v, marks), go[t]))
            for t in range(QUADS):
                gv.append(dot_nn(p_ref[j, t], go[t]))
            for t in range(QUADS):
                p = by_head(p_ref[j, t].astype(F32))
                now = by_head(gp[t])
                ds = p * (now - jnp.sum(now * p, axis=1, keepdims=True))
                low_ds.append(ds.reshape(4 * WIDE, 128).astype(LOW))
                scores_ref[t] += low_ds[t].astype(F32)
            for t in range(QUADS):
                q = qkv_ref[j, :, t * 128 : (t + 1) * 128]
                k = qkv_ref[j, :, D + t * 128 : D + (t + 1) * 128]
                gk.append(dot_nn(low_ds[t], diagonal(q)))
                gq.append(dot_tn(low_ds[t], spread_pair(k, marks)))
            for t in range(QUADS):
                left, right = slice(0, 128), slice(128, 256)
                keep(2, t, fold(gv[t][:, left], marks)[0:PAD], fold(gv[t][:, right], marks)[0:PAD])
            for t in range(QUADS):
                left, right = slice(0, 128), slice(128, 256)
                folded = fold(gk[t][:, left], marks), fold(gk[t][:, right], marks)
                keep(1, t, *[part[0:PAD] * SCORE_SCALE for part in folded])
                parts = gq[t][0:PAD, left], gq[t][WIDE : WIDE + PAD, right]
                keep(0, t, *[part * SCORE_SCALE for part in parts])
            return carry

        lax.fori_loop(0, bins // 2, window, 0, unroll=9)

    return pl.pallas_call(
        kernel,
        out_shape=(
            jax.ShapeDtypeStruct((rows, 3 * D), LOW),
            jax.ShapeDtypeStruct((QUADS, 4 * WIDE, 128), F32),
        ),
        in_specs=[smem()] + [vmem()] * 7,
        out_specs=[vmem()] * 2,
        scratch_shapes=[
            pltpu.VMEM((D, D), LOW),
            pltpu.VMEM((bins // 2, 2 * WIDE, D), LOW),
            pltpu.VMEM((spare, PAD, D), F32),
            pltpu.VMEM((spare, PAD, D), F32),
            pltpu.VMEM((spare, PAD, D), F32),
        ],
        compiler_params=params(11),
        cost_estimate=cost(1e10, 2e7),
        name="attn_backward",
    )(table, grad, qkv, probs, *weights)


def attn_grads(grad, a, attn, gqkv, scores, small_mlp, fc1_bias_grad, weights, norms):
    rows = grad.shape[0]

    def kernel(
        grad_ref, a_ref, attn_ref, gqkv_ref, scores_ref, mlp_ref, fc1b_ref, w0, w1, w2, w3, norm_ref,
        keep_ref, send_ref, wqkv, small,
    ):
        stack_qkv((w0, w1, w2, w3), wqkv)
        gain, shift = norm_ref[0:1], norm_ref[1:2]
        dqkv = dot_tn(a_ref[...], gqkv_ref[...])
        low_grad = grad_ref[...].astype(LOW)
        dproj = dot_tn(attn_ref[...], low_grad).astype(LOW)
        column_sums = jnp.sum(gqkv_ref[...].astype(F32), axis=0, keepdims=True)
        wide_sums = jnp.broadcast_to(column_sums, (16, 3 * D))
        dshift = sum(dot_nn(part, wqkv[...]) for part in split(wide_sums))[0:1]
        table_rows = scores_to_table(scores_ref)
        turned, match = [], jnp.zeros((1, D), F32)
        for c in range(3):
            back = dqkv[:, c * D : (c + 1) * D].T
            here = wqkv[c * D : (c + 1) * D].astype(F32)
            match = match + jnp.sum(back * here, axis=0, keepdims=True)
            turned.append(back.astype(LOW))
        small[...] = jnp.zeros((SMALL, D), F32)
        small[0:1] = (match - shift * dshift) / gain
        small[1:2] = dshift
        small[2:3] = jnp.sum(low_grad.astype(F32), axis=0, keepdims=True)
        small[3:6] = mlp_ref[0:3]
        gq_sum = jnp.broadcast_to(column_sums[:, 0:D], (8, D))
        gv_sum = jnp.broadcast_to(column_sums[:, 2 * D : 3 * D], (8, D))
        for k in range(4):
            dest = keep_ref if k < 2 else send_ref
            for c in range(3):
                dest[k % 2, c * 96 : (c + 1) * 96] = turned[c][k * 96 : (k + 1) * 96]
            dest[k % 2, 288:384] = dproj[k * 96 : (k + 1) * 96]
            small[6:7] = fc1b_ref[:, k * D : (k + 1) * D]
            small[7:8] = pltpu.roll(gq_sum, (D - k * 96) % D, 1)[0:1]
            small[8:9] = pltpu.roll(gv_sum, (D - k * 96) % D, 1)[0:1]
            for h in range(3):
                small[9 + h : 10 + h, 0:256] = table_rows[3 * k + h]
            dest[k % 2, D : D + SMALL] = small[...].astype(LOW)

    return pl.pallas_call(
        kernel,
        out_shape=(
            jax.ShapeDtypeStruct((2, D + SMALL, D), LOW),
            jax.ShapeDtypeStruct((2, D + SMALL, D), LOW),
        ),
        in_specs=[vmem()] * 12,
        out_specs=[vmem()] * 2,
        scratch_shapes=[
            pltpu.VMEM((3 * D, D), LOW),
            pltpu.VMEM((SMALL, D), F32),
        ],
        compiler_params=params(12),
        cost_estimate=cost(6e9, 2e7),
        name="attn_grads",
    )(grad, a, attn, gqkv, scores, small_mlp, fc1_bias_grad, *weights, norms)


def attn_input_grad(table, grad, hidden, gqkv, weights, norms, shifted, work):
    rows = hidden.shape[0]
    bins = rows // PAD
    chunk_slots = 6
    chunk = chunk_slots * PAD
    spare = bins if shifted else 2

    def kernel(
        table_ref, grad_ref, hidden_ref, gqkv_ref, w0, w1, w2, w3, norm_ref,
        out_ref, wqkv, wide, tmp, moved,
    ):
        stack_qkv((w0, w1, w2, w3), wqkv)
        gain = norm_ref[0:1]
        if shifted:
            for i in range(bins // chunk_slots):
                slots = slice(i * chunk_slots, (i + 1) * chunk_slots)
                ga = dot_nn(gqkv_ref[i * chunk : (i + 1) * chunk], wqkv[...])
                wide[slots] = ga.reshape(chunk_slots, PAD, D)
            move_windows(table_ref, wide, tmp, moved, True)

        for i in range(bins // chunk_slots):
            at = slice(i * chunk, (i + 1) * chunk)
            if shifted:
                ga = moved[i * chunk_slots : (i + 1) * chunk_slots].reshape(chunk, D)
            else:
                ga = dot_nn(gqkv_ref[at], wqkv[...])
            scaled, inverse = norm_rows(hidden_ref[at])
            out_ref[at] = grad_ref[at] + norm_back(ga, scaled, inverse, gain)

    return pl.pallas_call(
        kernel,
        out_shape=jax.ShapeDtypeStruct((rows, D), F32),
        in_specs=[smem()] + [vmem()] * 8,
        out_specs=vmem(),
        scratch_shapes=[pltpu.VMEM((3 * D, D), LOW)] + [pltpu.VMEM((spare, PAD, D), F32)] * 3,
        compiler_params=params(12),
        cost_estimate=cost(work, 1e7),
        name="attn_input_grad",
    )(table, grad, hidden, gqkv, *weights, norms)


def mlp_forward(mid, weights, fc1_bias, norms, layer):
    rows = mid.shape[0]
    chunk = 3 * PAD * 2
    steps = rows // chunk

    def kernel(
        mid_ref, w0, w1, w2, w3, fc1_bias_ref, norm_ref,
        out_ref, act_ref, slope_ref, fc1, fc2,
    ):
        stack_mlp((w0, w1, w2, w3), fc1, fc2)
        gain, shift, out_shift = norm_ref[0:1], norm_ref[1:2], norm_ref[2:3]

        def step(i, carry):
            at = pl.ds(pl.multiple_of(i * chunk, 16), chunk)
            rows_now = mid_ref[at]
            scaled, _ = norm_rows(rows_now)
            a = (scaled * gain + shift).astype(LOW)
            act, slope = gelu_parts(dot_nn(a, fc1[...]) + fc1_bias_ref[layer, 0:1])
            act = act.astype(LOW)
            act_ref[at] = act
            slope_ref[at] = slope.astype(LOW)
            out_ref[at] = rows_now + dot_nn(act, fc2[...]) + out_shift
            return carry

        lax.fori_loop(0, steps, step, 0, unroll=True)

    return pl.pallas_call(
        kernel,
        out_shape=(
            jax.ShapeDtypeStruct((rows, D), F32),
            jax.ShapeDtypeStruct((rows, FF), LOW),
            jax.ShapeDtypeStruct((rows, FF), LOW),
        ),
        in_specs=[vmem()] * 7,
        out_specs=[vmem()] * 3,
        scratch_shapes=[pltpu.VMEM((D, FF), LOW), pltpu.VMEM((FF, D), LOW)],
        compiler_params=params(14),
        cost_estimate=cost(7e9, 2e7),
        name="mlp_forward",
    )(mid, *weights, fc1_bias, norms)


def mlp_sums(gpre, a, act, low_grad, fc1, fc1_sums, grad_sums, norms, outs):
    keep_ref, send_ref, small_ref, bias_ref = outs
    gain, shift = norms[0:1], norms[1:2]
    ones = jnp.ones((16, D), LOW)
    match = jnp.zeros((16, D), F32)
    for k in range(4):
        dest = keep_ref if k < 2 else send_ref
        cols = slice(k * D, (k + 1) * D)
        dfc1 = dot_tn(a[...], gpre[:, cols])
        dest[k % 2, 0:D] = dfc1.astype(LOW)
        for part in split(dfc1 * fc1[:, cols].astype(F32)):
            match = match + dot_nt(ones, part)
        dest[k % 2, D : 2 * D] = dot_tn(low_grad[...], act[:, cols]).astype(LOW)
    wide_sums = jnp.broadcast_to(fc1_sums, (16, FF))
    dshift = sum(dot_nt(part, fc1[...]) for part in split(wide_sums))[0:1]
    small_ref[0:1] = (match[0:1] - shift * dshift) / gain
    small_ref[1:2] = dshift
    small_ref[2:3] = grad_sums
    small_ref[3:8] = jnp.zeros((5, D), F32)
    bias_ref[...] = fc1_sums


def sums_shapes():
    return (
        jax.ShapeDtypeStruct((2, 2 * D, D), LOW),
        jax.ShapeDtypeStruct((2, 2 * D, D), LOW),
        jax.ShapeDtypeStruct((8, D), F32),
        jax.ShapeDtypeStruct((1, FF), F32),
    )


def mlp_backward(grad, mid, act, slope, weights, norms):
    rows = mid.shape[0]
    chunk = 6 * PAD
    steps = rows // chunk

    def kernel(
        grad_ref, mid_ref, act_ref, slope_ref, w0, w1, w2, w3, norm_ref,
        gpre_ref, keep_ref, send_ref, small_ref, bias_ref, fc1, fc2, low_grad, a_ref,
    ):
        stack_mlp((w0, w1, w2, w3), fc1, fc2)
        gain, shift = norm_ref[0:1], norm_ref[1:2]
        fc1_sums, grad_sums = jnp.zeros((1, FF), F32), jnp.zeros((1, D), F32)
        for i in range(steps):
            at = slice(i * chunk, (i + 1) * chunk)
            gz = grad_ref[at].astype(LOW)
            low_grad[at] = gz
            gpre = (dot_nt(gz, fc2[...]) * slope_ref[at].astype(F32)).astype(LOW)
            gpre_ref[at] = gpre
            scaled, _ = norm_rows(mid_ref[at])
            a_ref[at] = (scaled * gain + shift).astype(LOW)
            fc1_sums = fc1_sums + jnp.sum(gpre.astype(F32), axis=0, keepdims=True)
            grad_sums = grad_sums + jnp.sum(gz.astype(F32), axis=0, keepdims=True)
        outs = keep_ref, send_ref, small_ref, bias_ref
        mlp_sums(gpre_ref, a_ref, act_ref, low_grad, fc1, fc1_sums, grad_sums, norm_ref, outs)

    return pl.pallas_call(
        kernel,
        out_shape=(jax.ShapeDtypeStruct((rows, FF), LOW), *sums_shapes()),
        in_specs=[vmem()] * 9,
        out_specs=[vmem()] * 5,
        scratch_shapes=[
            pltpu.VMEM((D, FF), LOW),
            pltpu.VMEM((FF, D), LOW),
            pltpu.VMEM((rows, D), LOW),
            pltpu.VMEM((rows, D), LOW),
        ],
        compiler_params=params(18),
        cost_estimate=cost(7e9, 2e7),
        name="mlp_backward",
    )(grad, mid, act, slope, *weights, norms)


def mlp_turn(mid, grad, weights, fc1_bias, norms, layer):
    rows = mid.shape[0]
    chunk = 6 * PAD
    steps = rows // chunk

    def kernel(
        mid_ref, grad_ref, w0, w1, w2, w3, fc1_bias_ref, norm_ref,
        out_ref, gpre_ref, keep_ref, send_ref, small_ref, bias_ref,
        fc1, fc2, a_all, act_all, low_grad,
    ):
        stack_mlp((w0, w1, w2, w3), fc1, fc2)
        gain, shift, out_shift = norm_ref[0:1], norm_ref[1:2], norm_ref[2:3]

        def step(i, totals):
            at = pl.ds(pl.multiple_of(i * chunk, 16), chunk)
            rows_now = mid_ref[at]
            scaled, _ = norm_rows(rows_now)
            a = (scaled * gain + shift).astype(LOW)
            a_all[at] = a
            act, slope = gelu_parts(dot_nn(a, fc1[...]) + fc1_bias_ref[layer, 0:1])
            act = act.astype(LOW)
            act_all[at] = act
            out_ref[at] = rows_now + dot_nn(act, fc2[...]) + out_shift
            gz = grad_ref[at].astype(LOW)
            low_grad[at] = gz
            gpre = (dot_nt(gz, fc2[...]) * slope).astype(LOW)
            gpre_ref[at] = gpre
            return (
                totals[0] + jnp.sum(gz.astype(F32), axis=0, keepdims=True),
                totals[1] + jnp.sum(gpre.astype(F32), axis=0, keepdims=True),
            )

        zeros = jnp.zeros((1, D), F32), jnp.zeros((1, FF), F32)
        grad_sums, fc1_sums = lax.fori_loop(0, steps, step, zeros)
        outs = keep_ref, send_ref, small_ref, bias_ref
        mlp_sums(gpre_ref, a_all, act_all, low_grad, fc1, fc1_sums, grad_sums, norm_ref, outs)

    return pl.pallas_call(
        kernel,
        out_shape=(
            jax.ShapeDtypeStruct((rows, D), F32),
            jax.ShapeDtypeStruct((rows, FF), LOW),
            *sums_shapes(),
        ),
        in_specs=[vmem()] * 8,
        out_specs=[vmem()] * 6,
        scratch_shapes=[
            pltpu.VMEM((D, FF), LOW),
            pltpu.VMEM((FF, D), LOW),
            pltpu.VMEM((rows, D), LOW),
            pltpu.VMEM((rows, FF), LOW),
            pltpu.VMEM((rows, D), LOW),
        ],
        compiler_params=params(18),
        cost_estimate=cost(1.5e10, 4e7),
        name="mlp_turn",
    )(mid, grad, *weights, fc1_bias, norms)


def mlp_input_grad(grad, mid, gpre, weights, norms):
    rows = mid.shape[0]
    chunk = 6 * PAD

    def kernel(grad_ref, mid_ref, gpre_ref, w0, w1, w2, w3, norm_ref, out_ref, fc1):
        for k, piece in enumerate((w0, w1, w2, w3)):
            fc1[:, k * D : (k + 1) * D] = piece[0:D]
        gain = norm_ref[0:1]
        for i in range(rows // chunk):
            at = slice(i * chunk, (i + 1) * chunk)
            ga = dot_nt(gpre_ref[at], fc1[...])
            scaled, inverse = norm_rows(mid_ref[at])
            out_ref[at] = grad_ref[at] + norm_back(ga, scaled, inverse, gain)

    return pl.pallas_call(
        kernel,
        out_shape=jax.ShapeDtypeStruct((rows, D), F32),
        in_specs=[vmem()] * 8,
        out_specs=vmem(),
        scratch_shapes=[pltpu.VMEM((D, FF), LOW)],
        compiler_params=params(8),
        cost_estimate=cost(3e12, 1e7),
        name="mlp_input_grad",
    )(grad, mid, gpre, *weights, norms)


def small_outputs(rows):
    def kernel(rows_ref, gains_ref, shifts_ref, fc1_ref, qv_ref, table_ref):
        for l in range(LAYERS):
            now = rows_ref[l]
            for i, row in enumerate((0, 3)):
                gains_ref[l, i : i + 1] = now[row : row + 1]
            for i, row in enumerate((1, 4, 2, 5)):
                shifts_ref[l, i : i + 1] = now[row : row + 1]
            fc1_ref[l : l + 1] = now[6:7]
            qv_ref[l] = now[7:9, 0:96]
            turned = rows_ref[l, 8:SMALL, 0:256].T
            table_ref[l] = turned[0:169, 1:4]

    return pl.pallas_call(
        kernel,
        out_shape=(
            jax.ShapeDtypeStruct((LAYERS, 2, D), F32),
            jax.ShapeDtypeStruct((LAYERS, 4, D), F32),
            jax.ShapeDtypeStruct((LAYERS, D), F32),
            jax.ShapeDtypeStruct((LAYERS, 2, 96), F32),
            jax.ShapeDtypeStruct((LAYERS, 169, 3), F32),
        ),
        in_specs=[vmem()],
        out_specs=[vmem()] * 5,
        compiler_params=params(4),
        cost_estimate=cost(0, 1e6),
        name="small_outputs",
    )(rows)


def swap_core(value):
    return lax.ppermute(value, "head", [(i, i ^ 1) for i in range(4)])


def swap_chip(value):
    return lax.ppermute(value, "head", [(i, i ^ 2) for i in range(4)])


def swap_border(value):
    return lax.ppermute(value, "head", [(1, 2), (2, 1)])


def swap_dp(value, step, size):
    return lax.ppermute(value, "dp", [(i, i ^ step) for i in range(size)])


def tie(*values):
    return lax.optimization_barrier(values)


def pick(first, one, other):
    first = first > 0
    return jnp.where(first, one, other), jnp.where(first, other, one)


def dp_masks(across):
    size = lax.axis_size("dp")
    upper = [(2 << b) - 2 for b in range(1, size.bit_length() - 1)]
    if across and upper:
        return [upper[-1], 1] + upper[:-1]
    return [1] + upper[::-1]


def dp_start(parts, sides, across=False):
    half = parts[0].shape[0] // 2
    low = sum(p[:half].astype(F32) for p in parts)
    high = sum(p[half:].astype(F32) for p in parts)
    masks = dp_masks(across)
    kept, sent = pick(sides[int(across)], low, high)
    return kept, swap_dp(sent.astype(LOW), masks[0], lax.axis_size("dp"))


def dp_next(kept, other, across, stage):
    masks = dp_masks(across)
    value = (kept.astype(F32) + other.astype(F32)).astype(LOW)
    return value, swap_dp(value, (masks + masks[:1])[stage], lax.axis_size("dp"))


def dp_join(value, other, sides, across=False):
    low, high = pick(sides[int(across)], value, other)
    return jnp.concatenate([low, high])


def body(
    tokens, outputs_grad, image_kind, qkv_weight, qv_bias, bias_table, proj_weight,
    fc1_weight, fc1_bias, fc2_weight, gains, shifts,
):
    own = tokens.shape[0] // PLACES
    bins = own + 2
    me = lax.axis_index("head").astype(jnp.int32)

    def border(value):
        edge = 4 * PLACES
        return swap_border(jnp.where(me == 1, value[-edge:], value[:edge]))

    def attn_pack(l):
        turned = jnp.transpose(qkv_weight[l], (1, 2, 0)).reshape(288, D)
        return jnp.concatenate([turned, proj_weight[l]], axis=0)

    def mlp_pack(l):
        return jnp.concatenate([fc1_weight[l], fc2_weight[l]], axis=0)

    def norm_pack(l, which, bias_row):
        rows = jnp.stack([gains[l, which], shifts[l, which], shifts[l, bias_row]])
        return jnp.pad(rows, ((0, 5), (0, 0)))

    partner = swap_core(tokens)
    rows = jnp.pad(jnp.transpose(bias_table, (0, 2, 1)).reshape(6, 169), ((0, 0), (0, D - 169)))
    small = jnp.concatenate([rows, qv_bias.reshape(1, D), fc1_bias])
    small = jnp.pad(small, ((0, SMALL - 9), (0, 0)))
    own_pack = [jnp.concatenate([attn_pack(0), *split(small)])]
    chip_pack = [swap_chip(own_pack[0])]
    edges, _ = tie(tokens, own_pack[0])
    halo = border(edges)
    place = lax.axis_index("dp")
    top = lax.axis_size("dp") // 2
    sides = [1 - (place & 1), (place < top).astype(jnp.int32)]
    first = jnp.broadcast_to(jnp.stack(sides).astype(jnp.int32)[:, None], (2, D))
    table = make_plan(image_kind, me, own, bins)
    mlp_first = mlp_pack(0)
    table, first, chip_pack[0], halo, partner, mlp_first = tie(
        table, first, chip_pack[0], halo, partner, mlp_first
    )
    sides = [first[0:1], first[1:2]]
    hidden = gather_slots(table, tokens, partner, halo, bins)

    def gathered(i):
        p, c = own_pack[i], chip_pack[i]
        return p, c, swap_core(p), swap_core(c)

    pack, _ = tie(mlp_first, chip_pack[0])
    own_pack.append(pack)
    chip_pack.append(swap_chip(pack))
    first_weights = gathered(0)
    bias, qkv_bias, fc1_all = spread_smalls(first_weights)

    saved, weights = [], []
    last = LAYERS - 1
    for l in range(LAYERS):
        norms, mlp_norms = norm_pack(l, 0, 2), norm_pack(l, 1, 3)
        weights.append(first_weights if l == 0 else gathered(2 * l))
        mid, a, qkv, probs, attn = attn_forward(
            table, hidden, weights[2 * l], qkv_bias, bias, norms, l
        )
        mid, chip_pack[2 * l + 1] = tie(mid, chip_pack[2 * l + 1])
        weights.append(gathered(2 * l + 1))
        if l == last:
            saved.append((hidden, mid, a, qkv, probs, attn, norms, mlp_norms))
            break
        pack, outputs_grad, mid = tie(attn_pack(1), outputs_grad, mid)
        grad_partner, grad_halo = swap_core(outputs_grad), border(outputs_grad)
        own_pack.append(pack)
        chip_pack.append(swap_chip(pack))
        out, act, slope = mlp_forward(mid, weights[2 * l + 1], fc1_all, mlp_norms, l)
        pack, out, chip_pack[2], grad_partner, grad_halo = tie(
            mlp_pack(1), out, chip_pack[2], grad_partner, grad_halo
        )
        own_pack.append(pack)
        chip_pack.append(swap_chip(pack))
        saved.append((hidden, mid, a, qkv, probs, attn, norms, mlp_norms, act, slope))
        hidden = out
    grad = gather_slots(table, outputs_grad, grad_partner, grad_halo, bins)

    def give_back(value):
        slots = value.reshape(bins, PAD, D)
        return slots, swap_core(slots), swap_border(border_slots(table, slots))

    def mlp_back(l, grad):
        return mlp_backward(
            grad, saved[l][1], saved[l][8], saved[l][9], weights[2 * l + 1], saved[l][7]
        )

    def mlp_input(l, grad, gpre):
        return mlp_input_grad(grad, saved[l][1], gpre, weights[2 * l + 1], saved[l][7])

    def attn_back(l, grad):
        return attn_backward(table, grad, saved[l][3], saved[l][4], weights[2 * l], l % 2 == 1)

    def attn_sums(l, grad, gqkv, scores, small_mlp, fc1_bias_grad):
        return attn_grads(
            grad, saved[l][2], saved[l][5], gqkv, scores, small_mlp, fc1_bias_grad,
            weights[2 * l], saved[l][6],
        )

    def attn_input(l, grad, gqkv):
        work = 6e9 if l == last else 3e12
        return attn_input_grad(
            table, grad, saved[l][0], gqkv, weights[2 * l], saved[l][6], l % 2 == 1, work
        )

    def core_sum(keep, other):
        return [(keep[i].astype(F32) + other[i].astype(F32)).astype(LOW) for i in range(2)]

    out, gpre, keep_a, send_a, small_mlp, fc1_bias_grad = mlp_turn(
        saved[last][1], grad, weights[2 * last + 1], fc1_all, saved[last][7], last
    )
    core_a = swap_core(send_a)
    grad = mlp_input(1, grad, gpre)
    grad, core_a = tie(grad, core_a)
    half_a, out_a = core_sum(keep_a, core_a)
    grad, out_a = tie(grad, out_a)
    chip_a = swap_chip(out_a)
    gqkv, scores = attn_back(1, grad)
    grad_after = attn_input(1, grad, gqkv)
    gqkv, _ = tie(gqkv, grad_after)
    keep_b, send_b = attn_sums(1, grad, gqkv, scores, small_mlp, fc1_bias_grad)
    grad, send_b, chip_a = tie(grad_after, send_b, chip_a)
    core_b = swap_core(send_b)
    state_a = dp_start((half_a, chip_a), sides)
    gpre, keep_c, send_c, small_mlp, fc1_bias_grad = mlp_back(0, grad)
    gpre, send_c, state_a, core_b = tie(gpre, send_c, state_a, core_b)
    core_c = swap_core(send_c)
    state_a = dp_next(*state_a, False, 1)
    half_b, out_b = core_sum(keep_b, core_b)
    gpre, out_b = tie(gpre, out_b)
    chip_b = swap_chip(out_b)
    grad = mlp_input(0, grad, gpre)
    grad, core_c = tie(grad, core_c)
    half_c, out_c = core_sum(keep_c, core_c)
    grad, out_c = tie(grad, out_c)
    chip_c = swap_chip(out_c)
    gqkv, scores = attn_back(0, grad)
    keep_d, send_d = attn_sums(0, grad, gqkv, scores, small_mlp, fc1_bias_grad)
    send_d, state_a, chip_b, chip_c = tie(send_d, state_a, chip_b, chip_c)
    core_d = swap_core(send_d)
    state_c = dp_start((half_c, chip_c), sides, True)
    state_a = dp_next(*state_a, False, 2)
    half_d, out_d = core_sum(keep_d, core_d)
    chip_d = swap_chip(out_d)
    gqkv, _ = tie(gqkv, out_d)
    grad = attn_input(0, grad, gqkv)
    out, _ = tie(out, out_d)
    output_parts = give_back(out)
    chip_d, state_a, state_c = tie(chip_d, state_a, state_c)
    half_bd = jnp.concatenate([half_b, half_d])
    state_d = dp_start((half_bd, jnp.concatenate([chip_b, chip_d])), sides, True)
    state_c = dp_next(*state_c, True, 1)
    tokens_parts = give_back(grad)
    state_d, state_c = tie(state_d, state_c)
    state_d = dp_next(*state_d, True, 1)
    state_c = dp_next(*state_c, True, 2)
    output = return_slots(table, *output_parts, own)
    state_d, state_c = tie(state_d, state_c)
    state_d = dp_next(*state_d, True, 2)
    state_c = dp_next(*state_c, True, 3)
    state_a = dp_next(*state_a, False, 3)
    tokens_grad = return_slots(table, *tokens_parts, own)
    state_d, state_c, state_a, output, tokens_grad = tie(
        state_d, state_c, state_a, output, tokens_grad
    )
    value_d, other_d = dp_next(*state_d, True, 3)
    total_a = dp_join(*state_a, sides)
    total_c = dp_join(*state_c, sides, True)
    mlp_all = jnp.stack([total_c, total_a]).astype(F32)
    fc1_out = mlp_all[:, :D]
    fc2_out = mlp_all[:, D:].transpose(0, 2, 1)
    total_bd = dp_join(value_d, other_d, sides, True)
    total_b, total_d = total_bd[: D + SMALL], total_bd[D + SMALL :]

    attn_all = jnp.stack([total_d, total_b]).astype(F32)
    gains_out, shifts_out, fc1_bias_out, qv_out, table_out = small_outputs(attn_all[:, D:])
    qkv_out = attn_all[:, 0:288].reshape(LAYERS, 3, 96, D).transpose(0, 3, 1, 2)
    proj_out = attn_all[:, 288:384]
    return (
        output, tokens_grad, qkv_out, qv_out, table_out, proj_out, fc1_out, fc1_bias_out,
        fc2_out, gains_out, shifts_out,
    )


def solution(mesh):
    rows = P(("dp", "head"), None)
    placed = (
        rows,
        rows,
        P("dp", None),
        P(None, None, None, "head"),
        P(None, None, "head"),
        P(None, None, "head"),
        P(None, "head", None),
        P(None, None, "head"),
        P(None, "head"),
        P(None, "head", None),
        P(),
        P(),
    )
    return jax.shard_map(
        body,
        mesh=mesh,
        in_specs=placed,
        out_specs=(
            rows,
            rows,
            P(None, None, None, "head"),
            P(None, None, "head"),
            P(None, None, "head"),
            P(None, "head", None),
            P(None, None, "head"),
            P(None, "head"),
            P(None, "head", None),
            P(),
            P(),
        ),
        check_vma=False,
    )
```

```python
import jax
import jax.numpy as jnp
from jax import lax
from jax.experimental import pallas as pl
from jax.experimental.pallas import tpu as pltpu
from jax.sharding import PartitionSpec as P

D = 384
FF = 1536
LAYERS = 2
PLACES = 49
PAD = 56
WIDE = 64
QUADS = 3
HEAD_DIM = 32
SCORE_SCALE = HEAD_DIM**-0.5
LN_EPS = 1e-05
LOW = jnp.bfloat16
F32 = jnp.float32
MIB = 1024 * 1024
SMALL = 16

SRC, SIDE, WROW, WCOL, FIRST, RET, SEND = 0, 24, 48, 72, 96, 120, 140
TABLE = 144


def vmem():
    return pl.BlockSpec(memory_space=pltpu.VMEM)


def smem():
    return pl.BlockSpec(memory_space=pltpu.SMEM)


def anywhere():
    return pl.BlockSpec(memory_space=pl.ANY)


def params(limit):
    return pltpu.CompilerParams(vmem_limit_bytes=limit * MIB)


def cost(flops, size):
    return pl.CostEstimate(flops=int(flops * 0.02), bytes_accessed=int(size * 0.02), transcendentals=0)


def dot_nn(a, b):
    return lax.dot_general(a, b, (((1,), (0,)), ((), ())), preferred_element_type=F32)


def dot_nt(a, b):
    return lax.dot_general(a, b, (((1,), (1,)), ((), ())), preferred_element_type=F32)


def dot_tn(a, b):
    return lax.dot_general(a, b, (((0,), (0,)), ((), ())), preferred_element_type=F32)


def plan_kernel(own, bins, kind_ref, me_ref, out_ref, load_ref):
    me = me_ref[0]
    half = 2 * own
    for i in range(TABLE):
        out_ref[i] = -1 if i < bins or RET <= i < RET + own else 0
    for i in range(bins):
        out_ref[SIDE + i] = 1
        out_ref[FIRST + i] = i
    for i in range(4):
        load_ref[i] = 0

    def place(start, count, side, bin_id):
        base = load_ref[bin_id]
        load_ref[bin_id] = base + count

        def step(k, carry):
            slot = start + k
            owner = slot // own
            inner = slot - owner * own
            local = base + k
            mine = bin_id == me
            halo = jnp.where(me == 1, slot - half, slot - half + 4)
            code = jnp.where(
                owner == me, inner, jnp.where(owner == (me ^ 1), own + inner, 2 * own + halo)
            )

            @pl.when(mine)
            def _():
                wrow = k // side
                out_ref[SRC + local] = code
                out_ref[SIDE + local] = side
                out_ref[WROW + local] = wrow
                out_ref[WCOL + local] = k - wrow * side
                out_ref[FIRST + local] = base

            @pl.when(owner == me)
            def _():
                back = jnp.where(me == 2, slot - half, k)
                out_ref[RET + inner] = jnp.where(
                    mine, local, jnp.where(bin_id == (me ^ 1), bins + local, 2 * bins + back)
                )

            return carry

        lax.fori_loop(0, count, step, 0)

    for turn in range(3):

        def visit(i, start, turn=turn):
            kind = kind_ref[0, i]
            count = jnp.where(kind == 2, 9, jnp.where(kind == 1, 4, 0))
            side = jnp.where(kind == 2, 3, 2)
            cut = half - start
            across = (cut > 0) & (cut < count)
            second = (start >= half) | (across & (cut < count - cut))
            chip = jnp.where(second, 1, 0)
            left, right = load_ref[2 * chip], load_ref[2 * chip + 1]
            emptier = 2 * chip + jnp.where(left <= right, 0, 1)
            if turn == 0:
                chosen, bin_id = across, 1 + chip
            else:
                chosen, bin_id = (kind == 3 - turn) & jnp.logical_not(across), emptier

            @pl.when(chosen)
            def _():
                place(start, count, side, bin_id)
                if turn == 0:
                    out_ref[SEND] = jnp.where((me == 1) & (chip == 0), cut, 0)

            return start + count

        lax.fori_loop(0, kind_ref.shape[1], visit, jnp.int32(0))


def gather_kernel(bins, table_ref, refs, out_ref, spread_ref):
    spread_ref[...] = jnp.zeros(spread_ref.shape, F32)
    at = 0
    for ref in refs:
        for s in range(ref.shape[0] // PLACES):
            spread_ref[at, 0:PLACES] = ref[s * PLACES : (s + 1) * PLACES].astype(F32)
            at += 1

    def step(j, carry):
        src = table_ref[SRC + j]

        @pl.when(src < 0)
        def _():
            out_ref[j] = jnp.zeros((PAD, D), F32)

        @pl.when(src >= 0)
        def _():
            out_ref[j] = spread_ref[src]

        return carry

    lax.fori_loop(0, bins, step, 0)


def make_plan(image_kind, me, own, bins):
    def kernel(kind_ref, me_ref, table_ref, load_ref):
        plan_kernel(own, bins, kind_ref, me_ref, table_ref, load_ref)

    return pl.pallas_call(
        kernel,
        out_shape=jax.ShapeDtypeStruct((TABLE,), jnp.int32),
        in_specs=[smem(), smem()],
        out_specs=smem(),
        scratch_shapes=[pltpu.SMEM((4,), jnp.int32)],
        compiler_params=params(1),
        cost_estimate=cost(0, 1.5e7),
        name="plan",
    )(image_kind, me.reshape(1))


def gather_slots(table, mine, partner, halo, bins):
    own = mine.shape[0] // PLACES

    def kernel(table_ref, *refs):
        gather_kernel(bins, table_ref, refs[:3], refs[3], refs[4])

    out = pl.pallas_call(
        kernel,
        out_shape=jax.ShapeDtypeStruct((bins, PAD, D), F32),
        in_specs=[smem()] + [vmem()] * 3,
        out_specs=vmem(),
        scratch_shapes=[pltpu.VMEM((2 * own + 4, PAD, D), F32)],
        compiler_params=params(8),
        cost_estimate=cost(0, 8e6),
        name="gather_slots",
    )(table, mine, partner, halo)
    return out.reshape(bins * PAD, D)


def border_slots(table, slots):
    def kernel(table_ref, slots_ref, out_ref):
        start = table_ref[SEND]
        for j in range(4):
            out_ref[j] = slots_ref[start + j]

    return pl.pallas_call(
        kernel,
        out_shape=jax.ShapeDtypeStruct((4,) + slots.shape[1:], F32),
        in_specs=[smem(), vmem()],
        out_specs=vmem(),
        compiler_params=params(4),
        cost_estimate=cost(0, 1e6),
        name="border_slots",
    )(table, slots)


def return_slots(table, mine, partner, halo, own):
    bins = mine.shape[0]

    def kernel(table_ref, mine_ref, partner_ref, halo_ref, out_ref):
        for s in range(own):
            src = table_ref[RET + s]
            rows = pl.ds(s * PLACES, PLACES)

            @pl.when(src < 0)
            def _():
                out_ref[rows] = jnp.zeros((PLACES, D), F32)

            @pl.when((src >= 0) & (src < bins))
            def _():
                out_ref[rows] = mine_ref[src, 0:PLACES]

            @pl.when((src >= bins) & (src < 2 * bins))
            def _():
                out_ref[rows] = partner_ref[src - bins, 0:PLACES]

            @pl.when(src >= 2 * bins)
            def _():
                out_ref[rows] = halo_ref[src - 2 * bins, 0:PLACES]

    return pl.pallas_call(
        kernel,
        out_shape=jax.ShapeDtypeStruct((own * PLACES, D), F32),
        in_specs=[smem(), vmem(), vmem(), vmem()],
        out_specs=vmem(),
        compiler_params=params(8),
        cost_estimate=cost(0, 8e6),
        name="return_slots",
    )(table, mine, partner, halo)


def norm_rows(rows):
    average = jnp.mean(rows, axis=-1, keepdims=True)
    centred = rows - average
    inverse = lax.rsqrt(jnp.mean(centred * centred, axis=-1, keepdims=True) + LN_EPS)
    return centred * inverse, inverse


def norm_back(incoming, scaled, inverse, gain):
    weighted = incoming * gain
    return inverse * (
        weighted
        - jnp.mean(weighted, axis=-1, keepdims=True)
        - scaled * jnp.mean(weighted * scaled, axis=-1, keepdims=True)
    )


def gelu_parts(x):
    t = 1.0 / (1.0 + 0.23164189 * jnp.abs(x))
    bell = jnp.exp2(x * x * -0.7213475204444817)
    poly = t * (
        0.127414796 + t * (-0.142248368 + t * (0.7107068705 + t * (-0.7265760135 + t * 0.5307027145)))
    )
    tail = poly * bell
    phi = jnp.where(x >= 0, 1.0 - tail, tail)
    return x * phi, phi + x * bell * 0.3989422804014327


def place_parts(shape, dim):
    place = lax.broadcasted_iota(jnp.int32, shape, dim)
    row = (place * 37) >> 8
    return place, row, place - 7 * row


def neighbour(table_ref, w, back, down):
    side, wrow, wcol = table_ref[SIDE + w], table_ref[WROW + w], table_ref[WCOL + w]
    at = wrow if down else wcol
    if back:
        other = jnp.where(at == 0, side - 1, at - 1)
    else:
        other = jnp.where(at == side - 1, 0, at + 1)
    if down:
        return table_ref[FIRST + w] + other * side + wcol
    return table_ref[FIRST + w] + wrow * side + other


def move_windows(table_ref, src, tmp, out, back):
    bins = src.shape[0]
    tmp[...] = jnp.zeros(tmp.shape, F32)
    out[...] = jnp.zeros(out.shape, F32)

    def rows(w, carry):
        other = neighbour(table_ref, w, back, True)
        if back:
            tmp[w, 21:49] = src[w, 0:28]
            tmp[w, 0:21] = src[other, 28:49]
        else:
            tmp[w, 0:28] = src[w, 21:49]
            tmp[w, 28:49] = src[other, 0:21]
        return carry

    lax.fori_loop(0, bins, rows, 0, unroll=2)
    _, _, col = place_parts((PAD, 1), 0)

    def cols(w, carry):
        other = neighbour(table_ref, w, back, False)
        if back:
            out[w, 0:49] = tmp[other, 4:53]
            out[w, 3:49] = jnp.where(col[3:49] >= 3, tmp[w, 0:46], out[w, 3:49])
        else:
            out[w, 0:49] = tmp[w, 3:52]
            out[w, 4:49] = jnp.where(col[4:49] < 4, out[w, 4:49], tmp[other, 0:45])
        return carry

    lax.fori_loop(0, bins, cols, 0, unroll=2)


def head_marks():
    lane = lax.broadcasted_iota(jnp.int32, (WIDE, 128), 1) // HEAD_DIM
    return [jnp.where(lane == h, 1.0, 0.0).astype(LOW) for h in range(4)]


def spread(block, marks):
    return jnp.concatenate([block * mark for mark in marks], axis=0)


def fold(product, marks):
    total = None
    for h, mark in enumerate(marks):
        part = product[h * WIDE : (h + 1) * WIDE] * mark.astype(F32)
        total = part if total is None else total + part
    return total


def spread_pair(block, marks):
    return jnp.concatenate([spread(block[0:WIDE], marks), spread(block[WIDE:], marks)], axis=1)


def diagonal(block):
    zero = jnp.zeros((WIDE, 128), block.dtype)
    top = jnp.concatenate([block[0:WIDE], zero], axis=1)
    return jnp.concatenate([top, jnp.concatenate([zero, block[WIDE:]], axis=1)], axis=0)


def by_head(values):
    return values.reshape(4, WIDE, 128)


def pad_rows(rows):
    return jnp.concatenate([rows, jnp.zeros((WIDE - PAD, rows.shape[1]), rows.dtype)], axis=0)


def split(values):
    high = values.astype(LOW)
    return high, (values - high.astype(F32)).astype(LOW)


def marks_where(rows, cols, test):
    row = lax.broadcasted_iota(jnp.int32, (rows, cols), 0)
    col = lax.broadcasted_iota(jnp.int32, (rows, cols), 1)
    return jnp.where(test(row, col), 1.0, 0.0).astype(LOW)


def far(place):
    row = (place * 37) >> 8
    return 13 * row + (place - 7 * row)


def spread_smalls(smalls):
    heads = LAYERS * 12

    def kernel(p0, p1, p2, p3, out_ref, qkv_ref, fc1_ref, table_ref, small_ref):
        quarters = []
        for k, ref in enumerate((p0, p1, p2, p3)):
            high, low = ref[D : D + SMALL], ref[D + SMALL : D + 2 * SMALL]
            small_ref[k] = high.astype(F32) + low.astype(F32)
            quarters.append(small_ref.at[k])
        for k, ref in enumerate(quarters):
            for l in range(LAYERS):
                at = l * 12 + k * 3
                table_ref[at : at + 3] = ref[l * 3 : l * 3 + 3, 0:256]
        lane = lax.broadcasted_iota(jnp.int32, (8, D), 1)
        for l in range(LAYERS):
            for c in range(3):
                total = jnp.zeros((8, D), F32)
                for k, ref in enumerate(quarters):
                    if c != 1:
                        row = jnp.broadcast_to(ref[6:7], (8, D))
                        row = pltpu.roll(row, (k * 96 - l * 192 - (c // 2) * 96) % D, 1)
                        own_lanes = (lane >= k * 96) & (lane < k * 96 + 96)
                        total = total + jnp.where(own_lanes, row, 0.0)
                qkv_ref[l, :, c * D : (c + 1) * D] = total
            for k, ref in enumerate(quarters):
                row = jnp.broadcast_to(ref[7 + l : 8 + l], (8, D))
                fc1_ref[l, :, k * D : (k + 1) * D] = row
        to_lane = marks_where(128, 128, lambda r, c: (far(c & 63) == r) & ((c & 63) < PLACES))
        to_row = marks_where(WIDE, 96, lambda r, c: (far(r) == c) & (r < PLACES))
        place = lax.broadcasted_iota(jnp.int32, (WIDE, 128), 0)
        empty = jnp.where(place < PLACES, 0.0, -1e30)
        turned = pltpu.roll(table_ref[...], 172, 1)
        skewed = []
        for n in range(heads):
            row = jnp.broadcast_to(turned[n : n + 1], (96, 256))
            skewed.append(pltpu.roll(row, 0, 1, stride=1, stride_axis=0)[:, 0:128])
        skewed = jnp.concatenate(skewed, axis=1)
        total = None
        for part in split(skewed):
            rows = dot_nn(to_row, part).astype(LOW)
            rows = jnp.concatenate([rows[:, n * 128 : (n + 1) * 128] for n in range(heads)], axis=0)
            part = dot_nn(rows, to_lane)
            total = part if total is None else total + part
        for n in range(heads):
            l, t, h = n // 12, n % 12 // 4, n % 4
            out_ref[l, t, h * WIDE : (h + 1) * WIDE] = total[n * WIDE : (n + 1) * WIDE] + empty

    return pl.pallas_call(
        kernel,
        out_shape=(
            jax.ShapeDtypeStruct((LAYERS, QUADS, 4 * WIDE, 128), F32),
            jax.ShapeDtypeStruct((LAYERS, 8, 3 * D), F32),
            jax.ShapeDtypeStruct((LAYERS, 8, FF), F32),
        ),
        in_specs=[vmem()] * 4,
        out_specs=[vmem()] * 3,
        scratch_shapes=[pltpu.VMEM((heads, 256), F32), pltpu.VMEM((4, SMALL, D), F32)],
        compiler_params=params(6),
        cost_estimate=cost(0, 1e7),
        name="spread_smalls",
    )(*smalls)


def scores_to_table(scores_ref):
    to_far = marks_where(128, 128, lambda r, c: (far(r & 63) == c) & ((r & 63) < PLACES))
    to_row = marks_where(96, WIDE, lambda r, c: (84 - far(c) == r) & (c < PLACES))
    wide = None
    for part in split(scores_ref[...].reshape(12 * WIDE, 128)):
        part = dot_nn(part, to_far)
        wide = part if wide is None else wide + part
    wide = jnp.concatenate([wide[h * WIDE : (h + 1) * WIDE] for h in range(12)], axis=1)
    rows = None
    for part in split(wide):
        part = dot_nn(to_row, part)
        rows = part if rows is None else rows + part
    out = []
    for h in range(12):
        one = rows[:, h * 128 : (h + 1) * 128]
        one = jnp.concatenate([one, jnp.zeros_like(one)], axis=1)
        one = pltpu.roll(one, 0, 1, stride=1, stride_axis=0)
        out.append(jnp.sum(one, axis=0, keepdims=True))
    return out


def stack_qkv(pieces, out_ref):
    for k, piece in enumerate(pieces):
        for c in range(3):
            out_ref[c * D + k * 96 : c * D + (k + 1) * 96] = piece[c * 96 : (c + 1) * 96]


def stack_proj(pieces, out_ref):
    for k, piece in enumerate(pieces):
        out_ref[k * 96 : (k + 1) * 96] = piece[288:384]


def stack_mlp(pieces, fc1_ref, fc2_ref):
    for k, piece in enumerate(pieces):
        fc1_ref[:, k * D : (k + 1) * D] = piece[0:D]
        fc2_ref[k * D : (k + 1) * D] = piece[D : 2 * D]


def attn_forward(table, hidden, weights, qv_bias, bias, norms, layer):
    shifted = layer % 2 == 1
    rows = hidden.shape[0]
    bins = rows // PAD
    chunk_slots = 6
    chunk = chunk_slots * PAD
    spare = bins if shifted else 2

    def kernel(
        table_ref, hidden_ref, w0, w1, w2, w3, qv_ref, bias_ref, norm_ref,
        mid_ref, a_ref, qkv_ref, p_ref, attn_ref,
        wqkv, wproj, wide, tmp, moved,
    ):
        pieces = (w0, w1, w2, w3)
        stack_qkv(pieces, wqkv)
        stack_proj(pieces, wproj)
        gain, shift, proj_shift = norm_ref[0:1], norm_ref[1:2], norm_ref[2:3]
        marks = head_marks()
        def norm_step(i, carry):
            at = pl.ds(pl.multiple_of(i * chunk, 16), chunk)
            scaled, _ = norm_rows(hidden_ref[at])
            normed = scaled * gain + shift
            if shifted:
                slots = pl.ds(i * chunk_slots, chunk_slots)
                wide[slots] = normed.reshape(chunk_slots, PAD, D)
            else:
                a_ref[at] = normed.astype(LOW)
            return carry

        lax.fori_loop(0, bins // chunk_slots, norm_step, 0)
        if shifted:
            move_windows(table_ref, wide, tmp, moved, False)
            a_ref[...] = moved[...].reshape(rows, D).astype(LOW)

        def qkv_step(i, carry):
            at = pl.ds(pl.multiple_of(i * chunk, 16), chunk)
            project = dot_nt(a_ref[at], wqkv[...]) + qv_ref[layer, 0:1]
            for j in range(chunk_slots):
                block = project[j * PAD : (j + 1) * PAD]
                at = pl.ds((j % 2) * WIDE, WIDE)
                qkv_ref[i * (chunk_slots // 2) + j // 2, at] = pad_rows(block).astype(LOW)
            return carry

        lax.fori_loop(0, bins // chunk_slots, qkv_step, 0)

        if shifted:
            _, qrow, qcol = place_parts((WIDE, 1), 0)
            lane = lax.broadcasted_iota(jnp.int32, (1, 128), 1)
            second = lane >= WIDE
            pplace = jnp.where(second, lane - WIDE, lane)
            prow = (pplace * 37) >> 8
            pcol = pplace - 7 * prow
            pband = 1 + (prow >= 4).astype(jnp.int32), 1 + (pcol >= 4).astype(jnp.int32)
            qband = 1 + (qrow >= 4).astype(jnp.int32), 1 + (qcol >= 4).astype(jnp.int32)

        def window(j, carry):
            if shifted:
                low = []
                for w in (2 * j, 2 * j + 1):
                    side = table_ref[SIDE + w]
                    low.append(
                        (
                            jnp.where(table_ref[WROW + w] == side - 1, 3, 0),
                            jnp.where(table_ref[WCOL + w] == side - 1, 1, 0),
                        )
                    )
                low_row = jnp.where(second, low[1][0], low[0][0])
                low_col = jnp.where(second, low[1][1], low[0][1])
                pregion = low_row * pband[0] + low_col * pband[1]
                qregion = low_row * qband[0] + low_col * qband[1]
                mask = jnp.where(pregion != qregion, -100.0, 0.0)[None]
            scores, probs = [], []
            for t in range(QUADS):
                q = qkv_ref[j, :, t * 128 : (t + 1) * 128]
                k = qkv_ref[j, :, D + t * 128 : D + (t + 1) * 128]
                scores.append(dot_nt(spread_pair(k, marks), diagonal(q)))
            for t in range(QUADS):
                now = by_head(scores[t] * SCORE_SCALE + bias_ref[layer, t])
                if shifted:
                    now = now + mask
                exponent = jnp.exp(now - jnp.max(now, axis=1, keepdims=True))
                total = jnp.sum(exponent, axis=1, keepdims=True)
                probs.append((exponent * (1.0 / total)).reshape(4 * WIDE, 128).astype(LOW))
                p_ref[j, t] = probs[t]
            for t in range(QUADS):
                cols = slice(t * 128, (t + 1) * 128)
                v = qkv_ref[j, :, 2 * D + t * 128 : 2 * D + (t + 1) * 128]
                both = dot_tn(probs[t], spread_pair(v, marks))
                wide[2 * j, :, cols] = both[0:PAD, 0:128]
                wide[2 * j + 1, :, cols] = both[WIDE : WIDE + PAD, 128:256]
            return carry

        lax.fori_loop(0, bins // 2, window, 0, unroll=9)
        if shifted:
            move_windows(table_ref, wide, tmp, moved, True)
            attn_ref[...] = moved[...].reshape(rows, D).astype(LOW)
        else:
            attn_ref[...] = wide[...].reshape(rows, D).astype(LOW)

        def proj_step(i, carry):
            at = pl.ds(pl.multiple_of(i * chunk, 16), chunk)
            mid_ref[at] = hidden_ref[at] + dot_nn(attn_ref[at], wproj[...]) + proj_shift
            return carry

        lax.fori_loop(0, bins // chunk_slots, proj_step, 0)

    return pl.pallas_call(
        kernel,
        out_shape=(
            jax.ShapeDtypeStruct((rows, D), F32),
            jax.ShapeDtypeStruct((rows, D), LOW),
            jax.ShapeDtypeStruct((bins // 2, 2 * WIDE, 3 * D), LOW),
            jax.ShapeDtypeStruct((bins // 2, QUADS, 4 * WIDE, 128), LOW),
            jax.ShapeDtypeStruct((rows, D), LOW),
        ),
        in_specs=[smem()] + [vmem()] * 8,
        out_specs=[vmem()] * 5,
        scratch_shapes=[
            pltpu.VMEM((3 * D, D), LOW),
            pltpu.VMEM((D, D), LOW),
            pltpu.VMEM((bins, PAD, D), F32),
            pltpu.VMEM((spare, PAD, D), F32),
            pltpu.VMEM((spare, PAD, D), F32),
        ],
        compiler_params=params(11),
        cost_estimate=cost(1e10, 2e7),
        name="attn_forward",
    )(table, hidden, *weights, qv_bias, bias, norms)


def attn_backward(table, grad, qkv, probs, weights, shifted):
    rows = grad.shape[0]
    bins = rows // PAD
    chunk_slots = 6
    chunk = chunk_slots * PAD
    spare = bins if shifted else 2

    def kernel(
        table_ref, grad_ref, qkv_ref, p_ref, w0, w1, w2, w3,
        gqkv_ref, scores_ref, wproj, wide_attn, wide, tmp, moved,
    ):
        stack_proj((w0, w1, w2, w3), wproj)
        marks = head_marks()
        steps = bins // chunk_slots
        def keep_windows(i, block_rows):
            for j in range(chunk_slots):
                block = block_rows[j * PAD : (j + 1) * PAD]
                dest = pl.ds((j % 2) * WIDE, WIDE)
                wide_attn[i * (chunk_slots // 2) + j // 2, dest] = pad_rows(block).astype(LOW)

        def proj_step(i, carry):
            at = pl.ds(pl.multiple_of(i * chunk, 16), chunk)
            gattn = dot_nt(grad_ref[at].astype(LOW), wproj[...])
            if shifted:
                slots = pl.ds(i * chunk_slots, chunk_slots)
                wide[slots] = gattn.reshape(chunk_slots, PAD, D)
            else:
                keep_windows(i, gattn)
            return carry

        lax.fori_loop(0, steps, proj_step, 0)
        if shifted:
            move_windows(table_ref, wide, tmp, moved, False)

            def move_step(i, carry):
                slots = pl.ds(i * chunk_slots, chunk_slots)
                keep_windows(i, moved[slots].reshape(chunk, D))
                return carry

            lax.fori_loop(0, steps, move_step, 0)

        scores_ref[...] = jnp.zeros((QUADS, 4 * WIDE, 128), F32)

        def window(j, carry):
            at = pl.ds(pl.multiple_of(j * 2 * PAD, 16), 2 * PAD)

            def keep(c, t, left, right):
                cols = slice(c * D + t * 128, c * D + (t + 1) * 128)
                gqkv_ref[at, cols] = jnp.concatenate([left, right], axis=0).astype(LOW)

            go, gp, gv, low_ds, gq, gk = [], [], [], [], [], []
            for t in range(QUADS):
                v = qkv_ref[j, :, 2 * D + t * 128 : 2 * D + (t + 1) * 128]
                go.append(diagonal(wide_attn[j, :, t * 128 : (t + 1) * 128]))
                gp.append(dot_nt(spread_pair(v, marks), go[t]))
            for t in range(QUADS):
                gv.append(dot_nn(p_ref[j, t], go[t]))
            for t in range(QUADS):
                p = by_head(p_ref[j, t].astype(F32))
                now = by_head(gp[t])
                ds = p * (now - jnp.sum(now * p, axis=1, keepdims=True))
                low_ds.append(ds.reshape(4 * WIDE, 128).astype(LOW))
                scores_ref[t] += low_ds[t].astype(F32)
            for t in range(QUADS):
                q = qkv_ref[j, :, t * 128 : (t + 1) * 128]
                k = qkv_ref[j, :, D + t * 128 : D + (t + 1) * 128]
                gk.append(dot_nn(low_ds[t], diagonal(q)))
                gq.append(dot_tn(low_ds[t], spread_pair(k, marks)))
            for t in range(QUADS):
                left, right = slice(0, 128), slice(128, 256)
                keep(2, t, fold(gv[t][:, left], marks)[0:PAD], fold(gv[t][:, right], marks)[0:PAD])
            for t in range(QUADS):
                left, right = slice(0, 128), slice(128, 256)
                folded = fold(gk[t][:, left], marks), fold(gk[t][:, right], marks)
                keep(1, t, *[part[0:PAD] * SCORE_SCALE for part in folded])
                parts = gq[t][0:PAD, left], gq[t][WIDE : WIDE + PAD, right]
                keep(0, t, *[part * SCORE_SCALE for part in parts])
            return carry

        lax.fori_loop(0, bins // 2, window, 0, unroll=9)

    return pl.pallas_call(
        kernel,
        out_shape=(
            jax.ShapeDtypeStruct((rows, 3 * D), LOW),
            jax.ShapeDtypeStruct((QUADS, 4 * WIDE, 128), F32),
        ),
        in_specs=[smem()] + [vmem()] * 7,
        out_specs=[vmem()] * 2,
        scratch_shapes=[
            pltpu.VMEM((D, D), LOW),
            pltpu.VMEM((bins // 2, 2 * WIDE, D), LOW),
            pltpu.VMEM((spare, PAD, D), F32),
            pltpu.VMEM((spare, PAD, D), F32),
            pltpu.VMEM((spare, PAD, D), F32),
        ],
        compiler_params=params(11),
        cost_estimate=cost(1e10, 2e7),
        name="attn_backward",
    )(table, grad, qkv, probs, *weights)


def attn_grads(grad, a, attn, gqkv, scores, small_mlp, fc1_bias_grad, weights, norms):
    rows = grad.shape[0]

    def kernel(
        grad_ref, a_ref, attn_ref, gqkv_ref, scores_ref, mlp_ref, fc1b_ref, w0, w1, w2, w3, norm_ref,
        keep_ref, send_ref, wqkv, small,
    ):
        stack_qkv((w0, w1, w2, w3), wqkv)
        gain, shift = norm_ref[0:1], norm_ref[1:2]
        dqkv = dot_tn(a_ref[...], gqkv_ref[...])
        low_grad = grad_ref[...].astype(LOW)
        dproj = dot_tn(attn_ref[...], low_grad).astype(LOW)
        column_sums = jnp.sum(gqkv_ref[...].astype(F32), axis=0, keepdims=True)
        wide_sums = jnp.broadcast_to(column_sums, (16, 3 * D))
        dshift = sum(dot_nn(part, wqkv[...]) for part in split(wide_sums))[0:1]
        table_rows = scores_to_table(scores_ref)
        turned, match = [], jnp.zeros((1, D), F32)
        for c in range(3):
            back = dqkv[:, c * D : (c + 1) * D].T
            here = wqkv[c * D : (c + 1) * D].astype(F32)
            match = match + jnp.sum(back * here, axis=0, keepdims=True)
            turned.append(back.astype(LOW))
        small[...] = jnp.zeros((SMALL, D), F32)
        small[0:1] = (match - shift * dshift) / gain
        small[1:2] = dshift
        small[2:3] = jnp.sum(low_grad.astype(F32), axis=0, keepdims=True)
        small[3:6] = mlp_ref[0:3]
        gq_sum = jnp.broadcast_to(column_sums[:, 0:D], (8, D))
        gv_sum = jnp.broadcast_to(column_sums[:, 2 * D : 3 * D], (8, D))
        for k in range(4):
            dest = keep_ref if k < 2 else send_ref
            for c in range(3):
                dest[k % 2, c * 96 : (c + 1) * 96] = turned[c][k * 96 : (k + 1) * 96]
            dest[k % 2, 288:384] = dproj[k * 96 : (k + 1) * 96]
            small[6:7] = fc1b_ref[:, k * D : (k + 1) * D]
            small[7:8] = pltpu.roll(gq_sum, (D - k * 96) % D, 1)[0:1]
            small[8:9] = pltpu.roll(gv_sum, (D - k * 96) % D, 1)[0:1]
            for h in range(3):
                small[9 + h : 10 + h, 0:256] = table_rows[3 * k + h]
            dest[k % 2, D : D + SMALL] = small[...].astype(LOW)

    return pl.pallas_call(
        kernel,
        out_shape=(
            jax.ShapeDtypeStruct((2, D + SMALL, D), LOW),
            jax.ShapeDtypeStruct((2, D + SMALL, D), LOW),
        ),
        in_specs=[vmem()] * 12,
        out_specs=[vmem()] * 2,
        scratch_shapes=[
            pltpu.VMEM((3 * D, D), LOW),
            pltpu.VMEM((SMALL, D), F32),
        ],
        compiler_params=params(12),
        cost_estimate=cost(6e9, 2e7),
        name="attn_grads",
    )(grad, a, attn, gqkv, scores, small_mlp, fc1_bias_grad, *weights, norms)


def attn_input_grad(table, grad, hidden, gqkv, weights, norms, shifted, work):
    rows = hidden.shape[0]
    bins = rows // PAD
    chunk_slots = 6
    chunk = chunk_slots * PAD
    spare = bins if shifted else 2

    def kernel(
        table_ref, grad_ref, hidden_ref, gqkv_ref, w0, w1, w2, w3, norm_ref,
        out_ref, wqkv, wide, tmp, moved,
    ):
        stack_qkv((w0, w1, w2, w3), wqkv)
        gain = norm_ref[0:1]
        if shifted:
            for i in range(bins // chunk_slots):
                slots = slice(i * chunk_slots, (i + 1) * chunk_slots)
                ga = dot_nn(gqkv_ref[i * chunk : (i + 1) * chunk], wqkv[...])
                wide[slots] = ga.reshape(chunk_slots, PAD, D)
            move_windows(table_ref, wide, tmp, moved, True)

        for i in range(bins // chunk_slots):
            at = slice(i * chunk, (i + 1) * chunk)
            if shifted:
                ga = moved[i * chunk_slots : (i + 1) * chunk_slots].reshape(chunk, D)
            else:
                ga = dot_nn(gqkv_ref[at], wqkv[...])
            scaled, inverse = norm_rows(hidden_ref[at])
            out_ref[at] = grad_ref[at] + norm_back(ga, scaled, inverse, gain)

    return pl.pallas_call(
        kernel,
        out_shape=jax.ShapeDtypeStruct((rows, D), F32),
        in_specs=[smem()] + [vmem()] * 8,
        out_specs=vmem(),
        scratch_shapes=[pltpu.VMEM((3 * D, D), LOW)] + [pltpu.VMEM((spare, PAD, D), F32)] * 3,
        compiler_params=params(12),
        cost_estimate=cost(work, 1e7),
        name="attn_input_grad",
    )(table, grad, hidden, gqkv, *weights, norms)


def mlp_forward(mid, weights, fc1_bias, norms, layer):
    rows = mid.shape[0]
    chunk = 3 * PAD * 2
    steps = rows // chunk

    def kernel(
        mid_ref, w0, w1, w2, w3, fc1_bias_ref, norm_ref,
        out_ref, act_ref, slope_ref, fc1, fc2,
    ):
        stack_mlp((w0, w1, w2, w3), fc1, fc2)
        gain, shift, out_shift = norm_ref[0:1], norm_ref[1:2], norm_ref[2:3]

        def step(i, carry):
            at = pl.ds(pl.multiple_of(i * chunk, 16), chunk)
            rows_now = mid_ref[at]
            scaled, _ = norm_rows(rows_now)
            a = (scaled * gain + shift).astype(LOW)
            act, slope = gelu_parts(dot_nn(a, fc1[...]) + fc1_bias_ref[layer, 0:1])
            act = act.astype(LOW)
            act_ref[at] = act
            slope_ref[at] = slope.astype(LOW)
            out_ref[at] = rows_now + dot_nn(act, fc2[...]) + out_shift
            return carry

        lax.fori_loop(0, steps, step, 0, unroll=True)

    return pl.pallas_call(
        kernel,
        out_shape=(
            jax.ShapeDtypeStruct((rows, D), F32),
            jax.ShapeDtypeStruct((rows, FF), LOW),
            jax.ShapeDtypeStruct((rows, FF), LOW),
        ),
        in_specs=[vmem()] * 7,
        out_specs=[vmem()] * 3,
        scratch_shapes=[pltpu.VMEM((D, FF), LOW), pltpu.VMEM((FF, D), LOW)],
        compiler_params=params(14),
        cost_estimate=cost(7e9, 2e7),
        name="mlp_forward",
    )(mid, *weights, fc1_bias, norms)


def mlp_sums(gpre, a, act, low_grad, fc1, fc1_sums, grad_sums, norms, outs):
    keep_ref, send_ref, small_ref, bias_ref = outs
    gain, shift = norms[0:1], norms[1:2]
    dfc1 = dot_tn(a[...], gpre[...])
    dfc2 = dot_tn(low_grad[...], act[...])
    column = jnp.sum(dfc1 * fc1[...].astype(F32), axis=1, keepdims=True)
    match = jnp.broadcast_to(column, (D, 128)).T
    for k in range(4):
        dest = keep_ref if k < 2 else send_ref
        cols = slice(k * D, (k + 1) * D)
        dest[k % 2, 0:D] = dfc1[:, cols].astype(LOW)
        dest[k % 2, D : 2 * D] = dfc2[:, cols].astype(LOW)
    wide_sums = jnp.broadcast_to(fc1_sums, (16, FF))
    dshift = sum(dot_nt(part, fc1[...]) for part in split(wide_sums))[0:1]
    small_ref[0:1] = (match[0:1] - shift * dshift) / gain
    small_ref[1:2] = dshift
    small_ref[2:3] = grad_sums
    small_ref[3:8] = jnp.zeros((5, D), F32)
    bias_ref[...] = fc1_sums


def sums_shapes():
    return (
        jax.ShapeDtypeStruct((2, 2 * D, D), LOW),
        jax.ShapeDtypeStruct((2, 2 * D, D), LOW),
        jax.ShapeDtypeStruct((8, D), F32),
        jax.ShapeDtypeStruct((1, FF), F32),
    )


def mlp_backward(grad, mid, act, slope, weights, norms):
    rows = mid.shape[0]
    chunk = 6 * PAD
    steps = rows // chunk

    def kernel(
        grad_ref, mid_ref, act_ref, slope_ref, w0, w1, w2, w3, norm_ref,
        gpre_ref, keep_ref, send_ref, small_ref, bias_ref, fc1, fc2, low_grad, a_ref,
    ):
        stack_mlp((w0, w1, w2, w3), fc1, fc2)
        gain, shift = norm_ref[0:1], norm_ref[1:2]
        fc1_sums, grad_sums = jnp.zeros((1, FF), F32), jnp.zeros((1, D), F32)
        for i in range(steps):
            at = slice(i * chunk, (i + 1) * chunk)
            gz = grad_ref[at].astype(LOW)
            low_grad[at] = gz
            gpre = (dot_nt(gz, fc2[...]) * slope_ref[at].astype(F32)).astype(LOW)
            gpre_ref[at] = gpre
            scaled, _ = norm_rows(mid_ref[at])
            a_ref[at] = (scaled * gain + shift).astype(LOW)
            fc1_sums = fc1_sums + jnp.sum(gpre.astype(F32), axis=0, keepdims=True)
            grad_sums = grad_sums + jnp.sum(gz.astype(F32), axis=0, keepdims=True)
        outs = keep_ref, send_ref, small_ref, bias_ref
        mlp_sums(gpre_ref, a_ref, act_ref, low_grad, fc1, fc1_sums, grad_sums, norm_ref, outs)

    return pl.pallas_call(
        kernel,
        out_shape=(jax.ShapeDtypeStruct((rows, FF), LOW), *sums_shapes()),
        in_specs=[vmem()] * 9,
        out_specs=[vmem()] * 5,
        scratch_shapes=[
            pltpu.VMEM((D, FF), LOW),
            pltpu.VMEM((FF, D), LOW),
            pltpu.VMEM((rows, D), LOW),
            pltpu.VMEM((rows, D), LOW),
        ],
        compiler_params=params(18),
        cost_estimate=cost(7e9, 2e7),
        name="mlp_backward",
    )(grad, mid, act, slope, *weights, norms)


def mlp_turn(mid, grad, weights, fc1_bias, norms, layer):
    rows = mid.shape[0]
    chunk = 6 * PAD
    steps = rows // chunk

    def kernel(
        mid_ref, grad_ref, w0, w1, w2, w3, fc1_bias_ref, norm_ref,
        out_ref, gpre_ref, keep_ref, send_ref, small_ref, bias_ref,
        fc1, fc2, a_all, act_all, low_grad,
    ):
        stack_mlp((w0, w1, w2, w3), fc1, fc2)
        gain, shift, out_shift = norm_ref[0:1], norm_ref[1:2], norm_ref[2:3]

        def step(i, totals):
            at = pl.ds(pl.multiple_of(i * chunk, 16), chunk)
            rows_now = mid_ref[at]
            scaled, _ = norm_rows(rows_now)
            a = (scaled * gain + shift).astype(LOW)
            a_all[at] = a
            act, slope = gelu_parts(dot_nn(a, fc1[...]) + fc1_bias_ref[layer, 0:1])
            act = act.astype(LOW)
            act_all[at] = act
            out_ref[at] = rows_now + dot_nn(act, fc2[...]) + out_shift
            gz = grad_ref[at].astype(LOW)
            low_grad[at] = gz
            gpre = (dot_nt(gz, fc2[...]) * slope).astype(LOW)
            gpre_ref[at] = gpre
            return (
                totals[0] + jnp.sum(gz.astype(F32), axis=0, keepdims=True),
                totals[1] + jnp.sum(gpre.astype(F32), axis=0, keepdims=True),
            )

        zeros = jnp.zeros((1, D), F32), jnp.zeros((1, FF), F32)
        grad_sums, fc1_sums = lax.fori_loop(0, steps, step, zeros)
        outs = keep_ref, send_ref, small_ref, bias_ref
        mlp_sums(gpre_ref, a_all, act_all, low_grad, fc1, fc1_sums, grad_sums, norm_ref, outs)

    return pl.pallas_call(
        kernel,
        out_shape=(
            jax.ShapeDtypeStruct((rows, D), F32),
            jax.ShapeDtypeStruct((rows, FF), LOW),
            *sums_shapes(),
        ),
        in_specs=[vmem()] * 8,
        out_specs=[vmem()] * 6,
        scratch_shapes=[
            pltpu.VMEM((D, FF), LOW),
            pltpu.VMEM((FF, D), LOW),
            pltpu.VMEM((rows, D), LOW),
            pltpu.VMEM((rows, FF), LOW),
            pltpu.VMEM((rows, D), LOW),
        ],
        compiler_params=params(18),
        cost_estimate=cost(1.5e10, 4e7),
        name="mlp_turn",
    )(mid, grad, *weights, fc1_bias, norms)


def mlp_input_grad(grad, mid, gpre, weights, norms):
    rows = mid.shape[0]
    chunk = 6 * PAD

    def kernel(grad_ref, mid_ref, gpre_ref, w0, w1, w2, w3, norm_ref, out_ref, fc1):
        for k, piece in enumerate((w0, w1, w2, w3)):
            fc1[:, k * D : (k + 1) * D] = piece[0:D]
        gain = norm_ref[0:1]
        for i in range(rows // chunk):
            at = slice(i * chunk, (i + 1) * chunk)
            ga = dot_nt(gpre_ref[at], fc1[...])
            scaled, inverse = norm_rows(mid_ref[at])
            out_ref[at] = grad_ref[at] + norm_back(ga, scaled, inverse, gain)

    return pl.pallas_call(
        kernel,
        out_shape=jax.ShapeDtypeStruct((rows, D), F32),
        in_specs=[vmem()] * 8,
        out_specs=vmem(),
        scratch_shapes=[pltpu.VMEM((D, FF), LOW)],
        compiler_params=params(8),
        cost_estimate=cost(3e12, 1e7),
        name="mlp_input_grad",
    )(grad, mid, gpre, *weights, norms)


def small_outputs(rows):
    def kernel(rows_ref, gains_ref, shifts_ref, fc1_ref, qv_ref, table_ref):
        for l in range(LAYERS):
            now = rows_ref[l]
            for i, row in enumerate((0, 3)):
                gains_ref[l, i : i + 1] = now[row : row + 1]
            for i, row in enumerate((1, 4, 2, 5)):
                shifts_ref[l, i : i + 1] = now[row : row + 1]
            fc1_ref[l : l + 1] = now[6:7]
            qv_ref[l] = now[7:9, 0:96]
            turned = rows_ref[l, 8:SMALL, 0:256].T
            table_ref[l] = turned[0:169, 1:4]

    return pl.pallas_call(
        kernel,
        out_shape=(
            jax.ShapeDtypeStruct((LAYERS, 2, D), F32),
            jax.ShapeDtypeStruct((LAYERS, 4, D), F32),
            jax.ShapeDtypeStruct((LAYERS, D), F32),
            jax.ShapeDtypeStruct((LAYERS, 2, 96), F32),
            jax.ShapeDtypeStruct((LAYERS, 169, 3), F32),
        ),
        in_specs=[vmem()],
        out_specs=[vmem()] * 5,
        compiler_params=params(4),
        cost_estimate=cost(0, 1e6),
        name="small_outputs",
    )(rows)


def swap_core(value):
    return lax.ppermute(value, "head", [(i, i ^ 1) for i in range(4)])


def swap_chip(value):
    return lax.ppermute(value, "head", [(i, i ^ 2) for i in range(4)])


def swap_border(value):
    return lax.ppermute(value, "head", [(1, 2), (2, 1)])


def swap_dp(value, step, size):
    return lax.ppermute(value, "dp", [(i, i ^ step) for i in range(size)])


def tie(*values):
    return lax.optimization_barrier(values)


def pick(first, one, other):
    first = first > 0
    return jnp.where(first, one, other), jnp.where(first, other, one)


def dp_masks(order):
    size = lax.axis_size("dp")
    upper = [(2 << b) - 2 for b in range(1, size.bit_length() - 1)]
    if order == 1 and upper:
        return [upper[-1]] + upper[:-1] + [1]
    return [1] + (upper if order == 2 else upper[::-1])


def dp_start(parts, sides, order):
    half = parts[0].shape[0] // 2
    low = sum(p[:half].astype(F32) for p in parts)
    high = sum(p[half:].astype(F32) for p in parts)
    masks = dp_masks(order)
    kept, sent = pick(sides[order % 2], low, high)
    return kept, swap_dp(sent.astype(LOW), masks[0], lax.axis_size("dp"))


def dp_next(kept, other, order, stage):
    masks = dp_masks(order)
    value = (kept.astype(F32) + other.astype(F32)).astype(LOW)
    return value, swap_dp(value, (masks + masks[:1])[stage], lax.axis_size("dp"))


def dp_join(value, other, sides, order):
    low, high = pick(sides[order % 2], value, other)
    return jnp.concatenate([low, high])


def body(
    tokens, outputs_grad, image_kind, qkv_weight, qv_bias, bias_table, proj_weight,
    fc1_weight, fc1_bias, fc2_weight, gains, shifts,
):
    own = tokens.shape[0] // PLACES
    bins = own + 2
    me = lax.axis_index("head").astype(jnp.int32)

    def border(value):
        edge = 4 * PLACES
        return swap_border(jnp.where(me == 1, value[-edge:], value[:edge]))

    def attn_pack(l):
        turned = jnp.transpose(qkv_weight[l], (1, 2, 0)).reshape(288, D)
        return jnp.concatenate([turned, proj_weight[l]], axis=0)

    def mlp_pack(l):
        return jnp.concatenate([fc1_weight[l], fc2_weight[l]], axis=0)

    def norm_pack(l, which, bias_row):
        rows = jnp.stack([gains[l, which], shifts[l, which], shifts[l, bias_row]])
        return jnp.pad(rows, ((0, 5), (0, 0)))

    partner = swap_core(tokens)
    rows = jnp.pad(jnp.transpose(bias_table, (0, 2, 1)).reshape(6, 169), ((0, 0), (0, D - 169)))
    small = jnp.concatenate([rows, qv_bias.reshape(1, D), fc1_bias])
    small = jnp.pad(small, ((0, SMALL - 9), (0, 0)))
    own_pack = [jnp.concatenate([attn_pack(0), *split(small)])]
    chip_pack = [swap_chip(own_pack[0])]
    edges, _ = tie(tokens, own_pack[0])
    halo = border(edges)
    place = lax.axis_index("dp")
    top = lax.axis_size("dp") // 2
    sides = [1 - (place & 1), (place < top).astype(jnp.int32)]
    first = jnp.broadcast_to(jnp.stack(sides).astype(jnp.int32)[:, None], (2, D))
    table = make_plan(image_kind, me, own, bins)
    mlp_first = mlp_pack(0)
    table, first, chip_pack[0], partner, mlp_first = tie(
        table, first, chip_pack[0], partner, mlp_first
    )
    sides = [first[0:1], first[1:2]]
    hidden = gather_slots(table, tokens, partner, halo, bins)

    def gathered(i):
        p, c = own_pack[i], chip_pack[i]
        return p, c, swap_core(p), swap_core(c)

    pack, halo, _ = tie(mlp_first, halo, chip_pack[0])
    own_pack.append(pack)
    chip_pack.append(swap_chip(pack))
    first_weights = gathered(0)
    bias, qkv_bias, fc1_all = spread_smalls(first_weights)

    saved, weights = [], []
    last = LAYERS - 1
    for l in range(LAYERS):
        norms, mlp_norms = norm_pack(l, 0, 2), norm_pack(l, 1, 3)
        weights.append(first_weights if l == 0 else gathered(2 * l))
        mid, a, qkv, probs, attn = attn_forward(
            table, hidden, weights[2 * l], qkv_bias, bias, norms, l
        )
        mid, chip_pack[2 * l + 1] = tie(mid, chip_pack[2 * l + 1])
        weights.append(gathered(2 * l + 1))
        if l == last:
            saved.append((hidden, mid, a, qkv, probs, attn, norms, mlp_norms))
            break
        pack, outputs_grad, mid = tie(attn_pack(1), outputs_grad, mid)
        grad_partner, grad_halo = swap_core(outputs_grad), border(outputs_grad)
        own_pack.append(pack)
        chip_pack.append(swap_chip(pack))
        out, act, slope = mlp_forward(mid, weights[2 * l + 1], fc1_all, mlp_norms, l)
        pack, out, chip_pack[2], grad_partner, grad_halo = tie(
            mlp_pack(1), out, chip_pack[2], grad_partner, grad_halo
        )
        own_pack.append(pack)
        chip_pack.append(swap_chip(pack))
        saved.append((hidden, mid, a, qkv, probs, attn, norms, mlp_norms, act, slope))
        hidden = out
    grad = gather_slots(table, outputs_grad, grad_partner, grad_halo, bins)

    def give_back(value):
        slots = value.reshape(bins, PAD, D)
        return slots, swap_core(slots), swap_border(border_slots(table, slots))

    def mlp_back(l, grad):
        return mlp_backward(
            grad, saved[l][1], saved[l][8], saved[l][9], weights[2 * l + 1], saved[l][7]
        )

    def mlp_input(l, grad, gpre):
        return mlp_input_grad(grad, saved[l][1], gpre, weights[2 * l + 1], saved[l][7])

    def attn_back(l, grad):
        return attn_backward(table, grad, saved[l][3], saved[l][4], weights[2 * l], l % 2 == 1)

    def attn_sums(l, grad, gqkv, scores, small_mlp, fc1_bias_grad):
        return attn_grads(
            grad, saved[l][2], saved[l][5], gqkv, scores, small_mlp, fc1_bias_grad,
            weights[2 * l], saved[l][6],
        )

    def attn_input(l, grad, gqkv):
        work = 6e9 if l == last else 3e12
        return attn_input_grad(
            table, grad, saved[l][0], gqkv, weights[2 * l], saved[l][6], l % 2 == 1, work
        )

    def core_sum(keep, other):
        return [(keep[i].astype(F32) + other[i].astype(F32)).astype(LOW) for i in range(2)]

    out, gpre, keep_a, send_a, small_mlp, fc1_bias_grad = mlp_turn(
        saved[last][1], grad, weights[2 * last + 1], fc1_all, saved[last][7], last
    )
    core_a = swap_core(send_a)
    grad = mlp_input(1, grad, gpre)
    grad, core_a = tie(grad, core_a)
    half_a, out_a = core_sum(keep_a, core_a)
    grad, out_a = tie(grad, out_a)
    chip_a = swap_chip(out_a)
    gqkv, scores = attn_back(1, grad)
    grad_after = attn_input(1, grad, gqkv)
    gqkv, _ = tie(gqkv, grad_after)
    keep_b, send_b = attn_sums(1, grad, gqkv, scores, small_mlp, fc1_bias_grad)
    grad, send_b, chip_a = tie(grad_after, send_b, chip_a)
    core_b = swap_core(send_b)
    state_a = dp_start((half_a, chip_a), sides, 0)
    gpre, keep_c, send_c, small_mlp, fc1_bias_grad = mlp_back(0, grad)
    gpre, send_c, state_a, core_b = tie(gpre, send_c, state_a, core_b)
    core_c = swap_core(send_c)
    state_a = dp_next(*state_a, 0, 1)
    half_b, out_b = core_sum(keep_b, core_b)
    gpre, out_b = tie(gpre, out_b)
    chip_b = swap_chip(out_b)
    grad = mlp_input(0, grad, gpre)
    grad, core_c = tie(grad, core_c)
    half_c, out_c = core_sum(keep_c, core_c)
    grad, out_c = tie(grad, out_c)
    chip_c = swap_chip(out_c)
    gqkv, scores = attn_back(0, grad)
    gqkv, state_a = tie(gqkv, state_a)
    state_a = dp_next(*state_a, 0, 2)
    keep_d, send_d = attn_sums(0, grad, gqkv, scores, small_mlp, fc1_bias_grad)
    core_d = swap_core(send_d)
    gqkv, state_a, chip_b, chip_c, _ = tie(gqkv, state_a, chip_b, chip_c, send_d)
    state_c = dp_start((half_c, chip_c), sides, 1)
    state_a = dp_next(*state_a, 0, 3)
    grad = attn_input(0, grad, gqkv)
    grad, core_d = tie(grad, core_d)
    half_d, out_d = core_sum(keep_d, core_d)
    chip_d = swap_chip(out_d)
    out, _ = tie(out, out_d)
    output_parts = give_back(out)
    chip_d, state_a, state_c = tie(chip_d, state_a, state_c)
    half_bd = jnp.concatenate([half_b, half_d])
    state_d = dp_start((half_bd, jnp.concatenate([chip_b, chip_d])), sides, 2)
    state_c = dp_next(*state_c, 1, 1)
    tokens_parts = give_back(grad)
    state_d, state_c = tie(state_d, state_c)
    state_d = dp_next(*state_d, 2, 1)
    state_c = dp_next(*state_c, 1, 2)
    output = return_slots(table, *output_parts, own)
    state_d, state_c = tie(state_d, state_c)
    state_d = dp_next(*state_d, 2, 2)
    state_c = dp_next(*state_c, 1, 3)
    tokens_grad = return_slots(table, *tokens_parts, own)
    state_d, state_c, output, tokens_grad = tie(state_d, state_c, output, tokens_grad)
    value_d, other_d = dp_next(*state_d, 2, 3)
    total_a = dp_join(*state_a, sides, 0)
    total_c = dp_join(*state_c, sides, 1)
    mlp_all = jnp.stack([total_c, total_a]).astype(F32)
    fc1_out = mlp_all[:, :D]
    fc2_out = mlp_all[:, D:].transpose(0, 2, 1)
    total_bd = dp_join(value_d, other_d, sides, 2)
    total_b, total_d = total_bd[: D + SMALL], total_bd[D + SMALL :]

    attn_all = jnp.stack([total_d, total_b]).astype(F32)
    gains_out, shifts_out, fc1_bias_out, qv_out, table_out = small_outputs(attn_all[:, D:])
    qkv_out = attn_all[:, 0:288].reshape(LAYERS, 3, 96, D).transpose(0, 3, 1, 2)
    proj_out = attn_all[:, 288:384]
    return (
        output, tokens_grad, qkv_out, qv_out, table_out, proj_out, fc1_out, fc1_bias_out,
        fc2_out, gains_out, shifts_out,
    )


def solution(mesh):
    rows = P(("dp", "head"), None)
    placed = (
        rows,
        rows,
        P("dp", None),
        P(None, None, None, "head"),
        P(None, None, "head"),
        P(None, None, "head"),
        P(None, "head", None),
        P(None, None, "head"),
        P(None, "head"),
        P(None, "head", None),
        P(),
        P(),
    )
    return jax.shard_map(
        body,
        mesh=mesh,
        in_specs=placed,
        out_specs=(
            rows,
            rows,
            P(None, None, None, "head"),
            P(None, None, "head"),
            P(None, None, "head"),
            P(None, "head", None),
            P(None, None, "head"),
            P(None, "head"),
            P(None, "head", None),
            P(),
            P(),
        ),
        check_vma=False,
    )
```

```python
import jax
import jax.numpy as jnp
from jax import lax
from jax.experimental import pallas as pl
from jax.experimental.pallas import tpu as pltpu
from jax.sharding import PartitionSpec as P

D = 384
FF = 1536
LAYERS = 2
PLACES = 49
PAD = 56
WIDE = 64
QUADS = 3
HEAD_DIM = 32
SCORE_SCALE = HEAD_DIM**-0.5
LN_EPS = 1e-05
LOW = jnp.bfloat16
F32 = jnp.float32
MIB = 1024 * 1024
SMALL = 16

SRC, SIDE, WROW, WCOL, FIRST, RET, SEND = 0, 24, 48, 72, 96, 120, 140
TABLE = 144


def vmem():
    return pl.BlockSpec(memory_space=pltpu.VMEM)


def smem():
    return pl.BlockSpec(memory_space=pltpu.SMEM)


def anywhere():
    return pl.BlockSpec(memory_space=pl.ANY)


def params(limit):
    return pltpu.CompilerParams(vmem_limit_bytes=limit * MIB)


def cost(flops, size):
    return pl.CostEstimate(flops=int(flops * 0.02), bytes_accessed=int(size * 0.02), transcendentals=0)


def dot_nn(a, b):
    return lax.dot_general(a, b, (((1,), (0,)), ((), ())), preferred_element_type=F32)


def dot_nt(a, b):
    return lax.dot_general(a, b, (((1,), (1,)), ((), ())), preferred_element_type=F32)


def dot_tn(a, b):
    return lax.dot_general(a, b, (((0,), (0,)), ((), ())), preferred_element_type=F32)


def plan_kernel(own, bins, kind_ref, me_ref, out_ref, load_ref):
    me = me_ref[0]
    half = 2 * own
    for i in range(TABLE):
        out_ref[i] = -1 if i < bins or RET <= i < RET + own else 0
    for i in range(bins):
        out_ref[SIDE + i] = 1
        out_ref[FIRST + i] = i
    for i in range(4):
        load_ref[i] = 0

    def place(start, count, side, bin_id):
        base = load_ref[bin_id]
        load_ref[bin_id] = base + count

        def step(k, carry):
            slot = start + k
            owner = slot // own
            inner = slot - owner * own
            local = base + k
            mine = bin_id == me
            halo = jnp.where(me == 1, slot - half, slot - half + 4)
            code = jnp.where(
                owner == me, inner, jnp.where(owner == (me ^ 1), own + inner, 2 * own + halo)
            )

            @pl.when(mine)
            def _():
                wrow = k // side
                out_ref[SRC + local] = code
                out_ref[SIDE + local] = side
                out_ref[WROW + local] = wrow
                out_ref[WCOL + local] = k - wrow * side
                out_ref[FIRST + local] = base

            @pl.when(owner == me)
            def _():
                back = jnp.where(me == 2, slot - half, k)
                out_ref[RET + inner] = jnp.where(
                    mine, local, jnp.where(bin_id == (me ^ 1), bins + local, 2 * bins + back)
                )

            return carry

        lax.fori_loop(0, count, step, 0)

    for turn in range(3):

        def visit(i, start, turn=turn):
            kind = kind_ref[0, i]
            count = jnp.where(kind == 2, 9, jnp.where(kind == 1, 4, 0))
            side = jnp.where(kind == 2, 3, 2)
            cut = half - start
            across = (cut > 0) & (cut < count)
            second = (start >= half) | (across & (cut < count - cut))
            chip = jnp.where(second, 1, 0)
            left, right = load_ref[2 * chip], load_ref[2 * chip + 1]
            emptier = 2 * chip + jnp.where(left <= right, 0, 1)
            if turn == 0:
                chosen, bin_id = across, 1 + chip
            else:
                chosen, bin_id = (kind == 3 - turn) & jnp.logical_not(across), emptier

            @pl.when(chosen)
            def _():
                place(start, count, side, bin_id)
                if turn == 0:
                    out_ref[SEND] = jnp.where((me == 1) & (chip == 0), cut, 0)

            return start + count

        lax.fori_loop(0, kind_ref.shape[1], visit, jnp.int32(0))


def gather_kernel(bins, table_ref, refs, out_ref, spread_ref):
    spread_ref[...] = jnp.zeros(spread_ref.shape, F32)
    at = 0
    for ref in refs:
        for s in range(ref.shape[0] // PLACES):
            spread_ref[at, 0:PLACES] = ref[s * PLACES : (s + 1) * PLACES].astype(F32)
            at += 1

    def step(j, carry):
        src = table_ref[SRC + j]

        @pl.when(src < 0)
        def _():
            out_ref[j] = jnp.zeros((PAD, D), F32)

        @pl.when(src >= 0)
        def _():
            out_ref[j] = spread_ref[src]

        return carry

    lax.fori_loop(0, bins, step, 0)


def make_plan(image_kind, me, own, bins):
    def kernel(kind_ref, me_ref, table_ref, load_ref):
        plan_kernel(own, bins, kind_ref, me_ref, table_ref, load_ref)

    return pl.pallas_call(
        kernel,
        out_shape=jax.ShapeDtypeStruct((TABLE,), jnp.int32),
        in_specs=[smem(), smem()],
        out_specs=smem(),
        scratch_shapes=[pltpu.SMEM((4,), jnp.int32)],
        compiler_params=params(1),
        cost_estimate=cost(0, 1.5e7),
        name="plan",
    )(image_kind, me.reshape(1))


def gather_slots(table, mine, partner, halo, bins):
    own = mine.shape[0] // PLACES

    def kernel(table_ref, *refs):
        gather_kernel(bins, table_ref, refs[:3], refs[3], refs[4])

    out = pl.pallas_call(
        kernel,
        out_shape=jax.ShapeDtypeStruct((bins, PAD, D), F32),
        in_specs=[smem()] + [vmem()] * 3,
        out_specs=vmem(),
        scratch_shapes=[pltpu.VMEM((2 * own + 4, PAD, D), F32)],
        compiler_params=params(8),
        cost_estimate=cost(0, 8e6),
        name="gather_slots",
    )(table, mine, partner, halo)
    return out.reshape(bins * PAD, D)


def border_slots(table, slots, work):
    def kernel(table_ref, slots_ref, out_ref):
        start = table_ref[SEND]
        for j in range(4):
            out_ref[j] = slots_ref[start + j]

    return pl.pallas_call(
        kernel,
        out_shape=jax.ShapeDtypeStruct((4,) + slots.shape[1:], F32),
        in_specs=[smem(), vmem()],
        out_specs=vmem(),
        compiler_params=params(4),
        cost_estimate=cost(work, 1e6),
        name="border_slots",
    )(table, slots)


def return_slots(table, mine, partner, halo, own):
    bins = mine.shape[0]

    def kernel(table_ref, mine_ref, partner_ref, halo_ref, out_ref):
        for s in range(own):
            src = table_ref[RET + s]
            rows = pl.ds(s * PLACES, PLACES)

            @pl.when(src < 0)
            def _():
                out_ref[rows] = jnp.zeros((PLACES, D), F32)

            @pl.when((src >= 0) & (src < bins))
            def _():
                out_ref[rows] = mine_ref[src, 0:PLACES]

            @pl.when((src >= bins) & (src < 2 * bins))
            def _():
                out_ref[rows] = partner_ref[src - bins, 0:PLACES]

            @pl.when(src >= 2 * bins)
            def _():
                out_ref[rows] = halo_ref[src - 2 * bins, 0:PLACES]

    return pl.pallas_call(
        kernel,
        out_shape=jax.ShapeDtypeStruct((own * PLACES, D), F32),
        in_specs=[smem(), vmem(), vmem(), vmem()],
        out_specs=vmem(),
        compiler_params=params(8),
        cost_estimate=cost(0, 8e6),
        name="return_slots",
    )(table, mine, partner, halo)


def norm_rows(rows):
    average = jnp.mean(rows, axis=-1, keepdims=True)
    centred = rows - average
    inverse = lax.rsqrt(jnp.mean(centred * centred, axis=-1, keepdims=True) + LN_EPS)
    return centred * inverse, inverse


def norm_back(incoming, scaled, inverse, gain):
    weighted = incoming * gain
    return inverse * (
        weighted
        - jnp.mean(weighted, axis=-1, keepdims=True)
        - scaled * jnp.mean(weighted * scaled, axis=-1, keepdims=True)
    )


def gelu_parts(x):
    t = 1.0 / (1.0 + 0.23164189 * jnp.abs(x))
    bell = jnp.exp2(x * x * -0.7213475204444817)
    poly = t * (
        0.127414796 + t * (-0.142248368 + t * (0.7107068705 + t * (-0.7265760135 + t * 0.5307027145)))
    )
    tail = poly * bell
    phi = jnp.where(x >= 0, 1.0 - tail, tail)
    return x * phi, phi + x * bell * 0.3989422804014327


def place_parts(shape, dim):
    place = lax.broadcasted_iota(jnp.int32, shape, dim)
    row = (place * 37) >> 8
    return place, row, place - 7 * row


def neighbour(table_ref, w, back, down):
    side, wrow, wcol = table_ref[SIDE + w], table_ref[WROW + w], table_ref[WCOL + w]
    at = wrow if down else wcol
    if back:
        other = jnp.where(at == 0, side - 1, at - 1)
    else:
        other = jnp.where(at == side - 1, 0, at + 1)
    if down:
        return table_ref[FIRST + w] + other * side + wcol
    return table_ref[FIRST + w] + wrow * side + other


def move_windows(table_ref, src, tmp, out, back):
    bins = src.shape[0]
    tmp[...] = jnp.zeros(tmp.shape, F32)
    out[...] = jnp.zeros(out.shape, F32)

    def rows(w, carry):
        other = neighbour(table_ref, w, back, True)
        if back:
            tmp[w, 21:49] = src[w, 0:28]
            tmp[w, 0:21] = src[other, 28:49]
        else:
            tmp[w, 0:28] = src[w, 21:49]
            tmp[w, 28:49] = src[other, 0:21]
        return carry

    lax.fori_loop(0, bins, rows, 0, unroll=2)
    _, _, col = place_parts((PAD, 1), 0)

    def cols(w, carry):
        other = neighbour(table_ref, w, back, False)
        if back:
            out[w, 0:49] = tmp[other, 4:53]
            out[w, 3:49] = jnp.where(col[3:49] >= 3, tmp[w, 0:46], out[w, 3:49])
        else:
            out[w, 0:49] = tmp[w, 3:52]
            out[w, 4:49] = jnp.where(col[4:49] < 4, out[w, 4:49], tmp[other, 0:45])
        return carry

    lax.fori_loop(0, bins, cols, 0, unroll=2)


def head_marks():
    lane = lax.broadcasted_iota(jnp.int32, (WIDE, 128), 1) // HEAD_DIM
    return [jnp.where(lane == h, 1.0, 0.0).astype(LOW) for h in range(4)]


def spread(block, marks):
    return jnp.concatenate([block * mark for mark in marks], axis=0)


def fold(product, marks):
    total = None
    for h, mark in enumerate(marks):
        part = product[h * WIDE : (h + 1) * WIDE] * mark.astype(F32)
        total = part if total is None else total + part
    return total


def spread_pair(block, marks):
    return jnp.concatenate([spread(block[0:WIDE], marks), spread(block[WIDE:], marks)], axis=1)


def diagonal(block):
    zero = jnp.zeros((WIDE, 128), block.dtype)
    top = jnp.concatenate([block[0:WIDE], zero], axis=1)
    return jnp.concatenate([top, jnp.concatenate([zero, block[WIDE:]], axis=1)], axis=0)


def by_head(values):
    return values.reshape(4, WIDE, 128)


def pad_rows(rows):
    return jnp.concatenate([rows, jnp.zeros((WIDE - PAD, rows.shape[1]), rows.dtype)], axis=0)


def split(values):
    high = values.astype(LOW)
    return high, (values - high.astype(F32)).astype(LOW)


def marks_where(rows, cols, test):
    row = lax.broadcasted_iota(jnp.int32, (rows, cols), 0)
    col = lax.broadcasted_iota(jnp.int32, (rows, cols), 1)
    return jnp.where(test(row, col), 1.0, 0.0).astype(LOW)


def far(place):
    row = (place * 37) >> 8
    return 13 * row + (place - 7 * row)


def spread_smalls(smalls):
    heads = LAYERS * 12

    def kernel(p0, p1, p2, p3, out_ref, qkv_ref, fc1_ref, table_ref, small_ref):
        quarters = []
        for k, ref in enumerate((p0, p1, p2, p3)):
            high, low = ref[D : D + SMALL], ref[D + SMALL : D + 2 * SMALL]
            small_ref[k] = high.astype(F32) + low.astype(F32)
            quarters.append(small_ref.at[k])
        for k, ref in enumerate(quarters):
            for l in range(LAYERS):
                at = l * 12 + k * 3
                table_ref[at : at + 3] = ref[l * 3 : l * 3 + 3, 0:256]
        lane = lax.broadcasted_iota(jnp.int32, (8, D), 1)
        for l in range(LAYERS):
            for c in range(3):
                total = jnp.zeros((8, D), F32)
                for k, ref in enumerate(quarters):
                    if c != 1:
                        row = jnp.broadcast_to(ref[6:7], (8, D))
                        row = pltpu.roll(row, (k * 96 - l * 192 - (c // 2) * 96) % D, 1)
                        own_lanes = (lane >= k * 96) & (lane < k * 96 + 96)
                        total = total + jnp.where(own_lanes, row, 0.0)
                qkv_ref[l, :, c * D : (c + 1) * D] = total
            for k, ref in enumerate(quarters):
                row = jnp.broadcast_to(ref[7 + l : 8 + l], (8, D))
                fc1_ref[l, :, k * D : (k + 1) * D] = row
        to_lane = marks_where(128, 128, lambda r, c: (far(c & 63) == r) & ((c & 63) < PLACES))
        to_row = marks_where(WIDE, 96, lambda r, c: (far(r) == c) & (r < PLACES))
        place = lax.broadcasted_iota(jnp.int32, (WIDE, 128), 0)
        empty = jnp.where(place < PLACES, 0.0, -1e30)
        turned = pltpu.roll(table_ref[...], 172, 1)
        skewed = []
        for n in range(heads):
            row = jnp.broadcast_to(turned[n : n + 1], (96, 256))
            skewed.append(pltpu.roll(row, 0, 1, stride=1, stride_axis=0)[:, 0:128])
        skewed = jnp.concatenate(skewed, axis=1)
        total = None
        for part in split(skewed):
            rows = dot_nn(to_row, part).astype(LOW)
            rows = jnp.concatenate([rows[:, n * 128 : (n + 1) * 128] for n in range(heads)], axis=0)
            part = dot_nn(rows, to_lane)
            total = part if total is None else total + part
        for n in range(heads):
            l, t, h = n // 12, n % 12 // 4, n % 4
            out_ref[l, t, h * WIDE : (h + 1) * WIDE] = total[n * WIDE : (n + 1) * WIDE] + empty

    return pl.pallas_call(
        kernel,
        out_shape=(
            jax.ShapeDtypeStruct((LAYERS, QUADS, 4 * WIDE, 128), F32),
            jax.ShapeDtypeStruct((LAYERS, 8, 3 * D), F32),
            jax.ShapeDtypeStruct((LAYERS, 8, FF), F32),
        ),
        in_specs=[vmem()] * 4,
        out_specs=[vmem()] * 3,
        scratch_shapes=[pltpu.VMEM((heads, 256), F32), pltpu.VMEM((4, SMALL, D), F32)],
        compiler_params=params(6),
        cost_estimate=cost(0, 1e7),
        name="spread_smalls",
    )(*smalls)


def scores_to_table(scores_ref):
    to_far = marks_where(128, 128, lambda r, c: (far(r & 63) == c) & ((r & 63) < PLACES))
    to_row = marks_where(96, WIDE, lambda r, c: (84 - far(c) == r) & (c < PLACES))
    wide = None
    for part in split(scores_ref[...].reshape(12 * WIDE, 128)):
        part = dot_nn(part, to_far)
        wide = part if wide is None else wide + part
    wide = jnp.concatenate([wide[h * WIDE : (h + 1) * WIDE] for h in range(12)], axis=1)
    rows = None
    for part in split(wide):
        part = dot_nn(to_row, part)
        rows = part if rows is None else rows + part
    out = []
    for h in range(12):
        one = rows[:, h * 128 : (h + 1) * 128]
        one = jnp.concatenate([one, jnp.zeros_like(one)], axis=1)
        one = pltpu.roll(one, 0, 1, stride=1, stride_axis=0)
        out.append(jnp.sum(one, axis=0, keepdims=True))
    return out


def stack_qkv(pieces, out_ref):
    for k, piece in enumerate(pieces):
        for c in range(3):
            out_ref[c * D + k * 96 : c * D + (k + 1) * 96] = piece[c * 96 : (c + 1) * 96]


def stack_proj(pieces, out_ref):
    for k, piece in enumerate(pieces):
        out_ref[k * 96 : (k + 1) * 96] = piece[288:384]


def stack_mlp(pieces, fc1_ref, fc2_ref):
    for k, piece in enumerate(pieces):
        fc1_ref[:, k * D : (k + 1) * D] = piece[0:D]
        fc2_ref[k * D : (k + 1) * D] = piece[D : 2 * D]


def attn_forward(table, hidden, weights, qv_bias, bias, norms, layer):
    shifted = layer % 2 == 1
    rows = hidden.shape[0]
    bins = rows // PAD
    chunk_slots = 6
    chunk = chunk_slots * PAD
    spare = bins if shifted else 2

    def kernel(
        table_ref, hidden_ref, w0, w1, w2, w3, qv_ref, bias_ref, norm_ref,
        mid_ref, a_ref, qkv_ref, p_ref, attn_ref,
        wqkv, wproj, wide, tmp, moved,
    ):
        pieces = (w0, w1, w2, w3)
        stack_qkv(pieces, wqkv)
        stack_proj(pieces, wproj)
        gain, shift, proj_shift = norm_ref[0:1], norm_ref[1:2], norm_ref[2:3]
        marks = head_marks()
        def norm_step(i, carry):
            at = pl.ds(pl.multiple_of(i * chunk, 16), chunk)
            scaled, _ = norm_rows(hidden_ref[at])
            normed = scaled * gain + shift
            if shifted:
                slots = pl.ds(i * chunk_slots, chunk_slots)
                wide[slots] = normed.reshape(chunk_slots, PAD, D)
            else:
                a_ref[at] = normed.astype(LOW)
            return carry

        lax.fori_loop(0, bins // chunk_slots, norm_step, 0)
        if shifted:
            move_windows(table_ref, wide, tmp, moved, False)
            a_ref[...] = moved[...].reshape(rows, D).astype(LOW)

        def qkv_step(i, carry):
            at = pl.ds(pl.multiple_of(i * chunk, 16), chunk)
            project = dot_nt(a_ref[at], wqkv[...]) + qv_ref[layer, 0:1]
            for j in range(chunk_slots):
                block = project[j * PAD : (j + 1) * PAD]
                at = pl.ds((j % 2) * WIDE, WIDE)
                qkv_ref[i * (chunk_slots // 2) + j // 2, at] = pad_rows(block).astype(LOW)
            return carry

        lax.fori_loop(0, bins // chunk_slots, qkv_step, 0)

        if shifted:
            _, qrow, qcol = place_parts((WIDE, 1), 0)
            lane = lax.broadcasted_iota(jnp.int32, (1, 128), 1)
            second = lane >= WIDE
            pplace = jnp.where(second, lane - WIDE, lane)
            prow = (pplace * 37) >> 8
            pcol = pplace - 7 * prow
            pband = 1 + (prow >= 4).astype(jnp.int32), 1 + (pcol >= 4).astype(jnp.int32)
            qband = 1 + (qrow >= 4).astype(jnp.int32), 1 + (qcol >= 4).astype(jnp.int32)

        def window(j, carry):
            if shifted:
                low = []
                for w in (2 * j, 2 * j + 1):
                    side = table_ref[SIDE + w]
                    low.append(
                        (
                            jnp.where(table_ref[WROW + w] == side - 1, 3, 0),
                            jnp.where(table_ref[WCOL + w] == side - 1, 1, 0),
                        )
                    )
                low_row = jnp.where(second, low[1][0], low[0][0])
                low_col = jnp.where(second, low[1][1], low[0][1])
                pregion = low_row * pband[0] + low_col * pband[1]
                qregion = low_row * qband[0] + low_col * qband[1]
                mask = jnp.where(pregion != qregion, -100.0, 0.0)[None]
            scores, probs = [], []
            for t in range(QUADS):
                q = qkv_ref[j, :, t * 128 : (t + 1) * 128]
                k = qkv_ref[j, :, D + t * 128 : D + (t + 1) * 128]
                scores.append(dot_nt(spread_pair(k, marks), diagonal(q)))
            for t in range(QUADS):
                now = by_head(scores[t] * SCORE_SCALE + bias_ref[layer, t])
                if shifted:
                    now = now + mask
                exponent = jnp.exp(now - jnp.max(now, axis=1, keepdims=True))
                total = jnp.sum(exponent, axis=1, keepdims=True)
                probs.append((exponent * (1.0 / total)).reshape(4 * WIDE, 128).astype(LOW))
                p_ref[j, t] = probs[t]
            for t in range(QUADS):
                cols = slice(t * 128, (t + 1) * 128)
                v = qkv_ref[j, :, 2 * D + t * 128 : 2 * D + (t + 1) * 128]
                both = dot_tn(probs[t], spread_pair(v, marks))
                wide[2 * j, :, cols] = both[0:PAD, 0:128]
                wide[2 * j + 1, :, cols] = both[WIDE : WIDE + PAD, 128:256]
            return carry

        lax.fori_loop(0, bins // 2, window, 0, unroll=9)
        if shifted:
            move_windows(table_ref, wide, tmp, moved, True)
            attn_ref[...] = moved[...].reshape(rows, D).astype(LOW)
        else:
            attn_ref[...] = wide[...].reshape(rows, D).astype(LOW)

        def proj_step(i, carry):
            at = pl.ds(pl.multiple_of(i * chunk, 16), chunk)
            mid_ref[at] = hidden_ref[at] + dot_nn(attn_ref[at], wproj[...]) + proj_shift
            return carry

        lax.fori_loop(0, bins // chunk_slots, proj_step, 0)

    return pl.pallas_call(
        kernel,
        out_shape=(
            jax.ShapeDtypeStruct((rows, D), F32),
            jax.ShapeDtypeStruct((rows, D), LOW),
            jax.ShapeDtypeStruct((bins // 2, 2 * WIDE, 3 * D), LOW),
            jax.ShapeDtypeStruct((bins // 2, QUADS, 4 * WIDE, 128), LOW),
            jax.ShapeDtypeStruct((rows, D), LOW),
        ),
        in_specs=[smem()] + [vmem()] * 8,
        out_specs=[vmem()] * 5,
        scratch_shapes=[
            pltpu.VMEM((3 * D, D), LOW),
            pltpu.VMEM((D, D), LOW),
            pltpu.VMEM((bins, PAD, D), F32),
            pltpu.VMEM((spare, PAD, D), F32),
            pltpu.VMEM((spare, PAD, D), F32),
        ],
        compiler_params=params(11),
        cost_estimate=cost(1e10, 2e7),
        name="attn_forward",
    )(table, hidden, *weights, qv_bias, bias, norms)


def attn_backward(table, grad, qkv, probs, weights, shifted):
    rows = grad.shape[0]
    bins = rows // PAD
    chunk_slots = 6
    chunk = chunk_slots * PAD
    spare = bins if shifted else 2

    def kernel(
        table_ref, grad_ref, qkv_ref, p_ref, w0, w1, w2, w3,
        gqkv_ref, scores_ref, wproj, wide_attn, wide, tmp, moved,
    ):
        stack_proj((w0, w1, w2, w3), wproj)
        marks = head_marks()
        steps = bins // chunk_slots
        def keep_windows(i, block_rows):
            for j in range(chunk_slots):
                block = block_rows[j * PAD : (j + 1) * PAD]
                dest = pl.ds((j % 2) * WIDE, WIDE)
                wide_attn[i * (chunk_slots // 2) + j // 2, dest] = pad_rows(block).astype(LOW)

        def proj_step(i, carry):
            at = pl.ds(pl.multiple_of(i * chunk, 16), chunk)
            gattn = dot_nt(grad_ref[at].astype(LOW), wproj[...])
            if shifted:
                slots = pl.ds(i * chunk_slots, chunk_slots)
                wide[slots] = gattn.reshape(chunk_slots, PAD, D)
            else:
                keep_windows(i, gattn)
            return carry

        lax.fori_loop(0, steps, proj_step, 0)
        if shifted:
            move_windows(table_ref, wide, tmp, moved, False)

            def move_step(i, carry):
                slots = pl.ds(i * chunk_slots, chunk_slots)
                keep_windows(i, moved[slots].reshape(chunk, D))
                return carry

            lax.fori_loop(0, steps, move_step, 0)

        scores_ref[...] = jnp.zeros((QUADS, 4 * WIDE, 128), F32)

        def window(j, carry):
            at = pl.ds(pl.multiple_of(j * 2 * PAD, 16), 2 * PAD)

            def keep(c, t, left, right):
                cols = slice(c * D + t * 128, c * D + (t + 1) * 128)
                gqkv_ref[at, cols] = jnp.concatenate([left, right], axis=0).astype(LOW)

            go, gp, gv, low_ds, gq, gk = [], [], [], [], [], []
            for t in range(QUADS):
                v = qkv_ref[j, :, 2 * D + t * 128 : 2 * D + (t + 1) * 128]
                go.append(diagonal(wide_attn[j, :, t * 128 : (t + 1) * 128]))
                gp.append(dot_nt(spread_pair(v, marks), go[t]))
            for t in range(QUADS):
                gv.append(dot_nn(p_ref[j, t], go[t]))
            for t in range(QUADS):
                p = by_head(p_ref[j, t].astype(F32))
                now = by_head(gp[t])
                ds = p * (now - jnp.sum(now * p, axis=1, keepdims=True))
                low_ds.append(ds.reshape(4 * WIDE, 128).astype(LOW))
                scores_ref[t] += low_ds[t].astype(F32)
            for t in range(QUADS):
                q = qkv_ref[j, :, t * 128 : (t + 1) * 128]
                k = qkv_ref[j, :, D + t * 128 : D + (t + 1) * 128]
                gk.append(dot_nn(low_ds[t], diagonal(q)))
                gq.append(dot_tn(low_ds[t], spread_pair(k, marks)))
            for t in range(QUADS):
                left, right = slice(0, 128), slice(128, 256)
                keep(2, t, fold(gv[t][:, left], marks)[0:PAD], fold(gv[t][:, right], marks)[0:PAD])
            for t in range(QUADS):
                left, right = slice(0, 128), slice(128, 256)
                folded = fold(gk[t][:, left], marks), fold(gk[t][:, right], marks)
                keep(1, t, *[part[0:PAD] * SCORE_SCALE for part in folded])
                parts = gq[t][0:PAD, left], gq[t][WIDE : WIDE + PAD, right]
                keep(0, t, *[part * SCORE_SCALE for part in parts])
            return carry

        lax.fori_loop(0, bins // 2, window, 0, unroll=9)

    return pl.pallas_call(
        kernel,
        out_shape=(
            jax.ShapeDtypeStruct((rows, 3 * D), LOW),
            jax.ShapeDtypeStruct((QUADS, 4 * WIDE, 128), F32),
        ),
        in_specs=[smem()] + [vmem()] * 7,
        out_specs=[vmem()] * 2,
        scratch_shapes=[
            pltpu.VMEM((D, D), LOW),
            pltpu.VMEM((bins // 2, 2 * WIDE, D), LOW),
            pltpu.VMEM((spare, PAD, D), F32),
            pltpu.VMEM((spare, PAD, D), F32),
            pltpu.VMEM((spare, PAD, D), F32),
        ],
        compiler_params=params(11),
        cost_estimate=cost(1e10, 2e7),
        name="attn_backward",
    )(table, grad, qkv, probs, *weights)


def attn_grads(grad, a, attn, gqkv, scores, small_mlp, fc1_bias_grad, weights, norms):
    rows = grad.shape[0]

    def kernel(
        grad_ref, a_ref, attn_ref, gqkv_ref, scores_ref, mlp_ref, fc1b_ref, w0, w1, w2, w3, norm_ref,
        keep_ref, send_ref, wqkv, small,
    ):
        stack_qkv((w0, w1, w2, w3), wqkv)
        gain, shift = norm_ref[0:1], norm_ref[1:2]
        dqkv = dot_tn(a_ref[...], gqkv_ref[...])
        low_grad = grad_ref[...].astype(LOW)
        dproj = dot_tn(attn_ref[...], low_grad).astype(LOW)
        column_sums = jnp.sum(gqkv_ref[...].astype(F32), axis=0, keepdims=True)
        wide_sums = jnp.broadcast_to(column_sums, (16, 3 * D))
        dshift = sum(dot_nn(part, wqkv[...]) for part in split(wide_sums))[0:1]
        table_rows = scores_to_table(scores_ref)
        turned, match = [], jnp.zeros((1, D), F32)
        for c in range(3):
            back = dqkv[:, c * D : (c + 1) * D].T
            here = wqkv[c * D : (c + 1) * D].astype(F32)
            match = match + jnp.sum(back * here, axis=0, keepdims=True)
            turned.append(back.astype(LOW))
        small[...] = jnp.zeros((SMALL, D), F32)
        small[0:1] = (match - shift * dshift) / gain
        small[1:2] = dshift
        small[2:3] = jnp.sum(low_grad.astype(F32), axis=0, keepdims=True)
        small[3:6] = mlp_ref[0:3]
        gq_sum = jnp.broadcast_to(column_sums[:, 0:D], (8, D))
        gv_sum = jnp.broadcast_to(column_sums[:, 2 * D : 3 * D], (8, D))
        for k in range(4):
            dest = keep_ref if k < 2 else send_ref
            for c in range(3):
                dest[k % 2, c * 96 : (c + 1) * 96] = turned[c][k * 96 : (k + 1) * 96]
            dest[k % 2, 288:384] = dproj[k * 96 : (k + 1) * 96]
            small[6:7] = fc1b_ref[:, k * D : (k + 1) * D]
            small[7:8] = pltpu.roll(gq_sum, (D - k * 96) % D, 1)[0:1]
            small[8:9] = pltpu.roll(gv_sum, (D - k * 96) % D, 1)[0:1]
            for h in range(3):
                small[9 + h : 10 + h, 0:256] = table_rows[3 * k + h]
            dest[k % 2, D : D + SMALL] = small[...].astype(LOW)

    return pl.pallas_call(
        kernel,
        out_shape=(
            jax.ShapeDtypeStruct((2, D + SMALL, D), LOW),
            jax.ShapeDtypeStruct((2, D + SMALL, D), LOW),
        ),
        in_specs=[vmem()] * 12,
        out_specs=[vmem()] * 2,
        scratch_shapes=[
            pltpu.VMEM((3 * D, D), LOW),
            pltpu.VMEM((SMALL, D), F32),
        ],
        compiler_params=params(12),
        cost_estimate=cost(6e9, 2e7),
        name="attn_grads",
    )(grad, a, attn, gqkv, scores, small_mlp, fc1_bias_grad, *weights, norms)


def attn_input_grad(table, grad, hidden, gqkv, weights, norms, shifted, work):
    rows = hidden.shape[0]
    bins = rows // PAD
    chunk_slots = 6
    chunk = chunk_slots * PAD
    spare = bins if shifted else 2

    def kernel(
        table_ref, grad_ref, hidden_ref, gqkv_ref, w0, w1, w2, w3, norm_ref,
        out_ref, wqkv, wide, tmp, moved,
    ):
        stack_qkv((w0, w1, w2, w3), wqkv)
        gain = norm_ref[0:1]
        if shifted:
            for i in range(bins // chunk_slots):
                slots = slice(i * chunk_slots, (i + 1) * chunk_slots)
                ga = dot_nn(gqkv_ref[i * chunk : (i + 1) * chunk], wqkv[...])
                wide[slots] = ga.reshape(chunk_slots, PAD, D)
            move_windows(table_ref, wide, tmp, moved, True)

        for i in range(bins // chunk_slots):
            at = slice(i * chunk, (i + 1) * chunk)
            if shifted:
                ga = moved[i * chunk_slots : (i + 1) * chunk_slots].reshape(chunk, D)
            else:
                ga = dot_nn(gqkv_ref[at], wqkv[...])
            scaled, inverse = norm_rows(hidden_ref[at])
            out_ref[at] = grad_ref[at] + norm_back(ga, scaled, inverse, gain)

    return pl.pallas_call(
        kernel,
        out_shape=jax.ShapeDtypeStruct((rows, D), F32),
        in_specs=[smem()] + [vmem()] * 8,
        out_specs=vmem(),
        scratch_shapes=[pltpu.VMEM((3 * D, D), LOW)] + [pltpu.VMEM((spare, PAD, D), F32)] * 3,
        compiler_params=params(12),
        cost_estimate=cost(work, 1e7),
        name="attn_input_grad",
    )(table, grad, hidden, gqkv, *weights, norms)


def mlp_forward(mid, weights, fc1_bias, norms, layer):
    rows = mid.shape[0]
    chunk = 3 * PAD * 2
    steps = rows // chunk

    def kernel(
        mid_ref, w0, w1, w2, w3, fc1_bias_ref, norm_ref,
        out_ref, act_ref, slope_ref, fc1, fc2,
    ):
        stack_mlp((w0, w1, w2, w3), fc1, fc2)
        gain, shift, out_shift = norm_ref[0:1], norm_ref[1:2], norm_ref[2:3]

        def step(i, carry):
            at = pl.ds(pl.multiple_of(i * chunk, 16), chunk)
            rows_now = mid_ref[at]
            scaled, _ = norm_rows(rows_now)
            a = (scaled * gain + shift).astype(LOW)
            act, slope = gelu_parts(dot_nn(a, fc1[...]) + fc1_bias_ref[layer, 0:1])
            act = act.astype(LOW)
            act_ref[at] = act
            slope_ref[at] = slope.astype(LOW)
            out_ref[at] = rows_now + dot_nn(act, fc2[...]) + out_shift
            return carry

        lax.fori_loop(0, steps, step, 0, unroll=True)

    return pl.pallas_call(
        kernel,
        out_shape=(
            jax.ShapeDtypeStruct((rows, D), F32),
            jax.ShapeDtypeStruct((rows, FF), LOW),
            jax.ShapeDtypeStruct((rows, FF), LOW),
        ),
        in_specs=[vmem()] * 7,
        out_specs=[vmem()] * 3,
        scratch_shapes=[pltpu.VMEM((D, FF), LOW), pltpu.VMEM((FF, D), LOW)],
        compiler_params=params(14),
        cost_estimate=cost(7e9, 2e7),
        name="mlp_forward",
    )(mid, *weights, fc1_bias, norms)


def mlp_sums(gpre, a, act, low_grad, fc1, fc1_sums, grad_sums, norms, outs):
    keep_ref, send_ref, small_ref, bias_ref = outs
    gain, shift = norms[0:1], norms[1:2]
    dfc1 = dot_tn(a[...], gpre[...])
    dfc2 = dot_tn(low_grad[...], act[...])
    column = jnp.sum(dfc1 * fc1[...].astype(F32), axis=1, keepdims=True)
    match = jnp.broadcast_to(column, (D, 128)).T
    for k in range(4):
        dest = keep_ref if k < 2 else send_ref
        cols = slice(k * D, (k + 1) * D)
        dest[k % 2, 0:D] = dfc1[:, cols].astype(LOW)
        dest[k % 2, D : 2 * D] = dfc2[:, cols].astype(LOW)
    wide_sums = jnp.broadcast_to(fc1_sums, (16, FF))
    dshift = sum(dot_nt(part, fc1[...]) for part in split(wide_sums))[0:1]
    small_ref[0:1] = (match[0:1] - shift * dshift) / gain
    small_ref[1:2] = dshift
    small_ref[2:3] = grad_sums
    small_ref[3:8] = jnp.zeros((5, D), F32)
    bias_ref[...] = fc1_sums


def sums_shapes():
    return (
        jax.ShapeDtypeStruct((2, 2 * D, D), LOW),
        jax.ShapeDtypeStruct((2, 2 * D, D), LOW),
        jax.ShapeDtypeStruct((8, D), F32),
        jax.ShapeDtypeStruct((1, FF), F32),
    )


def mlp_backward(grad, mid, act, slope, weights, norms):
    rows = mid.shape[0]
    chunk = 6 * PAD
    steps = rows // chunk

    def kernel(
        grad_ref, mid_ref, act_ref, slope_ref, w0, w1, w2, w3, norm_ref,
        gpre_ref, keep_ref, send_ref, small_ref, bias_ref, fc1, fc2, low_grad, a_ref,
    ):
        stack_mlp((w0, w1, w2, w3), fc1, fc2)
        gain, shift = norm_ref[0:1], norm_ref[1:2]
        fc1_sums, grad_sums = jnp.zeros((1, FF), F32), jnp.zeros((1, D), F32)
        for i in range(steps):
            at = slice(i * chunk, (i + 1) * chunk)
            gz = grad_ref[at].astype(LOW)
            low_grad[at] = gz
            gpre = (dot_nt(gz, fc2[...]) * slope_ref[at].astype(F32)).astype(LOW)
            gpre_ref[at] = gpre
            scaled, _ = norm_rows(mid_ref[at])
            a_ref[at] = (scaled * gain + shift).astype(LOW)
            fc1_sums = fc1_sums + jnp.sum(gpre.astype(F32), axis=0, keepdims=True)
            grad_sums = grad_sums + jnp.sum(gz.astype(F32), axis=0, keepdims=True)
        outs = keep_ref, send_ref, small_ref, bias_ref
        mlp_sums(gpre_ref, a_ref, act_ref, low_grad, fc1, fc1_sums, grad_sums, norm_ref, outs)

    return pl.pallas_call(
        kernel,
        out_shape=(jax.ShapeDtypeStruct((rows, FF), LOW), *sums_shapes()),
        in_specs=[vmem()] * 9,
        out_specs=[vmem()] * 5,
        scratch_shapes=[
            pltpu.VMEM((D, FF), LOW),
            pltpu.VMEM((FF, D), LOW),
            pltpu.VMEM((rows, D), LOW),
            pltpu.VMEM((rows, D), LOW),
        ],
        compiler_params=params(18),
        cost_estimate=cost(7e9, 2e7),
        name="mlp_backward",
    )(grad, mid, act, slope, *weights, norms)


def mlp_turn(mid, grad, weights, fc1_bias, norms, layer):
    rows = mid.shape[0]
    chunk = 6 * PAD
    steps = rows // chunk

    def kernel(
        mid_ref, grad_ref, w0, w1, w2, w3, fc1_bias_ref, norm_ref,
        out_ref, gpre_ref, keep_ref, send_ref, small_ref, bias_ref,
        fc1, fc2, a_all, act_all, low_grad,
    ):
        stack_mlp((w0, w1, w2, w3), fc1, fc2)
        gain, shift, out_shift = norm_ref[0:1], norm_ref[1:2], norm_ref[2:3]

        def step(i, totals):
            at = pl.ds(pl.multiple_of(i * chunk, 16), chunk)
            rows_now = mid_ref[at]
            scaled, _ = norm_rows(rows_now)
            a = (scaled * gain + shift).astype(LOW)
            a_all[at] = a
            act, slope = gelu_parts(dot_nn(a, fc1[...]) + fc1_bias_ref[layer, 0:1])
            act = act.astype(LOW)
            act_all[at] = act
            out_ref[at] = rows_now + dot_nn(act, fc2[...]) + out_shift
            gz = grad_ref[at].astype(LOW)
            low_grad[at] = gz
            gpre = (dot_nt(gz, fc2[...]) * slope).astype(LOW)
            gpre_ref[at] = gpre
            return (
                totals[0] + jnp.sum(gz.astype(F32), axis=0, keepdims=True),
                totals[1] + jnp.sum(gpre.astype(F32), axis=0, keepdims=True),
            )

        zeros = jnp.zeros((1, D), F32), jnp.zeros((1, FF), F32)
        grad_sums, fc1_sums = lax.fori_loop(0, steps, step, zeros)
        outs = keep_ref, send_ref, small_ref, bias_ref
        mlp_sums(gpre_ref, a_all, act_all, low_grad, fc1, fc1_sums, grad_sums, norm_ref, outs)

    return pl.pallas_call(
        kernel,
        out_shape=(
            jax.ShapeDtypeStruct((rows, D), F32),
            jax.ShapeDtypeStruct((rows, FF), LOW),
            *sums_shapes(),
        ),
        in_specs=[vmem()] * 8,
        out_specs=[vmem()] * 6,
        scratch_shapes=[
            pltpu.VMEM((D, FF), LOW),
            pltpu.VMEM((FF, D), LOW),
            pltpu.VMEM((rows, D), LOW),
            pltpu.VMEM((rows, FF), LOW),
            pltpu.VMEM((rows, D), LOW),
        ],
        compiler_params=params(18),
        cost_estimate=cost(1.5e10, 4e7),
        name="mlp_turn",
    )(mid, grad, *weights, fc1_bias, norms)


def mlp_input_grad(grad, mid, gpre, weights, norms):
    rows = mid.shape[0]
    chunk = 6 * PAD

    def kernel(grad_ref, mid_ref, gpre_ref, w0, w1, w2, w3, norm_ref, out_ref, fc1):
        for k, piece in enumerate((w0, w1, w2, w3)):
            fc1[:, k * D : (k + 1) * D] = piece[0:D]
        gain = norm_ref[0:1]
        for i in range(rows // chunk):
            at = slice(i * chunk, (i + 1) * chunk)
            ga = dot_nt(gpre_ref[at], fc1[...])
            scaled, inverse = norm_rows(mid_ref[at])
            out_ref[at] = grad_ref[at] + norm_back(ga, scaled, inverse, gain)

    return pl.pallas_call(
        kernel,
        out_shape=jax.ShapeDtypeStruct((rows, D), F32),
        in_specs=[vmem()] * 8,
        out_specs=vmem(),
        scratch_shapes=[pltpu.VMEM((D, FF), LOW)],
        compiler_params=params(8),
        cost_estimate=cost(3e12, 1e7),
        name="mlp_input_grad",
    )(grad, mid, gpre, *weights, norms)


def small_outputs(rows):
    def kernel(rows_ref, gains_ref, shifts_ref, fc1_ref, qv_ref, table_ref):
        for l in range(LAYERS):
            now = rows_ref[l]
            for i, row in enumerate((0, 3)):
                gains_ref[l, i : i + 1] = now[row : row + 1]
            for i, row in enumerate((1, 4, 2, 5)):
                shifts_ref[l, i : i + 1] = now[row : row + 1]
            fc1_ref[l : l + 1] = now[6:7]
            qv_ref[l] = now[7:9, 0:96]
            turned = rows_ref[l, 8:SMALL, 0:256].T
            table_ref[l] = turned[0:169, 1:4]

    return pl.pallas_call(
        kernel,
        out_shape=(
            jax.ShapeDtypeStruct((LAYERS, 2, D), F32),
            jax.ShapeDtypeStruct((LAYERS, 4, D), F32),
            jax.ShapeDtypeStruct((LAYERS, D), F32),
            jax.ShapeDtypeStruct((LAYERS, 2, 96), F32),
            jax.ShapeDtypeStruct((LAYERS, 169, 3), F32),
        ),
        in_specs=[vmem()],
        out_specs=[vmem()] * 5,
        compiler_params=params(4),
        cost_estimate=cost(0, 1e6),
        name="small_outputs",
    )(rows)


def swap_core(value):
    return lax.ppermute(value, "head", [(i, i ^ 1) for i in range(4)])


def swap_chip(value):
    return lax.ppermute(value, "head", [(i, i ^ 2) for i in range(4)])


def swap_border(value):
    return lax.ppermute(value, "head", [(1, 2), (2, 1)])


def swap_dp(value, step, size):
    return lax.ppermute(value, "dp", [(i, i ^ step) for i in range(size)])


def tie(*values):
    return lax.optimization_barrier(values)


def pick(first, one, other):
    first = first > 0
    return jnp.where(first, one, other), jnp.where(first, other, one)


def dp_masks(order):
    size = lax.axis_size("dp")
    upper = [(2 << b) - 2 for b in range(1, size.bit_length() - 1)]
    if order == 1 and upper:
        return [upper[-1]] + upper[:-1] + [1]
    return [1] + (upper if order == 2 else upper[::-1])


def dp_start(parts, sides, order):
    half = parts[0].shape[0] // 2
    low = sum(p[:half].astype(F32) for p in parts)
    high = sum(p[half:].astype(F32) for p in parts)
    masks = dp_masks(order)
    kept, sent = pick(sides[order % 2], low, high)
    return kept, swap_dp(sent.astype(LOW), masks[0], lax.axis_size("dp"))


def dp_next(kept, other, order, stage):
    masks = dp_masks(order)
    value = (kept.astype(F32) + other.astype(F32)).astype(LOW)
    return value, swap_dp(value, (masks + masks[:1])[stage], lax.axis_size("dp"))


def dp_join(value, other, sides, order):
    low, high = pick(sides[order % 2], value, other)
    return jnp.concatenate([low, high])


def body(
    tokens, outputs_grad, image_kind, qkv_weight, qv_bias, bias_table, proj_weight,
    fc1_weight, fc1_bias, fc2_weight, gains, shifts,
):
    own = tokens.shape[0] // PLACES
    bins = own + 2
    me = lax.axis_index("head").astype(jnp.int32)

    def border(value):
        edge = 4 * PLACES
        return swap_border(jnp.where(me == 1, value[-edge:], value[:edge]))

    turned = jnp.transpose(qkv_weight, (0, 2, 3, 1)).reshape(LAYERS, 288, D)

    def attn_pack(l):
        return jnp.concatenate([turned[l], proj_weight[l]], axis=0)

    def mlp_pack(l):
        return jnp.concatenate([fc1_weight[l], fc2_weight[l]], axis=0)

    def norm_pack(l, which, bias_row):
        rows = jnp.stack([gains[l, which], shifts[l, which], shifts[l, bias_row]])
        return jnp.pad(rows, ((0, 5), (0, 0)))

    partner = swap_core(tokens)
    rows = jnp.pad(jnp.transpose(bias_table, (0, 2, 1)).reshape(6, 169), ((0, 0), (0, D - 169)))
    small = jnp.concatenate([rows, qv_bias.reshape(1, D), fc1_bias])
    small = jnp.pad(small, ((0, SMALL - 9), (0, 0)))
    own_pack = [jnp.concatenate([attn_pack(0), *split(small)])]
    chip_pack = [swap_chip(own_pack[0])]
    edges, _ = tie(tokens, own_pack[0])
    halo = border(edges)
    place = lax.axis_index("dp")
    top = lax.axis_size("dp") // 2
    sides = [1 - (place & 1), (place < top).astype(jnp.int32)]
    first = jnp.broadcast_to(jnp.stack(sides).astype(jnp.int32)[:, None], (2, D))
    table = make_plan(image_kind, me, own, bins)
    mlp_first = mlp_pack(0)
    table, first, chip_pack[0], partner, mlp_first = tie(
        table, first, chip_pack[0], partner, mlp_first
    )
    sides = [first[0:1], first[1:2]]
    hidden = gather_slots(table, tokens, partner, halo, bins)

    def gathered(i):
        p, c = own_pack[i], chip_pack[i]
        return p, c, swap_core(p), swap_core(c)

    pack, halo, _ = tie(mlp_first, halo, chip_pack[0])
    own_pack.append(pack)
    chip_pack.append(swap_chip(pack))
    first_weights = gathered(0)
    bias, qkv_bias, fc1_all = spread_smalls(first_weights)

    saved, weights = [], []
    last = LAYERS - 1
    for l in range(LAYERS):
        norms, mlp_norms = norm_pack(l, 0, 2), norm_pack(l, 1, 3)
        weights.append(first_weights if l == 0 else gathered(2 * l))
        mid, a, qkv, probs, attn = attn_forward(
            table, hidden, weights[2 * l], qkv_bias, bias, norms, l
        )
        mid, chip_pack[2 * l + 1] = tie(mid, chip_pack[2 * l + 1])
        weights.append(gathered(2 * l + 1))
        if l == last:
            saved.append((hidden, mid, a, qkv, probs, attn, norms, mlp_norms))
            break
        pack, outputs_grad, mid = tie(attn_pack(1), outputs_grad, mid)
        grad_partner, grad_halo = swap_core(outputs_grad), border(outputs_grad)
        own_pack.append(pack)
        chip_pack.append(swap_chip(pack))
        out, act, slope = mlp_forward(mid, weights[2 * l + 1], fc1_all, mlp_norms, l)
        pack, out, chip_pack[2], grad_partner, grad_halo = tie(
            mlp_pack(1), out, chip_pack[2], grad_partner, grad_halo
        )
        own_pack.append(pack)
        chip_pack.append(swap_chip(pack))
        saved.append((hidden, mid, a, qkv, probs, attn, norms, mlp_norms, act, slope))
        hidden = out
    grad = gather_slots(table, outputs_grad, grad_partner, grad_halo, bins)

    def give_back(value):
        slots = value.reshape(bins, PAD, D)
        return slots, swap_core(slots), swap_border(border_slots(table, slots, 0))

    def mlp_back(l, grad):
        return mlp_backward(
            grad, saved[l][1], saved[l][8], saved[l][9], weights[2 * l + 1], saved[l][7]
        )

    def mlp_input(l, grad, gpre):
        return mlp_input_grad(grad, saved[l][1], gpre, weights[2 * l + 1], saved[l][7])

    def attn_back(l, grad):
        return attn_backward(table, grad, saved[l][3], saved[l][4], weights[2 * l], l % 2 == 1)

    def attn_sums(l, grad, gqkv, scores, small_mlp, fc1_bias_grad):
        return attn_grads(
            grad, saved[l][2], saved[l][5], gqkv, scores, small_mlp, fc1_bias_grad,
            weights[2 * l], saved[l][6],
        )

    def attn_input(l, grad, gqkv):
        work = 6e9 if l == last else 3e12
        return attn_input_grad(
            table, grad, saved[l][0], gqkv, weights[2 * l], saved[l][6], l % 2 == 1, work
        )

    def core_sum(keep, other):
        return [(keep[i].astype(F32) + other[i].astype(F32)).astype(LOW) for i in range(2)]

    out, gpre, keep_a, send_a, small_mlp, fc1_bias_grad = mlp_turn(
        saved[last][1], grad, weights[2 * last + 1], fc1_all, saved[last][7], last
    )
    core_a = swap_core(send_a)
    grad = mlp_input(1, grad, gpre)
    grad, core_a = tie(grad, core_a)
    half_a, out_a = core_sum(keep_a, core_a)
    grad, out_a = tie(grad, out_a)
    chip_a = swap_chip(out_a)
    gqkv, scores = attn_back(1, grad)
    grad_after = attn_input(1, grad, gqkv)
    gqkv, _ = tie(gqkv, grad_after)
    keep_b, send_b = attn_sums(1, grad, gqkv, scores, small_mlp, fc1_bias_grad)
    grad, send_b, chip_a = tie(grad_after, send_b, chip_a)
    core_b = swap_core(send_b)
    state_a = dp_start((half_a, chip_a), sides, 0)
    gpre, keep_c, send_c, small_mlp, fc1_bias_grad = mlp_back(0, grad)
    gpre, send_c, state_a, core_b = tie(gpre, send_c, state_a, core_b)
    core_c = swap_core(send_c)
    state_a = dp_next(*state_a, 0, 1)
    half_b, out_b = core_sum(keep_b, core_b)
    gpre, out_b = tie(gpre, out_b)
    chip_b = swap_chip(out_b)
    grad = mlp_input(0, grad, gpre)
    grad, core_c = tie(grad, core_c)
    half_c, out_c = core_sum(keep_c, core_c)
    grad, out_c = tie(grad, out_c)
    chip_c = swap_chip(out_c)
    gqkv, scores = attn_back(0, grad)
    gqkv, state_a = tie(gqkv, state_a)
    state_a = dp_next(*state_a, 0, 2)
    keep_d, send_d = attn_sums(0, grad, gqkv, scores, small_mlp, fc1_bias_grad)
    core_d = swap_core(send_d)
    out, state_a, chip_b, chip_c, _ = tie(out, state_a, chip_b, chip_c, send_d)
    state_c = dp_start((half_c, chip_c), sides, 2)
    out_slots = out.reshape(bins, PAD, D)
    out_edge, core_d = tie(border_slots(table, out_slots, 3e12), core_d)
    half_d, out_d = core_sum(keep_d, core_d)
    chip_d = swap_chip(out_d)
    gqkv, out_slots, out_edge, _ = tie(gqkv, out_slots, out_edge, out_d)
    grad = attn_input(0, grad, gqkv)
    output_parts = out_slots, swap_core(out_slots), swap_border(out_edge)
    chip_d, state_a, state_c = tie(chip_d, state_a, state_c)
    half_bd = jnp.concatenate([half_b, half_d])
    state_d = dp_start((half_bd, jnp.concatenate([chip_b, chip_d])), sides, 2)
    state_c = dp_next(*state_c, 2, 1)
    tokens_parts = give_back(grad)
    state_d, state_c = tie(state_d, state_c)
    state_d = dp_next(*state_d, 2, 1)
    state_c = dp_next(*state_c, 2, 2)
    state_a = dp_next(*state_a, 0, 3)
    output = return_slots(table, *output_parts, own)
    state_d, state_c, state_a = tie(state_d, state_c, state_a)
    state_d = dp_next(*state_d, 2, 2)
    state_c = dp_next(*state_c, 2, 3)
    tokens_grad = return_slots(table, *tokens_parts, own)
    state_d, state_c, output, tokens_grad = tie(state_d, state_c, output, tokens_grad)
    value_d, other_d = dp_next(*state_d, 2, 3)
    total_a = dp_join(*state_a, sides, 0)
    total_c = dp_join(*state_c, sides, 2)
    mlp_all = jnp.stack([total_c, total_a]).astype(F32)
    fc1_out = mlp_all[:, :D]
    fc2_out = mlp_all[:, D:].transpose(0, 2, 1)
    total_bd = dp_join(value_d, other_d, sides, 2)
    total_b, total_d = total_bd[: D + SMALL], total_bd[D + SMALL :]

    attn_all = jnp.stack([total_d, total_b]).astype(F32)
    gains_out, shifts_out, fc1_bias_out, qv_out, table_out = small_outputs(attn_all[:, D:])
    qkv_out = attn_all[:, 0:288].reshape(LAYERS, 3, 96, D).transpose(0, 3, 1, 2)
    proj_out = attn_all[:, 288:384]
    return (
        output, tokens_grad, qkv_out, qv_out, table_out, proj_out, fc1_out, fc1_bias_out,
        fc2_out, gains_out, shifts_out,
    )


def solution(mesh):
    rows = P(("dp", "head"), None)
    placed = (
        rows,
        rows,
        P("dp", None),
        P(None, None, None, "head"),
        P(None, None, "head"),
        P(None, None, "head"),
        P(None, "head", None),
        P(None, None, "head"),
        P(None, "head"),
        P(None, "head", None),
        P(),
        P(),
    )
    return jax.shard_map(
        body,
        mesh=mesh,
        in_specs=placed,
        out_specs=(
            rows,
            rows,
            P(None, None, None, "head"),
            P(None, None, "head"),
            P(None, None, "head"),
            P(None, "head", None),
            P(None, None, "head"),
            P(None, "head"),
            P(None, "head", None),
            P(),
            P(),
        ),
        check_vma=False,
    )
```

```python
import jax
import jax.numpy as jnp
from jax import lax
from jax.experimental import pallas as pl
from jax.experimental.pallas import tpu as pltpu
from jax.sharding import PartitionSpec as P

D = 384
FF = 1536
LAYERS = 2
PLACES = 49
PAD = 56
WIDE = 64
QUADS = 3
HEAD_DIM = 32
SCORE_SCALE = HEAD_DIM**-0.5
LN_EPS = 1e-05
LOW = jnp.bfloat16
F32 = jnp.float32
MIB = 1024 * 1024
SMALL = 16

SRC, SIDE, WROW, WCOL, FIRST, RET, SEND = 0, 24, 48, 72, 96, 120, 140
TABLE = 144


def vmem():
    return pl.BlockSpec(memory_space=pltpu.VMEM)


def smem():
    return pl.BlockSpec(memory_space=pltpu.SMEM)


def anywhere():
    return pl.BlockSpec(memory_space=pl.ANY)


def params(limit):
    return pltpu.CompilerParams(vmem_limit_bytes=limit * MIB)


def cost(flops, size):
    return pl.CostEstimate(flops=int(flops * 0.02), bytes_accessed=int(size * 0.02), transcendentals=0)


def dot_nn(a, b):
    return lax.dot_general(a, b, (((1,), (0,)), ((), ())), preferred_element_type=F32)


def dot_nt(a, b):
    return lax.dot_general(a, b, (((1,), (1,)), ((), ())), preferred_element_type=F32)


def dot_tn(a, b):
    return lax.dot_general(a, b, (((0,), (0,)), ((), ())), preferred_element_type=F32)


def plan_kernel(own, bins, kind_ref, me_ref, out_ref, load_ref):
    me = me_ref[0]
    half = 2 * own
    for i in range(TABLE):
        out_ref[i] = -1 if i < bins or RET <= i < RET + own else 0
    for i in range(bins):
        out_ref[SIDE + i] = 1
        out_ref[FIRST + i] = i
    for i in range(4):
        load_ref[i] = 0

    def place(start, count, side, bin_id):
        base = load_ref[bin_id]
        load_ref[bin_id] = base + count

        def step(k, carry):
            slot = start + k
            owner = slot // own
            inner = slot - owner * own
            local = base + k
            mine = bin_id == me
            halo = jnp.where(me == 1, slot - half, slot - half + 4)
            code = jnp.where(
                owner == me, inner, jnp.where(owner == (me ^ 1), own + inner, 2 * own + halo)
            )

            @pl.when(mine)
            def _():
                wrow = k // side
                out_ref[SRC + local] = code
                out_ref[SIDE + local] = side
                out_ref[WROW + local] = wrow
                out_ref[WCOL + local] = k - wrow * side
                out_ref[FIRST + local] = base

            @pl.when(owner == me)
            def _():
                back = jnp.where(me == 2, slot - half, k)
                out_ref[RET + inner] = jnp.where(
                    mine, local, jnp.where(bin_id == (me ^ 1), bins + local, 2 * bins + back)
                )

            return carry

        lax.fori_loop(0, count, step, 0)

    for turn in range(3):

        def visit(i, start, turn=turn):
            kind = kind_ref[0, i]
            count = jnp.where(kind == 2, 9, jnp.where(kind == 1, 4, 0))
            side = jnp.where(kind == 2, 3, 2)
            cut = half - start
            across = (cut > 0) & (cut < count)
            second = (start >= half) | (across & (cut < count - cut))
            chip = jnp.where(second, 1, 0)
            left, right = load_ref[2 * chip], load_ref[2 * chip + 1]
            emptier = 2 * chip + jnp.where(left <= right, 0, 1)
            if turn == 0:
                chosen, bin_id = across, 1 + chip
            else:
                chosen, bin_id = (kind == 3 - turn) & jnp.logical_not(across), emptier

            @pl.when(chosen)
            def _():
                place(start, count, side, bin_id)
                if turn == 0:
                    out_ref[SEND] = jnp.where((me == 1) & (chip == 0), cut, 0)

            return start + count

        lax.fori_loop(0, kind_ref.shape[1], visit, jnp.int32(0))


def gather_kernel(bins, table_ref, refs, out_ref, spread_ref):
    spread_ref[...] = jnp.zeros(spread_ref.shape, F32)
    at = 0
    for ref in refs:
        for s in range(ref.shape[0] // PLACES):
            spread_ref[at, 0:PLACES] = ref[s * PLACES : (s + 1) * PLACES].astype(F32)
            at += 1

    def step(j, carry):
        src = table_ref[SRC + j]

        @pl.when(src < 0)
        def _():
            out_ref[j] = jnp.zeros((PAD, D), F32)

        @pl.when(src >= 0)
        def _():
            out_ref[j] = spread_ref[src]

        return carry

    lax.fori_loop(0, bins, step, 0)


def make_plan(image_kind, me, own, bins):
    def kernel(kind_ref, me_ref, table_ref, load_ref):
        plan_kernel(own, bins, kind_ref, me_ref, table_ref, load_ref)

    return pl.pallas_call(
        kernel,
        out_shape=jax.ShapeDtypeStruct((TABLE,), jnp.int32),
        in_specs=[smem(), smem()],
        out_specs=smem(),
        scratch_shapes=[pltpu.SMEM((4,), jnp.int32)],
        compiler_params=params(1),
        cost_estimate=cost(0, 1.5e7),
        name="plan",
    )(image_kind, me.reshape(1))


def gather_slots(table, mine, partner, halo, bins):
    own = mine.shape[0] // PLACES

    def kernel(table_ref, *refs):
        gather_kernel(bins, table_ref, refs[:3], refs[3], refs[4])

    out = pl.pallas_call(
        kernel,
        out_shape=jax.ShapeDtypeStruct((bins, PAD, D), F32),
        in_specs=[smem()] + [vmem()] * 3,
        out_specs=vmem(),
        scratch_shapes=[pltpu.VMEM((2 * own + 4, PAD, D), F32)],
        compiler_params=params(8),
        cost_estimate=cost(0, 8e6),
        name="gather_slots",
    )(table, mine, partner, halo)
    return out.reshape(bins * PAD, D)


def border_slots(table, slots, work):
    def kernel(table_ref, slots_ref, out_ref):
        start = table_ref[SEND]
        for j in range(4):
            out_ref[j] = slots_ref[start + j]

    return pl.pallas_call(
        kernel,
        out_shape=jax.ShapeDtypeStruct((4,) + slots.shape[1:], F32),
        in_specs=[smem(), vmem()],
        out_specs=vmem(),
        compiler_params=params(4),
        cost_estimate=cost(work, 1e6),
        name="border_slots",
    )(table, slots)


def return_slots(table, mine, partner, halo, own):
    bins = mine.shape[0]

    def kernel(table_ref, mine_ref, partner_ref, halo_ref, out_ref):
        for s in range(own):
            src = table_ref[RET + s]
            rows = pl.ds(s * PLACES, PLACES)

            @pl.when(src < 0)
            def _():
                out_ref[rows] = jnp.zeros((PLACES, D), F32)

            @pl.when((src >= 0) & (src < bins))
            def _():
                out_ref[rows] = mine_ref[src, 0:PLACES]

            @pl.when((src >= bins) & (src < 2 * bins))
            def _():
                out_ref[rows] = partner_ref[src - bins, 0:PLACES]

            @pl.when(src >= 2 * bins)
            def _():
                out_ref[rows] = halo_ref[src - 2 * bins, 0:PLACES]

    return pl.pallas_call(
        kernel,
        out_shape=jax.ShapeDtypeStruct((own * PLACES, D), F32),
        in_specs=[smem(), vmem(), vmem(), vmem()],
        out_specs=vmem(),
        compiler_params=params(8),
        cost_estimate=cost(0, 8e6),
        name="return_slots",
    )(table, mine, partner, halo)


def norm_rows(rows):
    average = jnp.mean(rows, axis=-1, keepdims=True)
    centred = rows - average
    inverse = lax.rsqrt(jnp.mean(centred * centred, axis=-1, keepdims=True) + LN_EPS)
    return centred * inverse, inverse


def norm_back(incoming, scaled, inverse, gain):
    weighted = incoming * gain
    return inverse * (
        weighted
        - jnp.mean(weighted, axis=-1, keepdims=True)
        - scaled * jnp.mean(weighted * scaled, axis=-1, keepdims=True)
    )


def gelu_parts(x):
    t = 1.0 / (1.0 + 0.23164189 * jnp.abs(x))
    bell = jnp.exp2(x * x * -0.7213475204444817)
    poly = t * (
        0.127414796 + t * (-0.142248368 + t * (0.7107068705 + t * (-0.7265760135 + t * 0.5307027145)))
    )
    tail = poly * bell
    phi = jnp.where(x >= 0, 1.0 - tail, tail)
    return x * phi, phi + x * bell * 0.3989422804014327


def place_parts(shape, dim):
    place = lax.broadcasted_iota(jnp.int32, shape, dim)
    row = (place * 37) >> 8
    return place, row, place - 7 * row


def neighbour(table_ref, w, back, down):
    side, wrow, wcol = table_ref[SIDE + w], table_ref[WROW + w], table_ref[WCOL + w]
    at = wrow if down else wcol
    if back:
        other = jnp.where(at == 0, side - 1, at - 1)
    else:
        other = jnp.where(at == side - 1, 0, at + 1)
    if down:
        return table_ref[FIRST + w] + other * side + wcol
    return table_ref[FIRST + w] + wrow * side + other


def move_windows(table_ref, src, tmp, out, back):
    bins = src.shape[0]
    tmp[...] = jnp.zeros(tmp.shape, F32)
    out[...] = jnp.zeros(out.shape, F32)

    def rows(w, carry):
        other = neighbour(table_ref, w, back, True)
        if back:
            tmp[w, 21:49] = src[w, 0:28]
            tmp[w, 0:21] = src[other, 28:49]
        else:
            tmp[w, 0:28] = src[w, 21:49]
            tmp[w, 28:49] = src[other, 0:21]
        return carry

    lax.fori_loop(0, bins, rows, 0, unroll=2)
    _, _, col = place_parts((PAD, 1), 0)

    def cols(w, carry):
        other = neighbour(table_ref, w, back, False)
        if back:
            out[w, 0:49] = tmp[other, 4:53]
            out[w, 3:49] = jnp.where(col[3:49] >= 3, tmp[w, 0:46], out[w, 3:49])
        else:
            out[w, 0:49] = tmp[w, 3:52]
            out[w, 4:49] = jnp.where(col[4:49] < 4, out[w, 4:49], tmp[other, 0:45])
        return carry

    lax.fori_loop(0, bins, cols, 0, unroll=2)


def head_marks():
    lane = lax.broadcasted_iota(jnp.int32, (WIDE, 128), 1) // HEAD_DIM
    return [jnp.where(lane == h, 1.0, 0.0).astype(LOW) for h in range(4)]


def spread(block, marks):
    return jnp.concatenate([block * mark for mark in marks], axis=0)


def fold(product, marks):
    total = None
    for h, mark in enumerate(marks):
        part = product[h * WIDE : (h + 1) * WIDE] * mark.astype(F32)
        total = part if total is None else total + part
    return total


def spread_pair(block, marks):
    return jnp.concatenate([spread(block[0:WIDE], marks), spread(block[WIDE:], marks)], axis=1)


def diagonal(block):
    zero = jnp.zeros((WIDE, 128), block.dtype)
    top = jnp.concatenate([block[0:WIDE], zero], axis=1)
    return jnp.concatenate([top, jnp.concatenate([zero, block[WIDE:]], axis=1)], axis=0)


def by_head(values):
    return values.reshape(4, WIDE, 128)


def pad_rows(rows):
    return jnp.concatenate([rows, jnp.zeros((WIDE - PAD, rows.shape[1]), rows.dtype)], axis=0)


def split(values):
    high = values.astype(LOW)
    return high, (values - high.astype(F32)).astype(LOW)


def marks_where(rows, cols, test):
    row = lax.broadcasted_iota(jnp.int32, (rows, cols), 0)
    col = lax.broadcasted_iota(jnp.int32, (rows, cols), 1)
    return jnp.where(test(row, col), 1.0, 0.0).astype(LOW)


def far(place):
    row = (place * 37) >> 8
    return 13 * row + (place - 7 * row)


def spread_smalls(smalls):
    heads = LAYERS * 12

    def kernel(p0, p1, p2, p3, out_ref, qkv_ref, fc1_ref, table_ref, small_ref):
        quarters = []
        for k, ref in enumerate((p0, p1, p2, p3)):
            high, low = ref[D : D + SMALL], ref[D + SMALL : D + 2 * SMALL]
            small_ref[k] = high.astype(F32) + low.astype(F32)
            quarters.append(small_ref.at[k])
        for k, ref in enumerate(quarters):
            for l in range(LAYERS):
                at = l * 12 + k * 3
                table_ref[at : at + 3] = ref[l * 3 : l * 3 + 3, 0:256]
        lane = lax.broadcasted_iota(jnp.int32, (8, D), 1)
        for l in range(LAYERS):
            for c in range(3):
                total = jnp.zeros((8, D), F32)
                for k, ref in enumerate(quarters):
                    if c != 1:
                        row = jnp.broadcast_to(ref[6:7], (8, D))
                        row = pltpu.roll(row, (k * 96 - l * 192 - (c // 2) * 96) % D, 1)
                        own_lanes = (lane >= k * 96) & (lane < k * 96 + 96)
                        total = total + jnp.where(own_lanes, row, 0.0)
                qkv_ref[l, :, c * D : (c + 1) * D] = total
            for k, ref in enumerate(quarters):
                row = jnp.broadcast_to(ref[7 + l : 8 + l], (8, D))
                fc1_ref[l, :, k * D : (k + 1) * D] = row
        to_lane = marks_where(128, 128, lambda r, c: (far(c & 63) == r) & ((c & 63) < PLACES))
        to_row = marks_where(WIDE, 96, lambda r, c: (far(r) == c) & (r < PLACES))
        place = lax.broadcasted_iota(jnp.int32, (WIDE, 128), 0)
        empty = jnp.where(place < PLACES, 0.0, -1e30)
        turned = pltpu.roll(table_ref[...], 172, 1)
        skewed = []
        for n in range(heads):
            row = jnp.broadcast_to(turned[n : n + 1], (96, 256))
            skewed.append(pltpu.roll(row, 0, 1, stride=1, stride_axis=0)[:, 0:128])
        skewed = jnp.concatenate(skewed, axis=1)
        total = None
        for part in split(skewed):
            rows = dot_nn(to_row, part).astype(LOW)
            rows = jnp.concatenate([rows[:, n * 128 : (n + 1) * 128] for n in range(heads)], axis=0)
            part = dot_nn(rows, to_lane)
            total = part if total is None else total + part
        for n in range(heads):
            l, t, h = n // 12, n % 12 // 4, n % 4
            out_ref[l, t, h * WIDE : (h + 1) * WIDE] = total[n * WIDE : (n + 1) * WIDE] + empty

    return pl.pallas_call(
        kernel,
        out_shape=(
            jax.ShapeDtypeStruct((LAYERS, QUADS, 4 * WIDE, 128), F32),
            jax.ShapeDtypeStruct((LAYERS, 8, 3 * D), F32),
            jax.ShapeDtypeStruct((LAYERS, 8, FF), F32),
        ),
        in_specs=[vmem()] * 4,
        out_specs=[vmem()] * 3,
        scratch_shapes=[pltpu.VMEM((heads, 256), F32), pltpu.VMEM((4, SMALL, D), F32)],
        compiler_params=params(6),
        cost_estimate=cost(0, 1e7),
        name="spread_smalls",
    )(*smalls)


def scores_to_table(scores_ref):
    to_far = marks_where(128, 128, lambda r, c: (far(r & 63) == c) & ((r & 63) < PLACES))
    to_row = marks_where(96, WIDE, lambda r, c: (84 - far(c) == r) & (c < PLACES))
    wide = None
    for part in split(scores_ref[...].reshape(12 * WIDE, 128)):
        part = dot_nn(part, to_far)
        wide = part if wide is None else wide + part
    wide = jnp.concatenate([wide[h * WIDE : (h + 1) * WIDE] for h in range(12)], axis=1)
    rows = None
    for part in split(wide):
        part = dot_nn(to_row, part)
        rows = part if rows is None else rows + part
    out = []
    for h in range(12):
        one = rows[:, h * 128 : (h + 1) * 128]
        one = jnp.concatenate([one, jnp.zeros_like(one)], axis=1)
        one = pltpu.roll(one, 0, 1, stride=1, stride_axis=0)
        out.append(jnp.sum(one, axis=0, keepdims=True))
    return out


def stack_qkv(pieces, out_ref):
    for k, piece in enumerate(pieces):
        for c in range(3):
            out_ref[c * D + k * 96 : c * D + (k + 1) * 96] = piece[c * 96 : (c + 1) * 96]


def stack_proj(pieces, out_ref):
    for k, piece in enumerate(pieces):
        out_ref[k * 96 : (k + 1) * 96] = piece[288:384]


def stack_mlp(pieces, fc1_ref, fc2_ref):
    for k, piece in enumerate(pieces):
        fc1_ref[:, k * D : (k + 1) * D] = piece[0:D]
        fc2_ref[k * D : (k + 1) * D] = piece[D : 2 * D]


def attn_forward(table, hidden, weights, qv_bias, bias, norms, layer):
    shifted = layer % 2 == 1
    rows = hidden.shape[0]
    bins = rows // PAD
    chunk_slots = 6
    chunk = chunk_slots * PAD
    spare = bins if shifted else 2

    def kernel(
        table_ref, hidden_ref, w0, w1, w2, w3, qv_ref, bias_ref, norm_ref,
        mid_ref, a_ref, qkv_ref, p_ref, attn_ref,
        wqkv, wproj, wide, tmp, moved,
    ):
        pieces = (w0, w1, w2, w3)
        stack_qkv(pieces, wqkv)
        stack_proj(pieces, wproj)
        gain, shift, proj_shift = norm_ref[0:1], norm_ref[1:2], norm_ref[2:3]
        marks = head_marks()
        def norm_step(i, carry):
            at = pl.ds(pl.multiple_of(i * chunk, 16), chunk)
            scaled, _ = norm_rows(hidden_ref[at])
            normed = scaled * gain + shift
            if shifted:
                slots = pl.ds(i * chunk_slots, chunk_slots)
                wide[slots] = normed.reshape(chunk_slots, PAD, D)
            else:
                a_ref[at] = normed.astype(LOW)
            return carry

        lax.fori_loop(0, bins // chunk_slots, norm_step, 0)
        if shifted:
            move_windows(table_ref, wide, tmp, moved, False)
            a_ref[...] = moved[...].reshape(rows, D).astype(LOW)

        def qkv_step(i, carry):
            at = pl.ds(pl.multiple_of(i * chunk, 16), chunk)
            project = dot_nt(a_ref[at], wqkv[...]) + qv_ref[layer, 0:1]
            for j in range(chunk_slots):
                block = project[j * PAD : (j + 1) * PAD]
                at = pl.ds((j % 2) * WIDE, WIDE)
                qkv_ref[i * (chunk_slots // 2) + j // 2, at] = pad_rows(block).astype(LOW)
            return carry

        lax.fori_loop(0, bins // chunk_slots, qkv_step, 0)

        if shifted:
            _, qrow, qcol = place_parts((WIDE, 1), 0)
            lane = lax.broadcasted_iota(jnp.int32, (1, 128), 1)
            second = lane >= WIDE
            pplace = jnp.where(second, lane - WIDE, lane)
            prow = (pplace * 37) >> 8
            pcol = pplace - 7 * prow
            pband = 1 + (prow >= 4).astype(jnp.int32), 1 + (pcol >= 4).astype(jnp.int32)
            qband = 1 + (qrow >= 4).astype(jnp.int32), 1 + (qcol >= 4).astype(jnp.int32)

        def window(j, carry):
            if shifted:
                low = []
                for w in (2 * j, 2 * j + 1):
                    side = table_ref[SIDE + w]
                    low.append(
                        (
                            jnp.where(table_ref[WROW + w] == side - 1, 3, 0),
                            jnp.where(table_ref[WCOL + w] == side - 1, 1, 0),
                        )
                    )
                low_row = jnp.where(second, low[1][0], low[0][0])
                low_col = jnp.where(second, low[1][1], low[0][1])
                pregion = low_row * pband[0] + low_col * pband[1]
                qregion = low_row * qband[0] + low_col * qband[1]
                mask = jnp.where(pregion != qregion, -100.0, 0.0)[None]
            scores, probs = [], []
            for t in range(QUADS):
                q = qkv_ref[j, :, t * 128 : (t + 1) * 128]
                k = qkv_ref[j, :, D + t * 128 : D + (t + 1) * 128]
                scores.append(dot_nt(spread_pair(k, marks), diagonal(q)))
            for t in range(QUADS):
                now = by_head(scores[t] * SCORE_SCALE + bias_ref[layer, t])
                if shifted:
                    now = now + mask
                exponent = jnp.exp(now - jnp.max(now, axis=1, keepdims=True))
                total = jnp.sum(exponent, axis=1, keepdims=True)
                probs.append((exponent * (1.0 / total)).reshape(4 * WIDE, 128).astype(LOW))
                p_ref[j, t] = probs[t]
            for t in range(QUADS):
                cols = slice(t * 128, (t + 1) * 128)
                v = qkv_ref[j, :, 2 * D + t * 128 : 2 * D + (t + 1) * 128]
                both = dot_tn(probs[t], spread_pair(v, marks))
                wide[2 * j, :, cols] = both[0:PAD, 0:128]
                wide[2 * j + 1, :, cols] = both[WIDE : WIDE + PAD, 128:256]
            return carry

        lax.fori_loop(0, bins // 2, window, 0, unroll=9)
        if shifted:
            move_windows(table_ref, wide, tmp, moved, True)
            attn_ref[...] = moved[...].reshape(rows, D).astype(LOW)
        else:
            attn_ref[...] = wide[...].reshape(rows, D).astype(LOW)

        def proj_step(i, carry):
            at = pl.ds(pl.multiple_of(i * chunk, 16), chunk)
            mid_ref[at] = hidden_ref[at] + dot_nn(attn_ref[at], wproj[...]) + proj_shift
            return carry

        lax.fori_loop(0, bins // chunk_slots, proj_step, 0)

    return pl.pallas_call(
        kernel,
        out_shape=(
            jax.ShapeDtypeStruct((rows, D), F32),
            jax.ShapeDtypeStruct((rows, D), LOW),
            jax.ShapeDtypeStruct((bins // 2, 2 * WIDE, 3 * D), LOW),
            jax.ShapeDtypeStruct((bins // 2, QUADS, 4 * WIDE, 128), LOW),
            jax.ShapeDtypeStruct((rows, D), LOW),
        ),
        in_specs=[smem()] + [vmem()] * 8,
        out_specs=[vmem()] * 5,
        scratch_shapes=[
            pltpu.VMEM((3 * D, D), LOW),
            pltpu.VMEM((D, D), LOW),
            pltpu.VMEM((bins, PAD, D), F32),
            pltpu.VMEM((spare, PAD, D), F32),
            pltpu.VMEM((spare, PAD, D), F32),
        ],
        compiler_params=params(11),
        cost_estimate=cost(1e10, 2e7),
        name="attn_forward",
    )(table, hidden, *weights, qv_bias, bias, norms)


def attn_backward(table, grad, qkv, probs, weights, shifted):
    rows = grad.shape[0]
    bins = rows // PAD
    chunk_slots = 6
    chunk = chunk_slots * PAD
    spare = bins if shifted else 2

    def kernel(
        table_ref, grad_ref, qkv_ref, p_ref, w0, w1, w2, w3,
        gqkv_ref, scores_ref, wproj, wide_attn, wide, tmp, moved,
    ):
        stack_proj((w0, w1, w2, w3), wproj)
        marks = head_marks()
        steps = bins // chunk_slots
        def keep_windows(i, block_rows):
            for j in range(chunk_slots):
                block = block_rows[j * PAD : (j + 1) * PAD]
                dest = pl.ds((j % 2) * WIDE, WIDE)
                wide_attn[i * (chunk_slots // 2) + j // 2, dest] = pad_rows(block).astype(LOW)

        def proj_step(i, carry):
            at = pl.ds(pl.multiple_of(i * chunk, 16), chunk)
            gattn = dot_nt(grad_ref[at].astype(LOW), wproj[...])
            if shifted:
                slots = pl.ds(i * chunk_slots, chunk_slots)
                wide[slots] = gattn.reshape(chunk_slots, PAD, D)
            else:
                keep_windows(i, gattn)
            return carry

        lax.fori_loop(0, steps, proj_step, 0)
        if shifted:
            move_windows(table_ref, wide, tmp, moved, False)

            def move_step(i, carry):
                slots = pl.ds(i * chunk_slots, chunk_slots)
                keep_windows(i, moved[slots].reshape(chunk, D))
                return carry

            lax.fori_loop(0, steps, move_step, 0)

        scores_ref[...] = jnp.zeros((QUADS, 4 * WIDE, 128), F32)

        def window(j, carry):
            at = pl.ds(pl.multiple_of(j * 2 * PAD, 16), 2 * PAD)

            def keep(c, t, left, right):
                cols = slice(c * D + t * 128, c * D + (t + 1) * 128)
                gqkv_ref[at, cols] = jnp.concatenate([left, right], axis=0).astype(LOW)

            go, gp, gv, low_ds, gq, gk = [], [], [], [], [], []
            for t in range(QUADS):
                v = qkv_ref[j, :, 2 * D + t * 128 : 2 * D + (t + 1) * 128]
                go.append(diagonal(wide_attn[j, :, t * 128 : (t + 1) * 128]))
                gp.append(dot_nt(spread_pair(v, marks), go[t]))
            for t in range(QUADS):
                gv.append(dot_nn(p_ref[j, t], go[t]))
            for t in range(QUADS):
                p = by_head(p_ref[j, t].astype(F32))
                now = by_head(gp[t])
                ds = p * (now - jnp.sum(now * p, axis=1, keepdims=True))
                low_ds.append(ds.reshape(4 * WIDE, 128).astype(LOW))
                scores_ref[t] += low_ds[t].astype(F32)
            for t in range(QUADS):
                q = qkv_ref[j, :, t * 128 : (t + 1) * 128]
                k = qkv_ref[j, :, D + t * 128 : D + (t + 1) * 128]
                gk.append(dot_nn(low_ds[t], diagonal(q)))
                gq.append(dot_tn(low_ds[t], spread_pair(k, marks)))
            for t in range(QUADS):
                left, right = slice(0, 128), slice(128, 256)
                keep(2, t, fold(gv[t][:, left], marks)[0:PAD], fold(gv[t][:, right], marks)[0:PAD])
            for t in range(QUADS):
                left, right = slice(0, 128), slice(128, 256)
                folded = fold(gk[t][:, left], marks), fold(gk[t][:, right], marks)
                keep(1, t, *[part[0:PAD] * SCORE_SCALE for part in folded])
                parts = gq[t][0:PAD, left], gq[t][WIDE : WIDE + PAD, right]
                keep(0, t, *[part * SCORE_SCALE for part in parts])
            return carry

        lax.fori_loop(0, bins // 2, window, 0, unroll=9)

    return pl.pallas_call(
        kernel,
        out_shape=(
            jax.ShapeDtypeStruct((rows, 3 * D), LOW),
            jax.ShapeDtypeStruct((QUADS, 4 * WIDE, 128), F32),
        ),
        in_specs=[smem()] + [vmem()] * 7,
        out_specs=[vmem()] * 2,
        scratch_shapes=[
            pltpu.VMEM((D, D), LOW),
            pltpu.VMEM((bins // 2, 2 * WIDE, D), LOW),
            pltpu.VMEM((spare, PAD, D), F32),
            pltpu.VMEM((spare, PAD, D), F32),
            pltpu.VMEM((spare, PAD, D), F32),
        ],
        compiler_params=params(11),
        cost_estimate=cost(1e10, 2e7),
        name="attn_backward",
    )(table, grad, qkv, probs, *weights)


def attn_grads(grad, a, attn, gqkv, scores, small_mlp, fc1_bias_grad, weights, norms):
    rows = grad.shape[0]

    def kernel(
        grad_ref, a_ref, attn_ref, gqkv_ref, scores_ref, mlp_ref, fc1b_ref, w0, w1, w2, w3, norm_ref,
        keep_ref, send_ref, wqkv, small,
    ):
        stack_qkv((w0, w1, w2, w3), wqkv)
        gain, shift = norm_ref[0:1], norm_ref[1:2]
        dqkv = dot_tn(a_ref[...], gqkv_ref[...])
        low_grad = grad_ref[...].astype(LOW)
        dproj = dot_tn(attn_ref[...], low_grad).astype(LOW)
        column_sums = jnp.sum(gqkv_ref[...].astype(F32), axis=0, keepdims=True)
        wide_sums = jnp.broadcast_to(column_sums, (16, 3 * D))
        dshift = sum(dot_nn(part, wqkv[...]) for part in split(wide_sums))[0:1]
        table_rows = scores_to_table(scores_ref)
        turned, match = [], jnp.zeros((1, D), F32)
        for c in range(3):
            back = dqkv[:, c * D : (c + 1) * D].T
            here = wqkv[c * D : (c + 1) * D].astype(F32)
            match = match + jnp.sum(back * here, axis=0, keepdims=True)
            turned.append(back.astype(LOW))
        small[...] = jnp.zeros((SMALL, D), F32)
        small[0:1] = (match - shift * dshift) / gain
        small[1:2] = dshift
        small[2:3] = jnp.sum(low_grad.astype(F32), axis=0, keepdims=True)
        small[3:6] = mlp_ref[0:3]
        gq_sum = jnp.broadcast_to(column_sums[:, 0:D], (8, D))
        gv_sum = jnp.broadcast_to(column_sums[:, 2 * D : 3 * D], (8, D))
        for k in range(4):
            dest = keep_ref if k < 2 else send_ref
            for c in range(3):
                dest[k % 2, c * 96 : (c + 1) * 96] = turned[c][k * 96 : (k + 1) * 96]
            dest[k % 2, 288:384] = dproj[k * 96 : (k + 1) * 96]
            small[6:7] = fc1b_ref[:, k * D : (k + 1) * D]
            small[7:8] = pltpu.roll(gq_sum, (D - k * 96) % D, 1)[0:1]
            small[8:9] = pltpu.roll(gv_sum, (D - k * 96) % D, 1)[0:1]
            for h in range(3):
                small[9 + h : 10 + h, 0:256] = table_rows[3 * k + h]
            dest[k % 2, D : D + SMALL] = small[...].astype(LOW)

    return pl.pallas_call(
        kernel,
        out_shape=(
            jax.ShapeDtypeStruct((2, D + SMALL, D), LOW),
            jax.ShapeDtypeStruct((2, D + SMALL, D), LOW),
        ),
        in_specs=[vmem()] * 12,
        out_specs=[vmem()] * 2,
        scratch_shapes=[
            pltpu.VMEM((3 * D, D), LOW),
            pltpu.VMEM((SMALL, D), F32),
        ],
        compiler_params=params(12),
        cost_estimate=cost(6e9, 2e7),
        name="attn_grads",
    )(grad, a, attn, gqkv, scores, small_mlp, fc1_bias_grad, *weights, norms)


def attn_input_grad(table, grad, hidden, gqkv, weights, norms, shifted, work):
    rows = hidden.shape[0]
    bins = rows // PAD
    chunk_slots = 6
    chunk = chunk_slots * PAD
    spare = bins if shifted else 2

    def kernel(
        table_ref, grad_ref, hidden_ref, gqkv_ref, w0, w1, w2, w3, norm_ref,
        out_ref, wqkv, wide, tmp, moved,
    ):
        stack_qkv((w0, w1, w2, w3), wqkv)
        gain = norm_ref[0:1]
        if shifted:
            for i in range(bins // chunk_slots):
                slots = slice(i * chunk_slots, (i + 1) * chunk_slots)
                ga = dot_nn(gqkv_ref[i * chunk : (i + 1) * chunk], wqkv[...])
                wide[slots] = ga.reshape(chunk_slots, PAD, D)
            move_windows(table_ref, wide, tmp, moved, True)

        for i in range(bins // chunk_slots):
            at = slice(i * chunk, (i + 1) * chunk)
            if shifted:
                ga = moved[i * chunk_slots : (i + 1) * chunk_slots].reshape(chunk, D)
            else:
                ga = dot_nn(gqkv_ref[at], wqkv[...])
            scaled, inverse = norm_rows(hidden_ref[at])
            out_ref[at] = grad_ref[at] + norm_back(ga, scaled, inverse, gain)

    return pl.pallas_call(
        kernel,
        out_shape=jax.ShapeDtypeStruct((rows, D), F32),
        in_specs=[smem()] + [vmem()] * 8,
        out_specs=vmem(),
        scratch_shapes=[pltpu.VMEM((3 * D, D), LOW)] + [pltpu.VMEM((spare, PAD, D), F32)] * 3,
        compiler_params=params(12),
        cost_estimate=cost(work, 1e7),
        name="attn_input_grad",
    )(table, grad, hidden, gqkv, *weights, norms)


def mlp_forward(mid, weights, fc1_bias, norms, layer):
    rows = mid.shape[0]
    chunk = 3 * PAD * 2
    steps = rows // chunk

    def kernel(
        mid_ref, w0, w1, w2, w3, fc1_bias_ref, norm_ref,
        out_ref, act_ref, slope_ref, fc1, fc2,
    ):
        stack_mlp((w0, w1, w2, w3), fc1, fc2)
        gain, shift, out_shift = norm_ref[0:1], norm_ref[1:2], norm_ref[2:3]

        def step(i, carry):
            at = pl.ds(pl.multiple_of(i * chunk, 16), chunk)
            rows_now = mid_ref[at]
            scaled, _ = norm_rows(rows_now)
            a = (scaled * gain + shift).astype(LOW)
            act, slope = gelu_parts(dot_nn(a, fc1[...]) + fc1_bias_ref[layer, 0:1])
            act = act.astype(LOW)
            act_ref[at] = act
            slope_ref[at] = slope.astype(LOW)
            out_ref[at] = rows_now + dot_nn(act, fc2[...]) + out_shift
            return carry

        lax.fori_loop(0, steps, step, 0, unroll=True)

    return pl.pallas_call(
        kernel,
        out_shape=(
            jax.ShapeDtypeStruct((rows, D), F32),
            jax.ShapeDtypeStruct((rows, FF), LOW),
            jax.ShapeDtypeStruct((rows, FF), LOW),
        ),
        in_specs=[vmem()] * 7,
        out_specs=[vmem()] * 3,
        scratch_shapes=[pltpu.VMEM((D, FF), LOW), pltpu.VMEM((FF, D), LOW)],
        compiler_params=params(14),
        cost_estimate=cost(7e9, 2e7),
        name="mlp_forward",
    )(mid, *weights, fc1_bias, norms)


def mlp_sums(gpre, a, act, low_grad, fc1, fc1_sums, grad_sums, norms, outs):
    keep_ref, send_ref, small_ref, bias_ref = outs
    gain, shift = norms[0:1], norms[1:2]
    dfc1 = dot_tn(a[...], gpre[...])
    dfc2 = dot_tn(low_grad[...], act[...])
    column = jnp.sum(dfc1 * fc1[...].astype(F32), axis=1, keepdims=True)
    match = jnp.broadcast_to(column, (D, 128)).T
    for k in range(4):
        dest = keep_ref if k < 2 else send_ref
        cols = slice(k * D, (k + 1) * D)
        dest[k % 2, 0:D] = dfc1[:, cols].astype(LOW)
        dest[k % 2, D : 2 * D] = dfc2[:, cols].astype(LOW)
    wide_sums = jnp.broadcast_to(fc1_sums, (16, FF))
    dshift = sum(dot_nt(part, fc1[...]) for part in split(wide_sums))[0:1]
    small_ref[0:1] = (match[0:1] - shift * dshift) / gain
    small_ref[1:2] = dshift
    small_ref[2:3] = grad_sums
    small_ref[3:8] = jnp.zeros((5, D), F32)
    bias_ref[...] = fc1_sums


def sums_shapes():
    return (
        jax.ShapeDtypeStruct((2, 2 * D, D), LOW),
        jax.ShapeDtypeStruct((2, 2 * D, D), LOW),
        jax.ShapeDtypeStruct((8, D), F32),
        jax.ShapeDtypeStruct((1, FF), F32),
    )


def mlp_backward(grad, mid, act, slope, weights, norms):
    rows = mid.shape[0]
    chunk = 6 * PAD
    steps = rows // chunk

    def kernel(
        grad_ref, mid_ref, act_ref, slope_ref, w0, w1, w2, w3, norm_ref,
        gpre_ref, keep_ref, send_ref, small_ref, bias_ref, fc1, fc2, low_grad, a_ref,
    ):
        stack_mlp((w0, w1, w2, w3), fc1, fc2)
        gain, shift = norm_ref[0:1], norm_ref[1:2]
        fc1_sums, grad_sums = jnp.zeros((1, FF), F32), jnp.zeros((1, D), F32)
        for i in range(steps):
            at = slice(i * chunk, (i + 1) * chunk)
            gz = grad_ref[at].astype(LOW)
            low_grad[at] = gz
            gpre = (dot_nt(gz, fc2[...]) * slope_ref[at].astype(F32)).astype(LOW)
            gpre_ref[at] = gpre
            scaled, _ = norm_rows(mid_ref[at])
            a_ref[at] = (scaled * gain + shift).astype(LOW)
            fc1_sums = fc1_sums + jnp.sum(gpre.astype(F32), axis=0, keepdims=True)
            grad_sums = grad_sums + jnp.sum(gz.astype(F32), axis=0, keepdims=True)
        outs = keep_ref, send_ref, small_ref, bias_ref
        mlp_sums(gpre_ref, a_ref, act_ref, low_grad, fc1, fc1_sums, grad_sums, norm_ref, outs)

    return pl.pallas_call(
        kernel,
        out_shape=(jax.ShapeDtypeStruct((rows, FF), LOW), *sums_shapes()),
        in_specs=[vmem()] * 9,
        out_specs=[vmem()] * 5,
        scratch_shapes=[
            pltpu.VMEM((D, FF), LOW),
            pltpu.VMEM((FF, D), LOW),
            pltpu.VMEM((rows, D), LOW),
            pltpu.VMEM((rows, D), LOW),
        ],
        compiler_params=params(18),
        cost_estimate=cost(7e9, 2e7),
        name="mlp_backward",
    )(grad, mid, act, slope, *weights, norms)


def mlp_turn(mid, grad, weights, fc1_bias, norms, layer):
    rows = mid.shape[0]
    chunk = 6 * PAD
    steps = rows // chunk

    def kernel(
        mid_ref, grad_ref, w0, w1, w2, w3, fc1_bias_ref, norm_ref,
        out_ref, gpre_ref, keep_ref, send_ref, small_ref, bias_ref,
        fc1, fc2, a_all, act_all, low_grad,
    ):
        stack_mlp((w0, w1, w2, w3), fc1, fc2)
        gain, shift, out_shift = norm_ref[0:1], norm_ref[1:2], norm_ref[2:3]

        def step(i, totals):
            at = pl.ds(pl.multiple_of(i * chunk, 16), chunk)
            rows_now = mid_ref[at]
            scaled, _ = norm_rows(rows_now)
            a = (scaled * gain + shift).astype(LOW)
            a_all[at] = a
            act, slope = gelu_parts(dot_nn(a, fc1[...]) + fc1_bias_ref[layer, 0:1])
            act = act.astype(LOW)
            act_all[at] = act
            out_ref[at] = rows_now + dot_nn(act, fc2[...]) + out_shift
            gz = grad_ref[at].astype(LOW)
            low_grad[at] = gz
            gpre = (dot_nt(gz, fc2[...]) * slope).astype(LOW)
            gpre_ref[at] = gpre
            return (
                totals[0] + jnp.sum(gz.astype(F32), axis=0, keepdims=True),
                totals[1] + jnp.sum(gpre.astype(F32), axis=0, keepdims=True),
            )

        zeros = jnp.zeros((1, D), F32), jnp.zeros((1, FF), F32)
        grad_sums, fc1_sums = lax.fori_loop(0, steps, step, zeros)
        outs = keep_ref, send_ref, small_ref, bias_ref
        mlp_sums(gpre_ref, a_all, act_all, low_grad, fc1, fc1_sums, grad_sums, norm_ref, outs)

    return pl.pallas_call(
        kernel,
        out_shape=(
            jax.ShapeDtypeStruct((rows, D), F32),
            jax.ShapeDtypeStruct((rows, FF), LOW),
            *sums_shapes(),
        ),
        in_specs=[vmem()] * 8,
        out_specs=[vmem()] * 6,
        scratch_shapes=[
            pltpu.VMEM((D, FF), LOW),
            pltpu.VMEM((FF, D), LOW),
            pltpu.VMEM((rows, D), LOW),
            pltpu.VMEM((rows, FF), LOW),
            pltpu.VMEM((rows, D), LOW),
        ],
        compiler_params=params(18),
        cost_estimate=cost(1.5e10, 4e7),
        name="mlp_turn",
    )(mid, grad, *weights, fc1_bias, norms)


def mlp_input_grad(grad, mid, gpre, weights, norms):
    rows = mid.shape[0]
    chunk = 6 * PAD

    def kernel(grad_ref, mid_ref, gpre_ref, w0, w1, w2, w3, norm_ref, out_ref, fc1):
        for k, piece in enumerate((w0, w1, w2, w3)):
            fc1[:, k * D : (k + 1) * D] = piece[0:D]
        gain = norm_ref[0:1]
        for i in range(rows // chunk):
            at = slice(i * chunk, (i + 1) * chunk)
            ga = dot_nt(gpre_ref[at], fc1[...])
            scaled, inverse = norm_rows(mid_ref[at])
            out_ref[at] = grad_ref[at] + norm_back(ga, scaled, inverse, gain)

    return pl.pallas_call(
        kernel,
        out_shape=jax.ShapeDtypeStruct((rows, D), F32),
        in_specs=[vmem()] * 8,
        out_specs=vmem(),
        scratch_shapes=[pltpu.VMEM((D, FF), LOW)],
        compiler_params=params(8),
        cost_estimate=cost(3e12, 1e7),
        name="mlp_input_grad",
    )(grad, mid, gpre, *weights, norms)


def small_outputs(rows):
    def kernel(rows_ref, gains_ref, shifts_ref, fc1_ref, qv_ref, table_ref):
        for l in range(LAYERS):
            now = rows_ref[l]
            for i, row in enumerate((0, 3)):
                gains_ref[l, i : i + 1] = now[row : row + 1]
            for i, row in enumerate((1, 4, 2, 5)):
                shifts_ref[l, i : i + 1] = now[row : row + 1]
            fc1_ref[l : l + 1] = now[6:7]
            qv_ref[l] = now[7:9, 0:96]
            turned = rows_ref[l, 8:SMALL, 0:256].T
            table_ref[l] = turned[0:169, 1:4]

    return pl.pallas_call(
        kernel,
        out_shape=(
            jax.ShapeDtypeStruct((LAYERS, 2, D), F32),
            jax.ShapeDtypeStruct((LAYERS, 4, D), F32),
            jax.ShapeDtypeStruct((LAYERS, D), F32),
            jax.ShapeDtypeStruct((LAYERS, 2, 96), F32),
            jax.ShapeDtypeStruct((LAYERS, 169, 3), F32),
        ),
        in_specs=[vmem()],
        out_specs=[vmem()] * 5,
        compiler_params=params(4),
        cost_estimate=cost(0, 1e6),
        name="small_outputs",
    )(rows)


def swap_core(value):
    return lax.ppermute(value, "head", [(i, i ^ 1) for i in range(4)])


def swap_chip(value):
    return lax.ppermute(value, "head", [(i, i ^ 2) for i in range(4)])


def swap_border(value):
    return lax.ppermute(value, "head", [(1, 2), (2, 1)])


def swap_dp(value, step, size):
    return lax.ppermute(value, "dp", [(i, i ^ step) for i in range(size)])


def tie(*values):
    return lax.optimization_barrier(values)


def pick(first, one, other):
    first = first > 0
    return jnp.where(first, one, other), jnp.where(first, other, one)


def dp_masks(order):
    size = lax.axis_size("dp")
    upper = [(2 << b) - 2 for b in range(1, size.bit_length() - 1)]
    if order == 1 and upper:
        return [upper[-1]] + upper[:-1] + [1]
    return [1] + (upper if order == 2 else upper[::-1])


def dp_start(parts, sides, order):
    half = parts[0].shape[0] // 2
    low = sum(p[:half].astype(F32) for p in parts)
    high = sum(p[half:].astype(F32) for p in parts)
    masks = dp_masks(order)
    kept, sent = pick(sides[order % 2], low, high)
    return kept, swap_dp(sent.astype(LOW), masks[0], lax.axis_size("dp"))


def dp_next(kept, other, order, stage):
    masks = dp_masks(order)
    value = (kept.astype(F32) + other.astype(F32)).astype(LOW)
    return value, swap_dp(value, (masks + masks[:1])[stage], lax.axis_size("dp"))


def dp_whole(value, other, stage):
    masks = dp_masks(2)
    value = (value.astype(F32) + other.astype(F32)).astype(LOW)
    return value, swap_dp(value, masks[stage], lax.axis_size("dp"))


def dp_join(value, other, sides, order):
    low, high = pick(sides[order % 2], value, other)
    return jnp.concatenate([low, high])


def body(
    tokens, outputs_grad, image_kind, qkv_weight, qv_bias, bias_table, proj_weight,
    fc1_weight, fc1_bias, fc2_weight, gains, shifts,
):
    own = tokens.shape[0] // PLACES
    bins = own + 2
    me = lax.axis_index("head").astype(jnp.int32)

    def border(value):
        edge = 4 * PLACES
        return swap_border(jnp.where(me == 1, value[-edge:], value[:edge]))

    turned = jnp.transpose(qkv_weight, (0, 2, 3, 1)).reshape(LAYERS, 288, D)

    def attn_pack(l):
        return jnp.concatenate([turned[l], proj_weight[l]], axis=0)

    def mlp_pack(l):
        return jnp.concatenate([fc1_weight[l], fc2_weight[l]], axis=0)

    def norm_pack(l, which, bias_row):
        rows = jnp.stack([gains[l, which], shifts[l, which], shifts[l, bias_row]])
        return jnp.pad(rows, ((0, 5), (0, 0)))

    partner = swap_core(tokens)
    rows = jnp.pad(jnp.transpose(bias_table, (0, 2, 1)).reshape(6, 169), ((0, 0), (0, D - 169)))
    small = jnp.concatenate([rows, qv_bias.reshape(1, D), fc1_bias])
    small = jnp.pad(small, ((0, SMALL - 9), (0, 0)))
    own_pack = [jnp.concatenate([attn_pack(0), *split(small)])]
    chip_pack = [swap_chip(own_pack[0])]
    edges, _ = tie(tokens, own_pack[0])
    halo = border(edges)
    place = lax.axis_index("dp")
    top = lax.axis_size("dp") // 2
    sides = [1 - (place & 1), (place < top).astype(jnp.int32)]
    first = jnp.broadcast_to(jnp.stack(sides).astype(jnp.int32)[:, None], (2, D))
    table = make_plan(image_kind, me, own, bins)
    mlp_first = mlp_pack(0)
    table, first, chip_pack[0], partner, mlp_first = tie(
        table, first, chip_pack[0], partner, mlp_first
    )
    sides = [first[0:1], first[1:2]]
    hidden = gather_slots(table, tokens, partner, halo, bins)

    def gathered(i):
        p, c = own_pack[i], chip_pack[i]
        return p, c, swap_core(p), swap_core(c)

    pack, halo, _ = tie(mlp_first, halo, chip_pack[0])
    own_pack.append(pack)
    chip_pack.append(swap_chip(pack))
    first_weights = gathered(0)
    bias, qkv_bias, fc1_all = spread_smalls(first_weights)

    saved, weights = [], []
    last = LAYERS - 1
    for l in range(LAYERS):
        norms, mlp_norms = norm_pack(l, 0, 2), norm_pack(l, 1, 3)
        weights.append(first_weights if l == 0 else gathered(2 * l))
        mid, a, qkv, probs, attn = attn_forward(
            table, hidden, weights[2 * l], qkv_bias, bias, norms, l
        )
        mid, chip_pack[2 * l + 1] = tie(mid, chip_pack[2 * l + 1])
        weights.append(gathered(2 * l + 1))
        if l == last:
            saved.append((hidden, mid, a, qkv, probs, attn, norms, mlp_norms))
            break
        pack, outputs_grad, mid = tie(attn_pack(1), outputs_grad, mid)
        grad_partner, grad_halo = swap_core(outputs_grad), border(outputs_grad)
        own_pack.append(pack)
        chip_pack.append(swap_chip(pack))
        out, act, slope = mlp_forward(mid, weights[2 * l + 1], fc1_all, mlp_norms, l)
        pack, out, chip_pack[2], grad_partner, grad_halo = tie(
            mlp_pack(1), out, chip_pack[2], grad_partner, grad_halo
        )
        own_pack.append(pack)
        chip_pack.append(swap_chip(pack))
        saved.append((hidden, mid, a, qkv, probs, attn, norms, mlp_norms, act, slope))
        hidden = out
    grad = gather_slots(table, outputs_grad, grad_partner, grad_halo, bins)

    def give_back(value):
        slots = value.reshape(bins, PAD, D)
        return slots, swap_core(slots), swap_border(border_slots(table, slots, 0))

    def mlp_back(l, grad):
        return mlp_backward(
            grad, saved[l][1], saved[l][8], saved[l][9], weights[2 * l + 1], saved[l][7]
        )

    def mlp_input(l, grad, gpre):
        return mlp_input_grad(grad, saved[l][1], gpre, weights[2 * l + 1], saved[l][7])

    def attn_back(l, grad):
        return attn_backward(table, grad, saved[l][3], saved[l][4], weights[2 * l], l % 2 == 1)

    def attn_sums(l, grad, gqkv, scores, small_mlp, fc1_bias_grad):
        return attn_grads(
            grad, saved[l][2], saved[l][5], gqkv, scores, small_mlp, fc1_bias_grad,
            weights[2 * l], saved[l][6],
        )

    def attn_input(l, grad, gqkv):
        work = 6e9 if l == last else 3e12
        return attn_input_grad(
            table, grad, saved[l][0], gqkv, weights[2 * l], saved[l][6], l % 2 == 1, work
        )

    def core_sum(keep, other):
        return [(keep[i].astype(F32) + other[i].astype(F32)).astype(LOW) for i in range(2)]

    out, gpre, keep_a, send_a, small_mlp, fc1_bias_grad = mlp_turn(
        saved[last][1], grad, weights[2 * last + 1], fc1_all, saved[last][7], last
    )
    core_a = swap_core(send_a)
    grad = mlp_input(1, grad, gpre)
    grad, core_a = tie(grad, core_a)
    half_a, out_a = core_sum(keep_a, core_a)
    grad, out_a = tie(grad, out_a)
    chip_a = swap_chip(out_a)
    gqkv, scores = attn_back(1, grad)
    grad_after = attn_input(1, grad, gqkv)
    gqkv, _ = tie(gqkv, grad_after)
    keep_b, send_b = attn_sums(1, grad, gqkv, scores, small_mlp, fc1_bias_grad)
    grad, send_b, chip_a = tie(grad_after, send_b, chip_a)
    core_b = swap_core(send_b)
    state_a = dp_start((half_a, chip_a), sides, 2)
    half_b, out_b = core_sum(keep_b, core_b)
    grad, out_b = tie(grad, out_b)
    chip_b = swap_chip(out_b)
    gpre, keep_c, send_c, small_mlp, fc1_bias_grad = mlp_back(0, grad)
    gpre, send_c, state_a, chip_b = tie(gpre, send_c, state_a, chip_b)
    core_c = swap_core(send_c)
    state_a = dp_next(*state_a, 2, 1)
    grad = mlp_input(0, grad, gpre)
    grad, core_c = tie(grad, core_c)
    state_b = dp_start((half_b, chip_b), sides, 2)
    half_c, out_c = core_sum(keep_c, core_c)
    grad, out_c = tie(grad, out_c)
    chip_c = swap_chip(out_c)
    gqkv, scores = attn_back(0, grad)
    gqkv, state_a, state_b = tie(gqkv, state_a, state_b)
    state_a = dp_next(*state_a, 2, 2)
    state_b = dp_next(*state_b, 2, 1)
    keep_d, send_d = attn_sums(0, grad, gqkv, scores, small_mlp, fc1_bias_grad)
    core_d = swap_core(send_d)
    out, chip_c, _ = tie(out, chip_c, send_d)
    state_c = dp_start((half_c, chip_c), sides, 2)
    out_slots = out.reshape(bins, PAD, D)
    out_edge, core_d = tie(border_slots(table, out_slots, 3e12), core_d)
    half_d, out_d = core_sum(keep_d, core_d)
    chip_d = swap_chip(out_d)
    gqkv, out_slots, out_edge, _ = tie(gqkv, out_slots, out_edge, out_d)
    grad = attn_input(0, grad, gqkv)
    output_parts = out_slots, swap_core(out_slots), swap_border(out_edge)
    chip_d, state_a, state_b, state_c = tie(chip_d, state_a, state_b, state_c)
    state_d = dp_whole(half_d, chip_d, 0)
    state_c = dp_next(*state_c, 2, 1)
    state_b = dp_next(*state_b, 2, 2)
    tokens_parts = give_back(grad)
    state_d, state_c, state_b = tie(state_d, state_c, state_b)
    state_d = dp_whole(*state_d, 1)
    state_c = dp_next(*state_c, 2, 2)
    state_a = dp_next(*state_a, 2, 3)
    state_b = dp_next(*state_b, 2, 3)
    output = return_slots(table, *output_parts, own)
    state_d, state_c, state_a, state_b = tie(state_d, state_c, state_a, state_b)
    state_d = dp_whole(*state_d, 2)
    state_c = dp_next(*state_c, 2, 3)
    tokens_grad = return_slots(table, *tokens_parts, own)
    total_a = dp_join(*state_a, sides, 2)
    total_b = dp_join(*state_b, sides, 2).astype(F32)
    state_d, state_c, output, tokens_grad = tie(state_d, state_c, output, tokens_grad)
    total_c = dp_join(*state_c, sides, 2)
    mlp_all = jnp.stack([total_c, total_a]).astype(F32)
    fc1_out = mlp_all[:, :D]
    fc2_out = mlp_all[:, D:].transpose(0, 2, 1)
    total_d = state_d[0].astype(F32) + state_d[1].astype(F32)

    attn_all = jnp.stack([total_d, total_b])
    gains_out, shifts_out, fc1_bias_out, qv_out, table_out = small_outputs(attn_all[:, D:])
    qkv_out = attn_all[:, 0:288].reshape(LAYERS, 3, 96, D).transpose(0, 3, 1, 2)
    proj_out = attn_all[:, 288:384]
    return (
        output, tokens_grad, qkv_out, qv_out, table_out, proj_out, fc1_out, fc1_bias_out,
        fc2_out, gains_out, shifts_out,
    )


def solution(mesh):
    rows = P(("dp", "head"), None)
    placed = (
        rows,
        rows,
        P("dp", None),
        P(None, None, None, "head"),
        P(None, None, "head"),
        P(None, None, "head"),
        P(None, "head", None),
        P(None, None, "head"),
        P(None, "head"),
        P(None, "head", None),
        P(),
        P(),
    )
    return jax.shard_map(
        body,
        mesh=mesh,
        in_specs=placed,
        out_specs=(
            rows,
            rows,
            P(None, None, None, "head"),
            P(None, None, "head"),
            P(None, None, "head"),
            P(None, "head", None),
            P(None, None, "head"),
            P(None, "head"),
            P(None, "head", None),
            P(),
            P(),
        ),
        check_vma=False,
    )
```

```python
import jax
import jax.numpy as jnp
from jax import lax
from jax.experimental import pallas as pl
from jax.experimental.pallas import tpu as pltpu
from jax.sharding import PartitionSpec as P

D = 384
FF = 1536
LAYERS = 2
PLACES = 49
PAD = 56
WIDE = 64
QUADS = 3
HEAD_DIM = 32
SCORE_SCALE = HEAD_DIM**-0.5
LN_EPS = 1e-05
LOW = jnp.bfloat16
F32 = jnp.float32
MIB = 1024 * 1024
SMALL = 16

SRC, SIDE, WROW, WCOL, FIRST, RET, SEND = 0, 24, 48, 72, 96, 120, 140
TABLE = 144


def vmem():
    return pl.BlockSpec(memory_space=pltpu.VMEM)


def smem():
    return pl.BlockSpec(memory_space=pltpu.SMEM)


def anywhere():
    return pl.BlockSpec(memory_space=pl.ANY)


def params(limit):
    return pltpu.CompilerParams(vmem_limit_bytes=limit * MIB)


def cost(flops, size):
    return pl.CostEstimate(flops=int(flops * 0.02), bytes_accessed=int(size * 0.02), transcendentals=0)


def dot_nn(a, b):
    return lax.dot_general(a, b, (((1,), (0,)), ((), ())), preferred_element_type=F32)


def dot_nt(a, b):
    return lax.dot_general(a, b, (((1,), (1,)), ((), ())), preferred_element_type=F32)


def dot_tn(a, b):
    return lax.dot_general(a, b, (((0,), (0,)), ((), ())), preferred_element_type=F32)


def plan_kernel(own, bins, kind_ref, me_ref, out_ref, load_ref):
    me = me_ref[0]
    half = 2 * own
    for i in range(TABLE):
        out_ref[i] = -1 if i < bins or RET <= i < RET + own else 0
    for i in range(bins):
        out_ref[SIDE + i] = 1
        out_ref[FIRST + i] = i
    for i in range(4):
        load_ref[i] = 0

    def place(start, count, side, bin_id):
        base = load_ref[bin_id]
        load_ref[bin_id] = base + count

        def step(k, carry):
            slot = start + k
            owner = slot // own
            inner = slot - owner * own
            local = base + k
            mine = bin_id == me
            halo = jnp.where(me == 1, slot - half, slot - half + 4)
            code = jnp.where(
                owner == me, inner, jnp.where(owner == (me ^ 1), own + inner, 2 * own + halo)
            )

            @pl.when(mine)
            def _():
                wrow = k // side
                out_ref[SRC + local] = code
                out_ref[SIDE + local] = side
                out_ref[WROW + local] = wrow
                out_ref[WCOL + local] = k - wrow * side
                out_ref[FIRST + local] = base

            @pl.when(owner == me)
            def _():
                back = jnp.where(me == 2, slot - half, k)
                out_ref[RET + inner] = jnp.where(
                    mine, local, jnp.where(bin_id == (me ^ 1), bins + local, 2 * bins + back)
                )

            return carry

        lax.fori_loop(0, count, step, 0)

    for turn in range(3):

        def visit(i, start, turn=turn):
            kind = kind_ref[0, i]
            count = jnp.where(kind == 2, 9, jnp.where(kind == 1, 4, 0))
            side = jnp.where(kind == 2, 3, 2)
            cut = half - start
            across = (cut > 0) & (cut < count)
            second = (start >= half) | (across & (cut < count - cut))
            chip = jnp.where(second, 1, 0)
            left, right = load_ref[2 * chip], load_ref[2 * chip + 1]
            emptier = 2 * chip + jnp.where(left <= right, 0, 1)
            if turn == 0:
                chosen, bin_id = across, 1 + chip
            else:
                chosen, bin_id = (kind == 3 - turn) & jnp.logical_not(across), emptier

            @pl.when(chosen)
            def _():
                place(start, count, side, bin_id)
                if turn == 0:
                    out_ref[SEND] = jnp.where((me == 1) & (chip == 0), cut, 0)

            return start + count

        lax.fori_loop(0, kind_ref.shape[1], visit, jnp.int32(0))


def gather_kernel(bins, table_ref, refs, out_ref, spread_ref):
    spread_ref[...] = jnp.zeros(spread_ref.shape, F32)
    at = 0
    for ref in refs:
        for s in range(ref.shape[0] // PLACES):
            spread_ref[at, 0:PLACES] = ref[s * PLACES : (s + 1) * PLACES].astype(F32)
            at += 1

    def step(j, carry):
        src = table_ref[SRC + j]

        @pl.when(src < 0)
        def _():
            out_ref[j] = jnp.zeros((PAD, D), F32)

        @pl.when(src >= 0)
        def _():
            out_ref[j] = spread_ref[src]

        return carry

    lax.fori_loop(0, bins, step, 0)


def make_plan(image_kind, me, own, bins):
    def kernel(kind_ref, me_ref, table_ref, load_ref):
        plan_kernel(own, bins, kind_ref, me_ref, table_ref, load_ref)

    return pl.pallas_call(
        kernel,
        out_shape=jax.ShapeDtypeStruct((TABLE,), jnp.int32),
        in_specs=[smem(), smem()],
        out_specs=smem(),
        scratch_shapes=[pltpu.SMEM((4,), jnp.int32)],
        compiler_params=params(1),
        cost_estimate=cost(0, 1.5e7),
        name="plan",
    )(image_kind, me.reshape(1))


def gather_slots(table, mine, partner, halo, bins):
    own = mine.shape[0] // PLACES

    def kernel(table_ref, *refs):
        gather_kernel(bins, table_ref, refs[:3], refs[3], refs[4])

    out = pl.pallas_call(
        kernel,
        out_shape=jax.ShapeDtypeStruct((bins, PAD, D), F32),
        in_specs=[smem()] + [vmem()] * 3,
        out_specs=vmem(),
        scratch_shapes=[pltpu.VMEM((2 * own + 4, PAD, D), F32)],
        compiler_params=params(8),
        cost_estimate=cost(0, 8e6),
        name="gather_slots",
    )(table, mine, partner, halo)
    return out.reshape(bins * PAD, D)


def border_slots(table, slots, work):
    def kernel(table_ref, slots_ref, out_ref):
        start = table_ref[SEND]
        for j in range(4):
            out_ref[j] = slots_ref[start + j]

    return pl.pallas_call(
        kernel,
        out_shape=jax.ShapeDtypeStruct((4,) + slots.shape[1:], F32),
        in_specs=[smem(), vmem()],
        out_specs=vmem(),
        compiler_params=params(4),
        cost_estimate=cost(work, 1e6),
        name="border_slots",
    )(table, slots)


def return_slots(table, mine, partner, halo, own):
    bins = mine.shape[0]

    def kernel(table_ref, mine_ref, partner_ref, halo_ref, out_ref):
        for s in range(own):
            src = table_ref[RET + s]
            rows = pl.ds(s * PLACES, PLACES)

            @pl.when(src < 0)
            def _():
                out_ref[rows] = jnp.zeros((PLACES, D), F32)

            @pl.when((src >= 0) & (src < bins))
            def _():
                out_ref[rows] = mine_ref[src, 0:PLACES]

            @pl.when((src >= bins) & (src < 2 * bins))
            def _():
                out_ref[rows] = partner_ref[src - bins, 0:PLACES]

            @pl.when(src >= 2 * bins)
            def _():
                out_ref[rows] = halo_ref[src - 2 * bins, 0:PLACES]

    return pl.pallas_call(
        kernel,
        out_shape=jax.ShapeDtypeStruct((own * PLACES, D), F32),
        in_specs=[smem(), vmem(), vmem(), vmem()],
        out_specs=vmem(),
        compiler_params=params(8),
        cost_estimate=cost(0, 8e6),
        name="return_slots",
    )(table, mine, partner, halo)


def norm_rows(rows):
    average = jnp.mean(rows, axis=-1, keepdims=True)
    centred = rows - average
    inverse = lax.rsqrt(jnp.mean(centred * centred, axis=-1, keepdims=True) + LN_EPS)
    return centred * inverse, inverse


def norm_back(incoming, scaled, inverse, gain):
    weighted = incoming * gain
    return inverse * (
        weighted
        - jnp.mean(weighted, axis=-1, keepdims=True)
        - scaled * jnp.mean(weighted * scaled, axis=-1, keepdims=True)
    )


def gelu_parts(x):
    t = 1.0 / (1.0 + 0.23164189 * jnp.abs(x))
    bell = jnp.exp2(x * x * -0.7213475204444817)
    poly = t * (
        0.127414796 + t * (-0.142248368 + t * (0.7107068705 + t * (-0.7265760135 + t * 0.5307027145)))
    )
    tail = poly * bell
    phi = jnp.where(x >= 0, 1.0 - tail, tail)
    return x * phi, phi + x * bell * 0.3989422804014327


def place_parts(shape, dim):
    place = lax.broadcasted_iota(jnp.int32, shape, dim)
    row = (place * 37) >> 8
    return place, row, place - 7 * row


def neighbour(table_ref, w, back, down):
    side, wrow, wcol = table_ref[SIDE + w], table_ref[WROW + w], table_ref[WCOL + w]
    at = wrow if down else wcol
    if back:
        other = jnp.where(at == 0, side - 1, at - 1)
    else:
        other = jnp.where(at == side - 1, 0, at + 1)
    if down:
        return table_ref[FIRST + w] + other * side + wcol
    return table_ref[FIRST + w] + wrow * side + other


def move_windows(table_ref, src, tmp, out, back):
    bins = src.shape[0]
    tmp[...] = jnp.zeros(tmp.shape, F32)
    out[...] = jnp.zeros(out.shape, F32)

    def rows(w, carry):
        other = neighbour(table_ref, w, back, True)
        if back:
            tmp[w, 21:49] = src[w, 0:28]
            tmp[w, 0:21] = src[other, 28:49]
        else:
            tmp[w, 0:28] = src[w, 21:49]
            tmp[w, 28:49] = src[other, 0:21]
        return carry

    lax.fori_loop(0, bins, rows, 0, unroll=2)
    _, _, col = place_parts((PAD, 1), 0)

    def cols(w, carry):
        other = neighbour(table_ref, w, back, False)
        if back:
            out[w, 0:49] = tmp[other, 4:53]
            out[w, 3:49] = jnp.where(col[3:49] >= 3, tmp[w, 0:46], out[w, 3:49])
        else:
            out[w, 0:49] = tmp[w, 3:52]
            out[w, 4:49] = jnp.where(col[4:49] < 4, out[w, 4:49], tmp[other, 0:45])
        return carry

    lax.fori_loop(0, bins, cols, 0, unroll=2)


def head_marks():
    lane = lax.broadcasted_iota(jnp.int32, (WIDE, 128), 1) // HEAD_DIM
    return [jnp.where(lane == h, 1.0, 0.0).astype(LOW) for h in range(4)]


def spread(block, marks):
    return jnp.concatenate([block * mark for mark in marks], axis=0)


def fold(product, marks):
    total = None
    for h, mark in enumerate(marks):
        part = product[h * WIDE : (h + 1) * WIDE] * mark.astype(F32)
        total = part if total is None else total + part
    return total


def spread_pair(block, marks):
    return jnp.concatenate([spread(block[0:WIDE], marks), spread(block[WIDE:], marks)], axis=1)


def diagonal(block):
    zero = jnp.zeros((WIDE, 128), block.dtype)
    top = jnp.concatenate([block[0:WIDE], zero], axis=1)
    return jnp.concatenate([top, jnp.concatenate([zero, block[WIDE:]], axis=1)], axis=0)


def by_head(values):
    return values.reshape(4, WIDE, 128)


def pad_rows(rows):
    return jnp.concatenate([rows, jnp.zeros((WIDE - PAD, rows.shape[1]), rows.dtype)], axis=0)


def split(values):
    high = values.astype(LOW)
    return high, (values - high.astype(F32)).astype(LOW)


def marks_where(rows, cols, test):
    row = lax.broadcasted_iota(jnp.int32, (rows, cols), 0)
    col = lax.broadcasted_iota(jnp.int32, (rows, cols), 1)
    return jnp.where(test(row, col), 1.0, 0.0).astype(LOW)


def far(place):
    row = (place * 37) >> 8
    return 13 * row + (place - 7 * row)


def spread_smalls(smalls):
    heads = LAYERS * 12

    def kernel(p0, p1, p2, p3, out_ref, qkv_ref, fc1_ref, table_ref, small_ref):
        quarters = []
        for k, ref in enumerate((p0, p1, p2, p3)):
            high, low = ref[D : D + SMALL], ref[D + SMALL : D + 2 * SMALL]
            small_ref[k] = high.astype(F32) + low.astype(F32)
            quarters.append(small_ref.at[k])
        for k, ref in enumerate(quarters):
            for l in range(LAYERS):
                at = l * 12 + k * 3
                table_ref[at : at + 3] = ref[l * 3 : l * 3 + 3, 0:256]
        lane = lax.broadcasted_iota(jnp.int32, (8, D), 1)
        for l in range(LAYERS):
            for c in range(3):
                total = jnp.zeros((8, D), F32)
                for k, ref in enumerate(quarters):
                    if c != 1:
                        row = jnp.broadcast_to(ref[6:7], (8, D))
                        row = pltpu.roll(row, (k * 96 - l * 192 - (c // 2) * 96) % D, 1)
                        own_lanes = (lane >= k * 96) & (lane < k * 96 + 96)
                        total = total + jnp.where(own_lanes, row, 0.0)
                qkv_ref[l, :, c * D : (c + 1) * D] = total
            for k, ref in enumerate(quarters):
                row = jnp.broadcast_to(ref[7 + l : 8 + l], (8, D))
                fc1_ref[l, :, k * D : (k + 1) * D] = row
        to_lane = marks_where(128, 128, lambda r, c: (far(c & 63) == r) & ((c & 63) < PLACES))
        to_row = marks_where(WIDE, 96, lambda r, c: (far(r) == c) & (r < PLACES))
        place = lax.broadcasted_iota(jnp.int32, (WIDE, 128), 0)
        empty = jnp.where(place < PLACES, 0.0, -1e30)
        turned = pltpu.roll(table_ref[...], 172, 1)
        skewed = []
        for n in range(heads):
            row = jnp.broadcast_to(turned[n : n + 1], (96, 256))
            skewed.append(pltpu.roll(row, 0, 1, stride=1, stride_axis=0)[:, 0:128])
        skewed = jnp.concatenate(skewed, axis=1)
        total = None
        for part in split(skewed):
            rows = dot_nn(to_row, part).astype(LOW)
            rows = jnp.concatenate([rows[:, n * 128 : (n + 1) * 128] for n in range(heads)], axis=0)
            part = dot_nn(rows, to_lane)
            total = part if total is None else total + part
        for n in range(heads):
            l, t, h = n // 12, n % 12 // 4, n % 4
            out_ref[l, t, h * WIDE : (h + 1) * WIDE] = total[n * WIDE : (n + 1) * WIDE] + empty

    return pl.pallas_call(
        kernel,
        out_shape=(
            jax.ShapeDtypeStruct((LAYERS, QUADS, 4 * WIDE, 128), F32),
            jax.ShapeDtypeStruct((LAYERS, 8, 3 * D), F32),
            jax.ShapeDtypeStruct((LAYERS, 8, FF), F32),
        ),
        in_specs=[vmem()] * 4,
        out_specs=[vmem()] * 3,
        scratch_shapes=[pltpu.VMEM((heads, 256), F32), pltpu.VMEM((4, SMALL, D), F32)],
        compiler_params=params(6),
        cost_estimate=cost(0, 1e7),
        name="spread_smalls",
    )(*smalls)


def scores_to_table(scores_ref):
    to_far = marks_where(128, 128, lambda r, c: (far(r & 63) == c) & ((r & 63) < PLACES))
    to_row = marks_where(96, WIDE, lambda r, c: (84 - far(c) == r) & (c < PLACES))
    wide = None
    for part in split(scores_ref[...].reshape(12 * WIDE, 128)):
        part = dot_nn(part, to_far)
        wide = part if wide is None else wide + part
    wide = jnp.concatenate([wide[h * WIDE : (h + 1) * WIDE] for h in range(12)], axis=1)
    rows = None
    for part in split(wide):
        part = dot_nn(to_row, part)
        rows = part if rows is None else rows + part
    out = []
    for h in range(12):
        one = rows[:, h * 128 : (h + 1) * 128]
        one = jnp.concatenate([one, jnp.zeros_like(one)], axis=1)
        one = pltpu.roll(one, 0, 1, stride=1, stride_axis=0)
        out.append(jnp.sum(one, axis=0, keepdims=True))
    return out


def stack_qkv(pieces, out_ref):
    for k, piece in enumerate(pieces):
        for c in range(3):
            out_ref[c * D + k * 96 : c * D + (k + 1) * 96] = piece[c * 96 : (c + 1) * 96]


def stack_proj(pieces, out_ref):
    for k, piece in enumerate(pieces):
        out_ref[k * 96 : (k + 1) * 96] = piece[288:384]


def stack_mlp(pieces, fc1_ref, fc2_ref):
    for k, piece in enumerate(pieces):
        fc1_ref[:, k * D : (k + 1) * D] = piece[0:D]
        fc2_ref[k * D : (k + 1) * D] = piece[D : 2 * D]


def attn_forward(table, hidden, weights, qv_bias, bias, norms, layer):
    shifted = layer % 2 == 1
    rows = hidden.shape[0]
    bins = rows // PAD
    chunk_slots = 6
    chunk = chunk_slots * PAD
    spare = bins if shifted else 2

    def kernel(
        table_ref, hidden_ref, w0, w1, w2, w3, qv_ref, bias_ref, norm_ref,
        mid_ref, a_ref, qkv_ref, p_ref, attn_ref,
        wqkv, wproj, wide, tmp, moved,
    ):
        pieces = (w0, w1, w2, w3)
        stack_qkv(pieces, wqkv)
        stack_proj(pieces, wproj)
        gain, shift, proj_shift = norm_ref[0:1], norm_ref[1:2], norm_ref[2:3]
        marks = head_marks()
        def norm_step(i, carry):
            at = pl.ds(pl.multiple_of(i * chunk, 16), chunk)
            scaled, _ = norm_rows(hidden_ref[at])
            normed = scaled * gain + shift
            if shifted:
                slots = pl.ds(i * chunk_slots, chunk_slots)
                wide[slots] = normed.reshape(chunk_slots, PAD, D)
            else:
                a_ref[at] = normed.astype(LOW)
            return carry

        lax.fori_loop(0, bins // chunk_slots, norm_step, 0)
        if shifted:
            move_windows(table_ref, wide, tmp, moved, False)
            a_ref[...] = moved[...].reshape(rows, D).astype(LOW)

        def qkv_step(i, carry):
            at = pl.ds(pl.multiple_of(i * chunk, 16), chunk)
            project = dot_nt(a_ref[at], wqkv[...]) + qv_ref[layer, 0:1]
            for j in range(chunk_slots):
                block = project[j * PAD : (j + 1) * PAD]
                at = pl.ds((j % 2) * WIDE, WIDE)
                qkv_ref[i * (chunk_slots // 2) + j // 2, at] = pad_rows(block).astype(LOW)
            return carry

        lax.fori_loop(0, bins // chunk_slots, qkv_step, 0)

        if shifted:
            _, qrow, qcol = place_parts((WIDE, 1), 0)
            lane = lax.broadcasted_iota(jnp.int32, (1, 128), 1)
            second = lane >= WIDE
            pplace = jnp.where(second, lane - WIDE, lane)
            prow = (pplace * 37) >> 8
            pcol = pplace - 7 * prow
            pband = 1 + (prow >= 4).astype(jnp.int32), 1 + (pcol >= 4).astype(jnp.int32)
            qband = 1 + (qrow >= 4).astype(jnp.int32), 1 + (qcol >= 4).astype(jnp.int32)

        def window(j, carry):
            if shifted:
                low = []
                for w in (2 * j, 2 * j + 1):
                    side = table_ref[SIDE + w]
                    low.append(
                        (
                            jnp.where(table_ref[WROW + w] == side - 1, 3, 0),
                            jnp.where(table_ref[WCOL + w] == side - 1, 1, 0),
                        )
                    )
                low_row = jnp.where(second, low[1][0], low[0][0])
                low_col = jnp.where(second, low[1][1], low[0][1])
                pregion = low_row * pband[0] + low_col * pband[1]
                qregion = low_row * qband[0] + low_col * qband[1]
                mask = jnp.where(pregion != qregion, -100.0, 0.0)[None]
            scores, probs = [], []
            for t in range(QUADS):
                q = qkv_ref[j, :, t * 128 : (t + 1) * 128]
                k = qkv_ref[j, :, D + t * 128 : D + (t + 1) * 128]
                scores.append(dot_nt(spread_pair(k, marks), diagonal(q)))
            for t in range(QUADS):
                now = by_head(scores[t] * SCORE_SCALE + bias_ref[layer, t])
                if shifted:
                    now = now + mask
                exponent = jnp.exp(now - jnp.max(now, axis=1, keepdims=True))
                total = jnp.sum(exponent, axis=1, keepdims=True)
                probs.append((exponent * (1.0 / total)).reshape(4 * WIDE, 128).astype(LOW))
                p_ref[j, t] = probs[t]
            for t in range(QUADS):
                cols = slice(t * 128, (t + 1) * 128)
                v = qkv_ref[j, :, 2 * D + t * 128 : 2 * D + (t + 1) * 128]
                both = dot_tn(probs[t], spread_pair(v, marks))
                wide[2 * j, :, cols] = both[0:PAD, 0:128]
                wide[2 * j + 1, :, cols] = both[WIDE : WIDE + PAD, 128:256]
            return carry

        lax.fori_loop(0, bins // 2, window, 0, unroll=9)
        if shifted:
            move_windows(table_ref, wide, tmp, moved, True)
            attn_ref[...] = moved[...].reshape(rows, D).astype(LOW)
        else:
            attn_ref[...] = wide[...].reshape(rows, D).astype(LOW)

        def proj_step(i, carry):
            at = pl.ds(pl.multiple_of(i * chunk, 16), chunk)
            mid_ref[at] = hidden_ref[at] + dot_nn(attn_ref[at], wproj[...]) + proj_shift
            return carry

        lax.fori_loop(0, bins // chunk_slots, proj_step, 0)

    return pl.pallas_call(
        kernel,
        out_shape=(
            jax.ShapeDtypeStruct((rows, D), F32),
            jax.ShapeDtypeStruct((rows, D), LOW),
            jax.ShapeDtypeStruct((bins // 2, 2 * WIDE, 3 * D), LOW),
            jax.ShapeDtypeStruct((bins // 2, QUADS, 4 * WIDE, 128), LOW),
            jax.ShapeDtypeStruct((rows, D), LOW),
        ),
        in_specs=[smem()] + [vmem()] * 8,
        out_specs=[vmem()] * 5,
        scratch_shapes=[
            pltpu.VMEM((3 * D, D), LOW),
            pltpu.VMEM((D, D), LOW),
            pltpu.VMEM((bins, PAD, D), F32),
            pltpu.VMEM((spare, PAD, D), F32),
            pltpu.VMEM((spare, PAD, D), F32),
        ],
        compiler_params=params(11),
        cost_estimate=cost(1e10, 2e7),
        name="attn_forward",
    )(table, hidden, *weights, qv_bias, bias, norms)


def attn_backward(table, grad, qkv, probs, weights, shifted):
    rows = grad.shape[0]
    bins = rows // PAD
    chunk_slots = 6
    chunk = chunk_slots * PAD
    spare = bins if shifted else 2

    def kernel(
        table_ref, grad_ref, qkv_ref, p_ref, w0, w1, w2, w3,
        gqkv_ref, scores_ref, wproj, wide_attn, wide, tmp, moved,
    ):
        stack_proj((w0, w1, w2, w3), wproj)
        marks = head_marks()
        steps = bins // chunk_slots
        def keep_windows(i, block_rows):
            for j in range(chunk_slots):
                block = block_rows[j * PAD : (j + 1) * PAD]
                dest = pl.ds((j % 2) * WIDE, WIDE)
                wide_attn[i * (chunk_slots // 2) + j // 2, dest] = pad_rows(block).astype(LOW)

        def proj_step(i, carry):
            at = pl.ds(pl.multiple_of(i * chunk, 16), chunk)
            gattn = dot_nt(grad_ref[at].astype(LOW), wproj[...])
            if shifted:
                slots = pl.ds(i * chunk_slots, chunk_slots)
                wide[slots] = gattn.reshape(chunk_slots, PAD, D)
            else:
                keep_windows(i, gattn)
            return carry

        lax.fori_loop(0, steps, proj_step, 0)
        if shifted:
            move_windows(table_ref, wide, tmp, moved, False)

            def move_step(i, carry):
                slots = pl.ds(i * chunk_slots, chunk_slots)
                keep_windows(i, moved[slots].reshape(chunk, D))
                return carry

            lax.fori_loop(0, steps, move_step, 0)

        scores_ref[...] = jnp.zeros((QUADS, 4 * WIDE, 128), F32)

        def window(j, carry):
            at = pl.ds(pl.multiple_of(j * 2 * PAD, 16), 2 * PAD)

            def keep(c, t, left, right):
                cols = slice(c * D + t * 128, c * D + (t + 1) * 128)
                gqkv_ref[at, cols] = jnp.concatenate([left, right], axis=0).astype(LOW)

            go, gp, gv, low_ds, gq, gk = [], [], [], [], [], []
            for t in range(QUADS):
                v = qkv_ref[j, :, 2 * D + t * 128 : 2 * D + (t + 1) * 128]
                go.append(diagonal(wide_attn[j, :, t * 128 : (t + 1) * 128]))
                gp.append(dot_nt(spread_pair(v, marks), go[t]))
            for t in range(QUADS):
                gv.append(dot_nn(p_ref[j, t], go[t]))
            for t in range(QUADS):
                p = by_head(p_ref[j, t].astype(F32))
                now = by_head(gp[t])
                ds = p * (now - jnp.sum(now * p, axis=1, keepdims=True))
                low_ds.append(ds.reshape(4 * WIDE, 128).astype(LOW))
                scores_ref[t] += low_ds[t].astype(F32)
            for t in range(QUADS):
                q = qkv_ref[j, :, t * 128 : (t + 1) * 128]
                k = qkv_ref[j, :, D + t * 128 : D + (t + 1) * 128]
                gk.append(dot_nn(low_ds[t], diagonal(q)))
                gq.append(dot_tn(low_ds[t], spread_pair(k, marks)))
            for t in range(QUADS):
                left, right = slice(0, 128), slice(128, 256)
                keep(2, t, fold(gv[t][:, left], marks)[0:PAD], fold(gv[t][:, right], marks)[0:PAD])
            for t in range(QUADS):
                left, right = slice(0, 128), slice(128, 256)
                folded = fold(gk[t][:, left], marks), fold(gk[t][:, right], marks)
                keep(1, t, *[part[0:PAD] * SCORE_SCALE for part in folded])
                parts = gq[t][0:PAD, left], gq[t][WIDE : WIDE + PAD, right]
                keep(0, t, *[part * SCORE_SCALE for part in parts])
            return carry

        lax.fori_loop(0, bins // 2, window, 0, unroll=9)

    return pl.pallas_call(
        kernel,
        out_shape=(
            jax.ShapeDtypeStruct((rows, 3 * D), LOW),
            jax.ShapeDtypeStruct((QUADS, 4 * WIDE, 128), F32),
        ),
        in_specs=[smem()] + [vmem()] * 7,
        out_specs=[vmem()] * 2,
        scratch_shapes=[
            pltpu.VMEM((D, D), LOW),
            pltpu.VMEM((bins // 2, 2 * WIDE, D), LOW),
            pltpu.VMEM((spare, PAD, D), F32),
            pltpu.VMEM((spare, PAD, D), F32),
            pltpu.VMEM((spare, PAD, D), F32),
        ],
        compiler_params=params(11),
        cost_estimate=cost(1e10, 2e7),
        name="attn_backward",
    )(table, grad, qkv, probs, *weights)


def attn_grads(grad, a, attn, gqkv, scores, small_mlp, fc1_bias_grad, weights, norms):
    rows = grad.shape[0]

    def kernel(
        grad_ref, a_ref, attn_ref, gqkv_ref, scores_ref, mlp_ref, fc1b_ref, w0, w1, w2, w3, norm_ref,
        keep_ref, send_ref, wqkv, small,
    ):
        stack_qkv((w0, w1, w2, w3), wqkv)
        gain, shift = norm_ref[0:1], norm_ref[1:2]
        dqkv = dot_tn(a_ref[...], gqkv_ref[...])
        low_grad = grad_ref[...].astype(LOW)
        dproj = dot_tn(attn_ref[...], low_grad).astype(LOW)
        column_sums = jnp.sum(gqkv_ref[...].astype(F32), axis=0, keepdims=True)
        wide_sums = jnp.broadcast_to(column_sums, (16, 3 * D))
        dshift = sum(dot_nn(part, wqkv[...]) for part in split(wide_sums))[0:1]
        table_rows = scores_to_table(scores_ref)
        turned, match = [], jnp.zeros((1, D), F32)
        for c in range(3):
            back = dqkv[:, c * D : (c + 1) * D].T
            here = wqkv[c * D : (c + 1) * D].astype(F32)
            match = match + jnp.sum(back * here, axis=0, keepdims=True)
            turned.append(back.astype(LOW))
        small[...] = jnp.zeros((SMALL, D), F32)
        small[0:1] = (match - shift * dshift) / gain
        small[1:2] = dshift
        small[2:3] = jnp.sum(low_grad.astype(F32), axis=0, keepdims=True)
        small[3:6] = mlp_ref[0:3]
        gq_sum = jnp.broadcast_to(column_sums[:, 0:D], (8, D))
        gv_sum = jnp.broadcast_to(column_sums[:, 2 * D : 3 * D], (8, D))
        for k in range(4):
            dest = keep_ref if k < 2 else send_ref
            for c in range(3):
                dest[k % 2, c * 96 : (c + 1) * 96] = turned[c][k * 96 : (k + 1) * 96]
            dest[k % 2, 288:384] = dproj[k * 96 : (k + 1) * 96]
            small[6:7] = fc1b_ref[:, k * D : (k + 1) * D]
            small[7:8] = pltpu.roll(gq_sum, (D - k * 96) % D, 1)[0:1]
            small[8:9] = pltpu.roll(gv_sum, (D - k * 96) % D, 1)[0:1]
            for h in range(3):
                small[9 + h : 10 + h, 0:256] = table_rows[3 * k + h]
            dest[k % 2, D : D + SMALL] = small[...].astype(LOW)

    return pl.pallas_call(
        kernel,
        out_shape=(
            jax.ShapeDtypeStruct((2, D + SMALL, D), LOW),
            jax.ShapeDtypeStruct((2, D + SMALL, D), LOW),
        ),
        in_specs=[vmem()] * 12,
        out_specs=[vmem()] * 2,
        scratch_shapes=[
            pltpu.VMEM((3 * D, D), LOW),
            pltpu.VMEM((SMALL, D), F32),
        ],
        compiler_params=params(12),
        cost_estimate=cost(6e9, 2e7),
        name="attn_grads",
    )(grad, a, attn, gqkv, scores, small_mlp, fc1_bias_grad, *weights, norms)


def attn_input_grad(table, grad, hidden, gqkv, weights, norms, shifted, work):
    rows = hidden.shape[0]
    bins = rows // PAD
    chunk_slots = 6
    chunk = chunk_slots * PAD
    spare = bins if shifted else 2

    def kernel(
        table_ref, grad_ref, hidden_ref, gqkv_ref, w0, w1, w2, w3, norm_ref,
        out_ref, wqkv, wide, tmp, moved,
    ):
        stack_qkv((w0, w1, w2, w3), wqkv)
        gain = norm_ref[0:1]
        if shifted:
            for i in range(bins // chunk_slots):
                slots = slice(i * chunk_slots, (i + 1) * chunk_slots)
                ga = dot_nn(gqkv_ref[i * chunk : (i + 1) * chunk], wqkv[...])
                wide[slots] = ga.reshape(chunk_slots, PAD, D)
            move_windows(table_ref, wide, tmp, moved, True)

        for i in range(bins // chunk_slots):
            at = slice(i * chunk, (i + 1) * chunk)
            if shifted:
                ga = moved[i * chunk_slots : (i + 1) * chunk_slots].reshape(chunk, D)
            else:
                ga = dot_nn(gqkv_ref[at], wqkv[...])
            scaled, inverse = norm_rows(hidden_ref[at])
            out_ref[at] = grad_ref[at] + norm_back(ga, scaled, inverse, gain)

    return pl.pallas_call(
        kernel,
        out_shape=jax.ShapeDtypeStruct((rows, D), F32),
        in_specs=[smem()] + [vmem()] * 8,
        out_specs=vmem(),
        scratch_shapes=[pltpu.VMEM((3 * D, D), LOW)] + [pltpu.VMEM((spare, PAD, D), F32)] * 3,
        compiler_params=params(12),
        cost_estimate=cost(work, 1e7),
        name="attn_input_grad",
    )(table, grad, hidden, gqkv, *weights, norms)


def mlp_forward(mid, weights, fc1_bias, norms, layer):
    rows = mid.shape[0]
    chunk = 3 * PAD * 2
    steps = rows // chunk

    def kernel(
        mid_ref, w0, w1, w2, w3, fc1_bias_ref, norm_ref,
        out_ref, act_ref, slope_ref, fc1, fc2,
    ):
        stack_mlp((w0, w1, w2, w3), fc1, fc2)
        gain, shift, out_shift = norm_ref[0:1], norm_ref[1:2], norm_ref[2:3]

        def step(i, carry):
            at = pl.ds(pl.multiple_of(i * chunk, 16), chunk)
            rows_now = mid_ref[at]
            scaled, _ = norm_rows(rows_now)
            a = (scaled * gain + shift).astype(LOW)
            act, slope = gelu_parts(dot_nn(a, fc1[...]) + fc1_bias_ref[layer, 0:1])
            act = act.astype(LOW)
            act_ref[at] = act
            slope_ref[at] = slope.astype(LOW)
            out_ref[at] = rows_now + dot_nn(act, fc2[...]) + out_shift
            return carry

        lax.fori_loop(0, steps, step, 0, unroll=True)

    return pl.pallas_call(
        kernel,
        out_shape=(
            jax.ShapeDtypeStruct((rows, D), F32),
            jax.ShapeDtypeStruct((rows, FF), LOW),
            jax.ShapeDtypeStruct((rows, FF), LOW),
        ),
        in_specs=[vmem()] * 7,
        out_specs=[vmem()] * 3,
        scratch_shapes=[pltpu.VMEM((D, FF), LOW), pltpu.VMEM((FF, D), LOW)],
        compiler_params=params(14),
        cost_estimate=cost(7e9, 2e7),
        name="mlp_forward",
    )(mid, *weights, fc1_bias, norms)


def mlp_sums(gpre, a, act, low_grad, fc1, fc1_sums, grad_sums, norms, outs):
    keep_ref, send_ref, small_ref, bias_ref = outs
    gain, shift = norms[0:1], norms[1:2]
    dfc1 = dot_tn(a[...], gpre[...])
    dfc2 = dot_tn(low_grad[...], act[...])
    column = jnp.sum(dfc1 * fc1[...].astype(F32), axis=1, keepdims=True)
    match = jnp.broadcast_to(column, (D, 128)).T
    for k in range(4):
        dest = keep_ref if k < 2 else send_ref
        cols = slice(k * D, (k + 1) * D)
        dest[k % 2, 0:D] = dfc1[:, cols].astype(LOW)
        dest[k % 2, D : 2 * D] = dfc2[:, cols].astype(LOW)
    wide_sums = jnp.broadcast_to(fc1_sums, (16, FF))
    dshift = sum(dot_nt(part, fc1[...]) for part in split(wide_sums))[0:1]
    small_ref[0:1] = (match[0:1] - shift * dshift) / gain
    small_ref[1:2] = dshift
    small_ref[2:3] = grad_sums
    small_ref[3:8] = jnp.zeros((5, D), F32)
    bias_ref[...] = fc1_sums


def sums_shapes():
    return (
        jax.ShapeDtypeStruct((2, 2 * D, D), LOW),
        jax.ShapeDtypeStruct((2, 2 * D, D), LOW),
        jax.ShapeDtypeStruct((8, D), F32),
        jax.ShapeDtypeStruct((1, FF), F32),
    )


def mlp_backward(grad, mid, act, slope, weights, norms):
    rows = mid.shape[0]
    chunk = 6 * PAD
    steps = rows // chunk

    def kernel(
        grad_ref, mid_ref, act_ref, slope_ref, w0, w1, w2, w3, norm_ref,
        gpre_ref, keep_ref, send_ref, small_ref, bias_ref, fc1, fc2, low_grad, a_ref,
    ):
        stack_mlp((w0, w1, w2, w3), fc1, fc2)
        gain, shift = norm_ref[0:1], norm_ref[1:2]
        fc1_sums, grad_sums = jnp.zeros((1, FF), F32), jnp.zeros((1, D), F32)
        for i in range(steps):
            at = slice(i * chunk, (i + 1) * chunk)
            gz = grad_ref[at].astype(LOW)
            low_grad[at] = gz
            gpre = (dot_nt(gz, fc2[...]) * slope_ref[at].astype(F32)).astype(LOW)
            gpre_ref[at] = gpre
            scaled, _ = norm_rows(mid_ref[at])
            a_ref[at] = (scaled * gain + shift).astype(LOW)
            fc1_sums = fc1_sums + jnp.sum(gpre.astype(F32), axis=0, keepdims=True)
            grad_sums = grad_sums + jnp.sum(gz.astype(F32), axis=0, keepdims=True)
        outs = keep_ref, send_ref, small_ref, bias_ref
        mlp_sums(gpre_ref, a_ref, act_ref, low_grad, fc1, fc1_sums, grad_sums, norm_ref, outs)

    return pl.pallas_call(
        kernel,
        out_shape=(jax.ShapeDtypeStruct((rows, FF), LOW), *sums_shapes()),
        in_specs=[vmem()] * 9,
        out_specs=[vmem()] * 5,
        scratch_shapes=[
            pltpu.VMEM((D, FF), LOW),
            pltpu.VMEM((FF, D), LOW),
            pltpu.VMEM((rows, D), LOW),
            pltpu.VMEM((rows, D), LOW),
        ],
        compiler_params=params(18),
        cost_estimate=cost(7e9, 2e7),
        name="mlp_backward",
    )(grad, mid, act, slope, *weights, norms)


def mlp_turn(mid, grad, weights, fc1_bias, norms, layer):
    rows = mid.shape[0]
    chunk = 6 * PAD
    steps = rows // chunk

    def kernel(
        mid_ref, grad_ref, w0, w1, w2, w3, fc1_bias_ref, norm_ref,
        out_ref, gpre_ref, keep_ref, send_ref, small_ref, bias_ref,
        fc1, fc2, a_all, act_all, low_grad,
    ):
        stack_mlp((w0, w1, w2, w3), fc1, fc2)
        gain, shift, out_shift = norm_ref[0:1], norm_ref[1:2], norm_ref[2:3]

        def step(i, totals):
            at = pl.ds(pl.multiple_of(i * chunk, 16), chunk)
            rows_now = mid_ref[at]
            scaled, _ = norm_rows(rows_now)
            a = (scaled * gain + shift).astype(LOW)
            a_all[at] = a
            act, slope = gelu_parts(dot_nn(a, fc1[...]) + fc1_bias_ref[layer, 0:1])
            act = act.astype(LOW)
            act_all[at] = act
            out_ref[at] = rows_now + dot_nn(act, fc2[...]) + out_shift
            gz = grad_ref[at].astype(LOW)
            low_grad[at] = gz
            gpre = (dot_nt(gz, fc2[...]) * slope).astype(LOW)
            gpre_ref[at] = gpre
            return (
                totals[0] + jnp.sum(gz.astype(F32), axis=0, keepdims=True),
                totals[1] + jnp.sum(gpre.astype(F32), axis=0, keepdims=True),
            )

        zeros = jnp.zeros((1, D), F32), jnp.zeros((1, FF), F32)
        grad_sums, fc1_sums = lax.fori_loop(0, steps, step, zeros)
        outs = keep_ref, send_ref, small_ref, bias_ref
        mlp_sums(gpre_ref, a_all, act_all, low_grad, fc1, fc1_sums, grad_sums, norm_ref, outs)

    return pl.pallas_call(
        kernel,
        out_shape=(
            jax.ShapeDtypeStruct((rows, D), F32),
            jax.ShapeDtypeStruct((rows, FF), LOW),
            *sums_shapes(),
        ),
        in_specs=[vmem()] * 8,
        out_specs=[vmem()] * 6,
        scratch_shapes=[
            pltpu.VMEM((D, FF), LOW),
            pltpu.VMEM((FF, D), LOW),
            pltpu.VMEM((rows, D), LOW),
            pltpu.VMEM((rows, FF), LOW),
            pltpu.VMEM((rows, D), LOW),
        ],
        compiler_params=params(18),
        cost_estimate=cost(1.5e10, 4e7),
        name="mlp_turn",
    )(mid, grad, *weights, fc1_bias, norms)


def mlp_input_grad(grad, mid, gpre, weights, norms):
    rows = mid.shape[0]
    chunk = 6 * PAD

    def kernel(grad_ref, mid_ref, gpre_ref, w0, w1, w2, w3, norm_ref, out_ref, fc1):
        for k, piece in enumerate((w0, w1, w2, w3)):
            fc1[:, k * D : (k + 1) * D] = piece[0:D]
        gain = norm_ref[0:1]
        for i in range(rows // chunk):
            at = slice(i * chunk, (i + 1) * chunk)
            ga = dot_nt(gpre_ref[at], fc1[...])
            scaled, inverse = norm_rows(mid_ref[at])
            out_ref[at] = grad_ref[at] + norm_back(ga, scaled, inverse, gain)

    return pl.pallas_call(
        kernel,
        out_shape=jax.ShapeDtypeStruct((rows, D), F32),
        in_specs=[vmem()] * 8,
        out_specs=vmem(),
        scratch_shapes=[pltpu.VMEM((D, FF), LOW)],
        compiler_params=params(8),
        cost_estimate=cost(3e12, 1e7),
        name="mlp_input_grad",
    )(grad, mid, gpre, *weights, norms)


def finish(side, total_a, state_b, state_c, state_d):
    def kernel(
        side_ref, a_ref, b0, b1, c0, c1, d0, d1,
        qkv_ref, proj_ref, fc1_ref, fc2_ref, gains_ref, shifts_ref, fc1b_ref, qv_ref, table_ref,
        rows,
    ):
        first = side_ref[0:1] > 0

        def join(value, other):
            value, other = value[...].astype(F32), other[...].astype(F32)
            return jnp.where(first, value, other), jnp.where(first, other, value)

        half = (D + SMALL) // 2
        rows[0] = d0[...].astype(F32) + d1[...].astype(F32)
        rows[1, 0:half], rows[1, half:] = join(b0, b1)
        fc1_ref[0], fc2 = join(c0, c1)
        fc2_ref[0] = fc2.T
        fc1_ref[1] = a_ref[0:D].astype(F32)
        fc2_ref[1] = a_ref[D : 2 * D].astype(F32).T
        for l in range(LAYERS):
            qkv_ref[l] = rows[l, 0:288]
            proj_ref[l] = rows[l, 288:384]
            now = rows[l, D : D + SMALL]
            for i, row in enumerate((0, 3)):
                gains_ref[l, i : i + 1] = now[row : row + 1]
            for i, row in enumerate((1, 4, 2, 5)):
                shifts_ref[l, i : i + 1] = now[row : row + 1]
            fc1b_ref[l : l + 1] = now[6:7]
            qv_ref[l] = now[7:9, 0:96]
            turned = now[8:16, 0:256].T
            table_ref[l] = turned[0:169, 1:4]

    return pl.pallas_call(
        kernel,
        out_shape=(
            jax.ShapeDtypeStruct((LAYERS, 288, D), F32),
            jax.ShapeDtypeStruct((LAYERS, 96, D), F32),
            jax.ShapeDtypeStruct((LAYERS, D, D), F32),
            jax.ShapeDtypeStruct((LAYERS, D, D), F32),
            jax.ShapeDtypeStruct((LAYERS, 2, D), F32),
            jax.ShapeDtypeStruct((LAYERS, 4, D), F32),
            jax.ShapeDtypeStruct((LAYERS, D), F32),
            jax.ShapeDtypeStruct((LAYERS, 2, 96), F32),
            jax.ShapeDtypeStruct((LAYERS, 169, 3), F32),
        ),
        in_specs=[vmem()] * 8,
        out_specs=[vmem()] * 9,
        scratch_shapes=[pltpu.VMEM((LAYERS, D + SMALL, D), F32)],
        compiler_params=params(14),
        cost_estimate=cost(0, 1e6),
        name="finish",
    )(side, total_a, *state_b, *state_c, *state_d)


def swap_core(value):
    return lax.ppermute(value, "head", [(i, i ^ 1) for i in range(4)])


def swap_chip(value):
    return lax.ppermute(value, "head", [(i, i ^ 2) for i in range(4)])


def swap_border(value):
    return lax.ppermute(value, "head", [(1, 2), (2, 1)])


def swap_dp(value, step, size):
    return lax.ppermute(value, "dp", [(i, i ^ step) for i in range(size)])


def tie(*values):
    return lax.optimization_barrier(values)


def pick(first, one, other):
    first = first > 0
    return jnp.where(first, one, other), jnp.where(first, other, one)


def dp_masks(order):
    size = lax.axis_size("dp")
    upper = [(2 << b) - 2 for b in range(1, size.bit_length() - 1)]
    if order == 1 and upper:
        return [upper[-1]] + upper[:-1] + [1]
    return [1] + (upper if order == 2 else upper[::-1])


def dp_start(parts, sides, order):
    half = parts[0].shape[0] // 2
    low = sum(p[:half].astype(F32) for p in parts)
    high = sum(p[half:].astype(F32) for p in parts)
    masks = dp_masks(order)
    kept, sent = pick(sides[order % 2], low, high)
    return kept, swap_dp(sent.astype(LOW), masks[0], lax.axis_size("dp"))


def dp_next(kept, other, order, stage):
    masks = dp_masks(order)
    value = (kept.astype(F32) + other.astype(F32)).astype(LOW)
    return value, swap_dp(value, (masks + masks[:1])[stage], lax.axis_size("dp"))


def dp_whole(value, other, stage):
    masks = dp_masks(2)
    value = (value.astype(F32) + other.astype(F32)).astype(LOW)
    return value, swap_dp(value, masks[stage], lax.axis_size("dp"))


def dp_join(value, other, sides, order):
    low, high = pick(sides[order % 2], value, other)
    return jnp.concatenate([low, high])


def body(
    tokens, outputs_grad, image_kind, qkv_weight, qv_bias, bias_table, proj_weight,
    fc1_weight, fc1_bias, fc2_weight, gains, shifts,
):
    own = tokens.shape[0] // PLACES
    bins = own + 2
    me = lax.axis_index("head").astype(jnp.int32)

    def border(value):
        edge = 4 * PLACES
        return swap_border(jnp.where(me == 1, value[-edge:], value[:edge]))

    turned = jnp.transpose(qkv_weight, (0, 2, 3, 1)).reshape(LAYERS, 288, D)

    def attn_pack(l):
        return jnp.concatenate([turned[l], proj_weight[l]], axis=0)

    def mlp_pack(l):
        return jnp.concatenate([fc1_weight[l], fc2_weight[l]], axis=0)

    def norm_pack(l, which, bias_row):
        rows = jnp.stack([gains[l, which], shifts[l, which], shifts[l, bias_row]])
        return jnp.pad(rows, ((0, 5), (0, 0)))

    partner = swap_core(tokens)
    rows = jnp.pad(jnp.transpose(bias_table, (0, 2, 1)).reshape(6, 169), ((0, 0), (0, D - 169)))
    small = jnp.concatenate([rows, qv_bias.reshape(1, D), fc1_bias])
    small = jnp.pad(small, ((0, SMALL - 9), (0, 0)))
    own_pack = [jnp.concatenate([attn_pack(0), *split(small)])]
    chip_pack = [swap_chip(own_pack[0])]
    edges, _ = tie(tokens, own_pack[0])
    halo = border(edges)
    place = lax.axis_index("dp")
    top = lax.axis_size("dp") // 2
    sides = [1 - (place & 1), (place < top).astype(jnp.int32)]
    first = jnp.broadcast_to(jnp.stack(sides).astype(jnp.int32)[:, None], (2, D))
    table = make_plan(image_kind, me, own, bins)
    mlp_first = mlp_pack(0)
    table, first, chip_pack[0], partner, mlp_first = tie(
        table, first, chip_pack[0], partner, mlp_first
    )
    sides = [first[0:1], first[1:2]]
    hidden = gather_slots(table, tokens, partner, halo, bins)

    def gathered(i):
        p, c = own_pack[i], chip_pack[i]
        return p, c, swap_core(p), swap_core(c)

    pack, halo, _ = tie(mlp_first, halo, chip_pack[0])
    own_pack.append(pack)
    chip_pack.append(swap_chip(pack))
    first_weights = gathered(0)
    bias, qkv_bias, fc1_all = spread_smalls(first_weights)

    saved, weights = [], []
    last = LAYERS - 1
    for l in range(LAYERS):
        norms, mlp_norms = norm_pack(l, 0, 2), norm_pack(l, 1, 3)
        weights.append(first_weights if l == 0 else gathered(2 * l))
        mid, a, qkv, probs, attn = attn_forward(
            table, hidden, weights[2 * l], qkv_bias, bias, norms, l
        )
        mid, chip_pack[2 * l + 1] = tie(mid, chip_pack[2 * l + 1])
        weights.append(gathered(2 * l + 1))
        if l == last:
            saved.append((hidden, mid, a, qkv, probs, attn, norms, mlp_norms))
            break
        pack, outputs_grad, mid = tie(attn_pack(1), outputs_grad, mid)
        grad_partner, grad_halo = swap_core(outputs_grad), border(outputs_grad)
        own_pack.append(pack)
        chip_pack.append(swap_chip(pack))
        out, act, slope = mlp_forward(mid, weights[2 * l + 1], fc1_all, mlp_norms, l)
        pack, out, chip_pack[2], grad_partner, grad_halo = tie(
            mlp_pack(1), out, chip_pack[2], grad_partner, grad_halo
        )
        own_pack.append(pack)
        chip_pack.append(swap_chip(pack))
        saved.append((hidden, mid, a, qkv, probs, attn, norms, mlp_norms, act, slope))
        hidden = out
    grad = gather_slots(table, outputs_grad, grad_partner, grad_halo, bins)

    def give_back(value):
        slots = value.reshape(bins, PAD, D)
        return slots, swap_core(slots), swap_border(border_slots(table, slots, 0))

    def mlp_back(l, grad):
        return mlp_backward(
            grad, saved[l][1], saved[l][8], saved[l][9], weights[2 * l + 1], saved[l][7]
        )

    def mlp_input(l, grad, gpre):
        return mlp_input_grad(grad, saved[l][1], gpre, weights[2 * l + 1], saved[l][7])

    def attn_back(l, grad):
        return attn_backward(table, grad, saved[l][3], saved[l][4], weights[2 * l], l % 2 == 1)

    def attn_sums(l, grad, gqkv, scores, small_mlp, fc1_bias_grad):
        return attn_grads(
            grad, saved[l][2], saved[l][5], gqkv, scores, small_mlp, fc1_bias_grad,
            weights[2 * l], saved[l][6],
        )

    def attn_input(l, grad, gqkv):
        work = 6e9 if l == last else 3e12
        return attn_input_grad(
            table, grad, saved[l][0], gqkv, weights[2 * l], saved[l][6], l % 2 == 1, work
        )

    def core_sum(keep, other):
        return [(keep[i].astype(F32) + other[i].astype(F32)).astype(LOW) for i in range(2)]

    out, gpre, keep_a, send_a, small_mlp, fc1_bias_grad = mlp_turn(
        saved[last][1], grad, weights[2 * last + 1], fc1_all, saved[last][7], last
    )
    core_a = swap_core(send_a)
    grad = mlp_input(1, grad, gpre)
    grad, core_a = tie(grad, core_a)
    half_a, out_a = core_sum(keep_a, core_a)
    grad, out_a = tie(grad, out_a)
    chip_a = swap_chip(out_a)
    gqkv, scores = attn_back(1, grad)
    grad_after = attn_input(1, grad, gqkv)
    gqkv, _ = tie(gqkv, grad_after)
    keep_b, send_b = attn_sums(1, grad, gqkv, scores, small_mlp, fc1_bias_grad)
    grad, send_b, chip_a = tie(grad_after, send_b, chip_a)
    core_b = swap_core(send_b)
    state_a = dp_start((half_a, chip_a), sides, 2)
    half_b, out_b = core_sum(keep_b, core_b)
    grad, out_b = tie(grad, out_b)
    chip_b = swap_chip(out_b)
    gpre, keep_c, send_c, small_mlp, fc1_bias_grad = mlp_back(0, grad)
    gpre, send_c, state_a, chip_b = tie(gpre, send_c, state_a, chip_b)
    core_c = swap_core(send_c)
    state_a = dp_next(*state_a, 2, 1)
    grad = mlp_input(0, grad, gpre)
    grad, core_c = tie(grad, core_c)
    state_b = dp_start((half_b, chip_b), sides, 2)
    half_c, out_c = core_sum(keep_c, core_c)
    grad, out_c = tie(grad, out_c)
    chip_c = swap_chip(out_c)
    gqkv, scores = attn_back(0, grad)
    gqkv, state_a, state_b = tie(gqkv, state_a, state_b)
    state_a = dp_next(*state_a, 2, 2)
    state_b = dp_next(*state_b, 2, 1)
    keep_d, send_d = attn_sums(0, grad, gqkv, scores, small_mlp, fc1_bias_grad)
    core_d = swap_core(send_d)
    out, chip_c, _ = tie(out, chip_c, send_d)
    state_c = dp_start((half_c, chip_c), sides, 2)
    out_slots = out.reshape(bins, PAD, D)
    out_edge, core_d = tie(border_slots(table, out_slots, 3e12), core_d)
    half_d, out_d = core_sum(keep_d, core_d)
    chip_d = swap_chip(out_d)
    gqkv, out_slots, out_edge, _ = tie(gqkv, out_slots, out_edge, out_d)
    grad = attn_input(0, grad, gqkv)
    output_parts = out_slots, swap_core(out_slots), swap_border(out_edge)
    chip_d, state_a, state_b, state_c = tie(chip_d, state_a, state_b, state_c)
    state_d = dp_whole(half_d, chip_d, 0)
    state_c = dp_next(*state_c, 2, 1)
    state_b = dp_next(*state_b, 2, 2)
    tokens_parts = give_back(grad)
    state_d, state_c, state_b = tie(state_d, state_c, state_b)
    state_d = dp_whole(*state_d, 1)
    state_c = dp_next(*state_c, 2, 2)
    state_a = dp_next(*state_a, 2, 3)
    state_b = dp_next(*state_b, 2, 3)
    output = return_slots(table, *output_parts, own)
    state_d, state_c, state_a, state_b = tie(state_d, state_c, state_a, state_b)
    state_d = dp_whole(*state_d, 2)
    state_c = dp_next(*state_c, 2, 3)
    tokens_grad = return_slots(table, *tokens_parts, own)
    total_a = dp_join(*state_a, sides, 2)
    state_d, state_c, output, tokens_grad = tie(state_d, state_c, output, tokens_grad)
    qkv_out, proj_out, fc1_out, fc2_out, *smalls = finish(
        sides[0], total_a, state_b, state_c, state_d
    )
    gains_out, shifts_out, fc1_bias_out, qv_out, table_out = smalls
    qkv_out = qkv_out.reshape(LAYERS, 3, 96, D).transpose(0, 3, 1, 2)
    return (
        output, tokens_grad, qkv_out, qv_out, table_out, proj_out, fc1_out, fc1_bias_out,
        fc2_out, gains_out, shifts_out,
    )


def solution(mesh):
    rows = P(("dp", "head"), None)
    placed = (
        rows,
        rows,
        P("dp", None),
        P(None, None, None, "head"),
        P(None, None, "head"),
        P(None, None, "head"),
        P(None, "head", None),
        P(None, None, "head"),
        P(None, "head"),
        P(None, "head", None),
        P(),
        P(),
    )
    return jax.shard_map(
        body,
        mesh=mesh,
        in_specs=placed,
        out_specs=(
            rows,
            rows,
            P(None, None, None, "head"),
            P(None, None, "head"),
            P(None, None, "head"),
            P(None, "head", None),
            P(None, None, "head"),
            P(None, "head"),
            P(None, "head", None),
            P(),
            P(),
        ),
        check_vma=False,
    )
```

```python
import jax
import jax.numpy as jnp
from jax import lax
from jax.experimental import pallas as pl
from jax.experimental.pallas import tpu as pltpu
from jax.sharding import PartitionSpec as P

D = 384
FF = 1536
LAYERS = 2
PLACES = 49
PAD = 56
WIDE = 64
QUADS = 3
HEAD_DIM = 32
SCORE_SCALE = HEAD_DIM**-0.5
LN_EPS = 1e-05
LOW = jnp.bfloat16
F32 = jnp.float32
MIB = 1024 * 1024
SMALL = 16

SRC, SIDE, WROW, WCOL, FIRST, RET, SEND = 0, 24, 48, 72, 96, 120, 140
TABLE = 144


def vmem():
    return pl.BlockSpec(memory_space=pltpu.VMEM)


def smem():
    return pl.BlockSpec(memory_space=pltpu.SMEM)


def anywhere():
    return pl.BlockSpec(memory_space=pl.ANY)


def params(limit):
    return pltpu.CompilerParams(vmem_limit_bytes=limit * MIB)


def cost(flops, size):
    return pl.CostEstimate(flops=int(flops * 0.02), bytes_accessed=int(size * 0.02), transcendentals=0)


def dot_nn(a, b):
    return lax.dot_general(a, b, (((1,), (0,)), ((), ())), preferred_element_type=F32)


def dot_nt(a, b):
    return lax.dot_general(a, b, (((1,), (1,)), ((), ())), preferred_element_type=F32)


def dot_tn(a, b):
    return lax.dot_general(a, b, (((0,), (0,)), ((), ())), preferred_element_type=F32)


def plan_kernel(own, bins, kind_ref, me_ref, out_ref, load_ref):
    me = me_ref[0]
    half = 2 * own
    for i in range(TABLE):
        out_ref[i] = -1 if i < bins or RET <= i < RET + own else 0
    for i in range(bins):
        out_ref[SIDE + i] = 1
        out_ref[FIRST + i] = i
    for i in range(4):
        load_ref[i] = 0

    def place(start, count, side, bin_id):
        base = load_ref[bin_id]
        load_ref[bin_id] = base + count

        def step(k, carry):
            slot = start + k
            owner = slot // own
            inner = slot - owner * own
            local = base + k
            mine = bin_id == me
            halo = jnp.where(me == 1, slot - half, slot - half + 4)
            code = jnp.where(
                owner == me, inner, jnp.where(owner == (me ^ 1), own + inner, 2 * own + halo)
            )

            @pl.when(mine)
            def _():
                wrow = k // side
                out_ref[SRC + local] = code
                out_ref[SIDE + local] = side
                out_ref[WROW + local] = wrow
                out_ref[WCOL + local] = k - wrow * side
                out_ref[FIRST + local] = base

            @pl.when(owner == me)
            def _():
                back = jnp.where(me == 2, slot - half, k)
                out_ref[RET + inner] = jnp.where(
                    mine, local, jnp.where(bin_id == (me ^ 1), bins + local, 2 * bins + back)
                )

            return carry

        lax.fori_loop(0, count, step, 0)

    for turn in range(3):

        def visit(i, start, turn=turn):
            kind = kind_ref[0, i]
            count = jnp.where(kind == 2, 9, jnp.where(kind == 1, 4, 0))
            side = jnp.where(kind == 2, 3, 2)
            cut = half - start
            across = (cut > 0) & (cut < count)
            second = (start >= half) | (across & (cut < count - cut))
            chip = jnp.where(second, 1, 0)
            left, right = load_ref[2 * chip], load_ref[2 * chip + 1]
            emptier = 2 * chip + jnp.where(left <= right, 0, 1)
            if turn == 0:
                chosen, bin_id = across, 1 + chip
            else:
                chosen, bin_id = (kind == 3 - turn) & jnp.logical_not(across), emptier

            @pl.when(chosen)
            def _():
                place(start, count, side, bin_id)
                if turn == 0:
                    out_ref[SEND] = jnp.where((me == 1) & (chip == 0), cut, 0)

            return start + count

        lax.fori_loop(0, kind_ref.shape[1], visit, jnp.int32(0))


def gather_kernel(bins, table_ref, refs, out_ref, spread_ref):
    spread_ref[...] = jnp.zeros(spread_ref.shape, F32)
    at = 0
    for ref in refs:
        for s in range(ref.shape[0] // PLACES):
            spread_ref[at, 0:PLACES] = ref[s * PLACES : (s + 1) * PLACES].astype(F32)
            at += 1

    def step(j, carry):
        src = table_ref[SRC + j]

        @pl.when(src < 0)
        def _():
            out_ref[j] = jnp.zeros((PAD, D), F32)

        @pl.when(src >= 0)
        def _():
            out_ref[j] = spread_ref[src]

        return carry

    lax.fori_loop(0, bins, step, 0)


def make_plan(image_kind, me, own, bins):
    def kernel(kind_ref, me_ref, table_ref, load_ref):
        plan_kernel(own, bins, kind_ref, me_ref, table_ref, load_ref)

    return pl.pallas_call(
        kernel,
        out_shape=jax.ShapeDtypeStruct((TABLE,), jnp.int32),
        in_specs=[smem(), smem()],
        out_specs=smem(),
        scratch_shapes=[pltpu.SMEM((4,), jnp.int32)],
        compiler_params=params(1),
        cost_estimate=cost(0, 1.5e7),
        name="plan",
    )(image_kind, me.reshape(1))


def gather_slots(table, mine, partner, halo, bins):
    own = mine.shape[0] // PLACES

    def kernel(table_ref, *refs):
        gather_kernel(bins, table_ref, refs[:3], refs[3], refs[4])

    out = pl.pallas_call(
        kernel,
        out_shape=jax.ShapeDtypeStruct((bins, PAD, D), F32),
        in_specs=[smem()] + [vmem()] * 3,
        out_specs=vmem(),
        scratch_shapes=[pltpu.VMEM((2 * own + 4, PAD, D), F32)],
        compiler_params=params(8),
        cost_estimate=cost(0, 8e6),
        name="gather_slots",
    )(table, mine, partner, halo)
    return out.reshape(bins * PAD, D)


def border_slots(table, slots, work):
    def kernel(table_ref, slots_ref, out_ref):
        start = table_ref[SEND]
        for j in range(4):
            out_ref[j] = slots_ref[start + j]

    return pl.pallas_call(
        kernel,
        out_shape=jax.ShapeDtypeStruct((4,) + slots.shape[1:], F32),
        in_specs=[smem(), vmem()],
        out_specs=vmem(),
        compiler_params=params(4),
        cost_estimate=cost(work, 1e6),
        name="border_slots",
    )(table, slots)


def return_slots(table, mine, partner, halo, own):
    bins = mine.shape[0]

    def kernel(table_ref, mine_ref, partner_ref, halo_ref, out_ref):
        for s in range(own):
            src = table_ref[RET + s]
            rows = pl.ds(s * PLACES, PLACES)

            @pl.when(src < 0)
            def _():
                out_ref[rows] = jnp.zeros((PLACES, D), F32)

            @pl.when((src >= 0) & (src < bins))
            def _():
                out_ref[rows] = mine_ref[src, 0:PLACES]

            @pl.when((src >= bins) & (src < 2 * bins))
            def _():
                out_ref[rows] = partner_ref[src - bins, 0:PLACES]

            @pl.when(src >= 2 * bins)
            def _():
                out_ref[rows] = halo_ref[src - 2 * bins, 0:PLACES]

    return pl.pallas_call(
        kernel,
        out_shape=jax.ShapeDtypeStruct((own * PLACES, D), F32),
        in_specs=[smem(), vmem(), vmem(), vmem()],
        out_specs=vmem(),
        compiler_params=params(8),
        cost_estimate=cost(0, 8e6),
        name="return_slots",
    )(table, mine, partner, halo)


def norm_rows(rows):
    average = jnp.mean(rows, axis=-1, keepdims=True)
    centred = rows - average
    inverse = lax.rsqrt(jnp.mean(centred * centred, axis=-1, keepdims=True) + LN_EPS)
    return centred * inverse, inverse


def norm_back(incoming, scaled, inverse, gain):
    weighted = incoming * gain
    return inverse * (
        weighted
        - jnp.mean(weighted, axis=-1, keepdims=True)
        - scaled * jnp.mean(weighted * scaled, axis=-1, keepdims=True)
    )


def gelu_parts(x):
    t = 1.0 / (1.0 + 0.23164189 * jnp.abs(x))
    bell = jnp.exp2(x * x * -0.7213475204444817)
    poly = t * (
        0.127414796 + t * (-0.142248368 + t * (0.7107068705 + t * (-0.7265760135 + t * 0.5307027145)))
    )
    tail = poly * bell
    phi = jnp.where(x >= 0, 1.0 - tail, tail)
    return x * phi, phi + x * bell * 0.3989422804014327


def place_parts(shape, dim):
    place = lax.broadcasted_iota(jnp.int32, shape, dim)
    row = (place * 37) >> 8
    return place, row, place - 7 * row


def neighbour(table_ref, w, back, down):
    side, wrow, wcol = table_ref[SIDE + w], table_ref[WROW + w], table_ref[WCOL + w]
    at = wrow if down else wcol
    if back:
        other = jnp.where(at == 0, side - 1, at - 1)
    else:
        other = jnp.where(at == side - 1, 0, at + 1)
    if down:
        return table_ref[FIRST + w] + other * side + wcol
    return table_ref[FIRST + w] + wrow * side + other


def move_windows(table_ref, src, tmp, out, back):
    bins = src.shape[0]
    tmp[...] = jnp.zeros(tmp.shape, F32)
    out[...] = jnp.zeros(out.shape, F32)

    def rows(w, carry):
        other = neighbour(table_ref, w, back, True)
        if back:
            tmp[w, 21:49] = src[w, 0:28]
            tmp[w, 0:21] = src[other, 28:49]
        else:
            tmp[w, 0:28] = src[w, 21:49]
            tmp[w, 28:49] = src[other, 0:21]
        return carry

    lax.fori_loop(0, bins, rows, 0, unroll=2)
    _, _, col = place_parts((PAD, 1), 0)

    def cols(w, carry):
        other = neighbour(table_ref, w, back, False)
        if back:
            out[w, 0:49] = tmp[other, 4:53]
            out[w, 3:49] = jnp.where(col[3:49] >= 3, tmp[w, 0:46], out[w, 3:49])
        else:
            out[w, 0:49] = tmp[w, 3:52]
            out[w, 4:49] = jnp.where(col[4:49] < 4, out[w, 4:49], tmp[other, 0:45])
        return carry

    lax.fori_loop(0, bins, cols, 0, unroll=2)


def head_marks():
    lane = lax.broadcasted_iota(jnp.int32, (WIDE, 128), 1) // HEAD_DIM
    return [jnp.where(lane == h, 1.0, 0.0).astype(LOW) for h in range(4)]


def spread(block, marks):
    return jnp.concatenate([block * mark for mark in marks], axis=0)


def fold(product, marks):
    total = None
    for h, mark in enumerate(marks):
        part = product[h * WIDE : (h + 1) * WIDE] * mark.astype(F32)
        total = part if total is None else total + part
    return total


def spread_pair(block, marks):
    return jnp.concatenate([spread(block[0:WIDE], marks), spread(block[WIDE:], marks)], axis=1)


def diagonal(block):
    zero = jnp.zeros((WIDE, 128), block.dtype)
    top = jnp.concatenate([block[0:WIDE], zero], axis=1)
    return jnp.concatenate([top, jnp.concatenate([zero, block[WIDE:]], axis=1)], axis=0)


def by_head(values):
    return values.reshape(4, WIDE, 128)


def pad_rows(rows):
    return jnp.concatenate([rows, jnp.zeros((WIDE - PAD, rows.shape[1]), rows.dtype)], axis=0)


def split(values):
    high = values.astype(LOW)
    return high, (values - high.astype(F32)).astype(LOW)


def marks_where(rows, cols, test):
    row = lax.broadcasted_iota(jnp.int32, (rows, cols), 0)
    col = lax.broadcasted_iota(jnp.int32, (rows, cols), 1)
    return jnp.where(test(row, col), 1.0, 0.0).astype(LOW)


def far(place):
    row = (place * 37) >> 8
    return 13 * row + (place - 7 * row)


def spread_smalls(smalls):
    heads = LAYERS * 12

    def kernel(p0, p1, p2, p3, out_ref, qkv_ref, fc1_ref, table_ref, small_ref):
        quarters = []
        for k, ref in enumerate((p0, p1, p2, p3)):
            high, low = ref[D : D + SMALL], ref[D + SMALL : D + 2 * SMALL]
            small_ref[k] = high.astype(F32) + low.astype(F32)
            quarters.append(small_ref.at[k])
        for k, ref in enumerate(quarters):
            for l in range(LAYERS):
                at = l * 12 + k * 3
                table_ref[at : at + 3] = ref[l * 3 : l * 3 + 3, 0:256]
        lane = lax.broadcasted_iota(jnp.int32, (8, D), 1)
        for l in range(LAYERS):
            for c in range(3):
                total = jnp.zeros((8, D), F32)
                for k, ref in enumerate(quarters):
                    if c != 1:
                        row = jnp.broadcast_to(ref[6:7], (8, D))
                        row = pltpu.roll(row, (k * 96 - l * 192 - (c // 2) * 96) % D, 1)
                        own_lanes = (lane >= k * 96) & (lane < k * 96 + 96)
                        total = total + jnp.where(own_lanes, row, 0.0)
                qkv_ref[l, :, c * D : (c + 1) * D] = total
            for k, ref in enumerate(quarters):
                row = jnp.broadcast_to(ref[7 + l : 8 + l], (8, D))
                fc1_ref[l, :, k * D : (k + 1) * D] = row
        to_lane = marks_where(128, 128, lambda r, c: (far(c & 63) == r) & ((c & 63) < PLACES))
        to_row = marks_where(WIDE, 96, lambda r, c: (far(r) == c) & (r < PLACES))
        place = lax.broadcasted_iota(jnp.int32, (WIDE, 128), 0)
        empty = jnp.where(place < PLACES, 0.0, -1e30)
        turned = pltpu.roll(table_ref[...], 172, 1)
        skewed = []
        for n in range(heads):
            row = jnp.broadcast_to(turned[n : n + 1], (96, 256))
            skewed.append(pltpu.roll(row, 0, 1, stride=1, stride_axis=0)[:, 0:128])
        skewed = jnp.concatenate(skewed, axis=1)
        total = None
        for part in split(skewed):
            rows = dot_nn(to_row, part).astype(LOW)
            rows = jnp.concatenate([rows[:, n * 128 : (n + 1) * 128] for n in range(heads)], axis=0)
            part = dot_nn(rows, to_lane)
            total = part if total is None else total + part
        for n in range(heads):
            l, t, h = n // 12, n % 12 // 4, n % 4
            out_ref[l, t, h * WIDE : (h + 1) * WIDE] = total[n * WIDE : (n + 1) * WIDE] + empty

    return pl.pallas_call(
        kernel,
        out_shape=(
            jax.ShapeDtypeStruct((LAYERS, QUADS, 4 * WIDE, 128), F32),
            jax.ShapeDtypeStruct((LAYERS, 8, 3 * D), F32),
            jax.ShapeDtypeStruct((LAYERS, 8, FF), F32),
        ),
        in_specs=[vmem()] * 4,
        out_specs=[vmem()] * 3,
        scratch_shapes=[pltpu.VMEM((heads, 256), F32), pltpu.VMEM((4, SMALL, D), F32)],
        compiler_params=params(6),
        cost_estimate=cost(0, 1e7),
        name="spread_smalls",
    )(*smalls)


def scores_to_table(scores_ref):
    to_far = marks_where(128, 128, lambda r, c: (far(r & 63) == c) & ((r & 63) < PLACES))
    to_row = marks_where(96, WIDE, lambda r, c: (84 - far(c) == r) & (c < PLACES))
    wide = None
    for part in split(scores_ref[...].reshape(12 * WIDE, 128)):
        part = dot_nn(part, to_far)
        wide = part if wide is None else wide + part
    wide = jnp.concatenate([wide[h * WIDE : (h + 1) * WIDE] for h in range(12)], axis=1)
    rows = None
    for part in split(wide):
        part = dot_nn(to_row, part)
        rows = part if rows is None else rows + part
    out = []
    for h in range(12):
        one = rows[:, h * 128 : (h + 1) * 128]
        one = jnp.concatenate([one, jnp.zeros_like(one)], axis=1)
        one = pltpu.roll(one, 0, 1, stride=1, stride_axis=0)
        out.append(jnp.sum(one, axis=0, keepdims=True))
    return out


def stack_qkv(pieces, out_ref):
    for k, piece in enumerate(pieces):
        for c in range(3):
            out_ref[c * D + k * 96 : c * D + (k + 1) * 96] = piece[c * 96 : (c + 1) * 96]


def stack_proj(pieces, out_ref):
    for k, piece in enumerate(pieces):
        out_ref[k * 96 : (k + 1) * 96] = piece[288:384]


def stack_mlp(pieces, fc1_ref, fc2_ref):
    for k, piece in enumerate(pieces):
        fc1_ref[:, k * D : (k + 1) * D] = piece[0:D]
        fc2_ref[k * D : (k + 1) * D] = piece[D : 2 * D]


def attn_forward(table, hidden, weights, qv_bias, bias, norms, layer):
    shifted = layer % 2 == 1
    rows = hidden.shape[0]
    bins = rows // PAD
    chunk_slots = 6
    chunk = chunk_slots * PAD
    spare = bins if shifted else 2

    def kernel(
        table_ref, hidden_ref, w0, w1, w2, w3, qv_ref, bias_ref, norm_ref,
        mid_ref, a_ref, qkv_ref, p_ref, attn_ref,
        wqkv, wproj, wide, tmp, moved,
    ):
        pieces = (w0, w1, w2, w3)
        stack_qkv(pieces, wqkv)
        stack_proj(pieces, wproj)
        gain, shift, proj_shift = norm_ref[0:1], norm_ref[1:2], norm_ref[2:3]
        marks = head_marks()
        def norm_step(i, carry):
            at = pl.ds(pl.multiple_of(i * chunk, 16), chunk)
            scaled, _ = norm_rows(hidden_ref[at])
            normed = scaled * gain + shift
            if shifted:
                slots = pl.ds(i * chunk_slots, chunk_slots)
                wide[slots] = normed.reshape(chunk_slots, PAD, D)
            else:
                a_ref[at] = normed.astype(LOW)
            return carry

        lax.fori_loop(0, bins // chunk_slots, norm_step, 0)
        if shifted:
            move_windows(table_ref, wide, tmp, moved, False)
            a_ref[...] = moved[...].reshape(rows, D).astype(LOW)

        def qkv_step(i, carry):
            at = pl.ds(pl.multiple_of(i * chunk, 16), chunk)
            project = dot_nt(a_ref[at], wqkv[...]) + qv_ref[layer, 0:1]
            for j in range(chunk_slots):
                block = project[j * PAD : (j + 1) * PAD]
                at = pl.ds((j % 2) * WIDE, WIDE)
                qkv_ref[i * (chunk_slots // 2) + j // 2, at] = pad_rows(block).astype(LOW)
            return carry

        lax.fori_loop(0, bins // chunk_slots, qkv_step, 0)

        if shifted:
            _, qrow, qcol = place_parts((WIDE, 1), 0)
            lane = lax.broadcasted_iota(jnp.int32, (1, 128), 1)
            second = lane >= WIDE
            pplace = jnp.where(second, lane - WIDE, lane)
            prow = (pplace * 37) >> 8
            pcol = pplace - 7 * prow
            pband = 1 + (prow >= 4).astype(jnp.int32), 1 + (pcol >= 4).astype(jnp.int32)
            qband = 1 + (qrow >= 4).astype(jnp.int32), 1 + (qcol >= 4).astype(jnp.int32)

        def window(j, carry):
            if shifted:
                low = []
                for w in (2 * j, 2 * j + 1):
                    side = table_ref[SIDE + w]
                    low.append(
                        (
                            jnp.where(table_ref[WROW + w] == side - 1, 3, 0),
                            jnp.where(table_ref[WCOL + w] == side - 1, 1, 0),
                        )
                    )
                low_row = jnp.where(second, low[1][0], low[0][0])
                low_col = jnp.where(second, low[1][1], low[0][1])
                pregion = low_row * pband[0] + low_col * pband[1]
                qregion = low_row * qband[0] + low_col * qband[1]
                mask = jnp.where(pregion != qregion, -100.0, 0.0)[None]
            scores, probs = [], []
            for t in range(QUADS):
                q = qkv_ref[j, :, t * 128 : (t + 1) * 128]
                k = qkv_ref[j, :, D + t * 128 : D + (t + 1) * 128]
                scores.append(dot_nt(spread_pair(k, marks), diagonal(q)))
            for t in range(QUADS):
                now = by_head(scores[t] * SCORE_SCALE + bias_ref[layer, t])
                if shifted:
                    now = now + mask
                exponent = jnp.exp(now - jnp.max(now, axis=1, keepdims=True))
                total = jnp.sum(exponent, axis=1, keepdims=True)
                probs.append((exponent * (1.0 / total)).reshape(4 * WIDE, 128).astype(LOW))
                p_ref[j, t] = probs[t]
            for t in range(QUADS):
                cols = slice(t * 128, (t + 1) * 128)
                v = qkv_ref[j, :, 2 * D + t * 128 : 2 * D + (t + 1) * 128]
                both = dot_tn(probs[t], spread_pair(v, marks))
                wide[2 * j, :, cols] = both[0:PAD, 0:128]
                wide[2 * j + 1, :, cols] = both[WIDE : WIDE + PAD, 128:256]
            return carry

        lax.fori_loop(0, bins // 2, window, 0, unroll=9)
        if shifted:
            move_windows(table_ref, wide, tmp, moved, True)
            attn_ref[...] = moved[...].reshape(rows, D).astype(LOW)
        else:
            attn_ref[...] = wide[...].reshape(rows, D).astype(LOW)

        def proj_step(i, carry):
            at = pl.ds(pl.multiple_of(i * chunk, 16), chunk)
            mid_ref[at] = hidden_ref[at] + dot_nn(attn_ref[at], wproj[...]) + proj_shift
            return carry

        lax.fori_loop(0, bins // chunk_slots, proj_step, 0)

    return pl.pallas_call(
        kernel,
        out_shape=(
            jax.ShapeDtypeStruct((rows, D), F32),
            jax.ShapeDtypeStruct((rows, D), LOW),
            jax.ShapeDtypeStruct((bins // 2, 2 * WIDE, 3 * D), LOW),
            jax.ShapeDtypeStruct((bins // 2, QUADS, 4 * WIDE, 128), LOW),
            jax.ShapeDtypeStruct((rows, D), LOW),
        ),
        in_specs=[smem()] + [vmem()] * 8,
        out_specs=[vmem()] * 5,
        scratch_shapes=[
            pltpu.VMEM((3 * D, D), LOW),
            pltpu.VMEM((D, D), LOW),
            pltpu.VMEM((bins, PAD, D), F32),
            pltpu.VMEM((spare, PAD, D), F32),
            pltpu.VMEM((spare, PAD, D), F32),
        ],
        compiler_params=params(11),
        cost_estimate=cost(1e10, 2e7),
        name="attn_forward",
    )(table, hidden, *weights, qv_bias, bias, norms)


def attn_backward(table, grad, qkv, probs, weights, shifted):
    rows = grad.shape[0]
    bins = rows // PAD
    chunk_slots = 6
    chunk = chunk_slots * PAD
    spare = bins if shifted else 2

    def kernel(
        table_ref, grad_ref, qkv_ref, p_ref, w0, w1, w2, w3,
        gqkv_ref, scores_ref, wproj, wide_attn, wide, tmp, moved,
    ):
        stack_proj((w0, w1, w2, w3), wproj)
        marks = head_marks()
        steps = bins // chunk_slots
        def keep_windows(i, block_rows):
            for j in range(chunk_slots):
                block = block_rows[j * PAD : (j + 1) * PAD]
                dest = pl.ds((j % 2) * WIDE, WIDE)
                wide_attn[i * (chunk_slots // 2) + j // 2, dest] = pad_rows(block).astype(LOW)

        def proj_step(i, carry):
            at = pl.ds(pl.multiple_of(i * chunk, 16), chunk)
            gattn = dot_nt(grad_ref[at].astype(LOW), wproj[...])
            if shifted:
                slots = pl.ds(i * chunk_slots, chunk_slots)
                wide[slots] = gattn.reshape(chunk_slots, PAD, D)
            else:
                keep_windows(i, gattn)
            return carry

        lax.fori_loop(0, steps, proj_step, 0)
        if shifted:
            move_windows(table_ref, wide, tmp, moved, False)

            def move_step(i, carry):
                slots = pl.ds(i * chunk_slots, chunk_slots)
                keep_windows(i, moved[slots].reshape(chunk, D))
                return carry

            lax.fori_loop(0, steps, move_step, 0)

        scores_ref[...] = jnp.zeros((QUADS, 4 * WIDE, 128), F32)

        def window(j, carry):
            at = pl.ds(pl.multiple_of(j * 2 * PAD, 16), 2 * PAD)

            def keep(c, t, left, right):
                cols = slice(c * D + t * 128, c * D + (t + 1) * 128)
                gqkv_ref[at, cols] = jnp.concatenate([left, right], axis=0).astype(LOW)

            go, gp, gv, low_ds, gq, gk = [], [], [], [], [], []
            for t in range(QUADS):
                v = qkv_ref[j, :, 2 * D + t * 128 : 2 * D + (t + 1) * 128]
                go.append(diagonal(wide_attn[j, :, t * 128 : (t + 1) * 128]))
                gp.append(dot_nt(spread_pair(v, marks), go[t]))
            for t in range(QUADS):
                gv.append(dot_nn(p_ref[j, t], go[t]))
            for t in range(QUADS):
                p = by_head(p_ref[j, t].astype(F32))
                now = by_head(gp[t])
                ds = p * (now - jnp.sum(now * p, axis=1, keepdims=True))
                low_ds.append(ds.reshape(4 * WIDE, 128).astype(LOW))
                scores_ref[t] += low_ds[t].astype(F32)
            for t in range(QUADS):
                q = qkv_ref[j, :, t * 128 : (t + 1) * 128]
                k = qkv_ref[j, :, D + t * 128 : D + (t + 1) * 128]
                gk.append(dot_nn(low_ds[t], diagonal(q)))
                gq.append(dot_tn(low_ds[t], spread_pair(k, marks)))
            for t in range(QUADS):
                left, right = slice(0, 128), slice(128, 256)
                keep(2, t, fold(gv[t][:, left], marks)[0:PAD], fold(gv[t][:, right], marks)[0:PAD])
            for t in range(QUADS):
                left, right = slice(0, 128), slice(128, 256)
                folded = fold(gk[t][:, left], marks), fold(gk[t][:, right], marks)
                keep(1, t, *[part[0:PAD] * SCORE_SCALE for part in folded])
                parts = gq[t][0:PAD, left], gq[t][WIDE : WIDE + PAD, right]
                keep(0, t, *[part * SCORE_SCALE for part in parts])
            return carry

        lax.fori_loop(0, bins // 2, window, 0, unroll=9)

    return pl.pallas_call(
        kernel,
        out_shape=(
            jax.ShapeDtypeStruct((rows, 3 * D), LOW),
            jax.ShapeDtypeStruct((QUADS, 4 * WIDE, 128), F32),
        ),
        in_specs=[smem()] + [vmem()] * 7,
        out_specs=[vmem()] * 2,
        scratch_shapes=[
            pltpu.VMEM((D, D), LOW),
            pltpu.VMEM((bins // 2, 2 * WIDE, D), LOW),
            pltpu.VMEM((spare, PAD, D), F32),
            pltpu.VMEM((spare, PAD, D), F32),
            pltpu.VMEM((spare, PAD, D), F32),
        ],
        compiler_params=params(11),
        cost_estimate=cost(1e10, 2e7),
        name="attn_backward",
    )(table, grad, qkv, probs, *weights)


def attn_grads(grad, a, attn, gqkv, scores, small_mlp, fc1_bias_grad, weights, norms):
    rows = grad.shape[0]

    def kernel(
        grad_ref, a_ref, attn_ref, gqkv_ref, scores_ref, mlp_ref, fc1b_ref, w0, w1, w2, w3, norm_ref,
        keep_ref, send_ref, wqkv, small,
    ):
        stack_qkv((w0, w1, w2, w3), wqkv)
        gain, shift = norm_ref[0:1], norm_ref[1:2]
        dqkv = dot_tn(a_ref[...], gqkv_ref[...])
        low_grad = grad_ref[...].astype(LOW)
        dproj = dot_tn(attn_ref[...], low_grad).astype(LOW)
        column_sums = jnp.sum(gqkv_ref[...].astype(F32), axis=0, keepdims=True)
        wide_sums = jnp.broadcast_to(column_sums, (16, 3 * D))
        dshift = sum(dot_nn(part, wqkv[...]) for part in split(wide_sums))[0:1]
        table_rows = scores_to_table(scores_ref)
        turned, match = [], jnp.zeros((1, D), F32)
        for c in range(3):
            back = dqkv[:, c * D : (c + 1) * D].T
            here = wqkv[c * D : (c + 1) * D].astype(F32)
            match = match + jnp.sum(back * here, axis=0, keepdims=True)
            turned.append(back.astype(LOW))
        small[...] = jnp.zeros((SMALL, D), F32)
        small[0:1] = (match - shift * dshift) / gain
        small[1:2] = dshift
        small[2:3] = jnp.sum(low_grad.astype(F32), axis=0, keepdims=True)
        small[3:6] = mlp_ref[0:3]
        gq_sum = jnp.broadcast_to(column_sums[:, 0:D], (8, D))
        gv_sum = jnp.broadcast_to(column_sums[:, 2 * D : 3 * D], (8, D))
        for k in range(4):
            dest = keep_ref if k < 2 else send_ref
            for c in range(3):
                dest[k % 2, c * 96 : (c + 1) * 96] = turned[c][k * 96 : (k + 1) * 96]
            dest[k % 2, 288:384] = dproj[k * 96 : (k + 1) * 96]
            small[6:7] = fc1b_ref[:, k * D : (k + 1) * D]
            small[7:8] = pltpu.roll(gq_sum, (D - k * 96) % D, 1)[0:1]
            small[8:9] = pltpu.roll(gv_sum, (D - k * 96) % D, 1)[0:1]
            for h in range(3):
                small[9 + h : 10 + h, 0:256] = table_rows[3 * k + h]
            dest[k % 2, D : D + SMALL] = small[...].astype(LOW)

    return pl.pallas_call(
        kernel,
        out_shape=(
            jax.ShapeDtypeStruct((2, D + SMALL, D), LOW),
            jax.ShapeDtypeStruct((2, D + SMALL, D), LOW),
        ),
        in_specs=[vmem()] * 12,
        out_specs=[vmem()] * 2,
        scratch_shapes=[
            pltpu.VMEM((3 * D, D), LOW),
            pltpu.VMEM((SMALL, D), F32),
        ],
        compiler_params=params(12),
        cost_estimate=cost(6e9, 2e7),
        name="attn_grads",
    )(grad, a, attn, gqkv, scores, small_mlp, fc1_bias_grad, *weights, norms)


def attn_input_grad(table, grad, hidden, gqkv, weights, norms, shifted, work):
    rows = hidden.shape[0]
    bins = rows // PAD
    chunk_slots = 6
    chunk = chunk_slots * PAD
    spare = bins if shifted else 2

    def kernel(
        table_ref, grad_ref, hidden_ref, gqkv_ref, w0, w1, w2, w3, norm_ref,
        out_ref, wqkv, wide, tmp, moved,
    ):
        stack_qkv((w0, w1, w2, w3), wqkv)
        gain = norm_ref[0:1]
        if shifted:
            for i in range(bins // chunk_slots):
                slots = slice(i * chunk_slots, (i + 1) * chunk_slots)
                ga = dot_nn(gqkv_ref[i * chunk : (i + 1) * chunk], wqkv[...])
                wide[slots] = ga.reshape(chunk_slots, PAD, D)
            move_windows(table_ref, wide, tmp, moved, True)

        for i in range(bins // chunk_slots):
            at = slice(i * chunk, (i + 1) * chunk)
            if shifted:
                ga = moved[i * chunk_slots : (i + 1) * chunk_slots].reshape(chunk, D)
            else:
                ga = dot_nn(gqkv_ref[at], wqkv[...])
            scaled, inverse = norm_rows(hidden_ref[at])
            out_ref[at] = grad_ref[at] + norm_back(ga, scaled, inverse, gain)

    return pl.pallas_call(
        kernel,
        out_shape=jax.ShapeDtypeStruct((rows, D), F32),
        in_specs=[smem()] + [vmem()] * 8,
        out_specs=vmem(),
        scratch_shapes=[pltpu.VMEM((3 * D, D), LOW)] + [pltpu.VMEM((spare, PAD, D), F32)] * 3,
        compiler_params=params(12),
        cost_estimate=cost(work, 1e7),
        name="attn_input_grad",
    )(table, grad, hidden, gqkv, *weights, norms)


def mlp_forward(mid, weights, fc1_bias, norms, layer):
    rows = mid.shape[0]
    chunk = 3 * PAD * 2
    steps = rows // chunk

    def kernel(
        mid_ref, w0, w1, w2, w3, fc1_bias_ref, norm_ref,
        out_ref, act_ref, slope_ref, fc1, fc2,
    ):
        stack_mlp((w0, w1, w2, w3), fc1, fc2)
        gain, shift, out_shift = norm_ref[0:1], norm_ref[1:2], norm_ref[2:3]

        def step(i, carry):
            at = pl.ds(pl.multiple_of(i * chunk, 16), chunk)
            rows_now = mid_ref[at]
            scaled, _ = norm_rows(rows_now)
            a = (scaled * gain + shift).astype(LOW)
            act, slope = gelu_parts(dot_nn(a, fc1[...]) + fc1_bias_ref[layer, 0:1])
            act = act.astype(LOW)
            act_ref[at] = act
            slope_ref[at] = slope.astype(LOW)
            out_ref[at] = rows_now + dot_nn(act, fc2[...]) + out_shift
            return carry

        lax.fori_loop(0, steps, step, 0, unroll=True)

    return pl.pallas_call(
        kernel,
        out_shape=(
            jax.ShapeDtypeStruct((rows, D), F32),
            jax.ShapeDtypeStruct((rows, FF), LOW),
            jax.ShapeDtypeStruct((rows, FF), LOW),
        ),
        in_specs=[vmem()] * 7,
        out_specs=[vmem()] * 3,
        scratch_shapes=[pltpu.VMEM((D, FF), LOW), pltpu.VMEM((FF, D), LOW)],
        compiler_params=params(14),
        cost_estimate=cost(7e9, 2e7),
        name="mlp_forward",
    )(mid, *weights, fc1_bias, norms)


def mlp_sums(gpre, a, act, low_grad, fc1, fc1_sums, grad_sums, norms, outs):
    keep_ref, send_ref, small_ref, bias_ref = outs
    gain, shift = norms[0:1], norms[1:2]
    dfc1 = dot_tn(a[...], gpre[...])
    dfc2 = dot_tn(low_grad[...], act[...])
    column = jnp.sum(dfc1 * fc1[...].astype(F32), axis=1, keepdims=True)
    match = jnp.broadcast_to(column, (D, 128)).T
    for k in range(4):
        dest = keep_ref if k < 2 else send_ref
        cols = slice(k * D, (k + 1) * D)
        dest[k % 2, 0:D] = dfc1[:, cols].astype(LOW)
        dest[k % 2, D : 2 * D] = dfc2[:, cols].astype(LOW)
    wide_sums = jnp.broadcast_to(fc1_sums, (16, FF))
    dshift = sum(dot_nt(part, fc1[...]) for part in split(wide_sums))[0:1]
    small_ref[0:1] = (match[0:1] - shift * dshift) / gain
    small_ref[1:2] = dshift
    small_ref[2:3] = grad_sums
    small_ref[3:8] = jnp.zeros((5, D), F32)
    bias_ref[...] = fc1_sums


def sums_shapes():
    return (
        jax.ShapeDtypeStruct((2, 2 * D, D), LOW),
        jax.ShapeDtypeStruct((2, 2 * D, D), LOW),
        jax.ShapeDtypeStruct((8, D), F32),
        jax.ShapeDtypeStruct((1, FF), F32),
    )


def mlp_backward(grad, mid, act, slope, weights, norms):
    rows = mid.shape[0]
    chunk = 6 * PAD
    steps = rows // chunk

    def kernel(
        grad_ref, mid_ref, act_ref, slope_ref, w0, w1, w2, w3, norm_ref,
        gpre_ref, keep_ref, send_ref, small_ref, bias_ref, fc1, fc2, low_grad, a_ref,
    ):
        stack_mlp((w0, w1, w2, w3), fc1, fc2)
        gain, shift = norm_ref[0:1], norm_ref[1:2]
        fc1_sums, grad_sums = jnp.zeros((1, FF), F32), jnp.zeros((1, D), F32)
        for i in range(steps):
            at = slice(i * chunk, (i + 1) * chunk)
            gz = grad_ref[at].astype(LOW)
            low_grad[at] = gz
            gpre = (dot_nt(gz, fc2[...]) * slope_ref[at].astype(F32)).astype(LOW)
            gpre_ref[at] = gpre
            scaled, _ = norm_rows(mid_ref[at])
            a_ref[at] = (scaled * gain + shift).astype(LOW)
            fc1_sums = fc1_sums + jnp.sum(gpre.astype(F32), axis=0, keepdims=True)
            grad_sums = grad_sums + jnp.sum(gz.astype(F32), axis=0, keepdims=True)
        outs = keep_ref, send_ref, small_ref, bias_ref
        mlp_sums(gpre_ref, a_ref, act_ref, low_grad, fc1, fc1_sums, grad_sums, norm_ref, outs)

    return pl.pallas_call(
        kernel,
        out_shape=(jax.ShapeDtypeStruct((rows, FF), LOW), *sums_shapes()),
        in_specs=[vmem()] * 9,
        out_specs=[vmem()] * 5,
        scratch_shapes=[
            pltpu.VMEM((D, FF), LOW),
            pltpu.VMEM((FF, D), LOW),
            pltpu.VMEM((rows, D), LOW),
            pltpu.VMEM((rows, D), LOW),
        ],
        compiler_params=params(18),
        cost_estimate=cost(7e9, 2e7),
        name="mlp_backward",
    )(grad, mid, act, slope, *weights, norms)


def mlp_turn(mid, grad, weights, fc1_bias, norms, layer):
    rows = mid.shape[0]
    chunk = 6 * PAD
    steps = rows // chunk

    def kernel(
        mid_ref, grad_ref, w0, w1, w2, w3, fc1_bias_ref, norm_ref,
        out_ref, gpre_ref, keep_ref, send_ref, small_ref, bias_ref,
        fc1, fc2, a_all, act_all, low_grad,
    ):
        stack_mlp((w0, w1, w2, w3), fc1, fc2)
        gain, shift, out_shift = norm_ref[0:1], norm_ref[1:2], norm_ref[2:3]

        def step(i, totals):
            at = pl.ds(pl.multiple_of(i * chunk, 16), chunk)
            rows_now = mid_ref[at]
            scaled, _ = norm_rows(rows_now)
            a = (scaled * gain + shift).astype(LOW)
            a_all[at] = a
            act, slope = gelu_parts(dot_nn(a, fc1[...]) + fc1_bias_ref[layer, 0:1])
            act = act.astype(LOW)
            act_all[at] = act
            out_ref[at] = rows_now + dot_nn(act, fc2[...]) + out_shift
            gz = grad_ref[at].astype(LOW)
            low_grad[at] = gz
            gpre = (dot_nt(gz, fc2[...]) * slope).astype(LOW)
            gpre_ref[at] = gpre
            return (
                totals[0] + jnp.sum(gz.astype(F32), axis=0, keepdims=True),
                totals[1] + jnp.sum(gpre.astype(F32), axis=0, keepdims=True),
            )

        zeros = jnp.zeros((1, D), F32), jnp.zeros((1, FF), F32)
        grad_sums, fc1_sums = lax.fori_loop(0, steps, step, zeros, unroll=True)
        outs = keep_ref, send_ref, small_ref, bias_ref
        mlp_sums(gpre_ref, a_all, act_all, low_grad, fc1, fc1_sums, grad_sums, norm_ref, outs)

    return pl.pallas_call(
        kernel,
        out_shape=(
            jax.ShapeDtypeStruct((rows, D), F32),
            jax.ShapeDtypeStruct((rows, FF), LOW),
            *sums_shapes(),
        ),
        in_specs=[vmem()] * 8,
        out_specs=[vmem()] * 6,
        scratch_shapes=[
            pltpu.VMEM((D, FF), LOW),
            pltpu.VMEM((FF, D), LOW),
            pltpu.VMEM((rows, D), LOW),
            pltpu.VMEM((rows, FF), LOW),
            pltpu.VMEM((rows, D), LOW),
        ],
        compiler_params=params(22),
        cost_estimate=cost(1.5e10, 4e7),
        name="mlp_turn",
    )(mid, grad, *weights, fc1_bias, norms)


def mlp_input_grad(grad, mid, gpre, weights, norms):
    rows = mid.shape[0]
    chunk = 6 * PAD

    def kernel(grad_ref, mid_ref, gpre_ref, w0, w1, w2, w3, norm_ref, out_ref, fc1):
        for k, piece in enumerate((w0, w1, w2, w3)):
            fc1[:, k * D : (k + 1) * D] = piece[0:D]
        gain = norm_ref[0:1]
        for i in range(rows // chunk):
            at = slice(i * chunk, (i + 1) * chunk)
            ga = dot_nt(gpre_ref[at], fc1[...])
            scaled, inverse = norm_rows(mid_ref[at])
            out_ref[at] = grad_ref[at] + norm_back(ga, scaled, inverse, gain)

    return pl.pallas_call(
        kernel,
        out_shape=jax.ShapeDtypeStruct((rows, D), F32),
        in_specs=[vmem()] * 8,
        out_specs=vmem(),
        scratch_shapes=[pltpu.VMEM((D, FF), LOW)],
        compiler_params=params(8),
        cost_estimate=cost(3e12, 1e7),
        name="mlp_input_grad",
    )(grad, mid, gpre, *weights, norms)


def finish(side, total_a, state_b, state_c, state_d):
    def kernel(
        side_ref, a_ref, b0, b1, c0, c1, d0, d1,
        qkv_ref, proj_ref, fc1_ref, fc2_ref, gains_ref, shifts_ref, fc1b_ref, qv_ref, table_ref,
        rows,
    ):
        first = side_ref[0:1] > 0

        def join(value, other):
            value, other = value[...].astype(F32), other[...].astype(F32)
            return jnp.where(first, value, other), jnp.where(first, other, value)

        half = (D + SMALL) // 2
        rows[0] = d0[...].astype(F32) + d1[...].astype(F32)
        rows[1, 0:half], rows[1, half:] = join(b0, b1)
        fc1_ref[0], fc2 = join(c0, c1)
        fc2_ref[0] = fc2.T
        fc1_ref[1] = a_ref[0:D].astype(F32)
        fc2_ref[1] = a_ref[D : 2 * D].astype(F32).T
        for l in range(LAYERS):
            qkv_ref[l] = rows[l, 0:288]
            proj_ref[l] = rows[l, 288:384]
            now = rows[l, D : D + SMALL]
            for i, row in enumerate((0, 3)):
                gains_ref[l, i : i + 1] = now[row : row + 1]
            for i, row in enumerate((1, 4, 2, 5)):
                shifts_ref[l, i : i + 1] = now[row : row + 1]
            fc1b_ref[l : l + 1] = now[6:7]
            qv_ref[l] = now[7:9, 0:96]
            turned = now[8:16, 0:256].T
            table_ref[l] = turned[0:169, 1:4]

    return pl.pallas_call(
        kernel,
        out_shape=(
            jax.ShapeDtypeStruct((LAYERS, 288, D), F32),
            jax.ShapeDtypeStruct((LAYERS, 96, D), F32),
            jax.ShapeDtypeStruct((LAYERS, D, D), F32),
            jax.ShapeDtypeStruct((LAYERS, D, D), F32),
            jax.ShapeDtypeStruct((LAYERS, 2, D), F32),
            jax.ShapeDtypeStruct((LAYERS, 4, D), F32),
            jax.ShapeDtypeStruct((LAYERS, D), F32),
            jax.ShapeDtypeStruct((LAYERS, 2, 96), F32),
            jax.ShapeDtypeStruct((LAYERS, 169, 3), F32),
        ),
        in_specs=[vmem()] * 8,
        out_specs=[vmem()] * 9,
        scratch_shapes=[pltpu.VMEM((LAYERS, D + SMALL, D), F32)],
        compiler_params=params(14),
        cost_estimate=cost(0, 1e6),
        name="finish",
    )(side, total_a, *state_b, *state_c, *state_d)


def swap_core(value):
    return lax.ppermute(value, "head", [(i, i ^ 1) for i in range(4)])


def swap_chip(value):
    return lax.ppermute(value, "head", [(i, i ^ 2) for i in range(4)])


def swap_border(value):
    return lax.ppermute(value, "head", [(1, 2), (2, 1)])


def swap_dp(value, step, size):
    return lax.ppermute(value, "dp", [(i, i ^ step) for i in range(size)])


def tie(*values):
    return lax.optimization_barrier(values)


def pick(first, one, other):
    first = first > 0
    return jnp.where(first, one, other), jnp.where(first, other, one)


def dp_masks(order):
    size = lax.axis_size("dp")
    upper = [(2 << b) - 2 for b in range(1, size.bit_length() - 1)]
    if order == 1 and upper:
        return [upper[-1]] + upper[:-1] + [1]
    return [1] + (upper if order == 2 else upper[::-1])


def dp_start(parts, sides, order):
    half = parts[0].shape[0] // 2
    low = sum(p[:half].astype(F32) for p in parts)
    high = sum(p[half:].astype(F32) for p in parts)
    masks = dp_masks(order)
    kept, sent = pick(sides[order % 2], low, high)
    return kept, swap_dp(sent.astype(LOW), masks[0], lax.axis_size("dp"))


def dp_next(kept, other, order, stage):
    masks = dp_masks(order)
    value = (kept.astype(F32) + other.astype(F32)).astype(LOW)
    return value, swap_dp(value, (masks + masks[:1])[stage], lax.axis_size("dp"))


def dp_whole(value, other, stage):
    masks = dp_masks(2)
    value = (value.astype(F32) + other.astype(F32)).astype(LOW)
    return value, swap_dp(value, masks[stage], lax.axis_size("dp"))


def dp_join(value, other, sides, order):
    low, high = pick(sides[order % 2], value, other)
    return jnp.concatenate([low, high])


def body(
    tokens, outputs_grad, image_kind, qkv_weight, qv_bias, bias_table, proj_weight,
    fc1_weight, fc1_bias, fc2_weight, gains, shifts,
):
    own = tokens.shape[0] // PLACES
    bins = own + 2
    me = lax.axis_index("head").astype(jnp.int32)

    def border(value):
        edge = 4 * PLACES
        return swap_border(jnp.where(me == 1, value[-edge:], value[:edge]))

    turned = jnp.transpose(qkv_weight, (0, 2, 3, 1)).reshape(LAYERS, 288, D)

    def attn_pack(l):
        return jnp.concatenate([turned[l], proj_weight[l]], axis=0)

    def mlp_pack(l):
        return jnp.concatenate([fc1_weight[l], fc2_weight[l]], axis=0)

    def norm_pack(l, which, bias_row):
        rows = jnp.stack([gains[l, which], shifts[l, which], shifts[l, bias_row]])
        return jnp.pad(rows, ((0, 5), (0, 0)))

    partner = swap_core(tokens)
    rows = jnp.pad(jnp.transpose(bias_table, (0, 2, 1)).reshape(6, 169), ((0, 0), (0, D - 169)))
    small = jnp.concatenate([rows, qv_bias.reshape(1, D), fc1_bias])
    small = jnp.pad(small, ((0, SMALL - 9), (0, 0)))
    own_pack = [jnp.concatenate([attn_pack(0), *split(small)])]
    chip_pack = [swap_chip(own_pack[0])]
    edges, _ = tie(tokens, own_pack[0])
    halo = border(edges)
    place = lax.axis_index("dp")
    top = lax.axis_size("dp") // 2
    sides = [1 - (place & 1), (place < top).astype(jnp.int32)]
    first = jnp.broadcast_to(jnp.stack(sides).astype(jnp.int32)[:, None], (2, D))
    table = make_plan(image_kind, me, own, bins)
    mlp_first = mlp_pack(0)
    table, first, chip_pack[0], partner, mlp_first = tie(
        table, first, chip_pack[0], partner, mlp_first
    )
    sides = [first[0:1], first[1:2]]
    hidden = gather_slots(table, tokens, partner, halo, bins)

    def gathered(i):
        p, c = own_pack[i], chip_pack[i]
        return p, c, swap_core(p), swap_core(c)

    pack, halo, _ = tie(mlp_first, halo, chip_pack[0])
    own_pack.append(pack)
    chip_pack.append(swap_chip(pack))
    first_weights = gathered(0)
    bias, qkv_bias, fc1_all = spread_smalls(first_weights)

    saved, weights = [], []
    last = LAYERS - 1
    for l in range(LAYERS):
        norms, mlp_norms = norm_pack(l, 0, 2), norm_pack(l, 1, 3)
        weights.append(first_weights if l == 0 else gathered(2 * l))
        mid, a, qkv, probs, attn = attn_forward(
            table, hidden, weights[2 * l], qkv_bias, bias, norms, l
        )
        mid, chip_pack[2 * l + 1] = tie(mid, chip_pack[2 * l + 1])
        weights.append(gathered(2 * l + 1))
        if l == last:
            saved.append((hidden, mid, a, qkv, probs, attn, norms, mlp_norms))
            break
        pack, outputs_grad, mid = tie(attn_pack(1), outputs_grad, mid)
        grad_partner, grad_halo = swap_core(outputs_grad), border(outputs_grad)
        own_pack.append(pack)
        chip_pack.append(swap_chip(pack))
        out, act, slope = mlp_forward(mid, weights[2 * l + 1], fc1_all, mlp_norms, l)
        pack, out, chip_pack[2], grad_partner, grad_halo = tie(
            mlp_pack(1), out, chip_pack[2], grad_partner, grad_halo
        )
        own_pack.append(pack)
        chip_pack.append(swap_chip(pack))
        saved.append((hidden, mid, a, qkv, probs, attn, norms, mlp_norms, act, slope))
        hidden = out
    grad = gather_slots(table, outputs_grad, grad_partner, grad_halo, bins)

    def give_back(value):
        slots = value.reshape(bins, PAD, D)
        return slots, swap_core(slots), swap_border(border_slots(table, slots, 0))

    def mlp_back(l, grad):
        return mlp_backward(
            grad, saved[l][1], saved[l][8], saved[l][9], weights[2 * l + 1], saved[l][7]
        )

    def mlp_input(l, grad, gpre):
        return mlp_input_grad(grad, saved[l][1], gpre, weights[2 * l + 1], saved[l][7])

    def attn_back(l, grad):
        return attn_backward(table, grad, saved[l][3], saved[l][4], weights[2 * l], l % 2 == 1)

    def attn_sums(l, grad, gqkv, scores, small_mlp, fc1_bias_grad):
        return attn_grads(
            grad, saved[l][2], saved[l][5], gqkv, scores, small_mlp, fc1_bias_grad,
            weights[2 * l], saved[l][6],
        )

    def attn_input(l, grad, gqkv):
        work = 6e9 if l == last else 3e12
        return attn_input_grad(
            table, grad, saved[l][0], gqkv, weights[2 * l], saved[l][6], l % 2 == 1, work
        )

    def core_sum(keep, other):
        return [(keep[i].astype(F32) + other[i].astype(F32)).astype(LOW) for i in range(2)]

    out, gpre, keep_a, send_a, small_mlp, fc1_bias_grad = mlp_turn(
        saved[last][1], grad, weights[2 * last + 1], fc1_all, saved[last][7], last
    )
    core_a = swap_core(send_a)
    grad = mlp_input(1, grad, gpre)
    grad, core_a = tie(grad, core_a)
    half_a, out_a = core_sum(keep_a, core_a)
    grad, out_a = tie(grad, out_a)
    chip_a = swap_chip(out_a)
    gqkv, scores = attn_back(1, grad)
    grad_after = attn_input(1, grad, gqkv)
    gqkv, _ = tie(gqkv, grad_after)
    keep_b, send_b = attn_sums(1, grad, gqkv, scores, small_mlp, fc1_bias_grad)
    grad, send_b, chip_a = tie(grad_after, send_b, chip_a)
    core_b = swap_core(send_b)
    state_a = dp_start((half_a, chip_a), sides, 2)
    half_b, out_b = core_sum(keep_b, core_b)
    grad, out_b = tie(grad, out_b)
    chip_b = swap_chip(out_b)
    gpre, keep_c, send_c, small_mlp, fc1_bias_grad = mlp_back(0, grad)
    gpre, send_c, state_a, chip_b = tie(gpre, send_c, state_a, chip_b)
    core_c = swap_core(send_c)
    state_a = dp_next(*state_a, 2, 1)
    grad = mlp_input(0, grad, gpre)
    grad, core_c = tie(grad, core_c)
    state_b = dp_start((half_b, chip_b), sides, 2)
    half_c, out_c = core_sum(keep_c, core_c)
    grad, out_c = tie(grad, out_c)
    chip_c = swap_chip(out_c)
    gqkv, scores = attn_back(0, grad)
    gqkv, state_a, state_b = tie(gqkv, state_a, state_b)
    state_a = dp_next(*state_a, 2, 2)
    state_b = dp_next(*state_b, 2, 1)
    keep_d, send_d = attn_sums(0, grad, gqkv, scores, small_mlp, fc1_bias_grad)
    core_d = swap_core(send_d)
    out, chip_c, _ = tie(out, chip_c, send_d)
    state_c = dp_start((half_c, chip_c), sides, 2)
    out_slots = out.reshape(bins, PAD, D)
    out_edge, core_d = tie(border_slots(table, out_slots, 3e12), core_d)
    half_d, out_d = core_sum(keep_d, core_d)
    chip_d = swap_chip(out_d)
    gqkv, out_slots, out_edge, _ = tie(gqkv, out_slots, out_edge, out_d)
    grad = attn_input(0, grad, gqkv)
    output_parts = out_slots, swap_core(out_slots), swap_border(out_edge)
    chip_d, state_a, state_b, state_c = tie(chip_d, state_a, state_b, state_c)
    state_d = dp_whole(half_d, chip_d, 0)
    state_c = dp_next(*state_c, 2, 1)
    state_b = dp_next(*state_b, 2, 2)
    tokens_parts = give_back(grad)
    state_d, state_c, state_b = tie(state_d, state_c, state_b)
    state_d = dp_whole(*state_d, 1)
    state_c = dp_next(*state_c, 2, 2)
    state_a = dp_next(*state_a, 2, 3)
    state_b = dp_next(*state_b, 2, 3)
    output = return_slots(table, *output_parts, own)
    state_d, state_c, state_a, state_b = tie(state_d, state_c, state_a, state_b)
    state_d = dp_whole(*state_d, 2)
    state_c = dp_next(*state_c, 2, 3)
    tokens_grad = return_slots(table, *tokens_parts, own)
    total_a = dp_join(*state_a, sides, 2)
    state_d, state_c, output, tokens_grad = tie(state_d, state_c, output, tokens_grad)
    qkv_out, proj_out, fc1_out, fc2_out, *smalls = finish(
        sides[0], total_a, state_b, state_c, state_d
    )
    gains_out, shifts_out, fc1_bias_out, qv_out, table_out = smalls
    qkv_out = qkv_out.reshape(LAYERS, 3, 96, D).transpose(0, 3, 1, 2)
    return (
        output, tokens_grad, qkv_out, qv_out, table_out, proj_out, fc1_out, fc1_bias_out,
        fc2_out, gains_out, shifts_out,
    )


def solution(mesh):
    rows = P(("dp", "head"), None)
    placed = (
        rows,
        rows,
        P("dp", None),
        P(None, None, None, "head"),
        P(None, None, "head"),
        P(None, None, "head"),
        P(None, "head", None),
        P(None, None, "head"),
        P(None, "head"),
        P(None, "head", None),
        P(),
        P(),
    )
    return jax.shard_map(
        body,
        mesh=mesh,
        in_specs=placed,
        out_specs=(
            rows,
            rows,
            P(None, None, None, "head"),
            P(None, None, "head"),
            P(None, None, "head"),
            P(None, "head", None),
            P(None, None, "head"),
            P(None, "head"),
            P(None, "head", None),
            P(),
            P(),
        ),
        check_vma=False,
    )
```

```python
import jax
import jax.numpy as jnp
from jax import lax
from jax.experimental import pallas as pl
from jax.experimental.pallas import tpu as pltpu
from jax.sharding import PartitionSpec as P

D = 384
FF = 1536
LAYERS = 2
PLACES = 49
PAD = 56
WIDE = 64
QUADS = 3
HEAD_DIM = 32
SCORE_SCALE = HEAD_DIM**-0.5
LN_EPS = 1e-05
LOW = jnp.bfloat16
F32 = jnp.float32
MIB = 1024 * 1024
SMALL = 16

SRC, SIDE, WROW, WCOL, FIRST, RET, SEND = 0, 24, 48, 72, 96, 120, 140
TABLE = 144


def vmem():
    return pl.BlockSpec(memory_space=pltpu.VMEM)


def smem():
    return pl.BlockSpec(memory_space=pltpu.SMEM)


def anywhere():
    return pl.BlockSpec(memory_space=pl.ANY)


def params(limit):
    return pltpu.CompilerParams(vmem_limit_bytes=limit * MIB)


def cost(flops, size):
    return pl.CostEstimate(flops=int(flops * 0.02), bytes_accessed=int(size * 0.02), transcendentals=0)


def dot_nn(a, b):
    return lax.dot_general(a, b, (((1,), (0,)), ((), ())), preferred_element_type=F32)


def dot_nt(a, b):
    return lax.dot_general(a, b, (((1,), (1,)), ((), ())), preferred_element_type=F32)


def dot_tn(a, b):
    return lax.dot_general(a, b, (((0,), (0,)), ((), ())), preferred_element_type=F32)


def plan_kernel(own, bins, kind_ref, me_ref, out_ref, load_ref):
    me = me_ref[0]
    half = 2 * own
    for i in range(TABLE):
        out_ref[i] = -1 if i < bins or RET <= i < RET + own else 0
    for i in range(bins):
        out_ref[SIDE + i] = 1
        out_ref[FIRST + i] = i
    for i in range(4):
        load_ref[i] = 0

    def place(start, count, side, bin_id):
        base = load_ref[bin_id]
        load_ref[bin_id] = base + count

        def step(k, carry):
            slot = start + k
            owner = slot // own
            inner = slot - owner * own
            local = base + k
            mine = bin_id == me
            halo = jnp.where(me == 1, slot - half, slot - half + 4)
            code = jnp.where(
                owner == me, inner, jnp.where(owner == (me ^ 1), own + inner, 2 * own + halo)
            )

            @pl.when(mine)
            def _():
                wrow = k // side
                out_ref[SRC + local] = code
                out_ref[SIDE + local] = side
                out_ref[WROW + local] = wrow
                out_ref[WCOL + local] = k - wrow * side
                out_ref[FIRST + local] = base

            @pl.when(owner == me)
            def _():
                back = jnp.where(me == 2, slot - half, k)
                out_ref[RET + inner] = jnp.where(
                    mine, local, jnp.where(bin_id == (me ^ 1), bins + local, 2 * bins + back)
                )

            return carry

        lax.fori_loop(0, count, step, 0)

    for turn in range(3):

        def visit(i, start, turn=turn):
            kind = kind_ref[0, i]
            count = jnp.where(kind == 2, 9, jnp.where(kind == 1, 4, 0))
            side = jnp.where(kind == 2, 3, 2)
            cut = half - start
            across = (cut > 0) & (cut < count)
            second = (start >= half) | (across & (cut < count - cut))
            chip = jnp.where(second, 1, 0)
            left, right = load_ref[2 * chip], load_ref[2 * chip + 1]
            emptier = 2 * chip + jnp.where(left <= right, 0, 1)
            if turn == 0:
                chosen, bin_id = across, 1 + chip
            else:
                chosen, bin_id = (kind == 3 - turn) & jnp.logical_not(across), emptier

            @pl.when(chosen)
            def _():
                place(start, count, side, bin_id)
                if turn == 0:
                    out_ref[SEND] = jnp.where((me == 1) & (chip == 0), cut, 0)

            return start + count

        lax.fori_loop(0, kind_ref.shape[1], visit, jnp.int32(0))


def gather_kernel(bins, table_ref, refs, out_ref, spread_ref):
    spread_ref[...] = jnp.zeros(spread_ref.shape, F32)
    at = 0
    for ref in refs:
        for s in range(ref.shape[0] // PLACES):
            spread_ref[at, 0:PLACES] = ref[s * PLACES : (s + 1) * PLACES].astype(F32)
            at += 1

    def step(j, carry):
        src = table_ref[SRC + j]

        @pl.when(src < 0)
        def _():
            out_ref[j] = jnp.zeros((PAD, D), F32)

        @pl.when(src >= 0)
        def _():
            out_ref[j] = spread_ref[src]

        return carry

    lax.fori_loop(0, bins, step, 0)


def make_plan(image_kind, me, own, bins):
    def kernel(kind_ref, me_ref, table_ref, load_ref):
        plan_kernel(own, bins, kind_ref, me_ref, table_ref, load_ref)

    return pl.pallas_call(
        kernel,
        out_shape=jax.ShapeDtypeStruct((TABLE,), jnp.int32),
        in_specs=[smem(), smem()],
        out_specs=smem(),
        scratch_shapes=[pltpu.SMEM((4,), jnp.int32)],
        compiler_params=params(1),
        cost_estimate=cost(0, 1.5e7),
        name="plan",
    )(image_kind, me.reshape(1))


def gather_slots(table, mine, partner, halo, bins):
    own = mine.shape[0] // PLACES

    def kernel(table_ref, *refs):
        gather_kernel(bins, table_ref, refs[:3], refs[3], refs[4])

    out = pl.pallas_call(
        kernel,
        out_shape=jax.ShapeDtypeStruct((bins, PAD, D), F32),
        in_specs=[smem()] + [vmem()] * 3,
        out_specs=vmem(),
        scratch_shapes=[pltpu.VMEM((2 * own + 4, PAD, D), F32)],
        compiler_params=params(8),
        cost_estimate=cost(0, 8e6),
        name="gather_slots",
    )(table, mine, partner, halo)
    return out.reshape(bins * PAD, D)


def border_slots(table, slots, work):
    def kernel(table_ref, slots_ref, out_ref):
        start = table_ref[SEND]
        for j in range(4):
            out_ref[j] = slots_ref[start + j]

    return pl.pallas_call(
        kernel,
        out_shape=jax.ShapeDtypeStruct((4,) + slots.shape[1:], F32),
        in_specs=[smem(), vmem()],
        out_specs=vmem(),
        compiler_params=params(4),
        cost_estimate=cost(work, 1e6),
        name="border_slots",
    )(table, slots)


def return_slots(table, mine, partner, halo, own):
    bins = mine.shape[0]

    def kernel(table_ref, mine_ref, partner_ref, halo_ref, out_ref):
        for s in range(own):
            src = table_ref[RET + s]
            rows = pl.ds(s * PLACES, PLACES)

            @pl.when(src < 0)
            def _():
                out_ref[rows] = jnp.zeros((PLACES, D), F32)

            @pl.when((src >= 0) & (src < bins))
            def _():
                out_ref[rows] = mine_ref[src, 0:PLACES]

            @pl.when((src >= bins) & (src < 2 * bins))
            def _():
                out_ref[rows] = partner_ref[src - bins, 0:PLACES]

            @pl.when(src >= 2 * bins)
            def _():
                out_ref[rows] = halo_ref[src - 2 * bins, 0:PLACES]

    return pl.pallas_call(
        kernel,
        out_shape=jax.ShapeDtypeStruct((own * PLACES, D), F32),
        in_specs=[smem(), vmem(), vmem(), vmem()],
        out_specs=vmem(),
        compiler_params=params(8),
        cost_estimate=cost(0, 8e6),
        name="return_slots",
    )(table, mine, partner, halo)


def norm_rows(rows):
    average = jnp.mean(rows, axis=-1, keepdims=True)
    centred = rows - average
    inverse = lax.rsqrt(jnp.mean(centred * centred, axis=-1, keepdims=True) + LN_EPS)
    return centred * inverse, inverse


def norm_back(incoming, scaled, inverse, gain):
    weighted = incoming * gain
    return inverse * (
        weighted
        - jnp.mean(weighted, axis=-1, keepdims=True)
        - scaled * jnp.mean(weighted * scaled, axis=-1, keepdims=True)
    )


def gelu_parts(x):
    t = 1.0 / (1.0 + 0.23164189 * jnp.abs(x))
    bell = jnp.exp2(x * x * -0.7213475204444817)
    poly = t * (
        0.127414796 + t * (-0.142248368 + t * (0.7107068705 + t * (-0.7265760135 + t * 0.5307027145)))
    )
    tail = poly * bell
    phi = jnp.where(x >= 0, 1.0 - tail, tail)
    return x * phi, phi + x * bell * 0.3989422804014327


def place_parts(shape, dim):
    place = lax.broadcasted_iota(jnp.int32, shape, dim)
    row = (place * 37) >> 8
    return place, row, place - 7 * row


def neighbour(table_ref, w, back, down):
    side, wrow, wcol = table_ref[SIDE + w], table_ref[WROW + w], table_ref[WCOL + w]
    at = wrow if down else wcol
    if back:
        other = jnp.where(at == 0, side - 1, at - 1)
    else:
        other = jnp.where(at == side - 1, 0, at + 1)
    if down:
        return table_ref[FIRST + w] + other * side + wcol
    return table_ref[FIRST + w] + wrow * side + other


def move_windows(table_ref, src, tmp, out, back):
    bins = src.shape[0]
    tmp[...] = jnp.zeros(tmp.shape, F32)
    out[...] = jnp.zeros(out.shape, F32)

    def rows(w, carry):
        other = neighbour(table_ref, w, back, True)
        if back:
            tmp[w, 21:49] = src[w, 0:28]
            tmp[w, 0:21] = src[other, 28:49]
        else:
            tmp[w, 0:28] = src[w, 21:49]
            tmp[w, 28:49] = src[other, 0:21]
        return carry

    lax.fori_loop(0, bins, rows, 0, unroll=2)
    _, _, col = place_parts((PAD, 1), 0)

    def cols(w, carry):
        other = neighbour(table_ref, w, back, False)
        if back:
            out[w, 0:49] = tmp[other, 4:53]
            out[w, 3:49] = jnp.where(col[3:49] >= 3, tmp[w, 0:46], out[w, 3:49])
        else:
            out[w, 0:49] = tmp[w, 3:52]
            out[w, 4:49] = jnp.where(col[4:49] < 4, out[w, 4:49], tmp[other, 0:45])
        return carry

    lax.fori_loop(0, bins, cols, 0, unroll=2)


def head_marks():
    lane = lax.broadcasted_iota(jnp.int32, (WIDE, 128), 1) // HEAD_DIM
    return [jnp.where(lane == h, 1.0, 0.0).astype(LOW) for h in range(4)]


def spread(block, marks):
    return jnp.concatenate([block * mark for mark in marks], axis=0)


def fold(product, marks):
    total = None
    for h, mark in enumerate(marks):
        part = product[h * WIDE : (h + 1) * WIDE] * mark.astype(F32)
        total = part if total is None else total + part
    return total


def spread_pair(block, marks):
    return jnp.concatenate([spread(block[0:WIDE], marks), spread(block[WIDE:], marks)], axis=1)


def diagonal(block):
    zero = jnp.zeros((WIDE, 128), block.dtype)
    top = jnp.concatenate([block[0:WIDE], zero], axis=1)
    return jnp.concatenate([top, jnp.concatenate([zero, block[WIDE:]], axis=1)], axis=0)


def by_head(values):
    return values.reshape(4, WIDE, 128)


def pad_rows(rows):
    return jnp.concatenate([rows, jnp.zeros((WIDE - PAD, rows.shape[1]), rows.dtype)], axis=0)


def split(values):
    high = values.astype(LOW)
    return high, (values - high.astype(F32)).astype(LOW)


def marks_where(rows, cols, test):
    row = lax.broadcasted_iota(jnp.int32, (rows, cols), 0)
    col = lax.broadcasted_iota(jnp.int32, (rows, cols), 1)
    return jnp.where(test(row, col), 1.0, 0.0).astype(LOW)


def far(place):
    row = (place * 37) >> 8
    return 13 * row + (place - 7 * row)


def spread_smalls(smalls):
    heads = LAYERS * 12

    def kernel(p0, p1, p2, p3, out_ref, qkv_ref, fc1_ref, table_ref, small_ref):
        quarters = []
        for k, ref in enumerate((p0, p1, p2, p3)):
            high, low = ref[D : D + SMALL], ref[D + SMALL : D + 2 * SMALL]
            small_ref[k] = high.astype(F32) + low.astype(F32)
            quarters.append(small_ref.at[k])
        for k, ref in enumerate(quarters):
            for l in range(LAYERS):
                at = l * 12 + k * 3
                table_ref[at : at + 3] = ref[l * 3 : l * 3 + 3, 0:256]
        lane = lax.broadcasted_iota(jnp.int32, (8, D), 1)
        for l in range(LAYERS):
            for c in range(3):
                total = jnp.zeros((8, D), F32)
                for k, ref in enumerate(quarters):
                    if c != 1:
                        row = jnp.broadcast_to(ref[6:7], (8, D))
                        row = pltpu.roll(row, (k * 96 - l * 192 - (c // 2) * 96) % D, 1)
                        own_lanes = (lane >= k * 96) & (lane < k * 96 + 96)
                        total = total + jnp.where(own_lanes, row, 0.0)
                qkv_ref[l, :, c * D : (c + 1) * D] = total
            for k, ref in enumerate(quarters):
                row = jnp.broadcast_to(ref[7 + l : 8 + l], (8, D))
                fc1_ref[l, :, k * D : (k + 1) * D] = row
        to_lane = marks_where(128, 128, lambda r, c: (far(c & 63) == r) & ((c & 63) < PLACES))
        to_row = marks_where(WIDE, 96, lambda r, c: (far(r) == c) & (r < PLACES))
        place = lax.broadcasted_iota(jnp.int32, (WIDE, 128), 0)
        empty = jnp.where(place < PLACES, 0.0, -1e30)
        turned = pltpu.roll(table_ref[...], 172, 1)
        skewed = []
        for n in range(heads):
            row = jnp.broadcast_to(turned[n : n + 1], (96, 256))
            skewed.append(pltpu.roll(row, 0, 1, stride=1, stride_axis=0)[:, 0:128])
        skewed = jnp.concatenate(skewed, axis=1)
        total = None
        for part in split(skewed):
            rows = dot_nn(to_row, part).astype(LOW)
            rows = jnp.concatenate([rows[:, n * 128 : (n + 1) * 128] for n in range(heads)], axis=0)
            part = dot_nn(rows, to_lane)
            total = part if total is None else total + part
        for n in range(heads):
            l, t, h = n // 12, n % 12 // 4, n % 4
            out_ref[l, t, h * WIDE : (h + 1) * WIDE] = total[n * WIDE : (n + 1) * WIDE] + empty

    return pl.pallas_call(
        kernel,
        out_shape=(
            jax.ShapeDtypeStruct((LAYERS, QUADS, 4 * WIDE, 128), F32),
            jax.ShapeDtypeStruct((LAYERS, 8, 3 * D), F32),
            jax.ShapeDtypeStruct((LAYERS, 8, FF), F32),
        ),
        in_specs=[vmem()] * 4,
        out_specs=[vmem()] * 3,
        scratch_shapes=[pltpu.VMEM((heads, 256), F32), pltpu.VMEM((4, SMALL, D), F32)],
        compiler_params=params(6),
        cost_estimate=cost(0, 1e7),
        name="spread_smalls",
    )(*smalls)


def scores_to_table(scores_ref):
    to_far = marks_where(128, 128, lambda r, c: (far(r & 63) == c) & ((r & 63) < PLACES))
    to_row = marks_where(96, WIDE, lambda r, c: (84 - far(c) == r) & (c < PLACES))
    wide = None
    for part in split(scores_ref[...].reshape(12 * WIDE, 128)):
        part = dot_nn(part, to_far)
        wide = part if wide is None else wide + part
    wide = jnp.concatenate([wide[h * WIDE : (h + 1) * WIDE] for h in range(12)], axis=1)
    rows = None
    for part in split(wide):
        part = dot_nn(to_row, part)
        rows = part if rows is None else rows + part
    out = []
    for h in range(12):
        one = rows[:, h * 128 : (h + 1) * 128]
        one = jnp.concatenate([one, jnp.zeros_like(one)], axis=1)
        one = pltpu.roll(one, 0, 1, stride=1, stride_axis=0)
        out.append(jnp.sum(one, axis=0, keepdims=True))
    return out


def stack_qkv(pieces, out_ref):
    for k, piece in enumerate(pieces):
        for c in range(3):
            out_ref[c * D + k * 96 : c * D + (k + 1) * 96] = piece[c * 96 : (c + 1) * 96]


def stack_proj(pieces, out_ref):
    for k, piece in enumerate(pieces):
        out_ref[k * 96 : (k + 1) * 96] = piece[288:384]


def stack_mlp(pieces, fc1_ref, fc2_ref):
    for k, piece in enumerate(pieces):
        fc1_ref[:, k * D : (k + 1) * D] = piece[0:D]
        fc2_ref[k * D : (k + 1) * D] = piece[D : 2 * D]


def attn_forward(table, hidden, weights, qv_bias, bias, norms, layer):
    shifted = layer % 2 == 1
    rows = hidden.shape[0]
    bins = rows // PAD
    chunk_slots = 6
    chunk = chunk_slots * PAD
    spare = bins if shifted else 2

    def kernel(
        table_ref, hidden_ref, w0, w1, w2, w3, qv_ref, bias_ref, norm_ref,
        mid_ref, a_ref, qkv_ref, p_ref, attn_ref,
        wqkv, wproj, wide, tmp, moved,
    ):
        pieces = (w0, w1, w2, w3)
        stack_qkv(pieces, wqkv)
        stack_proj(pieces, wproj)
        gain, shift, proj_shift = norm_ref[0:1], norm_ref[1:2], norm_ref[2:3]
        marks = head_marks()
        def norm_step(i, carry):
            at = pl.ds(pl.multiple_of(i * chunk, 16), chunk)
            scaled, _ = norm_rows(hidden_ref[at])
            normed = scaled * gain + shift
            if shifted:
                slots = pl.ds(i * chunk_slots, chunk_slots)
                wide[slots] = normed.reshape(chunk_slots, PAD, D)
            else:
                a_ref[at] = normed.astype(LOW)
            return carry

        lax.fori_loop(0, bins // chunk_slots, norm_step, 0, unroll=True)
        if shifted:
            move_windows(table_ref, wide, tmp, moved, False)
            a_ref[...] = moved[...].reshape(rows, D).astype(LOW)

        def qkv_step(i, carry):
            at = pl.ds(pl.multiple_of(i * chunk, 16), chunk)
            project = dot_nt(a_ref[at], wqkv[...]) + qv_ref[layer, 0:1]
            for j in range(chunk_slots):
                block = project[j * PAD : (j + 1) * PAD]
                at = pl.ds((j % 2) * WIDE, WIDE)
                qkv_ref[i * (chunk_slots // 2) + j // 2, at] = pad_rows(block).astype(LOW)
            return carry

        lax.fori_loop(0, bins // chunk_slots, qkv_step, 0, unroll=True)

        if shifted:
            _, qrow, qcol = place_parts((WIDE, 1), 0)
            lane = lax.broadcasted_iota(jnp.int32, (1, 128), 1)
            second = lane >= WIDE
            pplace = jnp.where(second, lane - WIDE, lane)
            prow = (pplace * 37) >> 8
            pcol = pplace - 7 * prow
            pband = 1 + (prow >= 4).astype(jnp.int32), 1 + (pcol >= 4).astype(jnp.int32)
            qband = 1 + (qrow >= 4).astype(jnp.int32), 1 + (qcol >= 4).astype(jnp.int32)

        def window(j, carry):
            if shifted:
                low = []
                for w in (2 * j, 2 * j + 1):
                    side = table_ref[SIDE + w]
                    low.append(
                        (
                            jnp.where(table_ref[WROW + w] == side - 1, 3, 0),
                            jnp.where(table_ref[WCOL + w] == side - 1, 1, 0),
                        )
                    )
                low_row = jnp.where(second, low[1][0], low[0][0])
                low_col = jnp.where(second, low[1][1], low[0][1])
                pregion = low_row * pband[0] + low_col * pband[1]
                qregion = low_row * qband[0] + low_col * qband[1]
                mask = jnp.where(pregion != qregion, -100.0, 0.0)[None]
            scores, probs = [], []
            for t in range(QUADS):
                q = qkv_ref[j, :, t * 128 : (t + 1) * 128]
                k = qkv_ref[j, :, D + t * 128 : D + (t + 1) * 128]
                scores.append(dot_nt(spread_pair(k, marks), diagonal(q)))
            for t in range(QUADS):
                now = by_head(scores[t] * SCORE_SCALE + bias_ref[layer, t])
                if shifted:
                    now = now + mask
                exponent = jnp.exp(now - jnp.max(now, axis=1, keepdims=True))
                total = jnp.sum(exponent, axis=1, keepdims=True)
                probs.append((exponent * (1.0 / total)).reshape(4 * WIDE, 128).astype(LOW))
                p_ref[j, t] = probs[t]
            for t in range(QUADS):
                cols = slice(t * 128, (t + 1) * 128)
                v = qkv_ref[j, :, 2 * D + t * 128 : 2 * D + (t + 1) * 128]
                both = dot_tn(probs[t], spread_pair(v, marks))
                wide[2 * j, :, cols] = both[0:PAD, 0:128]
                wide[2 * j + 1, :, cols] = both[WIDE : WIDE + PAD, 128:256]
            return carry

        lax.fori_loop(0, bins // 2, window, 0, unroll=9)
        if shifted:
            move_windows(table_ref, wide, tmp, moved, True)
            attn_ref[...] = moved[...].reshape(rows, D).astype(LOW)
        else:
            attn_ref[...] = wide[...].reshape(rows, D).astype(LOW)

        def proj_step(i, carry):
            at = pl.ds(pl.multiple_of(i * chunk, 16), chunk)
            mid_ref[at] = hidden_ref[at] + dot_nn(attn_ref[at], wproj[...]) + proj_shift
            return carry

        lax.fori_loop(0, bins // chunk_slots, proj_step, 0, unroll=True)

    return pl.pallas_call(
        kernel,
        out_shape=(
            jax.ShapeDtypeStruct((rows, D), F32),
            jax.ShapeDtypeStruct((rows, D), LOW),
            jax.ShapeDtypeStruct((bins // 2, 2 * WIDE, 3 * D), LOW),
            jax.ShapeDtypeStruct((bins // 2, QUADS, 4 * WIDE, 128), LOW),
            jax.ShapeDtypeStruct((rows, D), LOW),
        ),
        in_specs=[smem()] + [vmem()] * 8,
        out_specs=[vmem()] * 5,
        scratch_shapes=[
            pltpu.VMEM((3 * D, D), LOW),
            pltpu.VMEM((D, D), LOW),
            pltpu.VMEM((bins, PAD, D), F32),
            pltpu.VMEM((spare, PAD, D), F32),
            pltpu.VMEM((spare, PAD, D), F32),
        ],
        compiler_params=params(14),
        cost_estimate=cost(1e10, 2e7),
        name="attn_forward",
    )(table, hidden, *weights, qv_bias, bias, norms)


def attn_backward(table, grad, qkv, probs, weights, shifted):
    rows = grad.shape[0]
    bins = rows // PAD
    chunk_slots = 6
    chunk = chunk_slots * PAD
    spare = bins if shifted else 2

    def kernel(
        table_ref, grad_ref, qkv_ref, p_ref, w0, w1, w2, w3,
        gqkv_ref, scores_ref, wproj, wide_attn, wide, tmp, moved,
    ):
        stack_proj((w0, w1, w2, w3), wproj)
        marks = head_marks()
        steps = bins // chunk_slots
        def keep_windows(i, block_rows):
            for j in range(chunk_slots):
                block = block_rows[j * PAD : (j + 1) * PAD]
                dest = pl.ds((j % 2) * WIDE, WIDE)
                wide_attn[i * (chunk_slots // 2) + j // 2, dest] = pad_rows(block).astype(LOW)

        def proj_step(i, carry):
            at = pl.ds(pl.multiple_of(i * chunk, 16), chunk)
            gattn = dot_nt(grad_ref[at].astype(LOW), wproj[...])
            if shifted:
                slots = pl.ds(i * chunk_slots, chunk_slots)
                wide[slots] = gattn.reshape(chunk_slots, PAD, D)
            else:
                keep_windows(i, gattn)
            return carry

        lax.fori_loop(0, steps, proj_step, 0, unroll=True)
        if shifted:
            move_windows(table_ref, wide, tmp, moved, False)

            def move_step(i, carry):
                slots = pl.ds(i * chunk_slots, chunk_slots)
                keep_windows(i, moved[slots].reshape(chunk, D))
                return carry

            lax.fori_loop(0, steps, move_step, 0, unroll=True)

        scores_ref[...] = jnp.zeros((QUADS, 4 * WIDE, 128), F32)

        def window(j, carry):
            at = pl.ds(pl.multiple_of(j * 2 * PAD, 16), 2 * PAD)

            def keep(c, t, left, right):
                cols = slice(c * D + t * 128, c * D + (t + 1) * 128)
                gqkv_ref[at, cols] = jnp.concatenate([left, right], axis=0).astype(LOW)

            go, gp, gv, low_ds, gq, gk = [], [], [], [], [], []
            for t in range(QUADS):
                v = qkv_ref[j, :, 2 * D + t * 128 : 2 * D + (t + 1) * 128]
                go.append(diagonal(wide_attn[j, :, t * 128 : (t + 1) * 128]))
                gp.append(dot_nt(spread_pair(v, marks), go[t]))
            for t in range(QUADS):
                gv.append(dot_nn(p_ref[j, t], go[t]))
            for t in range(QUADS):
                p = by_head(p_ref[j, t].astype(F32))
                now = by_head(gp[t])
                ds = p * (now - jnp.sum(now * p, axis=1, keepdims=True))
                low_ds.append(ds.reshape(4 * WIDE, 128).astype(LOW))
                scores_ref[t] += low_ds[t].astype(F32)
            for t in range(QUADS):
                q = qkv_ref[j, :, t * 128 : (t + 1) * 128]
                k = qkv_ref[j, :, D + t * 128 : D + (t + 1) * 128]
                gk.append(dot_nn(low_ds[t], diagonal(q)))
                gq.append(dot_tn(low_ds[t], spread_pair(k, marks)))
            for t in range(QUADS):
                left, right = slice(0, 128), slice(128, 256)
                keep(2, t, fold(gv[t][:, left], marks)[0:PAD], fold(gv[t][:, right], marks)[0:PAD])
            for t in range(QUADS):
                left, right = slice(0, 128), slice(128, 256)
                folded = fold(gk[t][:, left], marks), fold(gk[t][:, right], marks)
                keep(1, t, *[part[0:PAD] * SCORE_SCALE for part in folded])
                parts = gq[t][0:PAD, left], gq[t][WIDE : WIDE + PAD, right]
                keep(0, t, *[part * SCORE_SCALE for part in parts])
            return carry

        lax.fori_loop(0, bins // 2, window, 0, unroll=9)

    return pl.pallas_call(
        kernel,
        out_shape=(
            jax.ShapeDtypeStruct((rows, 3 * D), LOW),
            jax.ShapeDtypeStruct((QUADS, 4 * WIDE, 128), F32),
        ),
        in_specs=[smem()] + [vmem()] * 7,
        out_specs=[vmem()] * 2,
        scratch_shapes=[
            pltpu.VMEM((D, D), LOW),
            pltpu.VMEM((bins // 2, 2 * WIDE, D), LOW),
            pltpu.VMEM((spare, PAD, D), F32),
            pltpu.VMEM((spare, PAD, D), F32),
            pltpu.VMEM((spare, PAD, D), F32),
        ],
        compiler_params=params(13),
        cost_estimate=cost(1e10, 2e7),
        name="attn_backward",
    )(table, grad, qkv, probs, *weights)


def attn_grads(grad, a, attn, gqkv, scores, small_mlp, fc1_bias_grad, weights, norms):
    rows = grad.shape[0]

    def kernel(
        grad_ref, a_ref, attn_ref, gqkv_ref, scores_ref, mlp_ref, fc1b_ref, w0, w1, w2, w3, norm_ref,
        keep_ref, send_ref, wqkv, small,
    ):
        stack_qkv((w0, w1, w2, w3), wqkv)
        gain, shift = norm_ref[0:1], norm_ref[1:2]
        dqkv = dot_tn(a_ref[...], gqkv_ref[...])
        low_grad = grad_ref[...].astype(LOW)
        dproj = dot_tn(attn_ref[...], low_grad).astype(LOW)
        column_sums = jnp.sum(gqkv_ref[...].astype(F32), axis=0, keepdims=True)
        wide_sums = jnp.broadcast_to(column_sums, (16, 3 * D))
        dshift = sum(dot_nn(part, wqkv[...]) for part in split(wide_sums))[0:1]
        table_rows = scores_to_table(scores_ref)
        turned, match = [], jnp.zeros((1, D), F32)
        for c in range(3):
            back = dqkv[:, c * D : (c + 1) * D].T
            here = wqkv[c * D : (c + 1) * D].astype(F32)
            match = match + jnp.sum(back * here, axis=0, keepdims=True)
            turned.append(back.astype(LOW))
        small[...] = jnp.zeros((SMALL, D), F32)
        small[0:1] = (match - shift * dshift) / gain
        small[1:2] = dshift
        small[2:3] = jnp.sum(low_grad.astype(F32), axis=0, keepdims=True)
        small[3:6] = mlp_ref[0:3]
        gq_sum = jnp.broadcast_to(column_sums[:, 0:D], (8, D))
        gv_sum = jnp.broadcast_to(column_sums[:, 2 * D : 3 * D], (8, D))
        for k in range(4):
            dest = keep_ref if k < 2 else send_ref
            for c in range(3):
                dest[k % 2, c * 96 : (c + 1) * 96] = turned[c][k * 96 : (k + 1) * 96]
            dest[k % 2, 288:384] = dproj[k * 96 : (k + 1) * 96]
            small[6:7] = fc1b_ref[:, k * D : (k + 1) * D]
            small[7:8] = pltpu.roll(gq_sum, (D - k * 96) % D, 1)[0:1]
            small[8:9] = pltpu.roll(gv_sum, (D - k * 96) % D, 1)[0:1]
            for h in range(3):
                small[9 + h : 10 + h, 0:256] = table_rows[3 * k + h]
            dest[k % 2, D : D + SMALL] = small[...].astype(LOW)

    return pl.pallas_call(
        kernel,
        out_shape=(
            jax.ShapeDtypeStruct((2, D + SMALL, D), LOW),
            jax.ShapeDtypeStruct((2, D + SMALL, D), LOW),
        ),
        in_specs=[vmem()] * 12,
        out_specs=[vmem()] * 2,
        scratch_shapes=[
            pltpu.VMEM((3 * D, D), LOW),
            pltpu.VMEM((SMALL, D), F32),
        ],
        compiler_params=params(12),
        cost_estimate=cost(6e9, 2e7),
        name="attn_grads",
    )(grad, a, attn, gqkv, scores, small_mlp, fc1_bias_grad, *weights, norms)


def attn_input_grad(table, grad, hidden, gqkv, weights, norms, shifted, work):
    rows = hidden.shape[0]
    bins = rows // PAD
    chunk_slots = 6
    chunk = chunk_slots * PAD
    spare = bins if shifted else 2

    def kernel(
        table_ref, grad_ref, hidden_ref, gqkv_ref, w0, w1, w2, w3, norm_ref,
        out_ref, wqkv, wide, tmp, moved,
    ):
        stack_qkv((w0, w1, w2, w3), wqkv)
        gain = norm_ref[0:1]
        if shifted:
            for i in range(bins // chunk_slots):
                slots = slice(i * chunk_slots, (i + 1) * chunk_slots)
                ga = dot_nn(gqkv_ref[i * chunk : (i + 1) * chunk], wqkv[...])
                wide[slots] = ga.reshape(chunk_slots, PAD, D)
            move_windows(table_ref, wide, tmp, moved, True)

        for i in range(bins // chunk_slots):
            at = slice(i * chunk, (i + 1) * chunk)
            if shifted:
                ga = moved[i * chunk_slots : (i + 1) * chunk_slots].reshape(chunk, D)
            else:
                ga = dot_nn(gqkv_ref[at], wqkv[...])
            scaled, inverse = norm_rows(hidden_ref[at])
            out_ref[at] = grad_ref[at] + norm_back(ga, scaled, inverse, gain)

    return pl.pallas_call(
        kernel,
        out_shape=jax.ShapeDtypeStruct((rows, D), F32),
        in_specs=[smem()] + [vmem()] * 8,
        out_specs=vmem(),
        scratch_shapes=[pltpu.VMEM((3 * D, D), LOW)] + [pltpu.VMEM((spare, PAD, D), F32)] * 3,
        compiler_params=params(12),
        cost_estimate=cost(work, 1e7),
        name="attn_input_grad",
    )(table, grad, hidden, gqkv, *weights, norms)


def mlp_forward(mid, weights, fc1_bias, norms, layer):
    rows = mid.shape[0]
    chunk = 3 * PAD * 2
    steps = rows // chunk

    def kernel(
        mid_ref, w0, w1, w2, w3, fc1_bias_ref, norm_ref,
        out_ref, act_ref, slope_ref, fc1, fc2,
    ):
        stack_mlp((w0, w1, w2, w3), fc1, fc2)
        gain, shift, out_shift = norm_ref[0:1], norm_ref[1:2], norm_ref[2:3]

        def step(i, carry):
            at = pl.ds(pl.multiple_of(i * chunk, 16), chunk)
            rows_now = mid_ref[at]
            scaled, _ = norm_rows(rows_now)
            a = (scaled * gain + shift).astype(LOW)
            act, slope = gelu_parts(dot_nn(a, fc1[...]) + fc1_bias_ref[layer, 0:1])
            act = act.astype(LOW)
            act_ref[at] = act
            slope_ref[at] = slope.astype(LOW)
            out_ref[at] = rows_now + dot_nn(act, fc2[...]) + out_shift
            return carry

        lax.fori_loop(0, steps, step, 0, unroll=True)

    return pl.pallas_call(
        kernel,
        out_shape=(
            jax.ShapeDtypeStruct((rows, D), F32),
            jax.ShapeDtypeStruct((rows, FF), LOW),
            jax.ShapeDtypeStruct((rows, FF), LOW),
        ),
        in_specs=[vmem()] * 7,
        out_specs=[vmem()] * 3,
        scratch_shapes=[pltpu.VMEM((D, FF), LOW), pltpu.VMEM((FF, D), LOW)],
        compiler_params=params(14),
        cost_estimate=cost(7e9, 2e7),
        name="mlp_forward",
    )(mid, *weights, fc1_bias, norms)


def mlp_sums(gpre, a, act, low_grad, fc1, fc1_sums, grad_sums, norms, outs):
    keep_ref, send_ref, small_ref, bias_ref = outs
    gain, shift = norms[0:1], norms[1:2]
    dfc1 = dot_tn(a[...], gpre[...])
    dfc2 = dot_tn(low_grad[...], act[...])
    column = jnp.sum(dfc1 * fc1[...].astype(F32), axis=1, keepdims=True)
    match = jnp.broadcast_to(column, (D, 128)).T
    for k in range(4):
        dest = keep_ref if k < 2 else send_ref
        cols = slice(k * D, (k + 1) * D)
        dest[k % 2, 0:D] = dfc1[:, cols].astype(LOW)
        dest[k % 2, D : 2 * D] = dfc2[:, cols].astype(LOW)
    wide_sums = jnp.broadcast_to(fc1_sums, (16, FF))
    dshift = sum(dot_nt(part, fc1[...]) for part in split(wide_sums))[0:1]
    small_ref[0:1] = (match[0:1] - shift * dshift) / gain
    small_ref[1:2] = dshift
    small_ref[2:3] = grad_sums
    small_ref[3:8] = jnp.zeros((5, D), F32)
    bias_ref[...] = fc1_sums


def sums_shapes():
    return (
        jax.ShapeDtypeStruct((2, 2 * D, D), LOW),
        jax.ShapeDtypeStruct((2, 2 * D, D), LOW),
        jax.ShapeDtypeStruct((8, D), F32),
        jax.ShapeDtypeStruct((1, FF), F32),
    )


def mlp_backward(grad, mid, act, slope, weights, norms):
    rows = mid.shape[0]
    chunk = 6 * PAD
    steps = rows // chunk

    def kernel(
        grad_ref, mid_ref, act_ref, slope_ref, w0, w1, w2, w3, norm_ref,
        gpre_ref, keep_ref, send_ref, small_ref, bias_ref, fc1, fc2, low_grad, a_ref,
    ):
        stack_mlp((w0, w1, w2, w3), fc1, fc2)
        gain, shift = norm_ref[0:1], norm_ref[1:2]
        fc1_sums, grad_sums = jnp.zeros((1, FF), F32), jnp.zeros((1, D), F32)
        for i in range(steps):
            at = slice(i * chunk, (i + 1) * chunk)
            gz = grad_ref[at].astype(LOW)
            low_grad[at] = gz
            gpre = (dot_nt(gz, fc2[...]) * slope_ref[at].astype(F32)).astype(LOW)
            gpre_ref[at] = gpre
            scaled, _ = norm_rows(mid_ref[at])
            a_ref[at] = (scaled * gain + shift).astype(LOW)
            fc1_sums = fc1_sums + jnp.sum(gpre.astype(F32), axis=0, keepdims=True)
            grad_sums = grad_sums + jnp.sum(gz.astype(F32), axis=0, keepdims=True)
        outs = keep_ref, send_ref, small_ref, bias_ref
        mlp_sums(gpre_ref, a_ref, act_ref, low_grad, fc1, fc1_sums, grad_sums, norm_ref, outs)

    return pl.pallas_call(
        kernel,
        out_shape=(jax.ShapeDtypeStruct((rows, FF), LOW), *sums_shapes()),
        in_specs=[vmem()] * 9,
        out_specs=[vmem()] * 5,
        scratch_shapes=[
            pltpu.VMEM((D, FF), LOW),
            pltpu.VMEM((FF, D), LOW),
            pltpu.VMEM((rows, D), LOW),
            pltpu.VMEM((rows, D), LOW),
        ],
        compiler_params=params(18),
        cost_estimate=cost(7e9, 2e7),
        name="mlp_backward",
    )(grad, mid, act, slope, *weights, norms)


def mlp_turn(mid, grad, weights, fc1_bias, norms, layer):
    rows = mid.shape[0]
    chunk = 6 * PAD
    steps = rows // chunk

    def kernel(
        mid_ref, grad_ref, w0, w1, w2, w3, fc1_bias_ref, norm_ref,
        out_ref, gpre_ref, keep_ref, send_ref, small_ref, bias_ref,
        fc1, fc2, a_all, act_all, low_grad,
    ):
        stack_mlp((w0, w1, w2, w3), fc1, fc2)
        gain, shift, out_shift = norm_ref[0:1], norm_ref[1:2], norm_ref[2:3]

        def step(i, totals):
            at = pl.ds(pl.multiple_of(i * chunk, 16), chunk)
            rows_now = mid_ref[at]
            scaled, _ = norm_rows(rows_now)
            a = (scaled * gain + shift).astype(LOW)
            a_all[at] = a
            act, slope = gelu_parts(dot_nn(a, fc1[...]) + fc1_bias_ref[layer, 0:1])
            act = act.astype(LOW)
            act_all[at] = act
            out_ref[at] = rows_now + dot_nn(act, fc2[...]) + out_shift
            gz = grad_ref[at].astype(LOW)
            low_grad[at] = gz
            gpre = (dot_nt(gz, fc2[...]) * slope).astype(LOW)
            gpre_ref[at] = gpre
            return (
                totals[0] + jnp.sum(gz.astype(F32), axis=0, keepdims=True),
                totals[1] + jnp.sum(gpre.astype(F32), axis=0, keepdims=True),
            )

        zeros = jnp.zeros((1, D), F32), jnp.zeros((1, FF), F32)
        grad_sums, fc1_sums = lax.fori_loop(0, steps, step, zeros, unroll=True)
        outs = keep_ref, send_ref, small_ref, bias_ref
        mlp_sums(gpre_ref, a_all, act_all, low_grad, fc1, fc1_sums, grad_sums, norm_ref, outs)

    return pl.pallas_call(
        kernel,
        out_shape=(
            jax.ShapeDtypeStruct((rows, D), F32),
            jax.ShapeDtypeStruct((rows, FF), LOW),
            *sums_shapes(),
        ),
        in_specs=[vmem()] * 8,
        out_specs=[vmem()] * 6,
        scratch_shapes=[
            pltpu.VMEM((D, FF), LOW),
            pltpu.VMEM((FF, D), LOW),
            pltpu.VMEM((rows, D), LOW),
            pltpu.VMEM((rows, FF), LOW),
            pltpu.VMEM((rows, D), LOW),
        ],
        compiler_params=params(22),
        cost_estimate=cost(1.5e10, 4e7),
        name="mlp_turn",
    )(mid, grad, *weights, fc1_bias, norms)


def mlp_input_grad(grad, mid, gpre, weights, norms):
    rows = mid.shape[0]
    chunk = 6 * PAD

    def kernel(grad_ref, mid_ref, gpre_ref, w0, w1, w2, w3, norm_ref, out_ref, fc1):
        for k, piece in enumerate((w0, w1, w2, w3)):
            fc1[:, k * D : (k + 1) * D] = piece[0:D]
        gain = norm_ref[0:1]
        for i in range(rows // chunk):
            at = slice(i * chunk, (i + 1) * chunk)
            ga = dot_nt(gpre_ref[at], fc1[...])
            scaled, inverse = norm_rows(mid_ref[at])
            out_ref[at] = grad_ref[at] + norm_back(ga, scaled, inverse, gain)

    return pl.pallas_call(
        kernel,
        out_shape=jax.ShapeDtypeStruct((rows, D), F32),
        in_specs=[vmem()] * 8,
        out_specs=vmem(),
        scratch_shapes=[pltpu.VMEM((D, FF), LOW)],
        compiler_params=params(8),
        cost_estimate=cost(3e12, 1e7),
        name="mlp_input_grad",
    )(grad, mid, gpre, *weights, norms)


def finish(side, total_a, state_b, state_c, state_d):
    def kernel(
        side_ref, a_ref, b0, b1, c0, c1, d0, d1,
        qkv_ref, proj_ref, fc1_ref, fc2_ref, gains_ref, shifts_ref, fc1b_ref, qv_ref, table_ref,
        rows,
    ):
        first = side_ref[0:1] > 0

        def join(value, other):
            value, other = value[...].astype(F32), other[...].astype(F32)
            return jnp.where(first, value, other), jnp.where(first, other, value)

        half = (D + SMALL) // 2
        rows[0] = d0[...].astype(F32) + d1[...].astype(F32)
        rows[1, 0:half], rows[1, half:] = join(b0, b1)
        fc1_ref[0], fc2 = join(c0, c1)
        fc2_ref[0] = fc2.T
        fc1_ref[1] = a_ref[0:D].astype(F32)
        fc2_ref[1] = a_ref[D : 2 * D].astype(F32).T
        for l in range(LAYERS):
            qkv_ref[l] = rows[l, 0:288]
            proj_ref[l] = rows[l, 288:384]
            now = rows[l, D : D + SMALL]
            for i, row in enumerate((0, 3)):
                gains_ref[l, i : i + 1] = now[row : row + 1]
            for i, row in enumerate((1, 4, 2, 5)):
                shifts_ref[l, i : i + 1] = now[row : row + 1]
            fc1b_ref[l : l + 1] = now[6:7]
            qv_ref[l] = now[7:9, 0:96]
            turned = now[8:16, 0:256].T
            table_ref[l] = turned[0:169, 1:4]

    return pl.pallas_call(
        kernel,
        out_shape=(
            jax.ShapeDtypeStruct((LAYERS, 288, D), F32),
            jax.ShapeDtypeStruct((LAYERS, 96, D), F32),
            jax.ShapeDtypeStruct((LAYERS, D, D), F32),
            jax.ShapeDtypeStruct((LAYERS, D, D), F32),
            jax.ShapeDtypeStruct((LAYERS, 2, D), F32),
            jax.ShapeDtypeStruct((LAYERS, 4, D), F32),
            jax.ShapeDtypeStruct((LAYERS, D), F32),
            jax.ShapeDtypeStruct((LAYERS, 2, 96), F32),
            jax.ShapeDtypeStruct((LAYERS, 169, 3), F32),
        ),
        in_specs=[vmem()] * 8,
        out_specs=[vmem()] * 9,
        scratch_shapes=[pltpu.VMEM((LAYERS, D + SMALL, D), F32)],
        compiler_params=params(14),
        cost_estimate=cost(0, 1e6),
        name="finish",
    )(side, total_a, *state_b, *state_c, *state_d)


def swap_core(value):
    return lax.ppermute(value, "head", [(i, i ^ 1) for i in range(4)])


def swap_chip(value):
    return lax.ppermute(value, "head", [(i, i ^ 2) for i in range(4)])


def swap_border(value):
    return lax.ppermute(value, "head", [(1, 2), (2, 1)])


def swap_dp(value, step, size):
    return lax.ppermute(value, "dp", [(i, i ^ step) for i in range(size)])


def tie(*values):
    return lax.optimization_barrier(values)


def pick(first, one, other):
    first = first > 0
    return jnp.where(first, one, other), jnp.where(first, other, one)


def dp_masks(order):
    size = lax.axis_size("dp")
    upper = [(2 << b) - 2 for b in range(1, size.bit_length() - 1)]
    if order == 1 and upper:
        return [upper[-1]] + upper[:-1] + [1]
    return [1] + (upper if order == 2 else upper[::-1])


def dp_start(parts, sides, order):
    half = parts[0].shape[0] // 2
    low = sum(p[:half].astype(F32) for p in parts)
    high = sum(p[half:].astype(F32) for p in parts)
    masks = dp_masks(order)
    kept, sent = pick(sides[order % 2], low, high)
    return kept, swap_dp(sent.astype(LOW), masks[0], lax.axis_size("dp"))


def dp_next(kept, other, order, stage):
    masks = dp_masks(order)
    value = (kept.astype(F32) + other.astype(F32)).astype(LOW)
    return value, swap_dp(value, (masks + masks[:1])[stage], lax.axis_size("dp"))


def dp_whole(value, other, stage):
    masks = dp_masks(2)
    value = (value.astype(F32) + other.astype(F32)).astype(LOW)
    return value, swap_dp(value, masks[stage], lax.axis_size("dp"))


def dp_join(value, other, sides, order):
    low, high = pick(sides[order % 2], value, other)
    return jnp.concatenate([low, high])


def body(
    tokens, outputs_grad, image_kind, qkv_weight, qv_bias, bias_table, proj_weight,
    fc1_weight, fc1_bias, fc2_weight, gains, shifts,
):
    own = tokens.shape[0] // PLACES
    bins = own + 2
    me = lax.axis_index("head").astype(jnp.int32)

    def border(value):
        edge = 4 * PLACES
        return swap_border(jnp.where(me == 1, value[-edge:], value[:edge]))

    turned = jnp.transpose(qkv_weight, (0, 2, 3, 1)).reshape(LAYERS, 288, D)

    def attn_pack(l):
        return jnp.concatenate([turned[l], proj_weight[l]], axis=0)

    def mlp_pack(l):
        return jnp.concatenate([fc1_weight[l], fc2_weight[l]], axis=0)

    def norm_pack(l, which, bias_row):
        rows = jnp.stack([gains[l, which], shifts[l, which], shifts[l, bias_row]])
        return jnp.pad(rows, ((0, 5), (0, 0)))

    partner = swap_core(tokens)
    rows = jnp.pad(jnp.transpose(bias_table, (0, 2, 1)).reshape(6, 169), ((0, 0), (0, D - 169)))
    small = jnp.concatenate([rows, qv_bias.reshape(1, D), fc1_bias])
    small = jnp.pad(small, ((0, SMALL - 9), (0, 0)))
    own_pack = [jnp.concatenate([attn_pack(0), *split(small)])]
    chip_pack = [swap_chip(own_pack[0])]
    edges, _ = tie(tokens, own_pack[0])
    halo = border(edges)
    place = lax.axis_index("dp")
    top = lax.axis_size("dp") // 2
    sides = [1 - (place & 1), (place < top).astype(jnp.int32)]
    first = jnp.broadcast_to(jnp.stack(sides).astype(jnp.int32)[:, None], (2, D))
    table = make_plan(image_kind, me, own, bins)
    mlp_first = mlp_pack(0)
    table, first, chip_pack[0], partner, mlp_first = tie(
        table, first, chip_pack[0], partner, mlp_first
    )
    sides = [first[0:1], first[1:2]]
    hidden = gather_slots(table, tokens, partner, halo, bins)

    def gathered(i):
        p, c = own_pack[i], chip_pack[i]
        return p, c, swap_core(p), swap_core(c)

    pack, halo, _ = tie(mlp_first, halo, chip_pack[0])
    own_pack.append(pack)
    chip_pack.append(swap_chip(pack))
    first_weights = gathered(0)
    bias, qkv_bias, fc1_all = spread_smalls(first_weights)

    saved, weights = [], []
    last = LAYERS - 1
    for l in range(LAYERS):
        norms, mlp_norms = norm_pack(l, 0, 2), norm_pack(l, 1, 3)
        weights.append(first_weights if l == 0 else gathered(2 * l))
        mid, a, qkv, probs, attn = attn_forward(
            table, hidden, weights[2 * l], qkv_bias, bias, norms, l
        )
        mid, chip_pack[2 * l + 1] = tie(mid, chip_pack[2 * l + 1])
        weights.append(gathered(2 * l + 1))
        if l == last:
            saved.append((hidden, mid, a, qkv, probs, attn, norms, mlp_norms))
            break
        pack, outputs_grad, mid = tie(attn_pack(1), outputs_grad, mid)
        grad_partner, grad_halo = swap_core(outputs_grad), border(outputs_grad)
        own_pack.append(pack)
        chip_pack.append(swap_chip(pack))
        out, act, slope = mlp_forward(mid, weights[2 * l + 1], fc1_all, mlp_norms, l)
        pack, out, chip_pack[2], grad_partner, grad_halo = tie(
            mlp_pack(1), out, chip_pack[2], grad_partner, grad_halo
        )
        own_pack.append(pack)
        chip_pack.append(swap_chip(pack))
        saved.append((hidden, mid, a, qkv, probs, attn, norms, mlp_norms, act, slope))
        hidden = out
    grad = gather_slots(table, outputs_grad, grad_partner, grad_halo, bins)

    def give_back(value):
        slots = value.reshape(bins, PAD, D)
        return slots, swap_core(slots), swap_border(border_slots(table, slots, 0))

    def mlp_back(l, grad):
        return mlp_backward(
            grad, saved[l][1], saved[l][8], saved[l][9], weights[2 * l + 1], saved[l][7]
        )

    def mlp_input(l, grad, gpre):
        return mlp_input_grad(grad, saved[l][1], gpre, weights[2 * l + 1], saved[l][7])

    def attn_back(l, grad):
        return attn_backward(table, grad, saved[l][3], saved[l][4], weights[2 * l], l % 2 == 1)

    def attn_sums(l, grad, gqkv, scores, small_mlp, fc1_bias_grad):
        return attn_grads(
            grad, saved[l][2], saved[l][5], gqkv, scores, small_mlp, fc1_bias_grad,
            weights[2 * l], saved[l][6],
        )

    def attn_input(l, grad, gqkv):
        work = 6e9 if l == last else 3e12
        return attn_input_grad(
            table, grad, saved[l][0], gqkv, weights[2 * l], saved[l][6], l % 2 == 1, work
        )

    def core_sum(keep, other):
        return [(keep[i].astype(F32) + other[i].astype(F32)).astype(LOW) for i in range(2)]

    out, gpre, keep_a, send_a, small_mlp, fc1_bias_grad = mlp_turn(
        saved[last][1], grad, weights[2 * last + 1], fc1_all, saved[last][7], last
    )
    core_a = swap_core(send_a)
    grad = mlp_input(1, grad, gpre)
    grad, core_a = tie(grad, core_a)
    half_a, out_a = core_sum(keep_a, core_a)
    grad, out_a = tie(grad, out_a)
    chip_a = swap_chip(out_a)
    gqkv, scores = attn_back(1, grad)
    grad_after = attn_input(1, grad, gqkv)
    gqkv, _ = tie(gqkv, grad_after)
    keep_b, send_b = attn_sums(1, grad, gqkv, scores, small_mlp, fc1_bias_grad)
    grad, send_b, chip_a = tie(grad_after, send_b, chip_a)
    core_b = swap_core(send_b)
    state_a = dp_start((half_a, chip_a), sides, 2)
    half_b, out_b = core_sum(keep_b, core_b)
    grad, out_b = tie(grad, out_b)
    chip_b = swap_chip(out_b)
    gpre, keep_c, send_c, small_mlp, fc1_bias_grad = mlp_back(0, grad)
    gpre, send_c, state_a, chip_b = tie(gpre, send_c, state_a, chip_b)
    core_c = swap_core(send_c)
    state_a = dp_next(*state_a, 2, 1)
    grad = mlp_input(0, grad, gpre)
    grad, core_c = tie(grad, core_c)
    state_b = dp_start((half_b, chip_b), sides, 2)
    half_c, out_c = core_sum(keep_c, core_c)
    grad, out_c = tie(grad, out_c)
    chip_c = swap_chip(out_c)
    gqkv, scores = attn_back(0, grad)
    gqkv, state_a, state_b = tie(gqkv, state_a, state_b)
    state_a = dp_next(*state_a, 2, 2)
    state_b = dp_next(*state_b, 2, 1)
    keep_d, send_d = attn_sums(0, grad, gqkv, scores, small_mlp, fc1_bias_grad)
    core_d = swap_core(send_d)
    out, chip_c, _ = tie(out, chip_c, send_d)
    state_c = dp_start((half_c, chip_c), sides, 2)
    out_slots = out.reshape(bins, PAD, D)
    out_edge, core_d = tie(border_slots(table, out_slots, 3e12), core_d)
    half_d, out_d = core_sum(keep_d, core_d)
    chip_d = swap_chip(out_d)
    gqkv, out_slots, out_edge, _ = tie(gqkv, out_slots, out_edge, out_d)
    grad = attn_input(0, grad, gqkv)
    output_parts = out_slots, swap_core(out_slots), swap_border(out_edge)
    chip_d, state_a, state_b, state_c = tie(chip_d, state_a, state_b, state_c)
    state_d = dp_whole(half_d, chip_d, 0)
    state_c = dp_next(*state_c, 2, 1)
    state_b = dp_next(*state_b, 2, 2)
    tokens_parts = give_back(grad)
    state_d, state_c, state_b = tie(state_d, state_c, state_b)
    state_d = dp_whole(*state_d, 1)
    state_c = dp_next(*state_c, 2, 2)
    state_a = dp_next(*state_a, 2, 3)
    state_b = dp_next(*state_b, 2, 3)
    output = return_slots(table, *output_parts, own)
    state_d, state_c, state_a, state_b = tie(state_d, state_c, state_a, state_b)
    state_d = dp_whole(*state_d, 2)
    state_c = dp_next(*state_c, 2, 3)
    tokens_grad = return_slots(table, *tokens_parts, own)
    total_a = dp_join(*state_a, sides, 2)
    state_d, state_c, output, tokens_grad = tie(state_d, state_c, output, tokens_grad)
    qkv_out, proj_out, fc1_out, fc2_out, *smalls = finish(
        sides[0], total_a, state_b, state_c, state_d
    )
    gains_out, shifts_out, fc1_bias_out, qv_out, table_out = smalls
    qkv_out = qkv_out.reshape(LAYERS, 3, 96, D).transpose(0, 3, 1, 2)
    return (
        output, tokens_grad, qkv_out, qv_out, table_out, proj_out, fc1_out, fc1_bias_out,
        fc2_out, gains_out, shifts_out,
    )


def solution(mesh):
    rows = P(("dp", "head"), None)
    placed = (
        rows,
        rows,
        P("dp", None),
        P(None, None, None, "head"),
        P(None, None, "head"),
        P(None, None, "head"),
        P(None, "head", None),
        P(None, None, "head"),
        P(None, "head"),
        P(None, "head", None),
        P(),
        P(),
    )
    return jax.shard_map(
        body,
        mesh=mesh,
        in_specs=placed,
        out_specs=(
            rows,
            rows,
            P(None, None, None, "head"),
            P(None, None, "head"),
            P(None, None, "head"),
            P(None, "head", None),
            P(None, None, "head"),
            P(None, "head"),
            P(None, "head", None),
            P(),
            P(),
        ),
        check_vma=False,
    )
```
